32 devices in a mesh: lat: 4 (over y, x), lon: 8 (over z, core).
Axes of the slice: x: 2, y: 2, z: 4, core: 2. Of those that a mesh axis runs over, the one named last changes fastest.
Arguments:
- innovations: float32 [25, 16384], P(None, ('lat', 'lon')), may hold values from -6 to 6
- owners: int32 [16384, 1], P(('lat', 'lon')), may hold values from 0 to 31, as said below
- prof_row: int32 [16384], P(('lat', 'lon')), may hold values from 0 to 254
- prof_col: int32 [16384], P(('lat', 'lon')), may hold values from 0 to 126
- interp_weights: float32 [4, 16384], P(None, ('lat', 'lon')), may hold values from 0.1 to 1
- model_tiles: float32 [25, 1024, 8, 128], P(None, ('lat', 'lon')), may hold values from -6 to 6
- model_ids: int32 [1, 1024], P(None, ('lat', 'lon')), may hold values from 0 to 31, as said below
- face_x: float32 [1024, 1024], P('lat', 'lon'), may hold values from 0.02 to 0.12
- face_y: float32 [1024, 1024], P('lat', 'lon'), may hold values from 0.02 to 0.12
- cross_term: float32 [1024, 1024], P('lat', 'lon'), may hold values from -0.08 to 0.08
- wet_mask: int32 [1024, 1024], P('lat', 'lon'), may hold values 0 or 1
- norm_factor: float32 [25, 1024, 1024], P(None, 'lat', 'lon'), may hold values from 0.4 to 2.5
Outputs:
- smoothed: float32 [25, 1024, 1024], P(None, 'lat', 'lon')
- profile_values: float32 [25, 16384], P(None, ('lat', 'lon'))
The draws below stay inside these ranges and needn't reach their ends.
Inputs may be any that keep to these rules, and one draw needn't show every extreme that they name: `owners`: among the 512 profiles of one device no owner appears more than 32 times; in every draw one owner appears exactly 32 times among every device's profiles. Owners count analysis blocks in lat-major order. `model_ids`: the 32 slots of the model device at lat index i and lon index g form as many equal groups as the lon axis has devices; group j holds tiles of the analysis block at lat index i and lon index j, and every analysis block's 32 tiles appear exactly once over its lat row.
All inputs are finite; a program needn't handle non-finite values. No bound on the sum of `wet_mask` on one device may be relied on, other than what follows from the above.
Results may differ from the reference program's by a relative error of at most 0.00002.
Values sent between devices are 32-bit elements; how exact they have to be, the bound alone decides.
No kernel may reach another device: no remote copies, remote signals or barrier semaphores. Data moves between devices by JAX's collectives and lax.ppermute only.
A program may use at most 128 MiB of HBM per device.

```python
import math
import jax
import jax.numpy as jnp
from jax import lax

LEV = 25
LAT_DEV = 256
LON_DEV = 128
TILES_DEV = 32
TLAT = 8
TLON = 128
STEPS = 10
P_DEV = 512
CAP = 32
PROFILES = 16384
NLAT = 1024
NLON = 1024
MODEL_SLOTS = 1024
N_LAT = 4
N_LON = 8


def draw_owners(key, part):
    count = N_LAT * N_LON
    hottest = jax.random.randint(jax.random.fold_in(key, 1), (), 0, count)

    def block_owners(block):
        block_key = jax.random.fold_in(key, 100 + block)
        others = jax.random.permutation(jax.random.fold_in(block_key, 1), count - 1)
        others = others + (others >= hottest).astype(jnp.int32)
        position = jnp.arange(P_DEV, dtype=jnp.int32)
        picked = others[jnp.maximum(position - CAP, 0) % (count - 1)]
        chosen = jnp.where(position < CAP, hottest, picked)
        shuffle = jax.random.permutation(jax.random.fold_in(block_key, 2), P_DEV)
        return chosen[shuffle]
    blocks = jax.vmap(block_owners)(jnp.arange(count, dtype=jnp.int32))
    return blocks.reshape(count * P_DEV, 1).astype(jnp.int32)


def draw_model_ids(key, part):
    group_size = TILES_DEV // N_LON
    block_keys = jax.random.split(key, N_LAT * N_LON)
    orders = jax.vmap(lambda single_key: jax.random.permutation(single_key, TILES_DEV))(block_keys)
    orders = orders.reshape(N_LAT, N_LON, N_LON, group_size)
    placed = jnp.transpose(orders, (0, 2, 1, 3))
    return placed.reshape(1, -1).astype(jnp.int32)


def touch_ends(result, key, smallest, largest):
    spot = [jax.random.randint(jax.random.fold_in(key, axis), (), 0, length) for axis, length in enumerate(result.shape)]
    main_axis = result.shape.index(max(result.shape))
    neighbour = spot[:main_axis] + [(spot[main_axis] + 1) % result.shape[main_axis]] + spot[main_axis + 1:]
    return result.at[tuple(spot)].set(smallest).at[tuple(neighbour)].set(largest)


def steps_of(own_key, extent, cuts, least, top_value):
    factor_of = 1.0
    for dim, parts in cuts:
        steps = jax.random.uniform(jax.random.fold_in(jax.random.fold_in(own_key, 6), dim), (parts,), jnp.float32, least / len(cuts), top_value / len(cuts))
        factor_of = factor_of * jnp.repeat(jnp.exp(steps), extent[dim] // parts).reshape((-1,) + (1,) * (len(extent) - 1 - dim))
    return factor_of


def bell_draw(stream_key, dims, scale, bound, cuts=(), kind=jnp.bfloat16):
    array = scale * jax.random.normal(stream_key, dims, jnp.float32)
    if cuts:
        array = array * steps_of(stream_key, dims, cuts, -0.22, 0.18)
    return jnp.clip(array, -bound, bound).astype(kind)


def setup_inputs(seed: int = 0) -> dict:
    arg_keys = jax.random.split(jax.random.key(seed), 13)
    return {
        "innovations": bell_draw(arg_keys[0], (LEV, PROFILES), 1.0, 6.0, ((1, 32),), jnp.float32),
        "owners": draw_owners(jax.random.fold_in(arg_keys[12], 71), 0),
        "prof_row": touch_ends(jax.random.randint(arg_keys[2], (PROFILES,), 0, LAT_DEV - 1), jax.random.fold_in(arg_keys[2], 1), 0, (LAT_DEV - 1) - 1).astype(jnp.int32),
        "prof_col": touch_ends(jax.random.randint(arg_keys[3], (PROFILES,), 0, LON_DEV - 1), jax.random.fold_in(arg_keys[3], 1), 0, (LON_DEV - 1) - 1).astype(jnp.int32),
        "interp_weights": jnp.clip(0.1 + 0.9 * jax.random.uniform(arg_keys[4], (4, PROFILES), jnp.float32) ** steps_of(arg_keys[4], (4, PROFILES), ((1, 32),), -0.2, 0.2), 0.1, 1.0),
        "model_tiles": bell_draw(arg_keys[5], (LEV, MODEL_SLOTS, TLAT, TLON), 1.0, 6.0, ((1, 32),), jnp.float32),
        "model_ids": draw_model_ids(jax.random.fold_in(arg_keys[12], 71), 0),
        "face_x": jnp.clip(0.02 + 0.09999999776482582 * jax.random.uniform(arg_keys[7], (NLAT, NLON), jnp.float32) ** steps_of(arg_keys[7], (NLAT, NLON), ((0, 4), (1, 8)), -0.2, 0.2), 0.02, 0.12),
        "face_y": jnp.clip(0.02 + 0.09999999776482582 * jax.random.uniform(arg_keys[8], (NLAT, NLON), jnp.float32) ** steps_of(arg_keys[8], (NLAT, NLON), ((0, 4), (1, 8)), -0.2, 0.2), 0.02, 0.12),
        "cross_term": jnp.clip(jax.random.uniform(arg_keys[9], (NLAT, NLON), jnp.float32, -0.08, 0.08) * steps_of(arg_keys[9], (NLAT, NLON), ((0, 4), (1, 8)), -0.4, 0.0), -0.08, 0.08),
        "wet_mask": touch_ends((jax.random.randint(arg_keys[10], (NLAT, NLON), 0, 10) < 9).astype(jnp.int32), jax.random.fold_in(arg_keys[10], 1), 0, 1),
        "norm_factor": jnp.clip(jnp.exp(math.log(2.5) - 1.8325814 * jax.random.uniform(arg_keys[11], (LEV, NLAT, NLON), jnp.float32) ** steps_of(arg_keys[11], (LEV, NLAT, NLON), ((1, 4), (2, 8)), -0.2, 0.2)), 0.4, 2.5),
    }


def face_weights(stack):
    face_east = stack[0]
    face_north = stack[1]
    twist_field = stack[2]
    wet_cells = stack[3]
    east_face = face_east[1:-1, 1:-1] * wet_cells[1:-1, 1:-1] * wet_cells[1:-1, 2:]
    west_face = face_east[1:-1, :-2] * wet_cells[1:-1, :-2] * wet_cells[1:-1, 1:-1]
    north_face = face_north[1:-1, 1:-1] * wet_cells[1:-1, 1:-1] * wet_cells[2:, 1:-1]
    south_face = face_north[:-2, 1:-1] * wet_cells[:-2, 1:-1] * wet_cells[1:-1, 1:-1]
    twist_face = twist_field[1:-1, 1:-1] * wet_cells[1:-1, 1:-1]
    return (east_face, west_face, north_face, south_face, twist_face)


def widen(plane):
    padding = [(0, 0)] * (plane.ndim - 2) + [(1, 1), (0, 0)]
    padded = jnp.pad(plane, padding)
    return jnp.concatenate([padded[..., -1:], padded, padded[..., :1]], axis=-1)


def advance_level(padded, weights):
    east_face, west_face, north_face, south_face, twist_face = weights
    centre = padded[1:-1, 1:-1]
    return (centre + east_face * (padded[1:-1, 2:] - centre) + west_face * (padded[1:-1, :-2] - centre)
            + north_face * (padded[2:, 1:-1] - centre) + south_face * (padded[:-2, 1:-1] - centre)
            + 0.25 * twist_face * (padded[2:, 2:] - padded[2:, :-2] - padded[:-2, 2:] + padded[:-2, :-2]))


def reference(innovations, owners, prof_row, prof_col, interp_weights, model_tiles, model_ids, face_x, face_y, cross_term, wet_mask, norm_factor):
    lat_total = LAT_DEV * N_LAT
    lon_total = LON_DEV * N_LON
    group_size = TILES_DEV // N_LON
    slot_index = jnp.arange(MODEL_SLOTS, dtype=jnp.int32)
    model_device = slot_index // TILES_DEV
    target_lon = (slot_index % TILES_DEV) // group_size
    row_start = (model_device // N_LON) * LAT_DEV + model_ids[0] * TLAT
    col_start = target_lon * LON_DEV
    row_grid = row_start[:, None, None] + jnp.arange(TLAT, dtype=jnp.int32)[None, :, None]
    col_grid = col_start[:, None, None] + jnp.arange(TLON, dtype=jnp.int32)[None, None, :]
    increment = jnp.zeros((LEV, lat_total, lon_total), jnp.float32).at[:, row_grid, col_grid].set(model_tiles)

    owner_list = owners[:, 0]
    base_row = (owner_list // N_LON) * LAT_DEV + prof_row
    base_col = (owner_list % N_LON) * LON_DEV + prof_col
    base_cell = base_row * lon_total + base_col
    corner_cells = jnp.concatenate([base_cell, base_cell + 1, base_cell + lon_total, base_cell + lon_total + 1])
    spread = jnp.concatenate([innovations * interp_weights[corner][None, :] for corner in range(4)], axis=1)
    observed = jnp.zeros((LEV, lat_total * lon_total), jnp.float32).at[:, corner_cells].add(spread)
    observed = observed.reshape(LEV, lat_total, lon_total)
    field = norm_factor * (observed + increment)

    stacked = jnp.stack([face_x, face_y, cross_term, wet_mask.astype(jnp.float32)])
    weights = face_weights(widen(stacked))

    def smooth_level(plane):
        def one_step(number, values):
            return advance_level(widen(values), weights)
        return lax.fori_loop(0, STEPS, one_step, plane)

    field = lax.map(smooth_level, field)
    smoothed = norm_factor * field
    flat_field = smoothed.reshape(LEV, -1)
    sampled = (interp_weights[0][None, :] * flat_field[:, base_cell]
               + interp_weights[1][None, :] * flat_field[:, base_cell + 1]
               + interp_weights[2][None, :] * flat_field[:, base_cell + lon_total]
               + interp_weights[3][None, :] * flat_field[:, base_cell + lon_total + 1])
    return (smoothed, sampled)
```

```python
import functools
import jax
import jax.numpy as jnp
from jax import lax
from jax.experimental import pallas as pl
from jax.experimental.pallas import tpu as pltpu
from jax.sharding import PartitionSpec as P

STEPS = 10
SUB = 8
LANES = 128
FEATS = 32
PER_ROW = LANES // FEATS
UNROLL = 16
GROUPS = (7, 6, 6, 6)
CHUNKS = (1, 1, 1, 1)
WEIGHT_ROWS = (7, 14, 15, 22)
LOC_ROW = 23
ID_ROW = 30
VMEM_BYTES = 48 * 1024 * 1024


def group_starts():
    starts = []
    total = 0
    for count in GROUPS:
        starts.append(total)
        total += count
    return starts


def params():
    return pltpu.CompilerParams(vmem_limit_bytes=VMEM_BYTES)


def cost(micros):
    return pl.CostEstimate(flops=0, bytes_accessed=int(micros * 3.6e6), transcendentals=0)


def full(shape):
    zeros = (0,) * len(shape)
    return pl.BlockSpec(tuple(shape), lambda *_: zeros)


def iota(shape, dim):
    return lax.broadcasted_iota(jnp.int32, shape, dim)


def split3(values):
    high = values.astype(jnp.bfloat16)
    rest = values - high.astype(jnp.float32)
    middle = rest.astype(jnp.bfloat16)
    low = (rest - middle.astype(jnp.float32)).astype(jnp.bfloat16)
    return high, middle, low


def route_kernel(cap, group, starts, innov, weights, own_row, own_col, prow, pcol, ids, send, slot_out, pay):
    count = innov.shape[1]
    extra = ids.shape[1]
    same = own_col[...] == own_row[...]
    before = iota((count, count), 0) < iota((count, count), 1)
    ones = jnp.where(same & before, 1.0, 0.0)
    rank = jnp.sum(ones, axis=0, keepdims=True).astype(jnp.int32)
    slot = own_row[...] * cap + rank
    slot_out[...] = slot
    number = iota((1, extra), 1)
    id_slot = (number // group) * cap + number % group
    pay[...] = jnp.zeros_like(pay)
    for index, count_in in enumerate(GROUPS):
        pay[index * SUB : index * SUB + count_in, :count] = innov[starts[index] : starts[index] + count_in, :]
    for corner, row in enumerate(WEIGHT_ROWS):
        pay[row : row + 1, :count] = weights[corner : corner + 1, :]
    pay[LOC_ROW : LOC_ROW + 1, :count] = (prow[...] * LANES + pcol[...]).astype(jnp.float32)
    pay[ID_ROW : ID_ROW + 1, count:] = ids[...].astype(jnp.float32)
    slots = jnp.concatenate([slot, id_slot], axis=1)
    values = pay[...]
    part = slots % PER_ROW
    spread = jnp.concatenate([jnp.where(part == k, values, 0.0) for k in range(PER_ROW)], axis=0)
    rows = send.shape[0]
    hot = jnp.where(iota((rows, count + extra), 0) == slots // PER_ROW, 1.0, 0.0).astype(jnp.bfloat16)
    total = None
    for piece in split3(spread):
        term = lax.dot_general(hot, piece, (((1,), (1,)), ((), ())), preferred_element_type=jnp.float32)
        total = term if total is None else total + term
    send[...] = total


def unpack_kernel(starts, recv, slot, out):
    slots = slot[...]
    rows = recv.shape[0]
    hot = jnp.where(iota((rows, slots.shape[1]), 0) == slots // PER_ROW, 1.0, 0.0).astype(jnp.bfloat16)
    total = None
    for piece in split3(recv[...]):
        term = lax.dot_general(piece, hot, (((0,), (0,)), ((), ())), preferred_element_type=jnp.float32)
        total = term if total is None else total + term
    part = slots % PER_ROW
    picked = jnp.zeros((FEATS, slots.shape[1]), jnp.float32)
    for k in range(PER_ROW):
        picked = jnp.where(part == k, total[k * FEATS : (k + 1) * FEATS], picked)
    for index, count_in in enumerate(GROUPS):
        out[starts[index] : starts[index] + count_in, :] = picked[index * SUB : index * SUB + count_in]


def scatter_kernel(recv, obs, low, high, loc_out, turned, loc_v, loc_s, sem):
    rows = recv.shape[0]
    halves = rows // LANES
    for h in range(halves):
        turned[h] = recv[h * LANES : (h + 1) * LANES, :].T
    for k in range(PER_ROW):
        for h in range(halves):
            at = k * FEATS
            cut = slice(h * LANES, (h + 1) * LANES)
            loc_v[k : k + 1, cut] = turned[h, at + LOC_ROW : at + LOC_ROW + 1, :].astype(jnp.int32)
            loc_v[PER_ROW + k : PER_ROW + k + 1, cut] = turned[h, at + ID_ROW : at + ID_ROW + 1, :].astype(jnp.int32)
    loc_out[...] = loc_v[...]
    copy = pltpu.make_async_copy(loc_v, loc_s, sem)
    copy.start()
    lane = iota((rows, LANES), 1)
    for k in range(PER_ROW):
        at = k * FEATS
        col = recv[:, at + LOC_ROW : at + LOC_ROW + 1].astype(jnp.int32) % LANES
        w = [recv[:, at + row : at + row + 1] for row in WEIGHT_ROWS]
        here = lane == col
        after = lane == col + 1
        low[k * rows : (k + 1) * rows, :] = jnp.where(here, w[0], jnp.where(after, w[1], 0.0))
        high[k * rows : (k + 1) * rows, :] = jnp.where(here, w[2], jnp.where(after, w[3], 0.0))

    def clear(i, carry):
        for index in range(len(GROUPS)):
            obs[index, pl.ds(pl.multiple_of(i * 64, 64), 64), :] = jnp.zeros((64, LANES), jnp.float32)
        return carry

    lax.fori_loop(0, obs.shape[1] // 64, clear, 0)
    copy.wait()
    steps = LANES // SUB

    def body(i, carry):
        block_at = i // steps
        turn = i % steps
        h = block_at // PER_ROW
        k = block_at % PER_ROW
        block = turned[h, pl.ds(pl.multiple_of(k * FEATS, FEATS), FEATS), :]
        block = pltpu.roll(block, (LANES - turn * SUB) % LANES, 1)
        for u in range(SUB):
            row = h * LANES + turn * SUB + u
            at = pl.multiple_of((loc_s[k, row] // LANES) * SUB, SUB)
            lo = low[pl.ds(k * rows + row, 1), :]
            hi = high[pl.ds(k * rows + row, 1), :]
            for index in range(len(GROUPS)):
                value = block[index * SUB : (index + 1) * SUB, u : u + 1]
                old0 = obs[index, pl.ds(at, SUB), :]
                old1 = obs[index, pl.ds(at + SUB, SUB), :]
                obs[index, pl.ds(at, SUB), :] = old0 + value * lo
                obs[index, pl.ds(at + SUB, SUB), :] = old1 + value * hi
        return carry

    lax.fori_loop(0, halves * PER_ROW * steps, body, 0)


def pack_edges(field, up, down, east, west):
    edge = up.shape[0]
    total = field.shape[0]
    up[...] = field[total - edge :, :]
    down[...] = field[:edge, :]
    seats = LANES // 16
    span = total // SUB // seats
    lane = iota((SUB, LANES), 1)

    def body(m, carry):
        to_east = jnp.zeros((SUB, LANES), jnp.float32)
        to_west = jnp.zeros((SUB, LANES), jnp.float32)
        for q in range(seats):
            cells = field[pl.ds(pl.multiple_of((q * span + m) * SUB, SUB), SUB), :]
            mine = lane // 16 == q
            to_east = jnp.where(mine, pltpu.roll(cells, (16 * q + 16) % LANES, 1), to_east)
            to_west = jnp.where(mine, pltpu.roll(cells, 16 * q, 1) if q else cells, to_west)
        at = pl.ds(pl.multiple_of(m * SUB, SUB), SUB)
        east[at, :] = to_east
        west[at, :] = to_west
        return carry

    lax.fori_loop(0, span, body, 0)


def field_kernel(offset, levels, n_lon, group, cap, loc, lat, tiles, obs, norm, field, up, down, east, west):
    field[...] = jnp.zeros_like(field)

    def body(s, carry):
        j = s // group
        c = s % group
        slot = (lat[0] * n_lon + j) * cap + c
        t = loc[PER_ROW + slot % PER_ROW, slot // PER_ROW]
        for l in range(levels):
            at = pl.ds(t * (SUB * SUB) + l, SUB, stride=SUB)
            own = pl.ds(pl.multiple_of(t * SUB, SUB), SUB)
            field[at, :] = norm[l, own, :] * (obs[0, at, :] + tiles[j, offset + l, c])
        return carry

    lax.fori_loop(0, n_lon * group, body, 0)
    pack_edges(field, up, down, east, west)


def stack_kernel(face_x, face_y, cross, wet, field, up, down, east, west):
    field[...] = jnp.zeros_like(field)
    sources = (face_x, face_y, cross, wet)

    def body(t, carry):
        own = pl.ds(pl.multiple_of(t * SUB, SUB), SUB)
        for l, source in enumerate(sources):
            at = pl.ds(t * (SUB * SUB) + l, SUB, stride=SUB)
            field[at, :] = source[own, :].astype(jnp.float32)
        return carry

    lax.fori_loop(0, face_x.shape[0] // SUB, body, 0)
    pack_edges(field, up, down, east, west)


def row_at(index):
    return pl.ds(pl.multiple_of(index * SUB, SUB), SUB)


def build_windows(win, field, from_west, from_east, ups, downs):
    depth = STEPS
    rows = field.shape[0] // SUB
    lane = iota((SUB, LANES), 1)
    left = lane < depth
    right = lane >= LANES - depth
    seats = LANES // 16
    span = rows // seats

    def centre(m, carry):
        west = from_west[row_at(m), :]
        east = from_east[row_at(m), :]
        for q in range(seats):
            cells = field[row_at(q * span + m), :]
            at = row_at(q * span + m + depth)
            win[0, at, :] = jnp.where(
                left, pltpu.roll(west, (depth - 16 * q - 16) % LANES, 1), pltpu.roll(cells, depth, 1)
            )
            win[1, at, :] = jnp.where(
                right, pltpu.roll(east, (-depth - 16 * q) % LANES, 1), pltpu.roll(cells, LANES - depth, 1)
            )
        return carry

    lax.fori_loop(0, span, centre, 0)
    for base, parts in ((0, ups), (depth + rows, downs)):
        for m in range(depth):
            cut = slice(m * SUB, (m + 1) * SUB)
            mid, west, east = (part[cut, :] for part in parts)
            at = slice((base + m) * SUB, (base + m + 1) * SUB)
            win[0, at, :] = pltpu.roll(jnp.where(right, west, mid), depth, 1)
            win[1, at, :] = pltpu.roll(jnp.where(left, east, mid), LANES - depth, 1)
    first = (2 * depth + rows) * SUB
    for w in range(2):
        win[w, first:, :] = jnp.zeros((win.shape[1] - first, LANES), jnp.float32)


def coef_kernel(field, from_west, from_east, up0, up1, up2, down0, down1, down2, coef, win):
    build_windows(win, field, from_west, from_east, (up0, up1, up2), (down0, down1, down2))
    rows = coef.shape[1]

    def body(b, carry):
        base = b * (SUB * SUB)
        for w in range(2):
            fx, fy, ct, wet = (win[w, pl.ds(base + s, SUB, stride=SUB), :] for s in range(4))
            wet_n = win[w, pl.ds(base + SUB + 3, SUB, stride=SUB), :]
            x = fx * wet * pltpu.roll(wet, LANES - 1, 1)
            xw = pltpu.roll(x, 1, 1)
            y = fy * wet * wet_n
            twist = 0.25 * ct * wet
            own = pl.ds(pl.multiple_of(b * SUB, SUB), SUB)
            for c, value in enumerate((1.0 - x - xw, x, xw, y, twist)):
                coef[w * 5 + c, own, :] = value
        return carry

    lax.fori_loop(0, rows // SUB, body, 0)


def diffuse(win, coef, rows):
    whole = rows + 2 * STEPS

    def prepared(w, index):
        cells = win[w, row_at(index), :]
        east = pltpu.roll(cells, LANES - 1, 1)
        west = pltpu.roll(cells, 1, 1)
        return cells, east, west, east - west

    def weight(w, c, index):
        return coef[w * 5 + c, pl.ds(index, 1), :]

    def step(t, carry):
        first = t + 1
        blocks = (whole - 2 * first + UNROLL - 1) // UNROLL
        state = []
        for w in range(2):
            before = prepared(w, first - 1)
            now = prepared(w, first)
            flux = weight(w, 3, first - 1) * (now[0] - before[0])
            state.append((now, before[3], flux))

        def block(b, state):
            base = first + b * UNROLL
            state = list(state)
            for u in range(UNROLL):
                for w in range(2):
                    (cells, east, west, slope), slope_s, flux_s = state[w]
                    ahead = prepared(w, base + u + 1)
                    flux = weight(w, 3, base + u) * (ahead[0] - cells)
                    result = (
                        weight(w, 0, base + u) * cells
                        + weight(w, 1, base + u) * east
                        + weight(w, 2, base + u) * west
                        + (flux - flux_s)
                        + weight(w, 4, base + u) * (ahead[3] - slope_s)
                    )
                    win[w, row_at(base + u), :] = result
                    state[w] = (ahead, slope, flux)
            return tuple(state)

        lax.fori_loop(0, blocks, block, tuple(state))
        return carry

    lax.fori_loop(0, STEPS, step, 0)


def smooth_kernel(levels, aliased, *refs):
    (loc, field, from_west, from_east, up0, up1, up2, down0, down1, down2, coef, norm, low, high) = refs[:14]
    out, sampled, win, smooth = refs[14 + aliased :]
    rows = field.shape[0] // SUB
    build_windows(win, field, from_west, from_east, (up0, up1, up2), (down0, down1, down2))
    diffuse(win, coef, rows)
    lane = iota((SUB, LANES), 1)

    def merge(b, carry):
        for u in range(SUB):
            at = row_at(b * SUB + u + STEPS)
            a = pltpu.roll(win[0, at, :], LANES - STEPS, 1)
            z = pltpu.roll(win[1, at, :], STEPS, 1)
            smooth[row_at(b * SUB + u), :] = jnp.where(lane < LANES // 2, a, z)
        own = pl.ds(pl.multiple_of(b * SUB, SUB), SUB)
        for l in range(levels):
            at = pl.ds(b * (SUB * SUB) + l, SUB, stride=SUB)
            value = smooth[at, :] * norm[l, own, :]
            out[l, own, :] = value
            smooth[at, :] = value
        return carry

    lax.fori_loop(0, rows // SUB, merge, 0)
    count = low.shape[0] // PER_ROW
    halves = count // LANES
    turns = LANES // 16

    def samples(i, carry):
        h = i // PER_ROW
        k = i % PER_ROW

        def body(turn, kept):
            for u in range(16):
                row = h * LANES + turn * 16 + u
                at = pl.multiple_of((loc[k, row] // LANES) * SUB, SUB)
                value = (
                    smooth[pl.ds(at, SUB), :] * low[pl.ds(k * count + row, 1), :]
                    + smooth[pl.ds(at + SUB, SUB), :] * high[pl.ds(k * count + row, 1), :]
                )
                kept = jnp.where(lane == turn * 16 + u, jnp.sum(value, axis=1, keepdims=True), kept)
            return kept

        kept = lax.fori_loop(0, turns, body, jnp.zeros((SUB, LANES), jnp.float32))
        sampled[h, pl.ds(pl.multiple_of(k * SUB, SUB), SUB), :] = kept
        return carry

    lax.fori_loop(0, halves * PER_ROW, samples, 0)


def gather_kernel(*refs):
    out = refs[-2]
    turned = refs[-1]
    for h in range(turned.shape[0]):
        for index, part in enumerate(refs[:-2]):
            for k in range(PER_ROW):
                at = k * FEATS + index * SUB
                turned[h, at : at + SUB, :] = part[h, k * SUB : (k + 1) * SUB, :]
        out[h * LANES : (h + 1) * LANES, :] = turned[h].T


def shifted(value, d_lat, d_lon, n_lat, n_lon):
    pairs = []
    for i in range(n_lat):
        for j in range(n_lon):
            if 0 <= i + d_lat < n_lat:
                pairs.append((i * n_lon + j, (i + d_lat) * n_lon + (j + d_lon) % n_lon))
    return lax.ppermute(value, ("lat", "lon"), pairs)


def exchange(edges, n_lat, n_lon):
    up, down, east, west = edges
    send = functools.partial(shifted, n_lat=n_lat, n_lon=n_lon)
    from_west = send(east, 0, 1)
    from_east = send(west, 0, -1)
    ups = [send(up, 1, d) for d in (0, 1, -1)]
    downs = [send(down, -1, d) for d in (0, 1, -1)]
    return [from_west, from_east] + ups + downs


def on_device(
    innovations,
    owners,
    prof_row,
    prof_col,
    interp_weights,
    model_tiles,
    model_ids,
    face_x,
    face_y,
    cross_term,
    wet_mask,
    norm_factor,
):
    n_lat = lax.axis_size("lat")
    n_lon = lax.axis_size("lon")
    devices = n_lat * n_lon
    levels, lat_cells, lon_cells = norm_factor.shape
    tiles = model_tiles.shape[1]
    group = tiles // n_lon
    count = innovations.shape[1]
    cap = 2 * count // devices
    slots = devices * cap
    rows = slots // PER_ROW
    starts = group_starts()
    f32 = jnp.float32
    lat = lax.axis_index("lat").reshape(1)

    moved = []
    first = 0
    for taken in CHUNKS:
        begin = starts[first]
        size = sum(GROUPS[first : first + taken])
        piece = model_tiles[begin : begin + size].reshape(size, n_lon, group, SUB, LANES)
        piece = jnp.transpose(piece, (1, 0, 2, 3, 4))
        piece = lax.all_to_all(piece, "lon", split_axis=0, concat_axis=0, tiled=True)
        for index in range(first, first + taken):
            moved.append((piece, starts[index] - begin))
        first += taken

    send, slot = pl.pallas_call(
        functools.partial(route_kernel, cap, group, starts),
        out_shape=(
            jax.ShapeDtypeStruct((rows, LANES), f32),
            jax.ShapeDtypeStruct((1, count), jnp.int32),
        ),
        scratch_shapes=[pltpu.VMEM((FEATS, count + devices * group), f32)],
        compiler_params=params(),
        cost_estimate=cost(3),
        name="route",
    )(
        innovations,
        interp_weights,
        owners.reshape(1, count),
        owners,
        prof_row.reshape(1, count),
        prof_col.reshape(1, count),
        jnp.tile(model_ids, (1, n_lat)),
    )
    both = ("lat", "lon")
    recv = lax.all_to_all(
        send.reshape(devices, rows // devices, LANES), both, split_axis=0, concat_axis=0, tiled=True
    ).reshape(rows, LANES)

    edge_shapes = (
        jax.ShapeDtypeStruct((lat_cells * SUB, LANES), f32),
        jax.ShapeDtypeStruct((STEPS * SUB, LANES), f32),
        jax.ShapeDtypeStruct((STEPS * SUB, LANES), f32),
        jax.ShapeDtypeStruct((lat_cells * SUB // 8, LANES), f32),
        jax.ShapeDtypeStruct((lat_cells * SUB // 8, LANES), f32),
    )
    window_rows = 296 - 256 + lat_cells
    stacked = pl.pallas_call(
        stack_kernel,
        out_shape=edge_shapes,
        compiler_params=params(),
        cost_estimate=cost(3),
        name="stack",
    )(face_x, face_y, cross_term, wet_mask)
    coef = pl.pallas_call(
        coef_kernel,
        out_shape=jax.ShapeDtypeStruct((10, window_rows, LANES), f32),
        scratch_shapes=[pltpu.VMEM((2, (window_rows + 8) * SUB, LANES), f32)],
        compiler_params=params(),
        cost_estimate=cost(4),
        name="coef",
    )(stacked[0], *exchange(stacked[1:], n_lat, n_lon))

    obs, low, high, loc = pl.pallas_call(
        scatter_kernel,
        out_shape=(
            jax.ShapeDtypeStruct((len(GROUPS), lat_cells * SUB, LANES), f32),
            jax.ShapeDtypeStruct((slots, LANES), f32),
            jax.ShapeDtypeStruct((slots, LANES), f32),
            jax.ShapeDtypeStruct((2 * PER_ROW, rows), jnp.int32),
        ),
        scratch_shapes=[
            pltpu.VMEM((rows // LANES, LANES, LANES), f32),
            pltpu.VMEM((2 * PER_ROW, rows), jnp.int32),
            pltpu.SMEM((2 * PER_ROW, rows), jnp.int32),
            pltpu.SemaphoreType.DMA,
        ],
        compiler_params=params(),
        cost_estimate=cost(15),
        name="scatter",
    )(recv)

    smem = pl.BlockSpec(memory_space=pltpu.SMEM)
    smoothed = None
    sampled = []
    for index, (piece, offset) in enumerate(moved):
        size = GROUPS[index]
        begin = starts[index]
        norm_spec = pl.BlockSpec(
            (pl.Element(size), pl.Element(lat_cells), pl.Element(LANES)), lambda i, begin=begin: (begin, 0, 0)
        )
        field_out = pl.pallas_call(
            functools.partial(field_kernel, offset, size, n_lon, group, cap),
            out_shape=edge_shapes,
            grid=(1,),
            in_specs=[
                smem,
                smem,
                full(piece.shape),
                pl.BlockSpec((1, lat_cells * SUB, LANES), lambda i, index=index: (index, 0, 0)),
                norm_spec,
            ],
            out_specs=[full(shape.shape) for shape in edge_shapes],
            compiler_params=params(),
            cost_estimate=cost(4),
            name="field",
        )(loc, lat, piece, obs, norm_factor)
        halos = exchange(field_out[1:], n_lat, n_lon)
        operands = [loc, field_out[0], *halos, coef, norm_factor, low, high]
        specs = [smem] + [full(value.shape) for value in operands[1:-3]] + [norm_spec, full(low.shape), full(high.shape)]
        aliases = {}
        if smoothed is not None:
            aliases = {len(operands): 0}
            operands.append(smoothed)
            specs.append(pl.BlockSpec(memory_space=pl.ANY))
        smoothed, part = pl.pallas_call(
            functools.partial(smooth_kernel, size, len(aliases)),
            out_shape=(
                jax.ShapeDtypeStruct(norm_factor.shape, f32),
                jax.ShapeDtypeStruct((rows // LANES, PER_ROW * SUB, LANES), f32),
            ),
            grid=(1,),
            in_specs=specs,
            out_specs=[norm_spec, full((rows // LANES, PER_ROW * SUB, LANES))],
            scratch_shapes=[
                pltpu.VMEM((2, window_rows * SUB, LANES), f32),
                pltpu.VMEM((lat_cells * SUB, LANES), f32),
            ],
            input_output_aliases=aliases,
            compiler_params=params(),
            cost_estimate=cost(15),
            name="smooth",
        )(*operands)
        sampled.append(part)

    back = pl.pallas_call(
        gather_kernel,
        out_shape=jax.ShapeDtypeStruct((rows, LANES), f32),
        scratch_shapes=[pltpu.VMEM((rows // LANES, LANES, LANES), f32)],
        compiler_params=params(),
        name="gather",
    )(*sampled)
    returned = lax.all_to_all(
        back.reshape(devices, rows // devices, LANES), both, split_axis=0, concat_axis=0, tiled=True
    ).reshape(rows, LANES)
    profile_values = pl.pallas_call(
        functools.partial(unpack_kernel, starts),
        out_shape=jax.ShapeDtypeStruct((levels, count), f32),
        compiler_params=params(),
        name="unpack",
    )(returned, slot)
    return (smoothed, profile_values)


def solution(mesh):
    in_specs = (
        P(None, ("lat", "lon")),
        P(("lat", "lon"), None),
        P(("lat", "lon")),
        P(("lat", "lon")),
        P(None, ("lat", "lon")),
        P(None, ("lat", "lon"), None, None),
        P(None, ("lat", "lon")),
        P("lat", "lon"),
        P("lat", "lon"),
        P("lat", "lon"),
        P("lat", "lon"),
        P(None, "lat", "lon"),
    )
    out_specs = (P(None, "lat", "lon"), P(None, ("lat", "lon")))
    return jax.shard_map(
        on_device, mesh=mesh, in_specs=in_specs, out_specs=out_specs, check_vma=False
    )
```

```python
import functools
import jax
import jax.numpy as jnp
from jax import lax
from jax.experimental import pallas as pl
from jax.experimental.pallas import tpu as pltpu
from jax.sharding import PartitionSpec as P

STEPS = 10
SUB = 8
LANES = 128
FEATS = 32
PER_ROW = LANES // FEATS
UNROLL = 8
GROUPS = (7, 6, 6, 6)
CHUNKS = (1, 2, 1)
WEIGHT_ROWS = (7, 14, 15, 22)
LOC_ROW = 23
ID_ROW = 30
VMEM_BYTES = 48 * 1024 * 1024


def group_starts():
    starts = []
    total = 0
    for count in GROUPS:
        starts.append(total)
        total += count
    return starts


def params():
    return pltpu.CompilerParams(vmem_limit_bytes=VMEM_BYTES)


def cost(micros):
    return pl.CostEstimate(flops=0, bytes_accessed=int(micros * 3.6e6), transcendentals=0)


def full(shape):
    zeros = (0,) * len(shape)
    return pl.BlockSpec(tuple(shape), lambda *_: zeros)


def iota(shape, dim):
    return lax.broadcasted_iota(jnp.int32, shape, dim)


def split3(values):
    high = values.astype(jnp.bfloat16)
    rest = values - high.astype(jnp.float32)
    middle = rest.astype(jnp.bfloat16)
    low = (rest - middle.astype(jnp.float32)).astype(jnp.bfloat16)
    return high, middle, low


def route_kernel(cap, group, starts, innov, weights, own_row, own_col, prow, pcol, ids, send, slot_out, pay):
    count = innov.shape[1]
    extra = ids.shape[1]
    same = own_col[...] == own_row[...]
    before = iota((count, count), 0) < iota((count, count), 1)
    ones = jnp.where(same & before, 1.0, 0.0)
    rank = jnp.sum(ones, axis=0, keepdims=True).astype(jnp.int32)
    slot = own_row[...] * cap + rank
    slot_out[...] = slot
    number = iota((1, extra), 1)
    id_slot = (number // group) * cap + number % group
    pay[...] = jnp.zeros_like(pay)
    for index, count_in in enumerate(GROUPS):
        pay[index * SUB : index * SUB + count_in, :count] = innov[starts[index] : starts[index] + count_in, :]
    for corner, row in enumerate(WEIGHT_ROWS):
        pay[row : row + 1, :count] = weights[corner : corner + 1, :]
    pay[LOC_ROW : LOC_ROW + 1, :count] = (prow[...] * LANES + pcol[...]).astype(jnp.float32)
    pay[ID_ROW : ID_ROW + 1, count:] = ids[...].astype(jnp.float32)
    slots = jnp.concatenate([slot, id_slot], axis=1)
    values = pay[...]
    part = slots % PER_ROW
    spread = jnp.concatenate([jnp.where(part == k, values, 0.0) for k in range(PER_ROW)], axis=0)
    rows = send.shape[0]
    hot = jnp.where(iota((rows, count + extra), 0) == slots // PER_ROW, 1.0, 0.0).astype(jnp.bfloat16)
    total = None
    for piece in split3(spread):
        term = lax.dot_general(hot, piece, (((1,), (1,)), ((), ())), preferred_element_type=jnp.float32)
        total = term if total is None else total + term
    send[...] = total


def unpack_kernel(starts, recv, slot, out):
    slots = slot[...]
    rows = recv.shape[0]
    hot = jnp.where(iota((rows, slots.shape[1]), 0) == slots // PER_ROW, 1.0, 0.0).astype(jnp.bfloat16)
    total = None
    for piece in split3(recv[...]):
        term = lax.dot_general(piece, hot, (((0,), (0,)), ((), ())), preferred_element_type=jnp.float32)
        total = term if total is None else total + term
    part = slots % PER_ROW
    picked = jnp.zeros((FEATS, slots.shape[1]), jnp.float32)
    for k in range(PER_ROW):
        picked = jnp.where(part == k, total[k * FEATS : (k + 1) * FEATS], picked)
    for index, count_in in enumerate(GROUPS):
        out[starts[index] : starts[index] + count_in, :] = picked[index * SUB : index * SUB + count_in]


def scatter_kernel(recv, obs, low, high, loc_out, turned, loc_v, loc_s, sem):
    rows = recv.shape[0]
    halves = rows // LANES
    for h in range(halves):
        turned[h] = recv[h * LANES : (h + 1) * LANES, :].T
    for k in range(PER_ROW):
        for h in range(halves):
            at = k * FEATS
            cut = slice(h * LANES, (h + 1) * LANES)
            loc_v[k : k + 1, cut] = turned[h, at + LOC_ROW : at + LOC_ROW + 1, :].astype(jnp.int32)
            loc_v[PER_ROW + k : PER_ROW + k + 1, cut] = turned[h, at + ID_ROW : at + ID_ROW + 1, :].astype(jnp.int32)
    loc_out[...] = loc_v[...]
    copy = pltpu.make_async_copy(loc_v, loc_s, sem)
    copy.start()
    lane = iota((rows, LANES), 1)
    for k in range(PER_ROW):
        at = k * FEATS
        col = recv[:, at + LOC_ROW : at + LOC_ROW + 1].astype(jnp.int32) % LANES
        w = [recv[:, at + row : at + row + 1] for row in WEIGHT_ROWS]
        here = lane == col
        after = lane == col + 1
        low[k * rows : (k + 1) * rows, :] = jnp.where(here, w[0], jnp.where(after, w[1], 0.0))
        high[k * rows : (k + 1) * rows, :] = jnp.where(here, w[2], jnp.where(after, w[3], 0.0))

    def clear(i, carry):
        for index in range(len(GROUPS)):
            obs[index, pl.ds(pl.multiple_of(i * 64, 64), 64), :] = jnp.zeros((64, LANES), jnp.float32)
        return carry

    lax.fori_loop(0, obs.shape[1] // 64, clear, 0)
    copy.wait()
    steps = LANES // SUB
    groups = range(len(GROUPS))

    def body(i, carry):
        block_at = i // steps
        turn = i % steps
        h = block_at // PER_ROW
        k = block_at % PER_ROW
        block = turned[h, pl.ds(pl.multiple_of(k * FEATS, FEATS), FEATS), :]
        block = pltpu.roll(block, (LANES - turn * SUB) % LANES, 1)
        first = pl.multiple_of(k * rows + h * LANES + turn * SUB, SUB)
        lows = low[pl.ds(first, SUB), :]
        highs = high[pl.ds(first, SUB), :]
        for u in range(SUB):
            row = h * LANES + turn * SUB + u
            at = pl.multiple_of((loc_s[k, row] // LANES) * SUB, SUB)
            lo = lows[u : u + 1, :]
            hi = highs[u : u + 1, :]
            values = [block[index * SUB : (index + 1) * SUB, u : u + 1] for index in groups]
            old0 = [obs[index, pl.ds(at, SUB), :] for index in groups]
            old1 = [obs[index, pl.ds(at + SUB, SUB), :] for index in groups]
            for index in groups:
                obs[index, pl.ds(at, SUB), :] = old0[index] + values[index] * lo
                obs[index, pl.ds(at + SUB, SUB), :] = old1[index] + values[index] * hi
        return carry

    lax.fori_loop(0, halves * PER_ROW * steps, body, 0)


def row_at(index):
    return pl.ds(pl.multiple_of(index * SUB, SUB), SUB)


def rows_at(index, count):
    return pl.ds(pl.multiple_of(index * SUB, SUB), count * SUB)


def send_rows(field, up, down):
    edge = up.shape[1]
    total = field.shape[1]
    for g in range(field.shape[0]):
        up[g] = field[g, total - edge :, :]
        down[g] = field[g, :edge, :]


def field_kernel(sizes, n_lon, group, cap, loc, lat, tiles, obs, norm, field, up, down):
    field[...] = jnp.zeros_like(field)

    def body(s, carry):
        j = s // group
        c = s % group
        slot = (lat[0] * n_lon + j) * cap + c
        t = loc[PER_ROW + slot % PER_ROW, slot // PER_ROW]
        own = pl.ds(pl.multiple_of(t * SUB, SUB), SUB)
        done = []
        level = 0
        for g, size in enumerate(sizes):
            for l in range(size):
                at = pl.ds(t * (SUB * SUB) + l, SUB, stride=SUB)
                done.append((g, at, norm[level, own, :] * (obs[g, at, :] + tiles[j, level, c])))
                level += 1
        for g, at, value in done:
            field[g, at, :] = value
        return carry

    lax.fori_loop(0, n_lon * group, body, 0)
    send_rows(field, up, down)


def stack_kernel(face_x, face_y, cross, wet, field, up, down):
    field[...] = jnp.zeros_like(field)
    sources = (face_x, face_y, cross, wet)

    def body(t, carry):
        own = pl.ds(pl.multiple_of(t * SUB, SUB), SUB)
        values = [source[own, :].astype(jnp.float32) for source in sources]
        for l, value in enumerate(values):
            field[0, pl.ds(t * (SUB * SUB) + l, SUB, stride=SUB), :] = value
        return carry

    lax.fori_loop(0, face_x.shape[0] // SUB, body, 0)
    send_rows(field, up, down)


SEATS = 8
SEAT = LANES // SEATS


def span_of(rows):
    return (rows + 2 * STEPS + SEATS - 1) // SEATS


def edges_kernel(field, above, below, ext, east, west):
    groups, total, _ = field.shape
    halo = STEPS * SUB
    span = east.shape[1] // SUB
    lane = iota((SUB, LANES), 1)
    for g in range(groups):
        ext[g, :halo, :] = above[g]
        ext[g, halo : halo + total, :] = field[g]
        ext[g, halo + total : 2 * halo + total, :] = below[g]
        ext[g, 2 * halo + total :, :] = jnp.zeros((ext.shape[1] - 2 * halo - total, LANES), jnp.float32)

    def body(m, carry):
        for g in range(groups):
            to_east = None
            to_west = None
            for q in range(SEATS):
                cells = ext[g, row_at(q * span + m), :]
                one = pltpu.roll(cells, (SEAT * q + SEAT) % LANES, 1) if q < SEATS - 1 else cells
                two = pltpu.roll(cells, SEAT * q, 1) if q else cells
                mine = lane // SEAT == q
                to_east = one if q == 0 else jnp.where(mine, one, to_east)
                to_west = two if q == 0 else jnp.where(mine, two, to_west)
            east[g, row_at(m), :] = to_east
            west[g, row_at(m), :] = to_west
        return carry

    lax.fori_loop(0, span, body, 0)


STRIP = 32


def build_strips(win, ext, from_west, from_east):
    groups = ext.shape[0]
    span = from_west.shape[1] // SUB
    lane = iota((SUB, LANES), 1)
    place = lane % (2 * STRIP)
    depth = STEPS

    def body(m, carry):
        rows = []
        west = [from_west[g, row_at(m), :] for g in range(groups)]
        east = [from_east[g, row_at(m), :] for g in range(groups)]
        for q in range(SEATS):
            row = None
            for g in range(groups):
                base = 2 * STRIP * g
                cells = ext[g, row_at(q * span + m), :]
                a = pltpu.roll(west[g], (base + depth - SEAT - SEAT * q) % LANES, 1)
                b = pltpu.roll(cells, (base + depth) % LANES, 1)
                c = pltpu.roll(cells, (base + 2 * STRIP - depth) % LANES, 1)
                d = pltpu.roll(east[g], (base + 2 * STRIP - depth - SEAT * q) % LANES, 1)
                value = jnp.where(
                    place < STRIP,
                    jnp.where(place < depth, a, b),
                    jnp.where(place < 2 * STRIP - depth, c, d),
                )
                row = value if g == 0 else jnp.where(lane < 2 * STRIP, row, value)
            rows.append(row)
        for q in range(SEATS):
            win[row_at(q * span + m), :] = rows[q]
        return carry

    lax.fori_loop(0, span, body, 0)
    first = SEATS * span * SUB
    win[first:, :] = jnp.zeros((win.shape[0] - first, LANES), jnp.float32)


def coef_kernel(ext, from_west, from_east, coef, own, strip):
    total = ext.shape[1]
    own[:total, :] = ext[0]
    own[total:, :] = jnp.zeros((own.shape[0] - total, LANES), jnp.float32)
    build_strips(strip, ext, from_west, from_east)
    lane = iota((SUB, LANES), 1)
    rows = coef.shape[1]

    def body(b, carry):
        base = b * (SUB * SUB)
        at = pl.ds(pl.multiple_of(b * SUB, SUB), SUB)
        done = []
        for win in (own, strip):
            fx, fy, ct, wet = (win[pl.ds(base + s, SUB, stride=SUB), :] for s in range(4))
            wet_n = win[pl.ds(base + SUB + 3, SUB, stride=SUB), :]
            x = fx * wet * pltpu.roll(wet, LANES - 1, 1)
            xw = pltpu.roll(x, 1, 1)
            y = fy * wet * wet_n
            twist = 0.25 * ct * wet
            values = [1.0 - x - xw, x, xw, y, twist]
            if win is strip:
                values = [jnp.where(lane < 2 * STRIP, v, pltpu.roll(v, 2 * STRIP, 1)) for v in values]
            done.extend(values)
        for c, value in enumerate(done):
            coef[c, at, :] = value
        return carry

    lax.fori_loop(0, rows // SUB, body, 0)


def spread_weights(wide, coef, first):
    rows = coef.shape[1]

    def body(b, carry):
        for c in range(5):
            block = coef[first + c, pl.ds(pl.multiple_of(b * SUB, SUB), SUB), :]
            for s in range(SUB):
                wide[c, row_at(b * SUB + s), :] = jnp.broadcast_to(block[s : s + 1, :], (SUB, LANES))
        return carry

    lax.fori_loop(0, rows // SUB, body, 0)


def diffuse(wins, wide, rows):
    whole = rows + 2 * STEPS

    def rolled(cells):
        east = pltpu.roll(cells, LANES - 1, 1)
        west = pltpu.roll(cells, 1, 1)
        return cells, east, west, east - west

    def step(t, carry):
        first = t + 1
        blocks = (whole - 2 * first + UNROLL - 1) // UNROLL
        y_first = wide[3, row_at(first - 1), :]
        state = []
        for get, _ in wins:
            before = rolled(get(first - 1))
            now = rolled(get(first))
            state.append((now, before[3], y_first * (now[0] - before[0])))

        def block(b, state):
            base = first + b * UNROLL
            loaded = [[get(base + u + 1) for u in range(UNROLL)] for get, _ in wins]
            state = list(state)
            results = [[] for _ in wins]
            for u in range(UNROLL):
                weights = [wide[c, row_at(base + u), :] for c in range(5)]
                for w in range(len(wins)):
                    (cells, east, west, slope), slope_s, flux_s = state[w]
                    ahead = rolled(loaded[w][u])
                    flux = weights[3] * (ahead[0] - cells)
                    results[w].append(
                        (weights[0] * cells + weights[1] * east)
                        + (weights[2] * west + (flux - flux_s))
                        + weights[4] * (ahead[3] - slope_s)
                    )
                    state[w] = (ahead, slope, flux)
            for w, (_, put) in enumerate(wins):
                for u in range(UNROLL):
                    put(base + u, results[w][u])
            return tuple(state)

        lax.fori_loop(0, blocks, block, tuple(state))
        return carry

    lax.fori_loop(0, STEPS, step, 0)


def plane(ref, g):
    def get(index):
        return ref[g, row_at(index), :]

    def put(index, value):
        ref[g, row_at(index), :] = value

    return get, put


def own_kernel(ext, coef, mid, win, wide):
    groups, total, _ = ext.shape
    rows = mid.shape[1] // SUB
    halo = STEPS * SUB
    for g in range(groups):
        win[g, :total, :] = ext[g]
        win[g, total:, :] = jnp.zeros((win.shape[1] - total, LANES), jnp.float32)
    spread_weights(wide, coef, 0)
    diffuse([plane(win, g) for g in range(groups)], wide, rows)
    for g in range(groups):
        mid[g] = win[g, halo : halo + rows * SUB, :]


def strip_kernel(sizes, aliased, *refs):
    loc, ext, from_west, from_east, mid, coef, norm, low, high = refs[:9]
    out, sampled, win, wide, smooth = refs[9 + aliased :]
    groups = ext.shape[0]
    rows = mid.shape[1] // SUB
    build_strips(win.at[0], ext, from_west, from_east)
    spread_weights(wide, coef, 5)
    diffuse([plane(win, 0)], wide, rows)
    lane = iota((SUB, LANES), 1)
    depth = STEPS

    def merge(b, carry):
        done = []
        for g in range(groups):
            base = 2 * STRIP * g
            for u in range(SUB):
                strip = win[0, row_at(b * SUB + u + depth), :]
                west = pltpu.roll(strip, (-base - depth) % LANES, 1)
                east = pltpu.roll(strip, (depth - base - 2 * STRIP) % LANES, 1)
                cells = mid[g, row_at(b * SUB + u), :]
                done.append(jnp.where(lane < depth, west, jnp.where(lane >= LANES - depth, east, cells)))
        for g in range(groups):
            for u in range(SUB):
                smooth[g, row_at(b * SUB + u), :] = done[g * SUB + u]
        return carry

    lax.fori_loop(0, rows // SUB, merge, 0)

    def scale(b, carry):
        own = pl.ds(pl.multiple_of(b * SUB, SUB), SUB)
        done = []
        level = 0
        for g, size in enumerate(sizes):
            for l in range(size):
                at = pl.ds(b * (SUB * SUB) + l, SUB, stride=SUB)
                done.append((g, at, level, smooth[g, at, :] * norm[level, own, :]))
                level += 1
        for g, at, level, value in done:
            out[level, own, :] = value
            smooth[g, at, :] = value
        return carry

    lax.fori_loop(0, rows // SUB, scale, 0)
    count = low.shape[0] // PER_ROW
    halves = count // LANES

    def samples(i, carry):
        h = i // PER_ROW
        k = i % PER_ROW

        def body(turn, kept):
            kept = list(kept)
            first = pl.multiple_of(k * count + h * LANES + turn * SUB, SUB)
            lows = low[pl.ds(first, SUB), :]
            highs = high[pl.ds(first, SUB), :]
            for u in range(SUB):
                row = h * LANES + turn * SUB + u
                at = pl.multiple_of((loc[k, row] // LANES) * SUB, SUB)
                for g in range(groups):
                    value = (
                        smooth[g, pl.ds(at, SUB), :] * lows[u : u + 1, :]
                        + smooth[g, pl.ds(at + SUB, SUB), :] * highs[u : u + 1, :]
                    )
                    total = jnp.sum(value, axis=1, keepdims=True)
                    kept[g] = jnp.where(lane == turn * SUB + u, total, kept[g])
            return tuple(kept)

        start = tuple(jnp.zeros((SUB, LANES), jnp.float32) for _ in range(groups))
        kept = lax.fori_loop(0, LANES // SUB, body, start)
        for g in range(groups):
            sampled[h, g, row_at(k), :] = kept[g]
        return carry

    lax.fori_loop(0, halves * PER_ROW, samples, 0)


def gather_kernel(*refs):
    out = refs[-2]
    turned = refs[-1]
    for h in range(turned.shape[0]):
        index = 0
        for part in refs[:-2]:
            for g in range(part.shape[1]):
                for k in range(PER_ROW):
                    at = k * FEATS + index * SUB
                    turned[h, at : at + SUB, :] = part[h, g, k * SUB : (k + 1) * SUB, :]
                index += 1
        out[h * LANES : (h + 1) * LANES, :] = turned[h].T


def exchange_rows(up, down, n_lat):
    pairs = [(i, i + 1) for i in range(n_lat - 1)]
    back = [(i + 1, i) for i in range(n_lat - 1)]
    return lax.ppermute(up, "lat", pairs), lax.ppermute(down, "lat", back)


def exchange_columns(east, west, n_lon):
    pairs = [(i, (i + 1) % n_lon) for i in range(n_lon)]
    back = [((i + 1) % n_lon, i) for i in range(n_lon)]
    return lax.ppermute(east, "lon", pairs), lax.ppermute(west, "lon", back)


def on_device(
    innovations,
    owners,
    prof_row,
    prof_col,
    interp_weights,
    model_tiles,
    model_ids,
    face_x,
    face_y,
    cross_term,
    wet_mask,
    norm_factor,
):
    n_lat = lax.axis_size("lat")
    n_lon = lax.axis_size("lon")
    devices = n_lat * n_lon
    levels, lat_cells, lon_cells = norm_factor.shape
    tiles = model_tiles.shape[1]
    group = tiles // n_lon
    count = innovations.shape[1]
    cap = 2 * count // devices
    slots = devices * cap
    rows = slots // PER_ROW
    starts = group_starts()
    f32 = jnp.float32
    lat = lax.axis_index("lat").reshape(1)
    both = ("lat", "lon")
    span = span_of(lat_cells)
    ext_rows = SEATS * span
    win_rows = ext_rows + 2 * SUB

    def arrays(*shapes):
        return tuple(jax.ShapeDtypeStruct(shape, f32) for shape in shapes)

    def call(kernel, out_shape, micros, name, **kwargs):
        return pl.pallas_call(
            kernel,
            out_shape=out_shape,
            compiler_params=params(),
            cost_estimate=cost(micros),
            name=name,
            **kwargs,
        )

    def after(value, *others):
        return lax.optimization_barrier((value,) + others)[0]

    def tile_exchange(chunk, *others):
        first = sum(CHUNKS[:chunk])
        begin = starts[first]
        size = sum(GROUPS[first : first + CHUNKS[chunk]])
        piece = model_tiles[begin : begin + size].reshape(size, n_lon, group, SUB, LANES)
        piece = jnp.transpose(piece, (1, 0, 2, 3, 4))
        if others:
            piece = after(piece, *others)
        return lax.all_to_all(piece, "lon", split_axis=0, concat_axis=0, tiled=True)

    def halo(field, up, down, groups):
        above, below = exchange_rows(up, down, n_lat)
        ext, east, west = call(
            edges_kernel,
            arrays(
                (groups, ext_rows * SUB, LANES),
                (groups, span * SUB, LANES),
                (groups, span * SUB, LANES),
            ),
            3,
            "edges",
        )(field, above, below)
        return (ext,) + exchange_columns(east, west, n_lon)

    def field_shapes(groups):
        return arrays(
            (groups, lat_cells * SUB, LANES),
            (groups, STEPS * SUB, LANES),
            (groups, STEPS * SUB, LANES),
        )

    piece = tile_exchange(0)

    send, slot = call(
        functools.partial(route_kernel, cap, group, starts),
        (jax.ShapeDtypeStruct((rows, LANES), f32), jax.ShapeDtypeStruct((1, count), jnp.int32)),
        3,
        "route",
        scratch_shapes=[pltpu.VMEM((FEATS, count + devices * group), f32)],
    )(
        innovations,
        interp_weights,
        owners.reshape(1, count),
        owners,
        prof_row.reshape(1, count),
        prof_col.reshape(1, count),
        jnp.tile(model_ids, (1, n_lat)),
    )
    stacked = call(stack_kernel, field_shapes(1), 3, "stack")(face_x, face_y, cross_term, wet_mask)
    coef = call(
        coef_kernel,
        arrays((10, win_rows, LANES))[0],
        5,
        "coef",
        scratch_shapes=[
            pltpu.VMEM(((win_rows + SUB) * SUB, LANES), f32),
            pltpu.VMEM(((win_rows + SUB) * SUB, LANES), f32),
        ],
    )(*halo(*stacked, 1))

    send = after(send.reshape(devices, rows // devices, LANES), piece, coef)
    recv = lax.all_to_all(send, both, split_axis=0, concat_axis=0, tiled=True).reshape(rows, LANES)
    pieces = [piece, tile_exchange(1, recv)]

    obs, low, high, loc = call(
        scatter_kernel,
        arrays((len(GROUPS), lat_cells * SUB, LANES), (slots, LANES), (slots, LANES))
        + (jax.ShapeDtypeStruct((2 * PER_ROW, rows), jnp.int32),),
        15,
        "scatter",
        scratch_shapes=[
            pltpu.VMEM((rows // LANES, LANES, LANES), f32),
            pltpu.VMEM((2 * PER_ROW, rows), jnp.int32),
            pltpu.SMEM((2 * PER_ROW, rows), jnp.int32),
            pltpu.SemaphoreType.DMA,
        ],
    )(recv)

    smem = pl.BlockSpec(memory_space=pltpu.SMEM)
    smoothed = None
    sampled = []
    first = 0
    for chunk, groups in enumerate(CHUNKS):
        sizes = GROUPS[first : first + groups]
        begin = starts[first]
        piece = pieces[chunk]
        norm_spec = pl.BlockSpec(
            (pl.Element(sum(sizes)), pl.Element(lat_cells), pl.Element(LANES)),
            lambda i, begin=begin: (begin, 0, 0),
        )
        obs_spec = pl.BlockSpec(
            (pl.Element(groups), pl.Element(lat_cells * SUB), pl.Element(LANES)),
            lambda i, first=first: (first, 0, 0),
        )
        shapes = field_shapes(groups)
        field = call(
            functools.partial(field_kernel, sizes, n_lon, group, cap),
            shapes,
            4,
            "field",
            grid=(1,),
            in_specs=[smem, smem, full(piece.shape), obs_spec, norm_spec],
            out_specs=[full(shape.shape) for shape in shapes],
        )(loc, lat, piece, obs, norm_factor)
        ext, from_west, from_east = halo(*field, groups)
        mid = call(
            own_kernel,
            arrays((groups, lat_cells * SUB, LANES))[0],
            6 * groups,
            "own",
            grid=(1,),
            in_specs=[full(ext.shape), full(coef.shape)],
            out_specs=full((groups, lat_cells * SUB, LANES)),
            scratch_shapes=[
                pltpu.VMEM((groups, win_rows * SUB, LANES), f32),
                pltpu.VMEM((5, win_rows * SUB, LANES), f32),
            ],
        )(ext, coef)
        operands = [loc, ext, from_west, from_east, mid, coef, norm_factor, low, high]
        specs = [smem] + [full(value.shape) for value in operands[1:6]]
        specs += [norm_spec, full(low.shape), full(high.shape)]
        aliases = {}
        if smoothed is not None:
            aliases = {len(operands): 0}
            operands.append(smoothed)
            specs.append(pl.BlockSpec(memory_space=pl.ANY))
        part_shape = (rows // LANES, groups, PER_ROW * SUB, LANES)
        smoothed, part = call(
            functools.partial(strip_kernel, sizes, len(aliases)),
            arrays(norm_factor.shape, part_shape),
            12,
            "strips",
            grid=(1,),
            in_specs=specs,
            out_specs=[norm_spec, full(part_shape)],
            scratch_shapes=[
                pltpu.VMEM((1, win_rows * SUB, LANES), f32),
                pltpu.VMEM((5, win_rows * SUB, LANES), f32),
                pltpu.VMEM((groups, lat_cells * SUB, LANES), f32),
            ],
            input_output_aliases=aliases,
        )(*operands)
        sampled.append(part)
        first += groups
        if chunk + 2 < len(CHUNKS):
            pieces.append(tile_exchange(chunk + 2, pieces[chunk + 1], part))

    back = call(
        gather_kernel,
        arrays((rows, LANES))[0],
        1,
        "gather",
        scratch_shapes=[pltpu.VMEM((rows // LANES, LANES, LANES), f32)],
    )(*sampled)
    returned = lax.all_to_all(
        back.reshape(devices, rows // devices, LANES), both, split_axis=0, concat_axis=0, tiled=True
    ).reshape(rows, LANES)
    profile_values = call(
        functools.partial(unpack_kernel, starts),
        arrays((levels, count))[0],
        1,
        "unpack",
    )(returned, slot)
    return (smoothed, profile_values)


def solution(mesh):
    in_specs = (
        P(None, ("lat", "lon")),
        P(("lat", "lon"), None),
        P(("lat", "lon")),
        P(("lat", "lon")),
        P(None, ("lat", "lon")),
        P(None, ("lat", "lon"), None, None),
        P(None, ("lat", "lon")),
        P("lat", "lon"),
        P("lat", "lon"),
        P("lat", "lon"),
        P("lat", "lon"),
        P(None, "lat", "lon"),
    )
    out_specs = (P(None, "lat", "lon"), P(None, ("lat", "lon")))
    return jax.shard_map(
        on_device, mesh=mesh, in_specs=in_specs, out_specs=out_specs, check_vma=False
    )
```

```python
import functools
import jax
import jax.numpy as jnp
from jax import lax
from jax.experimental import pallas as pl
from jax.experimental.pallas import tpu as pltpu
from jax.sharding import PartitionSpec as P

STEPS = 10
SUB = 8
LANES = 128
FEATS = 32
PER_ROW = LANES // FEATS
GROUPS = (7, 6, 6, 6)
CHUNKS = (1, 2, 1)
WEIGHT_ROWS = (7, 14, 15, 22)
LOC_ROW = 23
ID_ROW = 30
VMEM_BYTES = 48 * 1024 * 1024


def group_starts():
    starts = []
    total = 0
    for count in GROUPS:
        starts.append(total)
        total += count
    return starts


def params():
    return pltpu.CompilerParams(vmem_limit_bytes=VMEM_BYTES)


def cost(micros):
    return pl.CostEstimate(flops=0, bytes_accessed=int(micros * 3.6e6), transcendentals=0)


def full(shape):
    zeros = (0,) * len(shape)
    return pl.BlockSpec(tuple(shape), lambda *_: zeros)


def iota(shape, dim):
    return lax.broadcasted_iota(jnp.int32, shape, dim)


def split3(values):
    high = values.astype(jnp.bfloat16)
    rest = values - high.astype(jnp.float32)
    middle = rest.astype(jnp.bfloat16)
    low = (rest - middle.astype(jnp.float32)).astype(jnp.bfloat16)
    return high, middle, low


def route_kernel(cap, group, starts, innov, weights, own_row, own_col, prow, pcol, ids, send, slot_out, pay):
    count = innov.shape[1]
    extra = ids.shape[1]
    same = own_col[...] == own_row[...]
    before = iota((count, count), 0) < iota((count, count), 1)
    ones = jnp.where(same & before, 1.0, 0.0)
    rank = jnp.sum(ones, axis=0, keepdims=True).astype(jnp.int32)
    slot = own_row[...] * cap + rank
    slot_out[...] = slot
    number = iota((1, extra), 1)
    id_slot = (number // group) * cap + number % group
    pay[...] = jnp.zeros_like(pay)
    for index, count_in in enumerate(GROUPS):
        pay[index * SUB : index * SUB + count_in, :count] = innov[starts[index] : starts[index] + count_in, :]
    for corner, row in enumerate(WEIGHT_ROWS):
        pay[row : row + 1, :count] = weights[corner : corner + 1, :]
    pay[LOC_ROW : LOC_ROW + 1, :count] = (prow[...] * LANES + pcol[...]).astype(jnp.float32)
    pay[ID_ROW : ID_ROW + 1, count:] = ids[...].astype(jnp.float32)
    slots = jnp.concatenate([slot, id_slot], axis=1)
    values = pay[...]
    part = slots % PER_ROW
    spread = jnp.concatenate([jnp.where(part == k, values, 0.0) for k in range(PER_ROW)], axis=0)
    rows = send.shape[0]
    hot = jnp.where(iota((rows, count + extra), 0) == slots // PER_ROW, 1.0, 0.0).astype(jnp.bfloat16)
    total = None
    for piece in split3(spread):
        term = lax.dot_general(hot, piece, (((1,), (1,)), ((), ())), preferred_element_type=jnp.float32)
        total = term if total is None else total + term
    send[...] = total


def unpack_kernel(starts, recv, slot, out):
    slots = slot[...]
    rows = recv.shape[0]
    hot = jnp.where(iota((rows, slots.shape[1]), 0) == slots // PER_ROW, 1.0, 0.0).astype(jnp.bfloat16)
    total = None
    for piece in split3(recv[...]):
        term = lax.dot_general(piece, hot, (((0,), (0,)), ((), ())), preferred_element_type=jnp.float32)
        total = term if total is None else total + term
    part = slots % PER_ROW
    picked = jnp.zeros((FEATS, slots.shape[1]), jnp.float32)
    for k in range(PER_ROW):
        picked = jnp.where(part == k, total[k * FEATS : (k + 1) * FEATS], picked)
    for index, count_in in enumerate(GROUPS):
        out[starts[index] : starts[index] + count_in, :] = picked[index * SUB : index * SUB + count_in]


def scatter_kernel(recv, obs, low, high, loc_out, turned, loc_v, loc_s, sem):
    rows = recv.shape[0]
    halves = rows // LANES
    for h in range(halves):
        turned[h] = recv[h * LANES : (h + 1) * LANES, :].T
    for k in range(PER_ROW):
        for h in range(halves):
            at = k * FEATS
            cut = slice(h * LANES, (h + 1) * LANES)
            loc_v[k : k + 1, cut] = turned[h, at + LOC_ROW : at + LOC_ROW + 1, :].astype(jnp.int32)
            loc_v[PER_ROW + k : PER_ROW + k + 1, cut] = turned[h, at + ID_ROW : at + ID_ROW + 1, :].astype(jnp.int32)
    loc_out[...] = loc_v[...]
    copy = pltpu.make_async_copy(loc_v, loc_s, sem)
    copy.start()
    lane = iota((rows, LANES), 1)
    for k in range(PER_ROW):
        at = k * FEATS
        col = recv[:, at + LOC_ROW : at + LOC_ROW + 1].astype(jnp.int32) % LANES
        w = [recv[:, at + row : at + row + 1] for row in WEIGHT_ROWS]
        here = lane == col
        after = lane == col + 1
        low[k * rows : (k + 1) * rows, :] = jnp.where(here, w[0], jnp.where(after, w[1], 0.0))
        high[k * rows : (k + 1) * rows, :] = jnp.where(here, w[2], jnp.where(after, w[3], 0.0))

    def clear(i, carry):
        for index in range(len(GROUPS)):
            obs[index, pl.ds(pl.multiple_of(i * 64, 64), 64), :] = jnp.zeros((64, LANES), jnp.float32)
        return carry

    lax.fori_loop(0, obs.shape[1] // 64, clear, 0)
    copy.wait()
    groups = range(len(GROUPS))

    def body(i, carry):
        h = i // PER_ROW
        k = i % PER_ROW
        block = turned[h, pl.ds(pl.multiple_of(k * FEATS, FEATS), FEATS), :]
        for turn in range(LANES // SUB):
            first = pl.multiple_of(k * rows + h * LANES + turn * SUB, SUB)
            lows = low[pl.ds(first, SUB), :]
            highs = high[pl.ds(first, SUB), :]
            for u in range(SUB):
                seat = turn * SUB + u
                at = pl.multiple_of((loc_s[k, h * LANES + seat] // LANES) * SUB, SUB)
                lo = lows[u : u + 1, :]
                hi = highs[u : u + 1, :]
                values = [block[index * SUB : (index + 1) * SUB, seat : seat + 1] for index in groups]
                old0 = [obs[index, pl.ds(at, SUB), :] for index in groups]
                old1 = [obs[index, pl.ds(at + SUB, SUB), :] for index in groups]
                for index in groups:
                    obs[index, pl.ds(at, SUB), :] = old0[index] + values[index] * lo
                    obs[index, pl.ds(at + SUB, SUB), :] = old1[index] + values[index] * hi
        return carry

    lax.fori_loop(0, halves * PER_ROW, body, 0)


def row_at(index):
    return pl.ds(pl.multiple_of(index * SUB, SUB), SUB)


def rows_at(index, count):
    return pl.ds(pl.multiple_of(index * SUB, SUB), count * SUB)


def send_rows(field, up, down):
    edge = up.shape[1]
    total = field.shape[1]
    for g in range(field.shape[0]):
        up[g] = field[g, total - edge :, :]
        down[g] = field[g, :edge, :]


def field_kernel(sizes, n_lon, group, cap, loc, lat, tiles, obs, norm, field, up, down):
    field[...] = jnp.zeros_like(field)

    def body(j, carry):
        done = []
        for c in range(group):
            slot = (lat[0] * n_lon + j) * cap + c
            t = loc[PER_ROW + slot % PER_ROW, slot // PER_ROW]
            own = pl.ds(pl.multiple_of(t * SUB, SUB), SUB)
            level = 0
            for g, size in enumerate(sizes):
                for l in range(size):
                    at = pl.ds(t * (SUB * SUB) + l, SUB, stride=SUB)
                    done.append((g, at, norm[level, own, :] * (obs[g, at, :] + tiles[j, level, c])))
                    level += 1
        for g, at, value in done:
            field[g, at, :] = value
        return carry

    lax.fori_loop(0, n_lon, body, 0)
    send_rows(field, up, down)


def stack_kernel(face_x, face_y, cross, wet, field, up, down):
    field[...] = jnp.zeros_like(field)
    sources = (face_x, face_y, cross, wet)

    def body(i, carry):
        values = []
        for n in range(4):
            t = i * 4 + n
            own = pl.ds(pl.multiple_of(t * SUB, SUB), SUB)
            values += [(t, l, source[own, :].astype(jnp.float32)) for l, source in enumerate(sources)]
        for t, l, value in values:
            field[0, pl.ds(t * (SUB * SUB) + l, SUB, stride=SUB), :] = value
        return carry

    lax.fori_loop(0, face_x.shape[0] // SUB // 4, body, 0)
    send_rows(field, up, down)


SEATS = 8
SEAT = LANES // SEATS


TURNS = 5


def span_of(rows):
    return -(-(rows + 2 * STEPS) // (SEATS * TURNS)) * TURNS


def edges_kernel(field, above, below, ext, east, west):
    groups, total, _ = field.shape
    halo = STEPS * SUB
    span = east.shape[1] // SUB
    lane = iota((SUB, LANES), 1)
    for g in range(groups):
        ext[g, :halo, :] = above[g]
        ext[g, halo : halo + total, :] = field[g]
        ext[g, halo + total : 2 * halo + total, :] = below[g]
        ext[g, 2 * halo + total :, :] = jnp.zeros((ext.shape[1] - 2 * halo - total, LANES), jnp.float32)

    def body(i, carry):
        done = []
        for n in range(TURNS):
            m = i * TURNS + n
            for g in range(groups):
                to_east = None
                to_west = None
                for q in range(SEATS):
                    cells = ext[g, row_at(q * span + m), :]
                    one = pltpu.roll(cells, (SEAT * q + SEAT) % LANES, 1) if q < SEATS - 1 else cells
                    two = pltpu.roll(cells, SEAT * q, 1) if q else cells
                    mine = lane // SEAT == q
                    to_east = one if q == 0 else jnp.where(mine, one, to_east)
                    to_west = two if q == 0 else jnp.where(mine, two, to_west)
                done.append((g, m, to_east, to_west))
        for g, m, to_east, to_west in done:
            east[g, row_at(m), :] = to_east
            west[g, row_at(m), :] = to_west
        return carry

    lax.fori_loop(0, span // TURNS, body, 0)


STRIP = 32


def build_strips(win, ext, from_west, from_east):
    groups = ext.shape[0]
    span = from_west.shape[1] // SUB
    lane = iota((SUB, LANES), 1)
    place = lane % (2 * STRIP)
    depth = STEPS

    def body(i, carry):
        done = []
        for n in range(TURNS):
            m = i * TURNS + n
            west = [from_west[g, row_at(m), :] for g in range(groups)]
            east = [from_east[g, row_at(m), :] for g in range(groups)]
            for q in range(SEATS):
                row = None
                for g in range(groups):
                    base = 2 * STRIP * g
                    cells = ext[g, row_at(q * span + m), :]
                    a = pltpu.roll(west[g], (base + depth - SEAT - SEAT * q) % LANES, 1)
                    b = pltpu.roll(cells, (base + depth) % LANES, 1)
                    c = pltpu.roll(cells, (base + 2 * STRIP - depth) % LANES, 1)
                    d = pltpu.roll(east[g], (base + 2 * STRIP - depth - SEAT * q) % LANES, 1)
                    value = jnp.where(
                        place < STRIP,
                        jnp.where(place < depth, a, b),
                        jnp.where(place < 2 * STRIP - depth, c, d),
                    )
                    row = value if g == 0 else jnp.where(lane < 2 * STRIP, row, value)
                done.append((q, m, row))
        for q, m, row in done:
            win[row_at(q * span + m), :] = row
        return carry

    lax.fori_loop(0, span // TURNS, body, 0)
    first = SEATS * span * SUB
    win[first:, :] = jnp.zeros((win.shape[0] - first, LANES), jnp.float32)


def coef_kernel(ext, from_west, from_east, coef, own, strip):
    total = ext.shape[1]
    own[:total, :] = ext[0]
    own[total:, :] = jnp.zeros((own.shape[0] - total, LANES), jnp.float32)
    build_strips(strip, ext, from_west, from_east)
    lane = iota((SUB, LANES), 1)
    rows = coef.shape[1]

    def body(i, carry):
        done = []
        for n in range(4):
            b = i * 4 + n
            base = b * (SUB * SUB)
            at = pl.ds(pl.multiple_of(b * SUB, SUB), SUB)
            for first, win in ((0, own), (5, strip)):
                fx, fy, ct, wet = (win[pl.ds(base + s, SUB, stride=SUB), :] for s in range(4))
                wet_n = win[pl.ds(base + SUB + 3, SUB, stride=SUB), :]
                if first:
                    fx, fy, ct, wet, wet_n = (
                        jnp.where(lane < 2 * STRIP, v, pltpu.roll(v, 2 * STRIP, 1)) for v in (fx, fy, ct, wet, wet_n)
                    )
                x = fx * wet * pltpu.roll(wet, LANES - 1, 1)
                xw = pltpu.roll(x, 1, 1)
                y = fy * wet * wet_n
                twist = 0.25 * ct * wet
                for c, value in enumerate((1.0 - x - xw, x, xw, y, twist)):
                    done.append((first + c, at, value))
        for c, at, value in done:
            coef[c, at, :] = value
        return carry

    lax.fori_loop(0, rows // (4 * SUB), body, 0)


def spread_weights(wide, coef, first):
    rows = coef.shape[1]

    def body(i, carry):
        for n in range(4):
            b = i * 4 + n
            for c in range(5):
                block = coef[first + c, pl.ds(pl.multiple_of(b * SUB, SUB), SUB), :]
                for s in range(SUB):
                    wide[c, row_at(b * SUB + s), :] = jnp.broadcast_to(block[s : s + 1, :], (SUB, LANES))
        return carry

    lax.fori_loop(0, rows // (4 * SUB), body, 0)


def advance(source, target, planes, wide, rows):
    last = rows + 2 * STEPS + 4
    unroll = last // (2 * planes)
    blocks = last // unroll

    def rolled(w, index):
        cells = source[w, row_at(index), :]
        east = pltpu.roll(cells, LANES - 1, 1)
        west = pltpu.roll(cells, 1, 1)
        return cells, east, west, east - west

    y_first = wide[3, row_at(0), :]
    state = []
    for w in range(planes):
        before = rolled(w, 0)
        now = rolled(w, 1)
        state.append((now, before[3], y_first * (now[0] - before[0])))

    def block(b, state):
        base = 1 + b * unroll
        state = list(state)
        for u in range(unroll):
            weights = [wide[c, row_at(base + u), :] for c in range(5)]
            for w in range(planes):
                (cells, east, west, slope), slope_s, flux_s = state[w]
                ahead = rolled(w, base + u + 1)
                flux = weights[3] * (ahead[0] - cells)
                target[w, row_at(base + u), :] = (
                    (weights[0] * cells + weights[1] * east)
                    + (weights[2] * west + (flux - flux_s))
                    + weights[4] * (ahead[3] - slope_s)
                )
                state[w] = (ahead, slope, flux)
        return tuple(state)

    lax.fori_loop(0, blocks, block, tuple(state))


def diffuse(win, other, planes, wide, rows):
    def two(t, carry):
        advance(win, other, planes, wide, rows)
        advance(other, win, planes, wide, rows)
        return carry

    for w in range(planes):
        other[w, :SUB, :] = jnp.zeros((SUB, LANES), jnp.float32)
        other[w, other.shape[1] - SUB * SUB :, :] = jnp.zeros((SUB * SUB, LANES), jnp.float32)
    lax.fori_loop(0, STEPS // 2, two, 0)


def own_kernel(ext, coef, mid, win, other, wide):
    groups, total, _ = ext.shape
    rows = mid.shape[1] // SUB
    halo = STEPS * SUB
    for g in range(groups):
        win[g, :total, :] = ext[g]
        win[g, total:, :] = jnp.zeros((win.shape[1] - total, LANES), jnp.float32)
    spread_weights(wide, coef, 0)
    diffuse(win, other, groups, wide, rows)
    for g in range(groups):
        mid[g] = win[g, halo : halo + rows * SUB, :]


MERGE = 32


def strip_kernel(sizes, aliased, *refs):
    loc, ext, from_west, from_east, mid, coef, norm, low, high = refs[:9]
    out, sampled, win, other, wide, smooth = refs[9 + aliased :]
    groups = ext.shape[0]
    rows = mid.shape[1] // SUB
    build_strips(win.at[0], ext, from_west, from_east)
    spread_weights(wide, coef, 5)
    diffuse(win, other, 1, wide, rows)
    lane = iota((SUB, LANES), 1)
    depth = STEPS

    def merge(b, carry):
        done = []
        for g in range(groups):
            base = 2 * STRIP * g
            for u in range(MERGE):
                strip = win[0, row_at(b * MERGE + u + depth), :]
                west = pltpu.roll(strip, (-base - depth) % LANES, 1)
                east = pltpu.roll(strip, (depth - base - 2 * STRIP) % LANES, 1)
                cells = mid[g, row_at(b * MERGE + u), :]
                done.append(jnp.where(lane < depth, west, jnp.where(lane >= LANES - depth, east, cells)))
        for g in range(groups):
            for u in range(MERGE):
                smooth[g, row_at(b * MERGE + u), :] = done[g * MERGE + u]
        return carry

    lax.fori_loop(0, rows // MERGE, merge, 0)

    def scale(i, carry):
        done = []
        for n in range(4):
            b = i * 4 + n
            own = pl.ds(pl.multiple_of(b * SUB, SUB), SUB)
            level = 0
            for g, size in enumerate(sizes):
                for l in range(size):
                    at = pl.ds(b * (SUB * SUB) + l, SUB, stride=SUB)
                    done.append((g, at, level, own, smooth[g, at, :] * norm[level, own, :]))
                    level += 1
        for g, at, level, own, value in done:
            out[level, own, :] = value
            smooth[g, at, :] = value
        return carry

    lax.fori_loop(0, rows // (4 * SUB), scale, 0)
    count = low.shape[0] // PER_ROW
    halves = count // LANES

    def samples(i, carry):
        h = i // PER_ROW
        k = i % PER_ROW
        kept = [[jnp.zeros((SUB, LANES), jnp.float32)] * 4 for _ in range(groups)]
        for turn in range(LANES // SUB):
            first = pl.multiple_of(k * count + h * LANES + turn * SUB, SUB)
            lows = low[pl.ds(first, SUB), :]
            highs = high[pl.ds(first, SUB), :]
            for u in range(SUB):
                seat = turn * SUB + u
                at = pl.multiple_of((loc[k, h * LANES + seat] // LANES) * SUB, SUB)
                for g in range(groups):
                    value = (
                        smooth[g, pl.ds(at, SUB), :] * lows[u : u + 1, :]
                        + smooth[g, pl.ds(at + SUB, SUB), :] * highs[u : u + 1, :]
                    )
                    total = jnp.sum(value, axis=1, keepdims=True)
                    kept[g][turn % 4] = jnp.where(lane == seat, total, kept[g][turn % 4])
        for g in range(groups):
            a, b, c, d = kept[g]
            sampled[h, g, row_at(k), :] = (a + b) + (c + d)
        return carry

    lax.fori_loop(0, halves * PER_ROW, samples, 0)


def gather_kernel(*refs):
    out = refs[-2]
    turned = refs[-1]
    for h in range(turned.shape[0]):
        index = 0
        for part in refs[:-2]:
            for g in range(part.shape[1]):
                for k in range(PER_ROW):
                    at = k * FEATS + index * SUB
                    turned[h, at : at + SUB, :] = part[h, g, k * SUB : (k + 1) * SUB, :]
                index += 1
        out[h * LANES : (h + 1) * LANES, :] = turned[h].T


def exchange_rows(up, down, n_lat):
    pairs = [(i, i + 1) for i in range(n_lat - 1)]
    back = [(i + 1, i) for i in range(n_lat - 1)]
    return lax.ppermute(up, "lat", pairs), lax.ppermute(down, "lat", back)


def exchange_columns(east, west, n_lon):
    pairs = [(i, (i + 1) % n_lon) for i in range(n_lon)]
    back = [((i + 1) % n_lon, i) for i in range(n_lon)]
    return lax.ppermute(east, "lon", pairs), lax.ppermute(west, "lon", back)


def on_device(
    innovations,
    owners,
    prof_row,
    prof_col,
    interp_weights,
    model_tiles,
    model_ids,
    face_x,
    face_y,
    cross_term,
    wet_mask,
    norm_factor,
):
    n_lat = lax.axis_size("lat")
    n_lon = lax.axis_size("lon")
    devices = n_lat * n_lon
    levels, lat_cells, lon_cells = norm_factor.shape
    tiles = model_tiles.shape[1]
    group = tiles // n_lon
    count = innovations.shape[1]
    cap = 2 * count // devices
    slots = devices * cap
    rows = slots // PER_ROW
    starts = group_starts()
    f32 = jnp.float32
    lat = lax.axis_index("lat").reshape(1)
    both = ("lat", "lon")
    span = span_of(lat_cells)
    ext_rows = SEATS * span
    win_rows = ext_rows + SUB

    def arrays(*shapes):
        return tuple(jax.ShapeDtypeStruct(shape, f32) for shape in shapes)

    def call(kernel, out_shape, micros, name, **kwargs):
        return pl.pallas_call(
            kernel,
            out_shape=out_shape,
            compiler_params=params(),
            cost_estimate=cost(micros),
            name=name,
            **kwargs,
        )

    def after(value, *others):
        return lax.optimization_barrier((value,) + others)[0]

    def tile_exchange(chunk, *others):
        first = sum(CHUNKS[:chunk])
        begin = starts[first]
        size = sum(GROUPS[first : first + CHUNKS[chunk]])
        piece = model_tiles[begin : begin + size].reshape(size, n_lon, group, SUB, LANES)
        piece = jnp.transpose(piece, (1, 0, 2, 3, 4))
        if others:
            piece = after(piece, *others)
        return lax.all_to_all(piece, "lon", split_axis=0, concat_axis=0, tiled=True)

    def halo(field, up, down, groups):
        above, below = exchange_rows(up, down, n_lat)
        ext, east, west = call(
            edges_kernel,
            arrays(
                (groups, ext_rows * SUB, LANES),
                (groups, span * SUB, LANES),
                (groups, span * SUB, LANES),
            ),
            3,
            "edges",
        )(field, above, below)
        return (ext,) + exchange_columns(east, west, n_lon)

    def field_shapes(groups):
        return arrays(
            (groups, lat_cells * SUB, LANES),
            (groups, STEPS * SUB, LANES),
            (groups, STEPS * SUB, LANES),
        )

    piece = tile_exchange(0)

    send, slot = call(
        functools.partial(route_kernel, cap, group, starts),
        (jax.ShapeDtypeStruct((rows, LANES), f32), jax.ShapeDtypeStruct((1, count), jnp.int32)),
        3,
        "route",
        scratch_shapes=[pltpu.VMEM((FEATS, count + devices * group), f32)],
    )(
        innovations,
        interp_weights,
        owners.reshape(1, count),
        owners,
        prof_row.reshape(1, count),
        prof_col.reshape(1, count),
        jnp.tile(model_ids, (1, n_lat)),
    )
    stacked = call(stack_kernel, field_shapes(1), 3, "stack")(face_x, face_y, cross_term, wet_mask)
    coef = call(
        coef_kernel,
        arrays((10, win_rows, LANES))[0],
        5,
        "coef",
        scratch_shapes=[
            pltpu.VMEM(((win_rows + SUB) * SUB, LANES), f32),
            pltpu.VMEM(((win_rows + SUB) * SUB, LANES), f32),
        ],
    )(*halo(*stacked, 1))

    send = after(send.reshape(devices, rows // devices, LANES), piece, coef)
    recv = lax.all_to_all(send, both, split_axis=0, concat_axis=0, tiled=True).reshape(rows, LANES)
    pieces = [piece, tile_exchange(1, recv)]

    obs, low, high, loc = call(
        scatter_kernel,
        arrays((len(GROUPS), lat_cells * SUB, LANES), (slots, LANES), (slots, LANES))
        + (jax.ShapeDtypeStruct((2 * PER_ROW, rows), jnp.int32),),
        15,
        "scatter",
        scratch_shapes=[
            pltpu.VMEM((rows // LANES, LANES, LANES), f32),
            pltpu.VMEM((2 * PER_ROW, rows), jnp.int32),
            pltpu.SMEM((2 * PER_ROW, rows), jnp.int32),
            pltpu.SemaphoreType.DMA,
        ],
    )(recv)

    smem = pl.BlockSpec(memory_space=pltpu.SMEM)
    smoothed = None
    sampled = []
    first = 0
    for chunk, groups in enumerate(CHUNKS):
        sizes = GROUPS[first : first + groups]
        begin = starts[first]
        piece = pieces[chunk]
        norm_spec = pl.BlockSpec(
            (pl.Element(sum(sizes)), pl.Element(lat_cells), pl.Element(LANES)),
            lambda i, begin=begin: (begin, 0, 0),
        )
        obs_spec = pl.BlockSpec(
            (pl.Element(groups), pl.Element(lat_cells * SUB), pl.Element(LANES)),
            lambda i, first=first: (first, 0, 0),
        )
        shapes = field_shapes(groups)
        field = call(
            functools.partial(field_kernel, sizes, n_lon, group, cap),
            shapes,
            4,
            "field",
            grid=(1,),
            in_specs=[smem, smem, full(piece.shape), obs_spec, norm_spec],
            out_specs=[full(shape.shape) for shape in shapes],
        )(loc, lat, piece, obs, norm_factor)
        ext, from_west, from_east = halo(*field, groups)
        mid = call(
            own_kernel,
            arrays((groups, lat_cells * SUB, LANES))[0],
            6 * groups,
            "own",
            grid=(1,),
            in_specs=[full(ext.shape), full(coef.shape)],
            out_specs=full((groups, lat_cells * SUB, LANES)),
            scratch_shapes=[
                pltpu.VMEM((groups, win_rows * SUB, LANES), f32),
                pltpu.VMEM((groups, win_rows * SUB, LANES), f32),
                pltpu.VMEM((5, win_rows * SUB, LANES), f32),
            ],
        )(ext, coef)
        operands = [loc, ext, from_west, from_east, mid, coef, norm_factor, low, high]
        specs = [smem] + [full(value.shape) for value in operands[1:6]]
        specs += [norm_spec, full(low.shape), full(high.shape)]
        aliases = {}
        if smoothed is not None:
            aliases = {len(operands): 0}
            operands.append(smoothed)
            specs.append(pl.BlockSpec(memory_space=pl.ANY))
        part_shape = (rows // LANES, groups, PER_ROW * SUB, LANES)
        smoothed, part = call(
            functools.partial(strip_kernel, sizes, len(aliases)),
            arrays(norm_factor.shape, part_shape),
            12,
            "strips",
            grid=(1,),
            in_specs=specs,
            out_specs=[norm_spec, full(part_shape)],
            scratch_shapes=[
                pltpu.VMEM((1, win_rows * SUB, LANES), f32),
                pltpu.VMEM((1, win_rows * SUB, LANES), f32),
                pltpu.VMEM((5, win_rows * SUB, LANES), f32),
                pltpu.VMEM((groups, lat_cells * SUB, LANES), f32),
            ],
            input_output_aliases=aliases,
        )(*operands)
        sampled.append(part)
        first += groups
        if chunk + 2 < len(CHUNKS):
            pieces.append(tile_exchange(chunk + 2, pieces[chunk + 1], part))

    back = call(
        gather_kernel,
        arrays((rows, LANES))[0],
        1,
        "gather",
        scratch_shapes=[pltpu.VMEM((rows // LANES, LANES, LANES), f32)],
    )(*sampled)
    returned = lax.all_to_all(
        back.reshape(devices, rows // devices, LANES), both, split_axis=0, concat_axis=0, tiled=True
    ).reshape(rows, LANES)
    profile_values = call(
        functools.partial(unpack_kernel, starts),
        arrays((levels, count))[0],
        1,
        "unpack",
    )(returned, slot)
    return (smoothed, profile_values)


def solution(mesh):
    in_specs = (
        P(None, ("lat", "lon")),
        P(("lat", "lon"), None),
        P(("lat", "lon")),
        P(("lat", "lon")),
        P(None, ("lat", "lon")),
        P(None, ("lat", "lon"), None, None),
        P(None, ("lat", "lon")),
        P("lat", "lon"),
        P("lat", "lon"),
        P("lat", "lon"),
        P("lat", "lon"),
        P(None, "lat", "lon"),
    )
    out_specs = (P(None, "lat", "lon"), P(None, ("lat", "lon")))
    return jax.shard_map(
        on_device, mesh=mesh, in_specs=in_specs, out_specs=out_specs, check_vma=False
    )
```

```python
import functools
import jax
import jax.numpy as jnp
from jax import lax
from jax.experimental import pallas as pl
from jax.experimental.pallas import tpu as pltpu
from jax.sharding import PartitionSpec as P

STEPS = 10
SUB = 8
LANES = 128
FEATS = 32
PER_ROW = LANES // FEATS
GROUPS = (6, 6, 7, 6)
CHUNKS = (2, 2)
WEIGHT_ROWS = (6, 7, 14, 15)
LOC_ROW = 23
ID_ROW = 30
VMEM_BYTES = 60 * 1024 * 1024


def group_starts():
    starts = []
    total = 0
    for count in GROUPS:
        starts.append(total)
        total += count
    return starts


def params():
    return pltpu.CompilerParams(vmem_limit_bytes=VMEM_BYTES)


def cost(micros):
    return pl.CostEstimate(flops=0, bytes_accessed=int(micros * 3.6e6), transcendentals=0)


def full(shape):
    zeros = (0,) * len(shape)
    return pl.BlockSpec(tuple(shape), lambda *_: zeros)


def iota(shape, dim):
    return lax.broadcasted_iota(jnp.int32, shape, dim)


def split3(values):
    high = values.astype(jnp.bfloat16)
    rest = values - high.astype(jnp.float32)
    middle = rest.astype(jnp.bfloat16)
    low = (rest - middle.astype(jnp.float32)).astype(jnp.bfloat16)
    return high, middle, low


def route_kernel(cap, group, starts, innov, weights, own_row, own_col, prow, pcol, ids, send, slot_out, pay):
    count = innov.shape[1]
    extra = ids.shape[1]
    same = own_col[...] == own_row[...]
    before = iota((count, count), 0) < iota((count, count), 1)
    ones = jnp.where(same & before, 1.0, 0.0)
    rank = jnp.sum(ones, axis=0, keepdims=True).astype(jnp.int32)
    slot = own_row[...] * cap + rank
    slot_out[...] = slot
    number = iota((1, extra), 1)
    id_slot = (number // group) * cap + number % group
    pay[...] = jnp.zeros_like(pay)
    for index, count_in in enumerate(GROUPS):
        pay[index * SUB : index * SUB + count_in, :count] = innov[starts[index] : starts[index] + count_in, :]
    for corner, row in enumerate(WEIGHT_ROWS):
        pay[row : row + 1, :count] = weights[corner : corner + 1, :]
    pay[LOC_ROW : LOC_ROW + 1, :count] = (prow[...] * LANES + pcol[...]).astype(jnp.float32)
    pay[ID_ROW : ID_ROW + 1, count:] = ids[...].astype(jnp.float32)
    slots = jnp.concatenate([slot, id_slot], axis=1)
    values = pay[...]
    part = slots % PER_ROW
    spread = jnp.concatenate([jnp.where(part == k, values, 0.0) for k in range(PER_ROW)], axis=0)
    rows = send.shape[0]
    hot = jnp.where(iota((rows, count + extra), 0) == slots // PER_ROW, 1.0, 0.0).astype(jnp.bfloat16)
    total = None
    for piece in split3(spread):
        term = lax.dot_general(hot, piece, (((1,), (1,)), ((), ())), preferred_element_type=jnp.float32)
        total = term if total is None else total + term
    send[...] = total


def unpack_kernel(starts, recv, slot, out):
    slots = slot[...]
    rows = recv.shape[0]
    hot = jnp.where(iota((rows, slots.shape[1]), 0) == slots // PER_ROW, 1.0, 0.0).astype(jnp.bfloat16)
    total = None
    for piece in split3(recv[...]):
        term = lax.dot_general(piece, hot, (((0,), (0,)), ((), ())), preferred_element_type=jnp.float32)
        total = term if total is None else total + term
    part = slots % PER_ROW
    picked = jnp.zeros((FEATS, slots.shape[1]), jnp.float32)
    for k in range(PER_ROW):
        picked = jnp.where(part == k, total[k * FEATS : (k + 1) * FEATS], picked)
    for index, count_in in enumerate(GROUPS):
        out[starts[index] : starts[index] + count_in, :] = picked[index * SUB : index * SUB + count_in]


def scatter_kernel(recv, obs, low, high, loc_out, turned, loc_v, loc_s, sem):
    rows = recv.shape[0]
    halves = rows // LANES
    for h in range(halves):
        turned[h] = recv[h * LANES : (h + 1) * LANES, :].T
    for k in range(PER_ROW):
        for h in range(halves):
            at = k * FEATS
            cut = slice(h * LANES, (h + 1) * LANES)
            cells = turned[h, at + LOC_ROW : at + LOC_ROW + 1, :].astype(jnp.int32)
            loc_v[k : k + 1, cut] = cells // LANES * SUB
            loc_v[PER_ROW + k : PER_ROW + k + 1, cut] = turned[h, at + ID_ROW : at + ID_ROW + 1, :].astype(jnp.int32)
    loc_out[...] = loc_v[...]
    copy = pltpu.make_async_copy(loc_v, loc_s, sem)
    copy.start()
    lane = iota((rows, LANES), 1)
    for k in range(PER_ROW):
        at = k * FEATS
        col = recv[:, at + LOC_ROW : at + LOC_ROW + 1].astype(jnp.int32) % LANES
        w = [recv[:, at + row : at + row + 1] for row in WEIGHT_ROWS]
        here = lane == col
        after = lane == col + 1
        low[k * rows : (k + 1) * rows, :] = jnp.where(here, w[0], jnp.where(after, w[1], 0.0))
        high[k * rows : (k + 1) * rows, :] = jnp.where(here, w[2], jnp.where(after, w[3], 0.0))

    def clear(i, carry):
        for index in range(len(GROUPS)):
            obs[index, pl.ds(pl.multiple_of(i * 64, 64), 64), :] = jnp.zeros((64, LANES), jnp.float32)
        return carry

    lax.fori_loop(0, obs.shape[1] // 64, clear, 0)
    copy.wait()
    groups = range(len(GROUPS))

    def body(i, carry):
        h = i // PER_ROW
        k = i % PER_ROW
        block = turned[h, pl.ds(pl.multiple_of(k * FEATS, FEATS), FEATS), :]
        for seat in range(LANES):
            at = pl.multiple_of(loc_s[k, h * LANES + seat], SUB)
            lo = low[pl.ds(k * rows + h * LANES + seat, 1), :]
            hi = high[pl.ds(k * rows + h * LANES + seat, 1), :]
            values = [block[index * SUB : (index + 1) * SUB, seat : seat + 1] for index in groups]
            old0 = [obs[index, pl.ds(at, SUB), :] for index in groups]
            old1 = [obs[index, pl.ds(at + SUB, SUB), :] for index in groups]
            for index in groups:
                obs[index, pl.ds(at, SUB), :] = old0[index] + values[index] * lo
                obs[index, pl.ds(at + SUB, SUB), :] = old1[index] + values[index] * hi
        return carry

    lax.fori_loop(0, halves * PER_ROW, body, 0)


def row_at(index):
    return pl.ds(pl.multiple_of(index * SUB, SUB), SUB)


def rows_at(index, count):
    return pl.ds(pl.multiple_of(index * SUB, SUB), count * SUB)


def send_rows(field, up, down):
    edge = up.shape[1]
    total = field.shape[1]
    for g in range(field.shape[0]):
        up[g] = field[g, total - edge :, :]
        down[g] = field[g, :edge, :]


def field_kernel(sizes, n_lon, group, cap, loc, lat, tiles, obs, norm, field, up, down):
    field[...] = jnp.zeros_like(field)

    def body(j, carry):
        done = []
        for c in range(group):
            slot = (lat[0] * n_lon + j) * cap + c
            t = loc[PER_ROW + slot % PER_ROW, slot // PER_ROW]
            own = pl.ds(pl.multiple_of(t * SUB, SUB), SUB)
            level = 0
            for g, size in enumerate(sizes):
                for l in range(size):
                    at = pl.ds(t * (SUB * SUB) + l, SUB, stride=SUB)
                    done.append((g, at, norm[level, own, :] * (obs[g, at, :] + tiles[j, level, c])))
                    level += 1
        for g, at, value in done:
            field[g, at, :] = value
        return carry

    lax.fori_loop(0, n_lon, body, 0)
    send_rows(field, up, down)


def stack_kernel(face_x, face_y, cross, wet, field, up, down):
    field[...] = jnp.zeros_like(field)
    sources = (face_x, face_y, cross, wet)

    def body(i, carry):
        values = []
        for n in range(4):
            t = i * 4 + n
            own = pl.ds(pl.multiple_of(t * SUB, SUB), SUB)
            values += [(t, l, source[own, :].astype(jnp.float32)) for l, source in enumerate(sources)]
        for t, l, value in values:
            field[0, pl.ds(t * (SUB * SUB) + l, SUB, stride=SUB), :] = value
        return carry

    lax.fori_loop(0, face_x.shape[0] // SUB // 4, body, 0)
    send_rows(field, up, down)


STRIP = 32
HALF = 2 * STRIP
SEAT = 16
SEATS = HALF // SEAT
TURNS = 10


def span_of(rows):
    return -(-(rows + 2 * STEPS) // (SEATS * TURNS)) * TURNS


def edges_kernel(field, above, below, ext, strips, east, west):
    groups, total, _ = field.shape
    halo = STEPS * SUB
    span = east.shape[0] // SUB
    lane = iota((SUB, LANES), 1)
    place = lane % HALF
    for g in range(groups):
        ext[g, :halo, :] = above[g]
        ext[g, halo : halo + total, :] = field[g]
        ext[g, halo + total : 2 * halo + total, :] = below[g]
        ext[g, 2 * halo + total :, :] = jnp.zeros((ext.shape[1] - 2 * halo - total, LANES), jnp.float32)

    def body(i, carry):
        done = []
        for n in range(TURNS // 2):
            m = i * (TURNS // 2) + n
            to_east = None
            to_west = None
            for q in range(SEATS):
                first = ext[0, row_at(q * span + m), :]
                second = pltpu.roll(ext[groups - 1, row_at(q * span + m), :], HALF, 1)
                left = jnp.where(lane < HALF, first, second)
                right = jnp.where(lane < HALF, second, first)
                row = jnp.where(place < STRIP, pltpu.roll(left, STEPS, 1), pltpu.roll(right, HALF - STEPS, 1))
                done.append((strips, q * span + m, row))
                right = pltpu.roll(right, SEAT * q + SEAT, 1)
                if q:
                    left = pltpu.roll(left, SEAT * q, 1)
                mine = place // SEAT == q
                to_east = right if q == 0 else jnp.where(mine, right, to_east)
                to_west = left if q == 0 else jnp.where(mine, left, to_west)
            done.append((east, m, to_east))
            done.append((west, m, to_west))
        for ref, m, value in done:
            ref[row_at(m), :] = value
        return carry

    lax.fori_loop(0, span // (TURNS // 2), body, 0)


def build_strips(win, strips, from_west, from_east):
    span = from_west.shape[0] // SUB
    place = iota((SUB, LANES), 1) % HALF

    def body(i, carry):
        done = []
        for n in range(TURNS):
            m = i * TURNS + n
            west = from_west[row_at(m), :]
            east = from_east[row_at(m), :]
            for q in range(SEATS):
                a = pltpu.roll(west, (STEPS - SEAT - SEAT * q) % LANES, 1)
                b = pltpu.roll(east, (HALF - STEPS - SEAT * q) % LANES, 1)
                row = strips[row_at(q * span + m), :]
                row = jnp.where(place < STEPS, a, jnp.where(place < HALF - STEPS, row, b))
                done.append((q * span + m, row))
        for m, row in done:
            win[row_at(m), :] = row
        return carry

    lax.fori_loop(0, span // TURNS, body, 0)
    first = SEATS * span * SUB
    win[first:, :] = jnp.zeros((win.shape[0] - first, LANES), jnp.float32)


def coef_kernel(ext, strips, from_west, from_east, coef, own, strip):
    total = ext.shape[1]
    own[:total, :] = ext[0]
    own[total:, :] = jnp.zeros((own.shape[0] - total, LANES), jnp.float32)
    build_strips(strip, strips, from_west, from_east)
    rows = coef.shape[1]

    def body(i, carry):
        done = []
        for n in range(4):
            b = i * 4 + n
            base = b * (SUB * SUB)
            at = pl.ds(pl.multiple_of(b * SUB, SUB), SUB)
            for first, win in ((0, own), (5, strip)):
                fx, fy, ct, wet = (win[pl.ds(base + s, SUB, stride=SUB), :] for s in range(4))
                wet_n = win[pl.ds(base + SUB + 3, SUB, stride=SUB), :]
                x = fx * wet * pltpu.roll(wet, LANES - 1, 1)
                xw = pltpu.roll(x, 1, 1)
                y = fy * wet * wet_n
                twist = 0.25 * ct * wet
                for c, value in enumerate((1.0 - x - xw, x, xw, y, twist)):
                    done.append((first + c, at, value))
        for c, at, value in done:
            coef[c, at, :] = value
        return carry

    lax.fori_loop(0, rows // (4 * SUB), body, 0)


def advance(source, target, planes, weight, rows):
    last = rows + 2 * STEPS + 4
    unroll = last // (2 * planes)
    blocks = last // unroll

    def rolled(w, index):
        cells = source[w, row_at(index), :]
        east = pltpu.roll(cells, LANES - 1, 1)
        west = pltpu.roll(cells, 1, 1)
        return cells, east, west, east - west

    y_first = weight(3, 0)
    state = []
    for w in range(planes):
        before = rolled(w, 0)
        now = rolled(w, 1)
        state.append((now, before[3], y_first * (now[0] - before[0])))

    def block(b, state):
        base = 1 + b * unroll
        state = list(state)
        for u in range(unroll):
            weights = [weight(c, base + u) for c in range(5)]
            for w in range(planes):
                (cells, east, west, slope), slope_s, flux_s = state[w]
                ahead = rolled(w, base + u + 1)
                flux = weights[3] * (ahead[0] - cells)
                target[w, row_at(base + u), :] = (
                    (weights[0] * cells + weights[1] * east)
                    + (weights[2] * west + (flux - flux_s))
                    + weights[4] * (ahead[3] - slope_s)
                )
                state[w] = (ahead, slope, flux)
        return tuple(state)

    lax.fori_loop(0, blocks, block, tuple(state))


def diffuse(win, other, planes, coef, first, rows):
    def weight(c, index):
        return coef[first + c, pl.ds(index, 1), :]

    def two(t, carry):
        advance(win, other, planes, weight, rows)
        advance(other, win, planes, weight, rows)
        return carry

    for w in range(planes):
        other[w, :SUB, :] = jnp.zeros((SUB, LANES), jnp.float32)
        other[w, other.shape[1] - SUB * SUB :, :] = jnp.zeros((SUB * SUB, LANES), jnp.float32)
    lax.fori_loop(0, STEPS // 2, two, 0)


def own_kernel(ext, coef, mid, win, other):
    groups, total, _ = ext.shape
    rows = mid.shape[1] // SUB
    halo = STEPS * SUB
    for g in range(groups):
        win[g, :total, :] = ext[g]
        win[g, total:, :] = jnp.zeros((win.shape[1] - total, LANES), jnp.float32)
    diffuse(win, other, groups, coef, 0, rows)
    for g in range(groups):
        mid[g] = win[g, halo : halo + rows * SUB, :]


MERGE = 32


def strip_kernel(sizes, begin, aliased, *refs):
    loc, strips, from_west, from_east, coef, mid_h, norm_h, low_h, high_h = refs[:9]
    out_h, sampled, win, other, smooth, norm, low, high, out, sems = refs[9 + aliased :]
    groups = mid_h.shape[0]
    rows = mid_h.shape[1] // SUB
    levels = pl.ds(begin, sum(sizes))
    pairs = ((mid_h, smooth), (norm_h.at[levels], norm), (low_h, low), (high_h, high))
    copies = [pltpu.make_async_copy(src, dst, sems.at[i]) for i, (src, dst) in enumerate(pairs)]
    for copy in copies:
        copy.start()
    build_strips(win.at[0], strips, from_west, from_east)
    diffuse(win, other, 1, coef, 5, rows)
    for copy in copies:
        copy.wait()
    lane = iota((SUB, LANES), 1)
    outer = LANES - STEPS

    def merge(b, carry):
        done = []
        for u in range(MERGE):
            at = row_at(b * MERGE + u)
            strip = win[0, row_at(b * MERGE + u + STEPS), :]
            west = pltpu.roll(strip, outer, 1)
            east = pltpu.roll(strip, HALF + STEPS, 1)
            cells = smooth[0, at, :]
            done.append((0, at, jnp.where(lane < STEPS, west, jnp.where(lane < outer, cells, east))))
            if groups == 2:
                both = pltpu.roll(jnp.where(lane < HALF, east, west), HALF, 1)
                cells = smooth[1, at, :]
                done.append((1, at, jnp.where((lane < STEPS) | (lane >= outer), both, cells)))
        for g, at, value in done:
            smooth[g, at, :] = value
        return carry

    lax.fori_loop(0, rows // MERGE, merge, 0)

    def scale(i, carry):
        done = []
        for n in range(4):
            b = i * 4 + n
            own = pl.ds(pl.multiple_of(b * SUB, SUB), SUB)
            level = 0
            for g, size in enumerate(sizes):
                for l in range(size):
                    at = pl.ds(b * (SUB * SUB) + l, SUB, stride=SUB)
                    done.append((g, at, level, own, smooth[g, at, :] * norm[level, own, :]))
                    level += 1
        for g, at, level, own, value in done:
            out[level, own, :] = value
            smooth[g, at, :] = value
        return carry

    lax.fori_loop(0, rows // (4 * SUB), scale, 0)
    back = pltpu.make_async_copy(out, out_h.at[levels], sems.at[4])
    back.start()
    count = low.shape[0] // PER_ROW
    halves = count // LANES

    def samples(i, carry):
        h = i // PER_ROW
        k = i % PER_ROW
        kept = [[jnp.zeros((SUB, LANES), jnp.float32)] * 4 for _ in range(groups)]
        for seat in range(LANES):
            at = pl.multiple_of(loc[k, h * LANES + seat], SUB)
            lo = low[pl.ds(k * count + h * LANES + seat, 1), :]
            hi = high[pl.ds(k * count + h * LANES + seat, 1), :]
            for g in range(groups):
                value = smooth[g, pl.ds(at, SUB), :] * lo + smooth[g, pl.ds(at + SUB, SUB), :] * hi
                total = jnp.sum(value, axis=1, keepdims=True)
                kept[g][seat % 4] = jnp.where(lane == seat, total, kept[g][seat % 4])
        for g in range(groups):
            a, b, c, d = kept[g]
            sampled[h, g, row_at(k), :] = (a + b) + (c + d)
        return carry

    lax.fori_loop(0, halves * PER_ROW, samples, 0)
    back.wait()


def gather_kernel(*refs):
    out = refs[-2]
    turned = refs[-1]
    for h in range(turned.shape[0]):
        index = 0
        for part in refs[:-2]:
            for g in range(part.shape[1]):
                for k in range(PER_ROW):
                    at = k * FEATS + index * SUB
                    turned[h, at : at + SUB, :] = part[h, g, k * SUB : (k + 1) * SUB, :]
                index += 1
        out[h * LANES : (h + 1) * LANES, :] = turned[h].T


def exchange_rows(up, down, n_lat):
    pairs = [(i, i + 1) for i in range(n_lat - 1)]
    back = [(i + 1, i) for i in range(n_lat - 1)]
    return lax.ppermute(up, "lat", pairs), lax.ppermute(down, "lat", back)


def exchange_columns(east, west, n_lon):
    pairs = [(i, (i + 1) % n_lon) for i in range(n_lon)]
    back = [((i + 1) % n_lon, i) for i in range(n_lon)]
    return lax.ppermute(east, "lon", pairs), lax.ppermute(west, "lon", back)


def on_device(
    innovations,
    owners,
    prof_row,
    prof_col,
    interp_weights,
    model_tiles,
    model_ids,
    face_x,
    face_y,
    cross_term,
    wet_mask,
    norm_factor,
):
    n_lat = lax.axis_size("lat")
    n_lon = lax.axis_size("lon")
    devices = n_lat * n_lon
    levels, lat_cells, lon_cells = norm_factor.shape
    tiles = model_tiles.shape[1]
    group = tiles // n_lon
    count = innovations.shape[1]
    cap = 2 * count // devices
    slots = devices * cap
    rows = slots // PER_ROW
    starts = group_starts()
    f32 = jnp.float32
    lat = lax.axis_index("lat").reshape(1)
    both = ("lat", "lon")
    span = span_of(lat_cells)
    ext_rows = SEATS * span
    win_rows = ext_rows + SUB

    def arrays(*shapes):
        return tuple(jax.ShapeDtypeStruct(shape, f32) for shape in shapes)

    def call(kernel, out_shape, micros, name, **kwargs):
        return pl.pallas_call(
            kernel,
            out_shape=out_shape,
            compiler_params=params(),
            cost_estimate=cost(micros),
            name=name,
            **kwargs,
        )

    def after(value, *others):
        return lax.optimization_barrier((value,) + others)[0]

    def tile_exchange(chunk, *others):
        first = sum(CHUNKS[:chunk])
        begin = starts[first]
        size = sum(GROUPS[first : first + CHUNKS[chunk]])
        piece = model_tiles[begin : begin + size].reshape(size, n_lon, group, SUB, LANES)
        piece = jnp.transpose(piece, (1, 0, 2, 3, 4))
        if others:
            piece = after(piece, *others)
        return lax.all_to_all(piece, "lon", split_axis=0, concat_axis=0, tiled=True)

    def halo(field, up, down, groups):
        above, below = exchange_rows(up, down, n_lat)
        ext, strips, east, west = call(
            edges_kernel,
            arrays(
                (groups, ext_rows * SUB, LANES),
                (ext_rows * SUB, LANES),
                (span * SUB, LANES),
                (span * SUB, LANES),
            ),
            3,
            "edges",
        )(field, above, below)
        return (ext, strips) + exchange_columns(east, west, n_lon)

    def field_shapes(groups):
        return arrays(
            (groups, lat_cells * SUB, LANES),
            (groups, STEPS * SUB, LANES),
            (groups, STEPS * SUB, LANES),
        )

    send, slot = call(
        functools.partial(route_kernel, cap, group, starts),
        (jax.ShapeDtypeStruct((rows, LANES), f32), jax.ShapeDtypeStruct((1, count), jnp.int32)),
        3,
        "route",
        scratch_shapes=[pltpu.VMEM((FEATS, count + devices * group), f32)],
    )(
        innovations,
        interp_weights,
        owners.reshape(1, count),
        owners,
        prof_row.reshape(1, count),
        prof_col.reshape(1, count),
        jnp.tile(model_ids, (1, n_lat)),
    )
    stacked = call(stack_kernel, field_shapes(1), 3, "stack")(face_x, face_y, cross_term, wet_mask)
    coef = call(
        coef_kernel,
        arrays((10, win_rows, LANES))[0],
        5,
        "coef",
        scratch_shapes=[
            pltpu.VMEM(((win_rows + SUB) * SUB, LANES), f32),
            pltpu.VMEM(((win_rows + SUB) * SUB, LANES), f32),
        ],
    )(*halo(*stacked, 1))

    recv = lax.all_to_all(
        send.reshape(devices, rows // devices, LANES), both, split_axis=0, concat_axis=0, tiled=True
    ).reshape(rows, LANES)
    pieces = [tile_exchange(0, recv)]

    obs, low, high, loc = call(
        scatter_kernel,
        arrays((len(GROUPS), lat_cells * SUB, LANES), (slots, LANES), (slots, LANES))
        + (jax.ShapeDtypeStruct((2 * PER_ROW, rows), jnp.int32),),
        15,
        "scatter",
        scratch_shapes=[
            pltpu.VMEM((rows // LANES, LANES, LANES), f32),
            pltpu.VMEM((2 * PER_ROW, rows), jnp.int32),
            pltpu.SMEM((2 * PER_ROW, rows), jnp.int32),
            pltpu.SemaphoreType.DMA,
        ],
    )(recv)

    pieces.append(tile_exchange(1, pieces[0], obs, coef))
    smem = pl.BlockSpec(memory_space=pltpu.SMEM)
    anywhere = pl.BlockSpec(memory_space=pl.ANY)
    smoothed = None
    sampled = []
    first = 0
    for chunk, groups in enumerate(CHUNKS):
        sizes = GROUPS[first : first + groups]
        begin = starts[first]
        piece = pieces[chunk]
        norm_spec = pl.BlockSpec(
            (pl.Element(sum(sizes)), pl.Element(lat_cells), pl.Element(LANES)),
            lambda i, begin=begin: (begin, 0, 0),
        )
        obs_spec = pl.BlockSpec(
            (pl.Element(groups), pl.Element(lat_cells * SUB), pl.Element(LANES)),
            lambda i, first=first: (first, 0, 0),
        )
        shapes = field_shapes(groups)
        field = call(
            functools.partial(field_kernel, sizes, n_lon, group, cap),
            shapes,
            4,
            "field",
            grid=(1,),
            in_specs=[smem, smem, full(piece.shape), obs_spec, norm_spec],
            out_specs=[full(shape.shape) for shape in shapes],
        )(loc, lat, piece, obs, norm_factor)
        ext, strips, from_west, from_east = halo(*field, groups)
        mid_shape = (groups, lat_cells * SUB, LANES)
        win_shape = (groups, win_rows * SUB, LANES)
        mid = call(
            own_kernel,
            arrays(mid_shape)[0],
            6 * groups,
            "own",
            grid=(1,),
            in_specs=[full(ext.shape), full(coef.shape)],
            out_specs=full(mid_shape),
            scratch_shapes=[pltpu.VMEM(win_shape, f32), pltpu.VMEM(win_shape, f32)],
        )(ext, coef)
        if chunk + 1 < len(CHUNKS):
            pieces[chunk + 1] = after(pieces[chunk + 1], mid)
        operands = [loc, strips, from_west, from_east, coef, mid, norm_factor, low, high]
        specs = [smem] + [full(value.shape) for value in operands[1:5]] + [anywhere] * 4
        aliases = {}
        if smoothed is not None:
            aliases = {len(operands): 0}
            operands.append(smoothed)
            specs.append(anywhere)
        part_shape = (rows // LANES, groups, PER_ROW * SUB, LANES)
        own_levels = (sum(sizes), lat_cells, LANES)
        smoothed, part = call(
            functools.partial(strip_kernel, sizes, begin, len(aliases)),
            arrays(norm_factor.shape, part_shape),
            12,
            "strips",
            grid=(1,),
            in_specs=specs,
            out_specs=[anywhere, full(part_shape)],
            scratch_shapes=[
                pltpu.VMEM((1,) + win_shape[1:], f32),
                pltpu.VMEM((1,) + win_shape[1:], f32),
                pltpu.VMEM(mid_shape, f32),
                pltpu.VMEM(own_levels, f32),
                pltpu.VMEM(low.shape, f32),
                pltpu.VMEM(high.shape, f32),
                pltpu.VMEM(own_levels, f32),
                pltpu.SemaphoreType.DMA((5,)),
            ],
            input_output_aliases=aliases,
        )(*operands)
        sampled.append(part)
        first += groups

    back = call(
        gather_kernel,
        arrays((rows, LANES))[0],
        1,
        "gather",
        scratch_shapes=[pltpu.VMEM((rows // LANES, LANES, LANES), f32)],
    )(*sampled)
    returned = lax.all_to_all(
        back.reshape(devices, rows // devices, LANES), both, split_axis=0, concat_axis=0, tiled=True
    ).reshape(rows, LANES)
    profile_values = call(
        functools.partial(unpack_kernel, starts),
        arrays((levels, count))[0],
        1,
        "unpack",
    )(returned, slot)
    return (smoothed, profile_values)


def solution(mesh):
    in_specs = (
        P(None, ("lat", "lon")),
        P(("lat", "lon"), None),
        P(("lat", "lon")),
        P(("lat", "lon")),
        P(None, ("lat", "lon")),
        P(None, ("lat", "lon"), None, None),
        P(None, ("lat", "lon")),
        P("lat", "lon"),
        P("lat", "lon"),
        P("lat", "lon"),
        P("lat", "lon"),
        P(None, "lat", "lon"),
    )
    out_specs = (P(None, "lat", "lon"), P(None, ("lat", "lon")))
    return jax.shard_map(
        on_device, mesh=mesh, in_specs=in_specs, out_specs=out_specs, check_vma=False
    )
```

```python
import functools
import jax
import jax.numpy as jnp
from jax import lax
from jax.experimental import pallas as pl
from jax.experimental.pallas import tpu as pltpu
from jax.sharding import PartitionSpec as P

STEPS = 10
SUB = 8
LANES = 128
FEATS = 32
PER_ROW = LANES // FEATS
GROUPS = (6, 6, 7, 6)
CHUNKS = (2, 2)
WEIGHT_ROWS = (6, 7, 14, 15)
LOC_ROW = 23
ID_ROW = 30
VMEM_BYTES = 20 * 1024 * 1024


def group_starts():
    starts = []
    total = 0
    for count in GROUPS:
        starts.append(total)
        total += count
    return starts


def params():
    return pltpu.CompilerParams(vmem_limit_bytes=VMEM_BYTES)


def cost(micros):
    return pl.CostEstimate(flops=0, bytes_accessed=int(micros * 3.6e6), transcendentals=0)


def iota(shape, dim):
    return lax.broadcasted_iota(jnp.int32, shape, dim)


def split3(values):
    high = values.astype(jnp.bfloat16)
    rest = values - high.astype(jnp.float32)
    middle = rest.astype(jnp.bfloat16)
    low = (rest - middle.astype(jnp.float32)).astype(jnp.bfloat16)
    return high, middle, low


def route_kernel(cap, group, starts, innov, weights, own_row, own_col, prow, pcol, ids, send, slot_out, pay):
    count = innov.shape[1]
    extra = ids.shape[1]
    same = own_col[...] == own_row[...]
    before = iota((count, count), 0) < iota((count, count), 1)
    ones = jnp.where(same & before, 1.0, 0.0)
    rank = jnp.sum(ones, axis=0, keepdims=True).astype(jnp.int32)
    slot = own_row[...] * cap + rank
    slot_out[...] = slot
    number = iota((1, extra), 1)
    id_slot = (number // group) * cap + number % group
    pay[...] = jnp.zeros_like(pay)
    for index, count_in in enumerate(GROUPS):
        pay[index * SUB : index * SUB + count_in, :count] = innov[starts[index] : starts[index] + count_in, :]
    for corner, row in enumerate(WEIGHT_ROWS):
        pay[row : row + 1, :count] = weights[corner : corner + 1, :]
    pay[LOC_ROW : LOC_ROW + 1, :count] = (prow[...] * LANES + pcol[...]).astype(jnp.float32)
    pay[ID_ROW : ID_ROW + 1, count:] = ids[...].astype(jnp.float32)
    slots = jnp.concatenate([slot, id_slot], axis=1)
    values = pay[...]
    part = slots % PER_ROW
    spread = jnp.concatenate([jnp.where(part == k, values, 0.0) for k in range(PER_ROW)], axis=0)
    rows = send.shape[0]
    hot = jnp.where(iota((rows, count + extra), 0) == slots // PER_ROW, 1.0, 0.0).astype(jnp.bfloat16)
    total = None
    for piece in split3(spread):
        term = lax.dot_general(hot, piece, (((1,), (1,)), ((), ())), preferred_element_type=jnp.float32)
        total = term if total is None else total + term
    send[...] = total


def unpack_kernel(starts, recv, slot, out):
    slots = slot[...]
    rows = recv.shape[0]
    hot = jnp.where(iota((rows, slots.shape[1]), 0) == slots // PER_ROW, 1.0, 0.0).astype(jnp.bfloat16)
    total = None
    for piece in split3(recv[...]):
        term = lax.dot_general(piece, hot, (((0,), (0,)), ((), ())), preferred_element_type=jnp.float32)
        total = term if total is None else total + term
    part = slots % PER_ROW
    picked = jnp.zeros((FEATS, slots.shape[1]), jnp.float32)
    for k in range(PER_ROW):
        picked = jnp.where(part == k, total[k * FEATS : (k + 1) * FEATS], picked)
    for index, count_in in enumerate(GROUPS):
        out[starts[index] : starts[index] + count_in, :] = picked[index * SUB : index * SUB + count_in]


def scatter_kernel(recv, obs, low, high, loc_out, turned, loc_v, loc_s, sem):
    rows = recv.shape[0]
    halves = rows // LANES
    for h in range(halves):
        turned[h] = recv[h * LANES : (h + 1) * LANES, :].T
    for k in range(PER_ROW):
        for h in range(halves):
            at = k * FEATS
            cut = slice(h * LANES, (h + 1) * LANES)
            cells = turned[h, at + LOC_ROW : at + LOC_ROW + 1, :].astype(jnp.int32)
            loc_v[k : k + 1, cut] = cells // LANES * SUB
            loc_v[PER_ROW + k : PER_ROW + k + 1, cut] = turned[h, at + ID_ROW : at + ID_ROW + 1, :].astype(jnp.int32)
    loc_out[...] = loc_v[...]
    copy = pltpu.make_async_copy(loc_v, loc_s, sem)
    copy.start()
    lane = iota((rows, LANES), 1)
    for k in range(PER_ROW):
        at = k * FEATS
        col = recv[:, at + LOC_ROW : at + LOC_ROW + 1].astype(jnp.int32) % LANES
        w = [recv[:, at + row : at + row + 1] for row in WEIGHT_ROWS]
        here = lane == col
        after = lane == col + 1
        low[k * rows : (k + 1) * rows, :] = jnp.where(here, w[0], jnp.where(after, w[1], 0.0))
        high[k * rows : (k + 1) * rows, :] = jnp.where(here, w[2], jnp.where(after, w[3], 0.0))

    def clear(i, carry):
        for index in range(len(GROUPS)):
            obs[index, pl.ds(pl.multiple_of(i * 64, 64), 64), :] = jnp.zeros((64, LANES), jnp.float32)
        return carry

    lax.fori_loop(0, obs.shape[1] // 64, clear, 0)
    copy.wait()
    groups = range(len(GROUPS))

    def body(i, carry):
        h = i // PER_ROW
        k = i % PER_ROW
        block = turned[h, pl.ds(pl.multiple_of(k * FEATS, FEATS), FEATS), :]
        for seat in range(LANES):
            at = pl.multiple_of(loc_s[k, h * LANES + seat], SUB)
            lo = low[pl.ds(k * rows + h * LANES + seat, 1), :]
            hi = high[pl.ds(k * rows + h * LANES + seat, 1), :]
            values = [block[index * SUB : (index + 1) * SUB, seat : seat + 1] for index in groups]
            old0 = [obs[index, pl.ds(at, SUB), :] for index in groups]
            old1 = [obs[index, pl.ds(at + SUB, SUB), :] for index in groups]
            for index in groups:
                obs[index, pl.ds(at, SUB), :] = old0[index] + values[index] * lo
                obs[index, pl.ds(at + SUB, SUB), :] = old1[index] + values[index] * hi
        return carry

    lax.fori_loop(0, halves * PER_ROW, body, 0)


def row_at(index):
    return pl.ds(pl.multiple_of(index * SUB, SUB), SUB)


def rows_at(index, count):
    return pl.ds(pl.multiple_of(index * SUB, SUB), count * SUB)


def send_rows(field, up, down):
    edge = up.shape[1]
    total = field.shape[1]
    for g in range(field.shape[0]):
        up[g] = field[g, total - edge :, :]
        down[g] = field[g, :edge, :]


def field_kernel(first, begin, sizes, n_lon, group, cap, loc, lat, tiles, obs, norm_h, field, up, down, norm, sem):
    copy = pltpu.make_async_copy(norm_h.at[pl.ds(begin, sum(sizes))], norm, sem)
    copy.start()
    field[...] = jnp.zeros_like(field)
    copy.wait()

    def body(j, carry):
        done = []
        for c in range(group):
            slot = (lat[0] * n_lon + j) * cap + c
            t = loc[PER_ROW + slot % PER_ROW, slot // PER_ROW]
            own = pl.ds(pl.multiple_of(t * SUB, SUB), SUB)
            level = 0
            for g, size in enumerate(sizes):
                for l in range(size):
                    at = pl.ds(t * (SUB * SUB) + l, SUB, stride=SUB)
                    done.append((g, at, norm[level, own, :] * (obs[first + g, at, :] + tiles[j, level, c])))
                    level += 1
        for g, at, value in done:
            field[g, at, :] = value
        return carry

    lax.fori_loop(0, n_lon, body, 0)
    send_rows(field, up, down)


def stack_kernel(face_x, face_y, cross, wet, field, up, down):
    field[...] = jnp.zeros_like(field)
    sources = (face_x, face_y, cross, wet)

    def body(i, carry):
        values = []
        for n in range(4):
            t = i * 4 + n
            own = pl.ds(pl.multiple_of(t * SUB, SUB), SUB)
            values += [(t, l, source[own, :].astype(jnp.float32)) for l, source in enumerate(sources)]
        for t, l, value in values:
            field[0, pl.ds(t * (SUB * SUB) + l, SUB, stride=SUB), :] = value
        return carry

    lax.fori_loop(0, face_x.shape[0] // SUB // 4, body, 0)
    send_rows(field, up, down)


STRIP = 32
HALF = 2 * STRIP
SEAT = 16
SEATS = HALF // SEAT
TURNS = 10


def span_of(rows):
    return -(-(rows + 2 * STEPS) // (SEATS * TURNS)) * TURNS


def extend(ext, field, above, below):
    groups, total, _ = field.shape
    halo = STEPS * SUB
    for g in range(groups):
        ext[g, :halo, :] = above[g]
        ext[g, halo : halo + total, :] = field[g]
        ext[g, halo + total : 2 * halo + total, :] = below[g]
        ext[g, 2 * halo + total :, :] = jnp.zeros((ext.shape[1] - 2 * halo - total, LANES), jnp.float32)


def edges_kernel(field, above, below, strips, east, west, ext):
    groups = field.shape[0]
    extend(ext, field, above, below)
    span = east.shape[0] // SUB
    lane = iota((SUB, LANES), 1)
    place = lane % HALF

    def body(i, carry):
        done = []
        for n in range(TURNS // 2):
            m = i * (TURNS // 2) + n
            to_east = None
            to_west = None
            for q in range(SEATS):
                first = ext[0, row_at(q * span + m), :]
                second = pltpu.roll(ext[groups - 1, row_at(q * span + m), :], HALF, 1)
                left = jnp.where(lane < HALF, first, second)
                right = jnp.where(lane < HALF, second, first)
                row = jnp.where(place < STRIP, pltpu.roll(left, STEPS, 1), pltpu.roll(right, HALF - STEPS, 1))
                done.append((strips, q * span + m, row))
                right = pltpu.roll(right, SEAT * q + SEAT, 1)
                if q:
                    left = pltpu.roll(left, SEAT * q, 1)
                mine = place // SEAT == q
                to_east = right if q == 0 else jnp.where(mine, right, to_east)
                to_west = left if q == 0 else jnp.where(mine, left, to_west)
            done.append((east, m, to_east))
            done.append((west, m, to_west))
        for ref, m, value in done:
            ref[row_at(m), :] = value
        return carry

    lax.fori_loop(0, span // (TURNS // 2), body, 0)


def build_strips(win, strips, from_west, from_east):
    span = from_west.shape[0] // SUB
    place = iota((SUB, LANES), 1) % HALF

    def body(i, carry):
        done = []
        for n in range(TURNS):
            m = i * TURNS + n
            west = from_west[row_at(m), :]
            east = from_east[row_at(m), :]
            for q in range(SEATS):
                a = pltpu.roll(west, (STEPS - SEAT - SEAT * q) % LANES, 1)
                b = pltpu.roll(east, (HALF - STEPS - SEAT * q) % LANES, 1)
                row = strips[row_at(q * span + m), :]
                row = jnp.where(place < STEPS, a, jnp.where(place < HALF - STEPS, row, b))
                done.append((q * span + m, row))
        for m, row in done:
            win[row_at(m), :] = row
        return carry

    lax.fori_loop(0, span // TURNS, body, 0)
    first = SEATS * span * SUB
    win[first:, :] = jnp.zeros((win.shape[0] - first, LANES), jnp.float32)


def coef_kernel(field, above, below, strips, from_west, from_east, coef, ext, strip):
    extend(ext, field, above, below)
    own = ext.at[0]
    build_strips(strip, strips, from_west, from_east)
    rows = coef.shape[1]

    def body(i, carry):
        done = []
        for n in range(4):
            b = i * 4 + n
            base = b * (SUB * SUB)
            at = pl.ds(pl.multiple_of(b * SUB, SUB), SUB)
            for first, win in ((0, own), (5, strip)):
                fx, fy, ct, wet = (win[pl.ds(base + s, SUB, stride=SUB), :] for s in range(4))
                wet_n = win[pl.ds(base + SUB + 3, SUB, stride=SUB), :]
                x = fx * wet * pltpu.roll(wet, LANES - 1, 1)
                xw = pltpu.roll(x, 1, 1)
                y = fy * wet * wet_n
                twist = 0.25 * ct * wet
                for c, value in enumerate((1.0 - x - xw, x, xw, y, twist)):
                    done.append((first + c, at, value))
        for c, at, value in done:
            coef[c, at, :] = value
        return carry

    lax.fori_loop(0, rows // (4 * SUB), body, 0)


def advance(source, target, planes, weight, rows):
    last = rows + 2 * STEPS + 4
    unroll = last // (2 * planes)
    blocks = last // unroll

    def rolled(w, index):
        cells = source[w, row_at(index), :]
        east = pltpu.roll(cells, LANES - 1, 1)
        west = pltpu.roll(cells, 1, 1)
        return cells, east, west, east - west

    y_first = weight(3, 0)
    state = []
    for w in range(planes):
        before = rolled(w, 0)
        now = rolled(w, 1)
        state.append((now, before[3], y_first * (now[0] - before[0])))

    def block(b, state):
        base = 1 + b * unroll
        state = list(state)
        for u in range(unroll):
            weights = [weight(c, base + u) for c in range(5)]
            for w in range(planes):
                (cells, east, west, slope), slope_s, flux_s = state[w]
                ahead = rolled(w, base + u + 1)
                flux = weights[3] * (ahead[0] - cells)
                target[w, row_at(base + u), :] = (
                    (weights[0] * cells + weights[1] * east)
                    + (weights[2] * west + (flux - flux_s))
                    + weights[4] * (ahead[3] - slope_s)
                )
                state[w] = (ahead, slope, flux)
        return tuple(state)

    lax.fori_loop(0, blocks, block, tuple(state))


def diffuse(win, other, planes, coef, first, rows):
    def weight(c, index):
        return coef[first + c, pl.ds(index, 1), :]

    def two(t, carry):
        advance(win, other, planes, weight, rows)
        advance(other, win, planes, weight, rows)
        return carry

    for w in range(planes):
        other[w, :SUB, :] = jnp.zeros((SUB, LANES), jnp.float32)
        other[w, other.shape[1] - SUB * SUB :, :] = jnp.zeros((SUB * SUB, LANES), jnp.float32)
    lax.fori_loop(0, STEPS // 2, two, 0)


def own_kernel(field, above, below, coef, mid, win, other):
    groups = field.shape[0]
    rows = mid.shape[1] // SUB
    halo = STEPS * SUB
    extend(win, field, above, below)
    diffuse(win, other, groups, coef, 0, rows)
    for g in range(groups):
        mid[g] = win[g, halo : halo + rows * SUB, :]


MERGE = 32


def strip_kernel(sizes, begin, aliased, earlier, *refs):
    loc, strips, from_west, from_east, coef, mid, low, high, norm_h = refs[:9]
    parts = refs[9 + aliased : 9 + aliased + earlier]
    refs = refs[9 + aliased + earlier :]
    if earlier:
        out_h, packed, sampled, turned = refs[:4]
    else:
        out_h, sampled = refs[:2]
    win, other, smooth, norm, out, sems = refs[-6:]
    groups = mid.shape[0]
    rows = mid.shape[1] // SUB
    levels = pl.ds(begin, sum(sizes))
    copy = pltpu.make_async_copy(norm_h.at[levels], norm, sems.at[0])
    copy.start()
    build_strips(win.at[0], strips, from_west, from_east)
    diffuse(win, other, 1, coef, 5, rows)
    copy.wait()
    lane = iota((SUB, LANES), 1)
    outer = LANES - STEPS

    def merge(b, carry):
        done = []
        for u in range(MERGE):
            at = row_at(b * MERGE + u)
            strip = win[0, row_at(b * MERGE + u + STEPS), :]
            west = pltpu.roll(strip, outer, 1)
            east = pltpu.roll(strip, HALF + STEPS, 1)
            cells = mid[0, at, :]
            done.append((0, at, jnp.where(lane < STEPS, west, jnp.where(lane < outer, cells, east))))
            if groups == 2:
                both = pltpu.roll(jnp.where(lane < HALF, east, west), HALF, 1)
                cells = mid[1, at, :]
                done.append((1, at, jnp.where((lane < STEPS) | (lane >= outer), both, cells)))
        for g, at, value in done:
            smooth[g, at, :] = value
        return carry

    lax.fori_loop(0, rows // MERGE, merge, 0)

    def scale(i, carry):
        done = []
        for n in range(4):
            b = i * 4 + n
            own = pl.ds(pl.multiple_of(b * SUB, SUB), SUB)
            level = 0
            for g, size in enumerate(sizes):
                for l in range(size):
                    at = pl.ds(b * (SUB * SUB) + l, SUB, stride=SUB)
                    done.append((g, at, level, own, smooth[g, at, :] * norm[level, own, :]))
                    level += 1
        for g, at, level, own, value in done:
            out[level, own, :] = value
            smooth[g, at, :] = value
        return carry

    lax.fori_loop(0, rows // (4 * SUB), scale, 0)
    back = pltpu.make_async_copy(out, out_h.at[levels], sems.at[1])
    back.start()
    count = low.shape[0] // PER_ROW
    halves = count // LANES

    def samples(i, carry):
        h = i // PER_ROW
        k = i % PER_ROW
        kept = [[jnp.zeros((SUB, LANES), jnp.float32)] * 4 for _ in range(groups)]
        for seat in range(LANES):
            at = pl.multiple_of(loc[k, h * LANES + seat], SUB)
            lo = low[pl.ds(k * count + h * LANES + seat, 1), :]
            hi = high[pl.ds(k * count + h * LANES + seat, 1), :]
            for g in range(groups):
                value = smooth[g, pl.ds(at, SUB), :] * lo + smooth[g, pl.ds(at + SUB, SUB), :] * hi
                total = jnp.sum(value, axis=1, keepdims=True)
                kept[g][seat % 4] = jnp.where(lane == seat, total, kept[g][seat % 4])
        for g in range(groups):
            a, b, c, d = kept[g]
            sampled[h, g, row_at(k), :] = (a + b) + (c + d)
        return carry

    lax.fori_loop(0, halves * PER_ROW, samples, 0)
    if earlier:
        pack_samples(parts + (sampled,), packed, turned)
    back.wait()


def pack_samples(parts, out, turned):
    for h in range(turned.shape[0]):
        index = 0
        for part in parts:
            for g in range(part.shape[1]):
                for k in range(PER_ROW):
                    at = k * FEATS + index * SUB
                    turned[h, at : at + SUB, :] = part[h, g, k * SUB : (k + 1) * SUB, :]
                index += 1
        out[h * LANES : (h + 1) * LANES, :] = turned[h].T


def exchange_rows(up, down, n_lat):
    pairs = [(i, i + 1) for i in range(n_lat - 1)]
    back = [(i + 1, i) for i in range(n_lat - 1)]
    return lax.ppermute(up, "lat", pairs), lax.ppermute(down, "lat", back)


def exchange_columns(east, west, n_lon):
    pairs = [(i, (i + 1) % n_lon) for i in range(n_lon)]
    back = [((i + 1) % n_lon, i) for i in range(n_lon)]
    return lax.ppermute(east, "lon", pairs), lax.ppermute(west, "lon", back)


def on_device(
    innovations,
    owners,
    prof_row,
    prof_col,
    interp_weights,
    model_tiles,
    model_ids,
    face_x,
    face_y,
    cross_term,
    wet_mask,
    norm_factor,
):
    n_lat = lax.axis_size("lat")
    n_lon = lax.axis_size("lon")
    devices = n_lat * n_lon
    levels, lat_cells, lon_cells = norm_factor.shape
    tiles = model_tiles.shape[1]
    group = tiles // n_lon
    count = innovations.shape[1]
    cap = 2 * count // devices
    slots = devices * cap
    rows = slots // PER_ROW
    starts = group_starts()
    f32 = jnp.float32
    lat = lax.axis_index("lat").reshape(1)
    both = ("lat", "lon")
    span = span_of(lat_cells)
    ext_rows = SEATS * span
    win_rows = ext_rows + SUB

    def arrays(*shapes):
        return tuple(jax.ShapeDtypeStruct(shape, f32) for shape in shapes)

    def call(kernel, out_shape, micros, name, **kwargs):
        return pl.pallas_call(
            kernel,
            out_shape=out_shape,
            compiler_params=params(),
            cost_estimate=cost(micros),
            name=name,
            **kwargs,
        )

    def after(value, *others):
        return lax.optimization_barrier((value,) + others)[0]

    def tile_exchange(chunk, *others):
        first = sum(CHUNKS[:chunk])
        begin = starts[first]
        size = sum(GROUPS[first : first + CHUNKS[chunk]])
        piece = model_tiles[begin : begin + size].reshape(size, n_lon, group, SUB, LANES)
        piece = jnp.transpose(piece, (1, 0, 2, 3, 4))
        if others:
            piece = after(piece, *others)
        return lax.all_to_all(piece, "lon", split_axis=0, concat_axis=0, tiled=True)

    def halo(field, up, down, groups):
        above, below = exchange_rows(up, down, n_lat)
        strips, east, west = call(
            edges_kernel,
            arrays((ext_rows * SUB, LANES), (span * SUB, LANES), (span * SUB, LANES)),
            3,
            "edges",
            scratch_shapes=[pltpu.VMEM((groups, ext_rows * SUB, LANES), f32)],
        )(field, above, below)
        return (field, above, below, strips) + exchange_columns(east, west, n_lon)

    def field_shapes(groups):
        return arrays(
            (groups, lat_cells * SUB, LANES),
            (groups, STEPS * SUB, LANES),
            (groups, STEPS * SUB, LANES),
        )

    send, slot = call(
        functools.partial(route_kernel, cap, group, starts),
        (jax.ShapeDtypeStruct((rows, LANES), f32), jax.ShapeDtypeStruct((1, count), jnp.int32)),
        3,
        "route",
        scratch_shapes=[pltpu.VMEM((FEATS, count + devices * group), f32)],
    )(
        innovations,
        interp_weights,
        owners.reshape(1, count),
        owners,
        prof_row.reshape(1, count),
        prof_col.reshape(1, count),
        jnp.tile(model_ids, (1, n_lat)),
    )
    stacked = call(stack_kernel, field_shapes(1), 3, "stack")(face_x, face_y, cross_term, wet_mask)
    coef = call(
        coef_kernel,
        arrays((10, win_rows, LANES))[0],
        5,
        "coef",
        scratch_shapes=[
            pltpu.VMEM((1, (win_rows + SUB) * SUB, LANES), f32),
            pltpu.VMEM(((win_rows + SUB) * SUB, LANES), f32),
        ],
    )(*halo(*stacked, 1))

    recv = lax.all_to_all(
        send.reshape(devices, rows // devices, LANES), both, split_axis=0, concat_axis=0, tiled=True
    ).reshape(rows, LANES)
    pieces = [tile_exchange(0, recv, stacked[0])]

    obs, low, high, loc = call(
        scatter_kernel,
        arrays((len(GROUPS), lat_cells * SUB, LANES), (slots, LANES), (slots, LANES))
        + (jax.ShapeDtypeStruct((2 * PER_ROW, rows), jnp.int32),),
        15,
        "scatter",
        scratch_shapes=[
            pltpu.VMEM((rows // LANES, LANES, LANES), f32),
            pltpu.VMEM((2 * PER_ROW, rows), jnp.int32),
            pltpu.SMEM((2 * PER_ROW, rows), jnp.int32),
            pltpu.SemaphoreType.DMA,
        ],
    )(recv)

    pieces.append(tile_exchange(1, pieces[0], obs, coef))
    smem = pl.BlockSpec(memory_space=pltpu.SMEM)
    vmem = pl.BlockSpec(memory_space=pltpu.VMEM)
    hbm = pl.BlockSpec(memory_space=pltpu.HBM)
    smoothed = None
    sampled = []
    first = 0
    for chunk, groups in enumerate(CHUNKS):
        sizes = GROUPS[first : first + groups]
        begin = starts[first]
        own_levels = (sum(sizes), lat_cells, LANES)
        field = call(
            functools.partial(field_kernel, first, begin, sizes, n_lon, group, cap),
            field_shapes(groups),
            4,
            "field",
            in_specs=[smem, smem, vmem, vmem, hbm],
            scratch_shapes=[pltpu.VMEM(own_levels, f32), pltpu.SemaphoreType.DMA],
        )(loc, lat, pieces[chunk], obs, norm_factor)
        field, above, below, strips, from_west, from_east = halo(*field, groups)
        mid_shape = (groups, lat_cells * SUB, LANES)
        win_shape = (groups, win_rows * SUB, LANES)
        mid = call(
            own_kernel,
            arrays(mid_shape)[0],
            6 * groups,
            "own",
            scratch_shapes=[pltpu.VMEM(win_shape, f32), pltpu.VMEM(win_shape, f32)],
        )(field, above, below, coef)
        if chunk + 1 < len(CHUNKS):
            pieces[chunk + 1] = after(pieces[chunk + 1], mid)
        operands = [loc, strips, from_west, from_east, coef, mid, low, high, norm_factor]
        specs = [smem] + [vmem] * 7 + [hbm]
        aliases = {}
        if smoothed is not None:
            aliases = {len(operands): 0}
            operands.append(smoothed)
            specs.append(hbm)
        last = chunk + 1 == len(CHUNKS)
        earlier = sampled if last else []
        part_shape = (rows // LANES, groups, PER_ROW * SUB, LANES)
        gathered = [pltpu.VMEM(part_shape, f32), pltpu.VMEM((rows // LANES, LANES, LANES), f32)]
        smoothed, part = call(
            functools.partial(strip_kernel, sizes, begin, len(aliases), len(earlier)),
            arrays(norm_factor.shape, (rows, LANES) if earlier else part_shape),
            12,
            "strips",
            in_specs=specs + [vmem] * len(earlier),
            out_specs=(hbm, vmem),
            scratch_shapes=(gathered if earlier else [])
            + [
                pltpu.VMEM((1,) + win_shape[1:], f32),
                pltpu.VMEM((1,) + win_shape[1:], f32),
                pltpu.VMEM(mid_shape, f32),
                pltpu.VMEM(own_levels, f32),
                pltpu.VMEM(own_levels, f32),
                pltpu.SemaphoreType.DMA((2,)),
            ],
            input_output_aliases=aliases,
        )(*operands, *earlier)
        sampled.append(part)
        first += groups

    back = sampled[-1]
    returned = lax.all_to_all(
        back.reshape(devices, rows // devices, LANES), both, split_axis=0, concat_axis=0, tiled=True
    ).reshape(rows, LANES)
    profile_values = call(
        functools.partial(unpack_kernel, starts),
        arrays((levels, count))[0],
        1,
        "unpack",
    )(returned, slot)
    return (smoothed, profile_values)


def solution(mesh):
    in_specs = (
        P(None, ("lat", "lon")),
        P(("lat", "lon"), None),
        P(("lat", "lon")),
        P(("lat", "lon")),
        P(None, ("lat", "lon")),
        P(None, ("lat", "lon"), None, None),
        P(None, ("lat", "lon")),
        P("lat", "lon"),
        P("lat", "lon"),
        P("lat", "lon"),
        P("lat", "lon"),
        P(None, "lat", "lon"),
    )
    out_specs = (P(None, "lat", "lon"), P(None, ("lat", "lon")))
    return jax.shard_map(
        on_device, mesh=mesh, in_specs=in_specs, out_specs=out_specs, check_vma=False
    )
```

```python
import functools
import jax
import jax.numpy as jnp
from jax import lax
from jax.experimental import pallas as pl
from jax.experimental.pallas import tpu as pltpu
from jax.sharding import PartitionSpec as P

STEPS = 10
SUB = 8
LANES = 128
FEATS = 32
PER_ROW = LANES // FEATS
GROUPS = (5, 5, 8, 7)
CHUNKS = (2, 2)
WEIGHT_ROWS = (5, 6, 13, 14)
LOC_ROW = 7
ID_ROW = 15
SMALL = 20 * 1024 * 1024
LARGE = 60 * 1024 * 1024


def group_starts():
    starts = []
    total = 0
    for count in GROUPS:
        starts.append(total)
        total += count
    return starts


def params(grant):
    return pltpu.CompilerParams(vmem_limit_bytes=grant)


def cost(micros):
    return pl.CostEstimate(flops=0, bytes_accessed=int(micros * 3.6e6), transcendentals=0)


def iota(shape, dim):
    return lax.broadcasted_iota(jnp.int32, shape, dim)


def split3(values):
    high = values.astype(jnp.bfloat16)
    rest = values - high.astype(jnp.float32)
    middle = rest.astype(jnp.bfloat16)
    low = (rest - middle.astype(jnp.float32)).astype(jnp.bfloat16)
    return high, middle, low


def route_kernel(cap, group, copies, starts, innov, weights, own_row, prow, pcol, ids, send, slot_out, pay):
    count = innov.shape[1]
    tiles = ids.shape[1]
    extra = tiles * copies
    owner = own_row[...]
    column = jnp.broadcast_to(owner.astype(jnp.float32), (SUB, count)).T[:, :1].astype(jnp.int32)
    same = column == owner
    before = iota((count, count), 0) < iota((count, count), 1)
    ones = jnp.where(same & before, 1.0, 0.0)
    rank = jnp.sum(ones, axis=0, keepdims=True).astype(jnp.int32)
    slot = owner * cap + rank
    slot_out[...] = slot
    number = iota((1, extra), 1)
    id_slot = (number // group) * cap + number % group
    pay[...] = jnp.zeros_like(pay)
    for index, count_in in enumerate(GROUPS):
        pay[index * SUB : index * SUB + count_in, :count] = innov[starts[index] : starts[index] + count_in, :]
    for corner, row in enumerate(WEIGHT_ROWS):
        pay[row : row + 1, :count] = weights[corner : corner + 1, :]
    pay[LOC_ROW : LOC_ROW + 1, :count] = (prow[...] * LANES + pcol[...]).astype(jnp.float32)
    for i in range(copies):
        at = count + i * tiles
        pay[ID_ROW : ID_ROW + 1, at : at + tiles] = ids[...].astype(jnp.float32)
    slots = jnp.concatenate([slot, id_slot], axis=1)
    values = pay[...]
    part = slots % PER_ROW
    spread = jnp.concatenate([jnp.where(part == k, values, 0.0) for k in range(PER_ROW)], axis=0)
    rows = send.shape[0]
    hot = jnp.where(iota((rows, count + extra), 0) == slots // PER_ROW, 1.0, 0.0).astype(jnp.bfloat16)
    total = None
    for piece in split3(spread):
        term = lax.dot_general(hot, piece, (((1,), (1,)), ((), ())), preferred_element_type=jnp.float32)
        total = term if total is None else total + term
    send[...] = total


def unpack_kernel(starts, recv, slot, out):
    slots = slot[...]
    rows = recv.shape[0]
    hot = jnp.where(iota((rows, slots.shape[1]), 0) == slots // PER_ROW, 1.0, 0.0).astype(jnp.bfloat16)
    total = None
    for piece in split3(recv[...]):
        term = lax.dot_general(piece, hot, (((0,), (0,)), ((), ())), preferred_element_type=jnp.float32)
        total = term if total is None else total + term
    part = slots % PER_ROW
    picked = jnp.zeros((FEATS, slots.shape[1]), jnp.float32)
    for k in range(PER_ROW):
        picked = jnp.where(part == k, total[k * FEATS : (k + 1) * FEATS], picked)
    for index, count_in in enumerate(GROUPS):
        out[starts[index] : starts[index] + count_in, :] = picked[index * SUB : index * SUB + count_in]


def scatter_kernel(recv, obs, low, high, loc_out, turned, loc_v, loc_s, sem):
    rows = recv.shape[0]
    halves = rows // LANES
    for h in range(halves):
        turned[h] = recv[h * LANES : (h + 1) * LANES, :].T
    for k in range(PER_ROW):
        for h in range(halves):
            at = k * FEATS
            cut = slice(h * LANES, (h + 1) * LANES)
            cells = turned[h, at + LOC_ROW : at + LOC_ROW + 1, :].astype(jnp.int32)
            loc_v[k : k + 1, cut] = cells // LANES * SUB
            loc_v[PER_ROW + k : PER_ROW + k + 1, cut] = turned[h, at + ID_ROW : at + ID_ROW + 1, :].astype(jnp.int32)
    loc_out[...] = loc_v[...]
    copy = pltpu.make_async_copy(loc_v, loc_s, sem)
    copy.start()
    lane = iota((rows, LANES), 1)
    for k in range(PER_ROW):
        at = k * FEATS
        col = recv[:, at + LOC_ROW : at + LOC_ROW + 1].astype(jnp.int32) % LANES
        w = [recv[:, at + row : at + row + 1] for row in WEIGHT_ROWS]
        here = lane == col
        after = lane == col + 1
        low[k * rows : (k + 1) * rows, :] = jnp.where(here, w[0], jnp.where(after, w[1], 0.0))
        high[k * rows : (k + 1) * rows, :] = jnp.where(here, w[2], jnp.where(after, w[3], 0.0))

    def clear(i, carry):
        for index in range(len(GROUPS)):
            obs[index, pl.ds(pl.multiple_of(i * 64, 64), 64), :] = jnp.zeros((64, LANES), jnp.float32)
        return carry

    lax.fori_loop(0, obs.shape[1] // 64, clear, 0)
    copy.wait()
    groups = range(len(GROUPS))

    def body(i, carry):
        h = i // PER_ROW
        k = i % PER_ROW
        block = turned[h, pl.ds(pl.multiple_of(k * FEATS, FEATS), FEATS), :]
        for seat in range(LANES):
            at = pl.multiple_of(loc_s[k, h * LANES + seat], SUB)
            lo = low[pl.ds(k * rows + h * LANES + seat, 1), :]
            hi = high[pl.ds(k * rows + h * LANES + seat, 1), :]
            values = [block[index * SUB : (index + 1) * SUB, seat : seat + 1] for index in groups]
            old0 = [obs[index, pl.ds(at, SUB), :] for index in groups]
            old1 = [obs[index, pl.ds(at + SUB, SUB), :] for index in groups]
            for index in groups:
                obs[index, pl.ds(at, SUB), :] = old0[index] + values[index] * lo
                obs[index, pl.ds(at + SUB, SUB), :] = old1[index] + values[index] * hi
        return carry

    lax.fori_loop(0, halves * PER_ROW, body, 0)


def row_at(index):
    return pl.ds(pl.multiple_of(index * SUB, SUB), SUB)


def rows_at(index, count):
    return pl.ds(pl.multiple_of(index * SUB, SUB), count * SUB)


def send_rows(field, up, down):
    edge = up.shape[1]
    total = field.shape[1]
    for g in range(field.shape[0]):
        up[g] = field[g, total - edge :, :]
        down[g] = field[g, :edge, :]


def field_kernel(first, begin, sizes, n_lon, group, cap, loc, lat, tiles, obs_h, norm_h, field, up, down, obs, norm, sems):
    copies = [
        pltpu.make_async_copy(obs_h.at[pl.ds(first, len(sizes))], obs, sems.at[0]),
        pltpu.make_async_copy(norm_h.at[pl.ds(begin, sum(sizes))], norm, sems.at[1]),
    ]
    for copy in copies:
        copy.start()
    field[...] = jnp.zeros_like(field)
    for copy in copies:
        copy.wait()

    def body(j, carry):
        done = []
        for c in range(group):
            slot = (lat[0] * n_lon + j) * cap + c
            t = loc[PER_ROW + slot % PER_ROW, slot // PER_ROW]
            own = pl.ds(pl.multiple_of(t * SUB, SUB), SUB)
            level = 0
            for g, size in enumerate(sizes):
                for l in range(size):
                    at = pl.ds(t * (SUB * SUB) + l, SUB, stride=SUB)
                    done.append((g, at, norm[level, own, :] * (obs[g, at, :] + tiles[j, level, c])))
                    level += 1
        for g, at, value in done:
            field[g, at, :] = value
        return carry

    lax.fori_loop(0, n_lon, body, 0)
    send_rows(field, up, down)


def stack_kernel(face_x, face_y, cross, wet, field, up, down):
    field[...] = jnp.zeros_like(field)
    sources = (face_x, face_y, cross, wet)

    def body(i, carry):
        values = []
        for n in range(4):
            t = i * 4 + n
            own = pl.ds(pl.multiple_of(t * SUB, SUB), SUB)
            values += [(t, l, source[own, :].astype(jnp.float32)) for l, source in enumerate(sources)]
        for t, l, value in values:
            field[0, pl.ds(t * (SUB * SUB) + l, SUB, stride=SUB), :] = value
        return carry

    lax.fori_loop(0, face_x.shape[0] // SUB // 4, body, 0)
    send_rows(field, up, down)


STRIP = 32
HALF = 2 * STRIP
SEAT = 16
SEATS = HALF // SEAT
TURNS = 10


def span_of(rows):
    return -(-(rows + 2 * STEPS) // (SEATS * TURNS)) * TURNS


def extend(ext, field, above, below):
    groups, total, _ = field.shape
    halo = STEPS * SUB
    for g in range(groups):
        ext[g, :halo, :] = above[g]
        ext[g, halo : halo + total, :] = field[g]
        ext[g, halo + total : 2 * halo + total, :] = below[g]
        ext[g, 2 * halo + total :, :] = jnp.zeros((ext.shape[1] - 2 * halo - total, LANES), jnp.float32)


def edges_kernel(field, above, below, strips, east, west, ext):
    groups = field.shape[0]
    extend(ext, field, above, below)
    span = east.shape[0] // SUB
    lane = iota((SUB, LANES), 1)
    place = lane % HALF

    def body(i, carry):
        done = []
        for n in range(TURNS // 2):
            m = i * (TURNS // 2) + n
            to_east = None
            to_west = None
            for q in range(SEATS):
                first = ext[0, row_at(q * span + m), :]
                second = pltpu.roll(ext[groups - 1, row_at(q * span + m), :], HALF, 1)
                left = jnp.where(lane < HALF, first, second)
                right = jnp.where(lane < HALF, second, first)
                row = jnp.where(place < STRIP, pltpu.roll(left, STEPS, 1), pltpu.roll(right, HALF - STEPS, 1))
                done.append((strips, q * span + m, row))
                right = pltpu.roll(right, SEAT * q + SEAT, 1)
                if q:
                    left = pltpu.roll(left, SEAT * q, 1)
                mine = place // SEAT == q
                to_east = right if q == 0 else jnp.where(mine, right, to_east)
                to_west = left if q == 0 else jnp.where(mine, left, to_west)
            done.append((east, m, to_east))
            done.append((west, m, to_west))
        for ref, m, value in done:
            ref[row_at(m), :] = value
        return carry

    lax.fori_loop(0, span // (TURNS // 2), body, 0)


def build_strips(win, strips, from_west, from_east):
    span = from_west.shape[0] // SUB
    place = iota((SUB, LANES), 1) % HALF

    def body(i, carry):
        done = []
        for n in range(TURNS):
            m = i * TURNS + n
            west = from_west[row_at(m), :]
            east = from_east[row_at(m), :]
            for q in range(SEATS):
                a = pltpu.roll(west, (STEPS - SEAT - SEAT * q) % LANES, 1)
                b = pltpu.roll(east, (HALF - STEPS - SEAT * q) % LANES, 1)
                row = strips[row_at(q * span + m), :]
                row = jnp.where(place < STEPS, a, jnp.where(place < HALF - STEPS, row, b))
                done.append((q * span + m, row))
        for m, row in done:
            win[row_at(m), :] = row
        return carry

    lax.fori_loop(0, span // TURNS, body, 0)
    first = SEATS * span * SUB
    win[first:, :] = jnp.zeros((win.shape[0] - first, LANES), jnp.float32)


def coef_kernel(field, above, below, strips, from_west, from_east, own_coef, strip_coef, ext, strip):
    extend(ext, field, above, below)
    own = ext.at[0]
    build_strips(strip, strips, from_west, from_east)
    rows = own_coef.shape[1]

    def body(i, carry):
        done = []
        for n in range(4):
            b = i * 4 + n
            base = b * (SUB * SUB)
            at = pl.ds(pl.multiple_of(b * SUB, SUB), SUB)
            for coef, win in ((own_coef, own), (strip_coef, strip)):
                fx, fy, ct, wet = (win[pl.ds(base + s, SUB, stride=SUB), :] for s in range(4))
                wet_n = win[pl.ds(base + SUB + 3, SUB, stride=SUB), :]
                x = fx * wet * pltpu.roll(wet, LANES - 1, 1)
                xw = pltpu.roll(x, 1, 1)
                y = fy * wet * wet_n
                twist = 0.25 * ct * wet
                for c, value in enumerate((1.0 - x - xw, x, xw, y, twist)):
                    done.append((coef, c, at, value))
        for coef, c, at, value in done:
            coef[c, at, :] = value
        return carry

    lax.fori_loop(0, rows // (4 * SUB), body, 0)


BY_MATMUL = 0.4


def fill_shift(shift):
    row = iota(shift.shape, 0) % LANES
    col = iota(shift.shape, 1)
    near = jnp.where(col < LANES, col + 1, col + LANES - 1) % LANES
    shift[...] = jnp.where(row == near, 1.0, 0.0).astype(jnp.bfloat16)


def advance(source, target, planes, weight, shift, rows):
    last = rows + 2 * STEPS + 4
    unroll = last // (2 * planes)
    blocks = last // unroll
    split = int(unroll * BY_MATMUL)

    def rolled(w, index):
        cells = source[w, row_at(index), :]
        east = pltpu.roll(cells, LANES - 1, 1)
        west = pltpu.roll(cells, 1, 1)
        return cells, east, west, east - west

    def shifted_rows(w, first):
        cells = source[w, rows_at(first, split), :]
        high = cells.astype(jnp.bfloat16)
        low = (cells - high.astype(jnp.float32)).astype(jnp.bfloat16)
        both = jnp.concatenate([high, low], axis=1)
        return jnp.dot(both, shift[...], preferred_element_type=jnp.float32)

    y_first = weight(3, 0)
    state = []
    for w in range(planes):
        before = rolled(w, 0)
        now = rolled(w, 1)
        state.append((now, before[3], y_first * (now[0] - before[0])))

    def block(b, state):
        base = 1 + b * unroll
        state = list(state)
        sides = [shifted_rows(w, base + 1) for w in range(planes)]
        for u in range(unroll):
            weights = [weight(c, base + u) for c in range(5)]
            for w in range(planes):
                (cells, east, west, slope), slope_s, flux_s = state[w]
                if u < split:
                    cells_n = source[w, row_at(base + u + 1), :]
                    east_n = sides[w][u * SUB : (u + 1) * SUB, :LANES]
                    west_n = sides[w][u * SUB : (u + 1) * SUB, LANES:]
                    ahead = (cells_n, east_n, west_n, east_n - west_n)
                else:
                    ahead = rolled(w, base + u + 1)
                flux = weights[3] * (ahead[0] - cells)
                target[w, row_at(base + u), :] = (
                    (weights[0] * cells + weights[1] * east)
                    + (weights[2] * west + (flux - flux_s))
                    + weights[4] * (ahead[3] - slope_s)
                )
                state[w] = (ahead, slope, flux)
        return tuple(state)

    lax.fori_loop(0, blocks, block, tuple(state))


def diffuse(win, other, planes, coef, shift, rows):
    fill_shift(shift)

    def weight(c, index):
        return coef[c, pl.ds(index, 1), :]

    def two(t, carry):
        advance(win, other, planes, weight, shift, rows)
        advance(other, win, planes, weight, shift, rows)
        return carry

    for w in range(planes):
        other[w, :SUB, :] = jnp.zeros((SUB, LANES), jnp.float32)
        other[w, other.shape[1] - SUB * SUB :, :] = jnp.zeros((SUB * SUB, LANES), jnp.float32)
    lax.fori_loop(0, STEPS // 2, two, 0)


def own_kernel(field, above, below, coef, mid, win, other, shift):
    groups = field.shape[0]
    rows = mid.shape[1] // SUB
    halo = STEPS * SUB
    extend(win, field, above, below)
    diffuse(win, other, groups, coef, shift, rows)
    for g in range(groups):
        mid[g] = win[g, halo : halo + rows * SUB, :]


MERGE = 32


def strip_kernel(sizes, begin, aliased, earlier, *refs):
    loc, strips, from_west, from_east, coef, mid, low, high, norm_h = refs[:9]
    parts = refs[9 + aliased : 9 + aliased + earlier]
    refs = refs[9 + aliased + earlier :]
    if earlier:
        out_h, packed, sampled, turned = refs[:4]
    else:
        out_h, sampled = refs[:2]
    win, other, shift, smooth, norm, out, sems = refs[-7:]
    groups = mid.shape[0]
    rows = mid.shape[1] // SUB
    levels = pl.ds(begin, sum(sizes))
    copy = pltpu.make_async_copy(norm_h.at[levels], norm, sems.at[0])
    copy.start()
    build_strips(win.at[0], strips, from_west, from_east)
    diffuse(win, other, 1, coef, shift, rows)
    copy.wait()
    lane = iota((SUB, LANES), 1)
    outer = LANES - STEPS

    def merge(b, carry):
        done = []
        for u in range(MERGE):
            at = row_at(b * MERGE + u)
            strip = win[0, row_at(b * MERGE + u + STEPS), :]
            west = pltpu.roll(strip, outer, 1)
            east = pltpu.roll(strip, HALF + STEPS, 1)
            cells = mid[0, at, :]
            done.append((0, at, jnp.where(lane < STEPS, west, jnp.where(lane < outer, cells, east))))
            if groups == 2:
                both = pltpu.roll(jnp.where(lane < HALF, east, west), HALF, 1)
                cells = mid[1, at, :]
                done.append((1, at, jnp.where((lane < STEPS) | (lane >= outer), both, cells)))
        for g, at, value in done:
            smooth[g, at, :] = value
        return carry

    lax.fori_loop(0, rows // MERGE, merge, 0)

    def scale(i, carry):
        done = []
        for n in range(4):
            b = i * 4 + n
            own = pl.ds(pl.multiple_of(b * SUB, SUB), SUB)
            level = 0
            for g, size in enumerate(sizes):
                for l in range(size):
                    at = pl.ds(b * (SUB * SUB) + l, SUB, stride=SUB)
                    done.append((g, at, level, own, smooth[g, at, :] * norm[level, own, :]))
                    level += 1
        for g, at, level, own, value in done:
            out[level, own, :] = value
            smooth[g, at, :] = value
        return carry

    lax.fori_loop(0, rows // (4 * SUB), scale, 0)
    back = pltpu.make_async_copy(out, out_h.at[levels], sems.at[1])
    back.start()
    count = low.shape[0] // PER_ROW
    halves = count // LANES

    def samples(i, carry):
        h = i // PER_ROW
        k = i % PER_ROW
        kept = [[jnp.zeros((SUB, LANES), jnp.float32)] * 4 for _ in range(groups)]
        for seat in range(LANES):
            at = pl.multiple_of(loc[k, h * LANES + seat], SUB)
            lo = low[pl.ds(k * count + h * LANES + seat, 1), :]
            hi = high[pl.ds(k * count + h * LANES + seat, 1), :]
            for g in range(groups):
                value = smooth[g, pl.ds(at, SUB), :] * lo + smooth[g, pl.ds(at + SUB, SUB), :] * hi
                total = jnp.sum(value, axis=1, keepdims=True)
                kept[g][seat % 4] = jnp.where(lane == seat, total, kept[g][seat % 4])
        for g in range(groups):
            a, b, c, d = kept[g]
            sampled[h, g, row_at(k), :] = (a + b) + (c + d)
        return carry

    lax.fori_loop(0, halves * PER_ROW, samples, 0)
    if earlier:
        pack_samples(parts + (sampled,), packed, turned)
    back.wait()


def pack_samples(parts, out, turned):
    for h in range(turned.shape[0]):
        index = 0
        for part in parts:
            for g in range(part.shape[1]):
                for k in range(PER_ROW):
                    at = k * FEATS + index * SUB
                    turned[h, at : at + SUB, :] = part[h, g, k * SUB : (k + 1) * SUB, :]
                index += 1
        out[h * LANES : (h + 1) * LANES, :] = turned[h].T


def exchange_rows(up, down, n_lat):
    pairs = [(i, i + 1) for i in range(n_lat - 1)]
    back = [(i + 1, i) for i in range(n_lat - 1)]
    return lax.ppermute(up, "lat", pairs), lax.ppermute(down, "lat", back)


def exchange_columns(east, west, n_lon):
    pairs = [(i, (i + 1) % n_lon) for i in range(n_lon)]
    back = [((i + 1) % n_lon, i) for i in range(n_lon)]
    return lax.ppermute(east, "lon", pairs), lax.ppermute(west, "lon", back)


def on_device(
    innovations,
    owners,
    prof_row,
    prof_col,
    interp_weights,
    model_tiles,
    model_ids,
    face_x,
    face_y,
    cross_term,
    wet_mask,
    norm_factor,
):
    n_lat = lax.axis_size("lat")
    n_lon = lax.axis_size("lon")
    devices = n_lat * n_lon
    levels, lat_cells, lon_cells = norm_factor.shape
    tiles = model_tiles.shape[1]
    group = tiles // n_lon
    count = innovations.shape[1]
    cap = 2 * count // devices
    slots = devices * cap
    rows = slots // PER_ROW
    starts = group_starts()
    f32 = jnp.float32
    lat = lax.axis_index("lat").reshape(1)
    both = ("lat", "lon")
    span = span_of(lat_cells)
    ext_rows = SEATS * span
    win_rows = ext_rows + SUB

    def arrays(*shapes):
        return tuple(jax.ShapeDtypeStruct(shape, f32) for shape in shapes)

    def call(kernel, out_shape, micros, name, grant=SMALL, **kwargs):
        return pl.pallas_call(
            kernel,
            out_shape=out_shape,
            compiler_params=params(grant),
            cost_estimate=cost(micros),
            name=name,
            **kwargs,
        )

    def after(value, *others):
        return lax.optimization_barrier((value,) + others)[0]

    def tile_exchange(chunk, *others):
        first = sum(CHUNKS[:chunk])
        begin = starts[first]
        size = sum(GROUPS[first : first + CHUNKS[chunk]])
        piece = model_tiles[begin : begin + size].reshape(size, n_lon, group, SUB, LANES)
        piece = jnp.transpose(piece, (1, 0, 2, 3, 4))
        if others:
            piece = after(piece, *others)
        return lax.all_to_all(piece, "lon", split_axis=0, concat_axis=0, tiled=True)

    def halo(field, up, down, groups):
        above, below = exchange_rows(up, down, n_lat)
        strips, east, west = call(
            edges_kernel,
            arrays((ext_rows * SUB, LANES), (span * SUB, LANES), (span * SUB, LANES)),
            3,
            "edges",
            scratch_shapes=[pltpu.VMEM((groups, ext_rows * SUB, LANES), f32)],
        )(field, above, below)
        return (field, above, below, strips) + exchange_columns(east, west, n_lon)

    def field_shapes(groups):
        return arrays(
            (groups, lat_cells * SUB, LANES),
            (groups, STEPS * SUB, LANES),
            (groups, STEPS * SUB, LANES),
        )

    send, slot = call(
        functools.partial(route_kernel, cap, group, n_lat, starts),
        (jax.ShapeDtypeStruct((rows, LANES), f32), jax.ShapeDtypeStruct((1, count), jnp.int32)),
        3,
        "route",
        LARGE,
        scratch_shapes=[pltpu.VMEM((FEATS, count + devices * group), f32)],
    )(
        innovations,
        interp_weights,
        owners.reshape(1, count),
        prof_row.reshape(1, count),
        prof_col.reshape(1, count),
        model_ids,
    )
    stacked = call(stack_kernel, field_shapes(1), 3, "stack")(face_x, face_y, cross_term, wet_mask)
    own_coef, strip_coef = call(
        coef_kernel,
        arrays((5, win_rows, LANES), (5, win_rows, LANES)),
        5,
        "coef",
        LARGE,
        scratch_shapes=[
            pltpu.VMEM((1, (win_rows + SUB) * SUB, LANES), f32),
            pltpu.VMEM(((win_rows + SUB) * SUB, LANES), f32),
        ],
    )(*halo(*stacked, 1))

    recv = lax.all_to_all(
        send.reshape(devices, rows // devices, LANES), both, split_axis=0, concat_axis=0, tiled=True
    ).reshape(rows, LANES)
    pieces = [tile_exchange(0, recv, stacked[0])]

    obs, low, high, loc = call(
        scatter_kernel,
        arrays((len(GROUPS), lat_cells * SUB, LANES), (slots, LANES), (slots, LANES))
        + (jax.ShapeDtypeStruct((2 * PER_ROW, rows), jnp.int32),),
        15,
        "scatter",
        LARGE,
        scratch_shapes=[
            pltpu.VMEM((rows // LANES, LANES, LANES), f32),
            pltpu.VMEM((2 * PER_ROW, rows), jnp.int32),
            pltpu.SMEM((2 * PER_ROW, rows), jnp.int32),
            pltpu.SemaphoreType.DMA,
        ],
    )(recv)

    pieces.append(tile_exchange(1, pieces[0], obs, own_coef))
    smem = pl.BlockSpec(memory_space=pltpu.SMEM)
    vmem = pl.BlockSpec(memory_space=pltpu.VMEM)
    hbm = pl.BlockSpec(memory_space=pltpu.HBM)
    shift_space = pltpu.VMEM((2 * LANES, 2 * LANES), jnp.bfloat16)
    smoothed = None
    sampled = []
    first = 0
    for chunk, groups in enumerate(CHUNKS):
        sizes = GROUPS[first : first + groups]
        begin = starts[first]
        own_levels = (sum(sizes), lat_cells, LANES)
        field = call(
            functools.partial(field_kernel, first, begin, sizes, n_lon, group, cap),
            field_shapes(groups),
            4,
            "field",
            LARGE,
            in_specs=[smem, smem, vmem, hbm, hbm],
            scratch_shapes=[
                pltpu.VMEM((groups, lat_cells * SUB, LANES), f32),
                pltpu.VMEM(own_levels, f32),
                pltpu.SemaphoreType.DMA((2,)),
            ],
        )(loc, lat, pieces[chunk], obs, norm_factor)
        field, above, below, strips, from_west, from_east = halo(*field, groups)
        mid_shape = (groups, lat_cells * SUB, LANES)
        win_shape = (groups, win_rows * SUB, LANES)
        mid = call(
            own_kernel,
            arrays(mid_shape)[0],
            6 * groups,
            "own",
            scratch_shapes=[pltpu.VMEM(win_shape, f32), pltpu.VMEM(win_shape, f32), shift_space],
        )(after(field, strips), above, below, own_coef)
        operands = [loc, strips, from_west, from_east, strip_coef, mid, low, high, norm_factor]
        specs = [smem] + [vmem] * 7 + [hbm]
        aliases = {}
        if smoothed is not None:
            aliases = {len(operands): 0}
            operands.append(smoothed)
            specs.append(hbm)
        last = chunk + 1 == len(CHUNKS)
        earlier = sampled if last else []
        part_shape = (rows // LANES, groups, PER_ROW * SUB, LANES)
        gathered = [pltpu.VMEM(part_shape, f32), pltpu.VMEM((rows // LANES, LANES, LANES), f32)]
        smoothed, part = call(
            functools.partial(strip_kernel, sizes, begin, len(aliases), len(earlier)),
            arrays(norm_factor.shape, (rows, LANES) if earlier else part_shape),
            12,
            "strips",
            in_specs=specs + [vmem] * len(earlier),
            out_specs=(hbm, vmem),
            scratch_shapes=(gathered if earlier else [])
            + [
                pltpu.VMEM((1,) + win_shape[1:], f32),
                pltpu.VMEM((1,) + win_shape[1:], f32),
                shift_space,
                pltpu.VMEM(mid_shape, f32),
                pltpu.VMEM(own_levels, f32),
                pltpu.VMEM(own_levels, f32),
                pltpu.SemaphoreType.DMA((2,)),
            ],
            input_output_aliases=aliases,
        )(*operands, *earlier)
        sampled.append(part)
        first += groups
        if not last:
            pieces[chunk + 1] = after(pieces[chunk + 1], part)

    back = sampled[-1]
    returned = lax.all_to_all(
        back.reshape(devices, rows // devices, LANES), both, split_axis=0, concat_axis=0, tiled=True
    ).reshape(rows, LANES)
    profile_values = call(
        functools.partial(unpack_kernel, starts),
        arrays((levels, count))[0],
        1,
        "unpack",
    )(returned, slot)
    return (smoothed, profile_values)


def solution(mesh):
    in_specs = (
        P(None, ("lat", "lon")),
        P(("lat", "lon"), None),
        P(("lat", "lon")),
        P(("lat", "lon")),
        P(None, ("lat", "lon")),
        P(None, ("lat", "lon"), None, None),
        P(None, ("lat", "lon")),
        P("lat", "lon"),
        P("lat", "lon"),
        P("lat", "lon"),
        P("lat", "lon"),
        P(None, "lat", "lon"),
    )
    out_specs = (P(None, "lat", "lon"), P(None, ("lat", "lon")))
    return jax.shard_map(
        on_device, mesh=mesh, in_specs=in_specs, out_specs=out_specs, check_vma=False
    )
```

```python
import functools
import jax
import jax.numpy as jnp
from jax import lax
from jax.experimental import pallas as pl
from jax.experimental.pallas import tpu as pltpu
from jax.sharding import PartitionSpec as P

STEPS = 10
SUB = 8
LANES = 128
FEATS = 32
PER_ROW = LANES // FEATS
GROUPS = (5, 4, 8, 8)
CHUNKS = (2, 2)
WEIGHT_ROWS = (5, 6, 12, 13)
LOC_ROW = 7
ID_ROW = 15
SMALL = 20 * 1024 * 1024
LARGE = 60 * 1024 * 1024


def group_starts():
    starts = []
    total = 0
    for count in GROUPS:
        starts.append(total)
        total += count
    return starts


def params(grant):
    return pltpu.CompilerParams(vmem_limit_bytes=grant)


def cost(micros):
    return pl.CostEstimate(flops=0, bytes_accessed=int(micros * 3.6e6), transcendentals=0)


def iota(shape, dim):
    return lax.broadcasted_iota(jnp.int32, shape, dim)


def split3(values):
    high = values.astype(jnp.bfloat16)
    rest = values - high.astype(jnp.float32)
    middle = rest.astype(jnp.bfloat16)
    low = (rest - middle.astype(jnp.float32)).astype(jnp.bfloat16)
    return high, middle, low


def route_kernel(cap, group, copies, starts, innov, weights, own_row, prow, pcol, ids, send, slot_out, pay):
    count = innov.shape[1]
    tiles = ids.shape[1]
    extra = tiles * copies
    owner = own_row[...]
    column = jnp.broadcast_to(owner.astype(jnp.float32), (SUB, count)).T[:, :1].astype(jnp.int32)
    same = column == owner
    before = iota((count, count), 0) < iota((count, count), 1)
    ones = jnp.where(same & before, 1.0, 0.0)
    rank = jnp.sum(ones, axis=0, keepdims=True).astype(jnp.int32)
    slot = owner * cap + rank
    slot_out[...] = slot
    number = iota((1, extra), 1)
    id_slot = (number // group) * cap + number % group
    pay[...] = jnp.zeros_like(pay)
    for index, count_in in enumerate(GROUPS):
        pay[index * SUB : index * SUB + count_in, :count] = innov[starts[index] : starts[index] + count_in, :]
    for corner, row in enumerate(WEIGHT_ROWS):
        pay[row : row + 1, :count] = weights[corner : corner + 1, :]
    pay[LOC_ROW : LOC_ROW + 1, :count] = (prow[...] * LANES + pcol[...]).astype(jnp.float32)
    for i in range(copies):
        at = count + i * tiles
        pay[ID_ROW : ID_ROW + 1, at : at + tiles] = ids[...].astype(jnp.float32)
    slots = jnp.concatenate([slot, id_slot], axis=1)
    values = pay[...]
    part = slots % PER_ROW
    spread = jnp.concatenate([jnp.where(part == k, values, 0.0) for k in range(PER_ROW)], axis=0)
    rows = send.shape[0]
    hot = jnp.where(iota((rows, count + extra), 0) == slots // PER_ROW, 1.0, 0.0).astype(jnp.bfloat16)
    total = None
    for piece in split3(spread):
        term = lax.dot_general(hot, piece, (((1,), (1,)), ((), ())), preferred_element_type=jnp.float32)
        total = term if total is None else total + term
    send[...] = total


def unpack_kernel(starts, recv, slot, out):
    slots = slot[...]
    rows = recv.shape[0]
    hot = jnp.where(iota((rows, slots.shape[1]), 0) == slots // PER_ROW, 1.0, 0.0).astype(jnp.bfloat16)
    total = None
    for piece in split3(recv[...]):
        term = lax.dot_general(piece, hot, (((0,), (0,)), ((), ())), preferred_element_type=jnp.float32)
        total = term if total is None else total + term
    part = slots % PER_ROW
    picked = jnp.zeros((FEATS, slots.shape[1]), jnp.float32)
    for k in range(PER_ROW):
        picked = jnp.where(part == k, total[k * FEATS : (k + 1) * FEATS], picked)
    for index, count_in in enumerate(GROUPS):
        out[starts[index] : starts[index] + count_in, :] = picked[index * SUB : index * SUB + count_in]


def turn_slots(recv, turned):
    for h in range(recv.shape[0] // LANES):
        turned[h] = recv[h * LANES : (h + 1) * LANES, :].T


def place_kernel(recv, low, high, loc_out, turned):
    rows = recv.shape[0]
    turn_slots(recv, turned)
    for k in range(PER_ROW):
        for h in range(rows // LANES):
            at = k * FEATS
            cut = slice(h * LANES, (h + 1) * LANES)
            cells = turned[h, at + LOC_ROW : at + LOC_ROW + 1, :].astype(jnp.int32)
            loc_out[k : k + 1, cut] = cells // LANES * SUB
            loc_out[PER_ROW + k : PER_ROW + k + 1, cut] = turned[h, at + ID_ROW : at + ID_ROW + 1, :].astype(jnp.int32)
    lane = iota((rows, LANES), 1)
    for k in range(PER_ROW):
        at = k * FEATS
        col = recv[:, at + LOC_ROW : at + LOC_ROW + 1].astype(jnp.int32) % LANES
        w = [recv[:, at + row : at + row + 1] for row in WEIGHT_ROWS]
        here = lane == col
        after = lane == col + 1
        low[k * rows : (k + 1) * rows, :] = jnp.where(here, w[0], jnp.where(after, w[1], 0.0))
        high[k * rows : (k + 1) * rows, :] = jnp.where(here, w[2], jnp.where(after, w[3], 0.0))


def scatter_kernel(first, loc, recv, low, high, obs, turned):
    rows = recv.shape[0]
    groups = range(obs.shape[0])
    turn_slots(recv, turned)

    def clear(i, carry):
        for g in groups:
            obs[g, pl.ds(pl.multiple_of(i * 64, 64), 64), :] = jnp.zeros((64, LANES), jnp.float32)
        return carry

    lax.fori_loop(0, obs.shape[1] // 64, clear, 0)

    def body(i, carry):
        h = i // PER_ROW
        k = i % PER_ROW
        size = len(groups) * SUB
        block = turned[h, pl.ds(pl.multiple_of(k * FEATS + first * SUB, SUB), size), :]
        for seat in range(LANES):
            at = pl.multiple_of(loc[k, h * LANES + seat], SUB)
            lo = low[pl.ds(k * rows + h * LANES + seat, 1), :]
            hi = high[pl.ds(k * rows + h * LANES + seat, 1), :]
            values = [block[g * SUB : (g + 1) * SUB, seat : seat + 1] for g in groups]
            old0 = [obs[g, pl.ds(at, SUB), :] for g in groups]
            old1 = [obs[g, pl.ds(at + SUB, SUB), :] for g in groups]
            for g in groups:
                obs[g, pl.ds(at, SUB), :] = old0[g] + values[g] * lo
                obs[g, pl.ds(at + SUB, SUB), :] = old1[g] + values[g] * hi
        return carry

    lax.fori_loop(0, (rows // LANES) * PER_ROW, body, 0)


def row_at(index):
    return pl.ds(pl.multiple_of(index * SUB, SUB), SUB)


def rows_at(index, count):
    return pl.ds(pl.multiple_of(index * SUB, SUB), count * SUB)


def send_rows(field, up, down):
    edge = up.shape[1]
    total = field.shape[1]
    for g in range(field.shape[0]):
        up[g] = field[g, total - edge :, :]
        down[g] = field[g, :edge, :]


def field_kernel(begin, sizes, n_lon, group, cap, loc, lat, tiles, obs, norm_h, field, up, down, norm, sem):
    copy = pltpu.make_async_copy(norm_h.at[pl.ds(begin, sum(sizes))], norm, sem)
    copy.start()
    field[...] = jnp.zeros_like(field)
    copy.wait()

    def body(j, carry):
        done = []
        for c in range(group):
            slot = (lat[0] * n_lon + j) * cap + c
            t = loc[PER_ROW + slot % PER_ROW, slot // PER_ROW]
            own = pl.ds(pl.multiple_of(t * SUB, SUB), SUB)
            level = 0
            for g, size in enumerate(sizes):
                for l in range(size):
                    at = pl.ds(t * (SUB * SUB) + l, SUB, stride=SUB)
                    done.append((g, at, norm[level, own, :] * (obs[g, at, :] + tiles[j, level, c])))
                    level += 1
        for g, at, value in done:
            field[g, at, :] = value
        return carry

    lax.fori_loop(0, n_lon, body, 0)
    send_rows(field, up, down)


def stack_kernel(face_x, face_y, cross, wet, field, up, down):
    field[...] = jnp.zeros_like(field)
    sources = (face_x, face_y, cross, wet)

    def body(i, carry):
        values = []
        for n in range(4):
            t = i * 4 + n
            own = pl.ds(pl.multiple_of(t * SUB, SUB), SUB)
            values += [(t, l, source[own, :].astype(jnp.float32)) for l, source in enumerate(sources)]
        for t, l, value in values:
            field[0, pl.ds(t * (SUB * SUB) + l, SUB, stride=SUB), :] = value
        return carry

    lax.fori_loop(0, face_x.shape[0] // SUB // 4, body, 0)
    send_rows(field, up, down)


STRIP = 32
HALF = 2 * STRIP
SEAT = 16
SEATS = HALF // SEAT
TURNS = 10


def span_of(rows):
    return -(-(rows + 2 * STEPS) // (SEATS * TURNS)) * TURNS


def extend(ext, field, above, below):
    groups, total, _ = field.shape
    halo = STEPS * SUB
    for g in range(groups):
        ext[g, :halo, :] = above[g]
        ext[g, halo : halo + total, :] = field[g]
        ext[g, halo + total : 2 * halo + total, :] = below[g]
        ext[g, 2 * halo + total :, :] = jnp.zeros((ext.shape[1] - 2 * halo - total, LANES), jnp.float32)


def edges_kernel(field, above, below, strips, east, west, ext):
    groups = field.shape[0]
    extend(ext, field, above, below)
    span = east.shape[0] // SUB
    lane = iota((SUB, LANES), 1)
    place = lane % HALF

    def body(i, carry):
        done = []
        for n in range(TURNS // 2):
            m = i * (TURNS // 2) + n
            to_east = None
            to_west = None
            for q in range(SEATS):
                first = ext[0, row_at(q * span + m), :]
                second = pltpu.roll(ext[groups - 1, row_at(q * span + m), :], HALF, 1)
                left = jnp.where(lane < HALF, first, second)
                right = jnp.where(lane < HALF, second, first)
                row = jnp.where(place < STRIP, pltpu.roll(left, STEPS, 1), pltpu.roll(right, HALF - STEPS, 1))
                done.append((strips, q * span + m, row))
                right = pltpu.roll(right, SEAT * q + SEAT, 1)
                if q:
                    left = pltpu.roll(left, SEAT * q, 1)
                mine = place // SEAT == q
                to_east = right if q == 0 else jnp.where(mine, right, to_east)
                to_west = left if q == 0 else jnp.where(mine, left, to_west)
            done.append((east, m, to_east))
            done.append((west, m, to_west))
        for ref, m, value in done:
            ref[row_at(m), :] = value
        return carry

    lax.fori_loop(0, span // (TURNS // 2), body, 0)


def build_strips(win, strips, from_west, from_east):
    span = from_west.shape[0] // SUB
    place = iota((SUB, LANES), 1) % HALF

    def body(i, carry):
        done = []
        for n in range(TURNS):
            m = i * TURNS + n
            west = from_west[row_at(m), :]
            east = from_east[row_at(m), :]
            for q in range(SEATS):
                a = pltpu.roll(west, (STEPS - SEAT - SEAT * q) % LANES, 1)
                b = pltpu.roll(east, (HALF - STEPS - SEAT * q) % LANES, 1)
                row = strips[row_at(q * span + m), :]
                row = jnp.where(place < STEPS, a, jnp.where(place < HALF - STEPS, row, b))
                done.append((q * span + m, row))
        for m, row in done:
            win[row_at(m), :] = row
        return carry

    lax.fori_loop(0, span // TURNS, body, 0)
    first = SEATS * span * SUB
    win[first:, :] = jnp.zeros((win.shape[0] - first, LANES), jnp.float32)


def fill_coef(coef, win):
    rows = coef.shape[1]

    def body(i, carry):
        done = []
        for n in range(4):
            b = i * 4 + n
            base = b * (SUB * SUB)
            at = pl.ds(pl.multiple_of(b * SUB, SUB), SUB)
            fx, fy, ct, wet = (win[pl.ds(base + s, SUB, stride=SUB), :] for s in range(4))
            wet_n = win[pl.ds(base + SUB + 3, SUB, stride=SUB), :]
            x = fx * wet * pltpu.roll(wet, LANES - 1, 1)
            xw = pltpu.roll(x, 1, 1)
            y = fy * wet * wet_n
            twist = 0.25 * ct * wet
            for c, value in enumerate((1.0 - x - xw, x, xw, y, twist)):
                done.append((c, at, value))
        for c, at, value in done:
            coef[c, at, :] = value
        return carry

    lax.fori_loop(0, rows // (4 * SUB), body, 0)


def own_coef_kernel(field, above, below, coef, ext):
    extend(ext, field, above, below)
    fill_coef(coef, ext.at[0])


def strip_coef_kernel(strips, from_west, from_east, coef, win):
    build_strips(win, strips, from_west, from_east)
    fill_coef(coef, win)


BY_MATMUL = 0.25


def fill_shift(shift):
    row = iota(shift.shape, 0) % LANES
    col = iota(shift.shape, 1)
    near = jnp.where(col < LANES, col + 1, col + LANES - 1) % LANES
    shift[...] = jnp.where(row == near, 1.0, 0.0).astype(jnp.bfloat16)


def advance(source, target, planes, weight, shift, rows):
    last = rows + 2 * STEPS + 4
    unroll = last // planes
    blocks = last // unroll
    split = int(unroll * BY_MATMUL)

    def rolled(w, index):
        cells = source[w, row_at(index), :]
        east = pltpu.roll(cells, LANES - 1, 1)
        west = pltpu.roll(cells, 1, 1)
        return cells, east, west, east - west

    def shifted_rows(w, first):
        cells = source[w, rows_at(first, split), :]
        high = cells.astype(jnp.bfloat16)
        low = (cells - high.astype(jnp.float32)).astype(jnp.bfloat16)
        both = jnp.concatenate([high, low], axis=1)
        return jnp.dot(both, shift[...], preferred_element_type=jnp.float32)

    y_first = weight(3, 0)
    state = []
    for w in range(planes):
        before = rolled(w, 0)
        now = rolled(w, 1)
        state.append((now, before[3], y_first * (now[0] - before[0])))

    def block(b, state):
        base = 1 + b * unroll
        state = list(state)
        sides = [shifted_rows(w, base + 1) for w in range(planes)]
        for u in range(unroll):
            weights = [weight(c, base + u) for c in range(5)]
            for w in range(planes):
                (cells, east, west, slope), slope_s, flux_s = state[w]
                if u < split:
                    cells_n = source[w, row_at(base + u + 1), :]
                    east_n = sides[w][u * SUB : (u + 1) * SUB, :LANES]
                    west_n = sides[w][u * SUB : (u + 1) * SUB, LANES:]
                    ahead = (cells_n, east_n, west_n, east_n - west_n)
                else:
                    ahead = rolled(w, base + u + 1)
                flux = weights[3] * (ahead[0] - cells)
                target[w, row_at(base + u), :] = (
                    (weights[0] * cells + weights[1] * east)
                    + (weights[2] * west + (flux - flux_s))
                    + weights[4] * (ahead[3] - slope_s)
                )
                state[w] = (ahead, slope, flux)
        return tuple(state)

    lax.fori_loop(0, blocks, block, tuple(state))


def diffuse(win, other, planes, coef, shift, rows):
    fill_shift(shift)

    def weight(c, index):
        return coef[c, pl.ds(index, 1), :]

    def two(t, carry):
        advance(win, other, planes, weight, shift, rows)
        advance(other, win, planes, weight, shift, rows)
        return carry

    for w in range(planes):
        other[w, :SUB, :] = jnp.zeros((SUB, LANES), jnp.float32)
        other[w, other.shape[1] - SUB * SUB :, :] = jnp.zeros((SUB * SUB, LANES), jnp.float32)
    lax.fori_loop(0, STEPS // 2, two, 0)


def own_kernel(field, above, below, coef, mid, win, other, shift):
    groups = field.shape[0]
    rows = mid.shape[1] // SUB
    halo = STEPS * SUB
    extend(win, field, above, below)
    diffuse(win, other, groups, coef, shift, rows)
    for g in range(groups):
        mid[g] = win[g, halo : halo + rows * SUB, :]


MERGE = 32


def strip_kernel(sizes, begin, aliased, earlier, *refs):
    loc, strips, from_west, from_east, coef, mid, low, high, norm_h = refs[:9]
    parts = refs[9 + aliased : 9 + aliased + earlier]
    refs = refs[9 + aliased + earlier :]
    if earlier:
        out_h, packed, sampled, turned = refs[:4]
    else:
        out_h, sampled = refs[:2]
    win, other, shift, smooth, norm, out, sems = refs[-7:]
    groups = mid.shape[0]
    rows = mid.shape[1] // SUB
    levels = pl.ds(begin, sum(sizes))
    copy = pltpu.make_async_copy(norm_h.at[levels], norm, sems.at[0])
    copy.start()
    build_strips(win.at[0], strips, from_west, from_east)
    diffuse(win, other, 1, coef, shift, rows)
    copy.wait()
    lane = iota((SUB, LANES), 1)
    outer = LANES - STEPS

    def merge(b, carry):
        done = []
        for u in range(MERGE):
            at = row_at(b * MERGE + u)
            strip = win[0, row_at(b * MERGE + u + STEPS), :]
            west = pltpu.roll(strip, outer, 1)
            east = pltpu.roll(strip, HALF + STEPS, 1)
            cells = mid[0, at, :]
            done.append((0, at, jnp.where(lane < STEPS, west, jnp.where(lane < outer, cells, east))))
            if groups == 2:
                both = pltpu.roll(jnp.where(lane < HALF, east, west), HALF, 1)
                cells = mid[1, at, :]
                done.append((1, at, jnp.where((lane < STEPS) | (lane >= outer), both, cells)))
        for g, at, value in done:
            smooth[g, at, :] = value
        return carry

    lax.fori_loop(0, rows // MERGE, merge, 0)

    def scale(i, carry):
        done = []
        for n in range(4):
            b = i * 4 + n
            own = pl.ds(pl.multiple_of(b * SUB, SUB), SUB)
            level = 0
            for g, size in enumerate(sizes):
                for l in range(size):
                    at = pl.ds(b * (SUB * SUB) + l, SUB, stride=SUB)
                    done.append((g, at, level, own, smooth[g, at, :] * norm[level, own, :]))
                    level += 1
        for g, at, level, own, value in done:
            out[level, own, :] = value
            smooth[g, at, :] = value
        return carry

    lax.fori_loop(0, rows // (4 * SUB), scale, 0)
    back = pltpu.make_async_copy(out, out_h.at[levels], sems.at[1])
    back.start()
    count = low.shape[0] // PER_ROW
    halves = count // LANES

    def samples(i, carry):
        h = i // PER_ROW
        k = i % PER_ROW
        kept = [[jnp.zeros((SUB, LANES), jnp.float32)] * 4 for _ in range(groups)]
        for seat in range(LANES):
            at = pl.multiple_of(loc[k, h * LANES + seat], SUB)
            lo = low[pl.ds(k * count + h * LANES + seat, 1), :]
            hi = high[pl.ds(k * count + h * LANES + seat, 1), :]
            for g in range(groups):
                value = smooth[g, pl.ds(at, SUB), :] * lo + smooth[g, pl.ds(at + SUB, SUB), :] * hi
                total = jnp.sum(value, axis=1, keepdims=True)
                kept[g][seat % 4] = jnp.where(lane == seat, total, kept[g][seat % 4])
        for g in range(groups):
            a, b, c, d = kept[g]
            sampled[h, g, row_at(k), :] = (a + b) + (c + d)
        return carry

    lax.fori_loop(0, halves * PER_ROW, samples, 0)
    if earlier:
        pack_samples(parts + (sampled,), packed, turned)
    back.wait()


def pack_samples(parts, out, turned):
    for h in range(turned.shape[0]):
        index = 0
        for part in parts:
            for g in range(part.shape[1]):
                for k in range(PER_ROW):
                    at = k * FEATS + index * SUB
                    turned[h, at : at + SUB, :] = part[h, g, k * SUB : (k + 1) * SUB, :]
                index += 1
        out[h * LANES : (h + 1) * LANES, :] = turned[h].T


def exchange_rows(up, down, n_lat):
    pairs = [(i, i + 1) for i in range(n_lat - 1)]
    back = [(i + 1, i) for i in range(n_lat - 1)]
    return lax.ppermute(up, "lat", pairs), lax.ppermute(down, "lat", back)


def exchange_columns(east, west, n_lon):
    pairs = [(i, (i + 1) % n_lon) for i in range(n_lon)]
    back = [((i + 1) % n_lon, i) for i in range(n_lon)]
    return lax.ppermute(east, "lon", pairs), lax.ppermute(west, "lon", back)


def on_device(
    innovations,
    owners,
    prof_row,
    prof_col,
    interp_weights,
    model_tiles,
    model_ids,
    face_x,
    face_y,
    cross_term,
    wet_mask,
    norm_factor,
):
    n_lat = lax.axis_size("lat")
    n_lon = lax.axis_size("lon")
    devices = n_lat * n_lon
    levels, lat_cells, lon_cells = norm_factor.shape
    tiles = model_tiles.shape[1]
    group = tiles // n_lon
    count = innovations.shape[1]
    cap = 2 * count // devices
    slots = devices * cap
    rows = slots // PER_ROW
    starts = group_starts()
    f32 = jnp.float32
    lat = lax.axis_index("lat").reshape(1)
    both = ("lat", "lon")
    span = span_of(lat_cells)
    ext_rows = SEATS * span
    win_rows = ext_rows + SUB

    def arrays(*shapes):
        return tuple(jax.ShapeDtypeStruct(shape, f32) for shape in shapes)

    def call(kernel, out_shape, micros, name, grant=SMALL, **kwargs):
        return pl.pallas_call(
            kernel,
            out_shape=out_shape,
            compiler_params=params(grant),
            cost_estimate=cost(micros),
            name=name,
            **kwargs,
        )

    def after(value, *others):
        return lax.optimization_barrier((value,) + others)[0]

    def tile_exchange(chunk, *others):
        first = sum(CHUNKS[:chunk])
        begin = starts[first]
        size = sum(GROUPS[first : first + CHUNKS[chunk]])
        piece = model_tiles[begin : begin + size].reshape(size, n_lon, group, SUB, LANES)
        piece = jnp.transpose(piece, (1, 0, 2, 3, 4))
        if others:
            piece = after(piece, *others)
        return lax.all_to_all(piece, "lon", split_axis=0, concat_axis=0, tiled=True)

    def halo(field, up, down, groups):
        above, below = exchange_rows(up, down, n_lat)
        strips, east, west = call(
            edges_kernel,
            arrays((ext_rows * SUB, LANES), (span * SUB, LANES), (span * SUB, LANES)),
            3,
            "edges",
            scratch_shapes=[pltpu.VMEM((groups, ext_rows * SUB, LANES), f32)],
        )(field, above, below)
        return (field, above, below, strips) + exchange_columns(east, west, n_lon)

    def field_shapes(groups):
        return arrays(
            (groups, lat_cells * SUB, LANES),
            (groups, STEPS * SUB, LANES),
            (groups, STEPS * SUB, LANES),
        )

    send, slot = call(
        functools.partial(route_kernel, cap, group, n_lat, starts),
        (jax.ShapeDtypeStruct((rows, LANES), f32), jax.ShapeDtypeStruct((1, count), jnp.int32)),
        3,
        "route",
        LARGE,
        scratch_shapes=[pltpu.VMEM((FEATS, count + devices * group), f32)],
    )(
        innovations,
        interp_weights,
        owners.reshape(1, count),
        prof_row.reshape(1, count),
        prof_col.reshape(1, count),
        model_ids,
    )
    stacked = call(stack_kernel, field_shapes(1), 3, "stack")(face_x, face_y, cross_term, wet_mask)
    stack, above, below, strips, from_west, from_east = halo(*stacked, 1)
    own_coef = call(
        own_coef_kernel,
        arrays((5, win_rows, LANES))[0],
        3,
        "own_coef",
        scratch_shapes=[pltpu.VMEM((1, (win_rows + SUB) * SUB, LANES), f32)],
    )(stack, above, below)
    strip_coef = call(
        strip_coef_kernel,
        arrays((5, win_rows, LANES))[0],
        3,
        "strip_coef",
        scratch_shapes=[pltpu.VMEM(((win_rows + SUB) * SUB, LANES), f32)],
    )(strips, from_west, from_east)

    recv = lax.all_to_all(
        send.reshape(devices, rows // devices, LANES), both, split_axis=0, concat_axis=0, tiled=True
    ).reshape(rows, LANES)
    pieces = [tile_exchange(0, recv, stacked[0])]

    smem = pl.BlockSpec(memory_space=pltpu.SMEM)
    vmem = pl.BlockSpec(memory_space=pltpu.VMEM)
    hbm = pl.BlockSpec(memory_space=pltpu.HBM)
    turned = pltpu.VMEM((rows // LANES, LANES, LANES), f32)
    low, high, loc = call(
        place_kernel,
        arrays((slots, LANES), (slots, LANES)) + (jax.ShapeDtypeStruct((2 * PER_ROW, rows), jnp.int32),),
        2,
        "place",
        LARGE,
        scratch_shapes=[turned],
    )(recv)

    def scatter(chunk, grant):
        first = sum(CHUNKS[:chunk])
        return call(
            functools.partial(scatter_kernel, first),
            arrays((CHUNKS[chunk], lat_cells * SUB, LANES))[0],
            9,
            "scatter",
            grant,
            in_specs=[smem, vmem, vmem, vmem],
            scratch_shapes=[turned],
        )(loc, recv, low, high)

    observed = [scatter(0, LARGE), scatter(1, SMALL)]
    pieces.append(tile_exchange(1, pieces[0], observed[0], own_coef))
    shift_space = pltpu.VMEM((2 * LANES, 2 * LANES), jnp.bfloat16)
    smoothed = None
    sampled = []
    first = 0
    for chunk, groups in enumerate(CHUNKS):
        sizes = GROUPS[first : first + groups]
        begin = starts[first]
        own_levels = (sum(sizes), lat_cells, LANES)
        field = call(
            functools.partial(field_kernel, begin, sizes, n_lon, group, cap),
            field_shapes(groups),
            4,
            "field",
            in_specs=[smem, smem, vmem, vmem, hbm],
            scratch_shapes=[pltpu.VMEM(own_levels, f32), pltpu.SemaphoreType.DMA],
        )(loc, lat, pieces[chunk], observed[chunk], norm_factor)
        field, above, below, strips, from_west, from_east = halo(*field, groups)
        mid_shape = (groups, lat_cells * SUB, LANES)
        win_shape = (groups, win_rows * SUB, LANES)
        mid = call(
            own_kernel,
            arrays(mid_shape)[0],
            6 * groups,
            "own",
            scratch_shapes=[pltpu.VMEM(win_shape, f32), pltpu.VMEM(win_shape, f32), shift_space],
        )(after(field, strips), above, below, own_coef)
        if chunk == 0:
            strips = after(strips, *observed[1:], strip_coef)
        operands = [loc, strips, from_west, from_east, strip_coef, mid, low, high, norm_factor]
        specs = [smem] + [vmem] * 7 + [hbm]
        aliases = {}
        if smoothed is not None:
            aliases = {len(operands): 0}
            operands.append(smoothed)
            specs.append(hbm)
        last = chunk + 1 == len(CHUNKS)
        earlier = sampled if last else []
        part_shape = (rows // LANES, groups, PER_ROW * SUB, LANES)
        gathered = [pltpu.VMEM(part_shape, f32), pltpu.VMEM((rows // LANES, LANES, LANES), f32)]
        smoothed, part = call(
            functools.partial(strip_kernel, sizes, begin, len(aliases), len(earlier)),
            arrays(norm_factor.shape, (rows, LANES) if earlier else part_shape),
            12,
            "strips",
            in_specs=specs + [vmem] * len(earlier),
            out_specs=(hbm, vmem),
            scratch_shapes=(gathered if earlier else [])
            + [
                pltpu.VMEM((1,) + win_shape[1:], f32),
                pltpu.VMEM((1,) + win_shape[1:], f32),
                shift_space,
                pltpu.VMEM(mid_shape, f32),
                pltpu.VMEM(own_levels, f32),
                pltpu.VMEM(own_levels, f32),
                pltpu.SemaphoreType.DMA((2,)),
            ],
            input_output_aliases=aliases,
        )(*operands, *earlier)
        sampled.append(part)
        first += groups
        if not last:
            pieces[chunk + 1] = after(pieces[chunk + 1], part)

    back = sampled[-1]
    returned = lax.all_to_all(
        back.reshape(devices, rows // devices, LANES), both, split_axis=0, concat_axis=0, tiled=True
    ).reshape(rows, LANES)
    profile_values = call(
        functools.partial(unpack_kernel, starts),
        arrays((levels, count))[0],
        1,
        "unpack",
    )(returned, slot)
    return (smoothed, profile_values)


def solution(mesh):
    in_specs = (
        P(None, ("lat", "lon")),
        P(("lat", "lon"), None),
        P(("lat", "lon")),
        P(("lat", "lon")),
        P(None, ("lat", "lon")),
        P(None, ("lat", "lon"), None, None),
        P(None, ("lat", "lon")),
        P("lat", "lon"),
        P("lat", "lon"),
        P("lat", "lon"),
        P("lat", "lon"),
        P(None, "lat", "lon"),
    )
    out_specs = (P(None, "lat", "lon"), P(None, ("lat", "lon")))
    return jax.shard_map(
        on_device, mesh=mesh, in_specs=in_specs, out_specs=out_specs, check_vma=False
    )
```

```python
import functools
import jax
import jax.numpy as jnp
from jax import lax
from jax.experimental import pallas as pl
from jax.experimental.pallas import tpu as pltpu
from jax.sharding import PartitionSpec as P

STEPS = 10
SUB = 8
LANES = 128
FEATS = 32
PER_ROW = LANES // FEATS
GROUPS = (5, 4, 8, 8)
CHUNKS = (2, 2)
WEIGHT_ROWS = (5, 6, 12, 13)
LOC_ROW = 7
ID_ROW = 15
SMALL = 20 * 1024 * 1024
LARGE = 60 * 1024 * 1024


def group_starts():
    starts = []
    total = 0
    for count in GROUPS:
        starts.append(total)
        total += count
    return starts


def params(grant):
    return pltpu.CompilerParams(vmem_limit_bytes=grant)


def cost(micros):
    return pl.CostEstimate(flops=0, bytes_accessed=int(micros * 3.6e6), transcendentals=0)


def iota(shape, dim):
    return lax.broadcasted_iota(jnp.int32, shape, dim)


def split3(values):
    high = values.astype(jnp.bfloat16)
    rest = values - high.astype(jnp.float32)
    middle = rest.astype(jnp.bfloat16)
    low = (rest - middle.astype(jnp.float32)).astype(jnp.bfloat16)
    return high, middle, low


def route_kernel(cap, group, copies, starts, innov, weights, own_row, prow, pcol, ids, send, slot_out, pay):
    count = innov.shape[1]
    tiles = ids.shape[1]
    extra = tiles * copies
    owner = own_row[...]
    column = jnp.broadcast_to(owner.astype(jnp.float32), (SUB, count)).T[:, :1].astype(jnp.int32)
    same = column == owner
    before = iota((count, count), 0) < iota((count, count), 1)
    ones = jnp.where(same & before, 1.0, 0.0)
    rank = jnp.sum(ones, axis=0, keepdims=True).astype(jnp.int32)
    slot = owner * cap + rank
    slot_out[...] = slot
    number = iota((1, extra), 1)
    id_slot = (number // group) * cap + number % group
    pay[...] = jnp.zeros_like(pay)
    for index, count_in in enumerate(GROUPS):
        pay[index * SUB : index * SUB + count_in, :count] = innov[starts[index] : starts[index] + count_in, :]
    for corner, row in enumerate(WEIGHT_ROWS):
        pay[row : row + 1, :count] = weights[corner : corner + 1, :]
    pay[LOC_ROW : LOC_ROW + 1, :count] = (prow[...] * LANES + pcol[...]).astype(jnp.float32)
    for i in range(copies):
        at = count + i * tiles
        pay[ID_ROW : ID_ROW + 1, at : at + tiles] = ids[...].astype(jnp.float32)
    slots = jnp.concatenate([slot, id_slot], axis=1)
    values = pay[...]
    part = slots % PER_ROW
    spread = jnp.concatenate([jnp.where(part == k, values, 0.0) for k in range(PER_ROW)], axis=0)
    rows = send.shape[0]
    hot = jnp.where(iota((rows, count + extra), 0) == slots // PER_ROW, 1.0, 0.0).astype(jnp.bfloat16)
    total = None
    for piece in split3(spread):
        term = lax.dot_general(hot, piece, (((1,), (1,)), ((), ())), preferred_element_type=jnp.float32)
        total = term if total is None else total + term
    send[...] = total


def unpack_kernel(starts, recv, slot, out):
    slots = slot[...]
    rows = recv.shape[0]
    hot = jnp.where(iota((rows, slots.shape[1]), 0) == slots // PER_ROW, 1.0, 0.0).astype(jnp.bfloat16)
    total = None
    for piece in split3(recv[...]):
        term = lax.dot_general(piece, hot, (((0,), (0,)), ((), ())), preferred_element_type=jnp.float32)
        total = term if total is None else total + term
    part = slots % PER_ROW
    picked = jnp.zeros((FEATS, slots.shape[1]), jnp.float32)
    for k in range(PER_ROW):
        picked = jnp.where(part == k, total[k * FEATS : (k + 1) * FEATS], picked)
    for index, count_in in enumerate(GROUPS):
        out[starts[index] : starts[index] + count_in, :] = picked[index * SUB : index * SUB + count_in]


def turn_slots(recv, turned):
    for h in range(recv.shape[0] // LANES):
        turned[h] = recv[h * LANES : (h + 1) * LANES, :].T


def place_kernel(recv, low, high, loc_out, turned):
    rows = recv.shape[0]
    turn_slots(recv, turned)
    for k in range(PER_ROW):
        for h in range(rows // LANES):
            at = k * FEATS
            cut = slice(h * LANES, (h + 1) * LANES)
            cells = turned[h, at + LOC_ROW : at + LOC_ROW + 1, :].astype(jnp.int32)
            loc_out[k : k + 1, cut] = cells // LANES * SUB
            loc_out[PER_ROW + k : PER_ROW + k + 1, cut] = turned[h, at + ID_ROW : at + ID_ROW + 1, :].astype(jnp.int32)
    lane = iota((rows, LANES), 1)
    for k in range(PER_ROW):
        at = k * FEATS
        col = recv[:, at + LOC_ROW : at + LOC_ROW + 1].astype(jnp.int32) % LANES
        w = [recv[:, at + row : at + row + 1] for row in WEIGHT_ROWS]
        here = lane == col
        after = lane == col + 1
        low[k * rows : (k + 1) * rows, :] = jnp.where(here, w[0], jnp.where(after, w[1], 0.0))
        high[k * rows : (k + 1) * rows, :] = jnp.where(here, w[2], jnp.where(after, w[3], 0.0))


def scatter_kernel(first, loc, recv, low, high, obs, turned):
    rows = recv.shape[0]
    groups = range(obs.shape[0])
    turn_slots(recv, turned)

    def clear(i, carry):
        for g in groups:
            obs[g, pl.ds(pl.multiple_of(i * 64, 64), 64), :] = jnp.zeros((64, LANES), jnp.float32)
        return carry

    lax.fori_loop(0, obs.shape[1] // 64, clear, 0)

    def body(i, carry):
        h = i // PER_ROW
        k = i % PER_ROW
        size = len(groups) * SUB
        block = turned[h, pl.ds(pl.multiple_of(k * FEATS + first * SUB, SUB), size), :]
        for seat in range(LANES):
            at = pl.multiple_of(loc[k, h * LANES + seat], SUB)
            lo = low[pl.ds(k * rows + h * LANES + seat, 1), :]
            hi = high[pl.ds(k * rows + h * LANES + seat, 1), :]
            values = [block[g * SUB : (g + 1) * SUB, seat : seat + 1] for g in groups]
            old0 = [obs[g, pl.ds(at, SUB), :] for g in groups]
            old1 = [obs[g, pl.ds(at + SUB, SUB), :] for g in groups]
            for g in groups:
                obs[g, pl.ds(at, SUB), :] = old0[g] + values[g] * lo
                obs[g, pl.ds(at + SUB, SUB), :] = old1[g] + values[g] * hi
        return carry

    lax.fori_loop(0, (rows // LANES) * PER_ROW, body, 0)


def row_at(index):
    return pl.ds(pl.multiple_of(index * SUB, SUB), SUB)


def rows_at(index, count):
    return pl.ds(pl.multiple_of(index * SUB, SUB), count * SUB)


def send_rows(field, up, down):
    edge = up.shape[1]
    total = field.shape[1]
    for g in range(field.shape[0]):
        up[g] = field[g, total - edge :, :]
        down[g] = field[g, :edge, :]


def field_kernel(begin, sizes, n_lon, group, cap, loc, lat, tiles, obs, norm_h, field, up, down, norm, sem):
    copy = pltpu.make_async_copy(norm_h.at[pl.ds(begin, sum(sizes))], norm, sem)
    copy.start()
    field[...] = jnp.zeros_like(field)
    copy.wait()

    def body(j, carry):
        done = []
        for c in range(group):
            slot = (lat[0] * n_lon + j) * cap + c
            t = loc[PER_ROW + slot % PER_ROW, slot // PER_ROW]
            own = pl.ds(pl.multiple_of(t * SUB, SUB), SUB)
            level = 0
            for g, size in enumerate(sizes):
                for l in range(size):
                    at = pl.ds(t * (SUB * SUB) + l, SUB, stride=SUB)
                    done.append((g, at, norm[level, own, :] * (obs[g, at, :] + tiles[j, level, c])))
                    level += 1
        for g, at, value in done:
            field[g, at, :] = value
        return carry

    lax.fori_loop(0, n_lon, body, 0)
    send_rows(field, up, down)


def stack_kernel(face_x, face_y, cross, wet, field, up, down):
    field[...] = jnp.zeros_like(field)
    sources = (face_x, face_y, cross, wet)

    def body(i, carry):
        values = []
        for n in range(4):
            t = i * 4 + n
            own = pl.ds(pl.multiple_of(t * SUB, SUB), SUB)
            values += [(t, l, source[own, :].astype(jnp.float32)) for l, source in enumerate(sources)]
        for t, l, value in values:
            field[0, pl.ds(t * (SUB * SUB) + l, SUB, stride=SUB), :] = value
        return carry

    lax.fori_loop(0, face_x.shape[0] // SUB // 4, body, 0)
    send_rows(field, up, down)


STRIP = 32
HALF = 2 * STRIP
SEAT = 16
SEATS = HALF // SEAT
TURNS = 35


def span_of(rows):
    return -(-(rows + 2 * STEPS) // (SEATS * TURNS)) * TURNS


def extend(ext, field, above, below):
    groups, total, _ = field.shape
    halo = STEPS * SUB
    for g in range(groups):
        ext[g, :halo, :] = above[g]
        ext[g, halo : halo + total, :] = field[g]
        ext[g, halo + total : 2 * halo + total, :] = below[g]
        ext[g, 2 * halo + total :, :] = jnp.zeros((ext.shape[1] - 2 * halo - total, LANES), jnp.float32)


def edges_kernel(field, above, below, strips, east, west, ext):
    groups = field.shape[0]
    extend(ext, field, above, below)
    span = east.shape[0] // SUB
    lane = iota((SUB, LANES), 1)
    place = lane % HALF

    def body(i, carry):
        done = []
        for n in range(TURNS):
            m = i * TURNS + n
            to_east = None
            to_west = None
            for q in range(SEATS):
                first = ext[0, row_at(q * span + m), :]
                second = pltpu.roll(ext[groups - 1, row_at(q * span + m), :], HALF, 1)
                left = jnp.where(lane < HALF, first, second)
                right = jnp.where(lane < HALF, second, first)
                row = jnp.where(place < STRIP, pltpu.roll(left, STEPS, 1), pltpu.roll(right, HALF - STEPS, 1))
                done.append((strips, q * span + m, row))
                right = pltpu.roll(right, SEAT * q + SEAT, 1)
                if q:
                    left = pltpu.roll(left, SEAT * q, 1)
                mine = place // SEAT == q
                to_east = right if q == 0 else jnp.where(mine, right, to_east)
                to_west = left if q == 0 else jnp.where(mine, left, to_west)
            done.append((east, m, to_east))
            done.append((west, m, to_west))
        for ref, m, value in done:
            ref[row_at(m), :] = value
        return carry

    lax.fori_loop(0, span // TURNS, body, 0)


def build_strips(win, strips, from_west, from_east):
    span = from_west.shape[0] // SUB
    place = iota((SUB, LANES), 1) % HALF

    def body(i, carry):
        done = []
        for n in range(TURNS):
            m = i * TURNS + n
            west = from_west[row_at(m), :]
            east = from_east[row_at(m), :]
            for q in range(SEATS):
                a = pltpu.roll(west, (STEPS - SEAT - SEAT * q) % LANES, 1)
                b = pltpu.roll(east, (HALF - STEPS - SEAT * q) % LANES, 1)
                row = strips[row_at(q * span + m), :]
                row = jnp.where(place < STEPS, a, jnp.where(place < HALF - STEPS, row, b))
                done.append((q * span + m, row))
        for m, row in done:
            win[row_at(m), :] = row
        return carry

    lax.fori_loop(0, span // TURNS, body, 0)
    first = SEATS * span * SUB
    win[first:, :] = jnp.zeros((win.shape[0] - first, LANES), jnp.float32)


def fill_coef(coef, win):
    rows = coef.shape[1]

    def body(i, carry):
        done = []
        for n in range(12):
            b = i * 12 + n
            base = b * (SUB * SUB)
            at = pl.ds(pl.multiple_of(b * SUB, SUB), SUB)
            fx, fy, ct, wet = (win[pl.ds(base + s, SUB, stride=SUB), :] for s in range(4))
            wet_n = win[pl.ds(base + SUB + 3, SUB, stride=SUB), :]
            x = fx * wet * pltpu.roll(wet, LANES - 1, 1)
            xw = pltpu.roll(x, 1, 1)
            y = fy * wet * wet_n
            twist = 0.25 * ct * wet
            for c, value in enumerate((1.0 - x - xw, x, xw, y, twist)):
                done.append((c, at, value))
        for c, at, value in done:
            coef[c, at, :] = value
        return carry

    lax.fori_loop(0, rows // (12 * SUB), body, 0)


def own_coef_kernel(field, above, below, coef, ext):
    extend(ext, field, above, below)
    fill_coef(coef, ext.at[0])


def strip_coef_kernel(strips, from_west, from_east, coef, win):
    build_strips(win, strips, from_west, from_east)
    fill_coef(coef, win)


def advance(source, target, planes, weight, rows):
    last = rows + 2 * STEPS + 4
    unroll = last // planes
    blocks = last // unroll

    def rolled(w, index):
        cells = source[w, row_at(index), :]
        east = pltpu.roll(cells, LANES - 1, 1)
        west = pltpu.roll(cells, 1, 1)
        return cells, east, west, east - west

    y_first = weight(3, 0)
    state = []
    for w in range(planes):
        before = rolled(w, 0)
        now = rolled(w, 1)
        state.append((now, before[3], y_first * (now[0] - before[0])))

    def block(b, state):
        base = 1 + b * unroll
        state = list(state)
        for u in range(unroll):
            weights = [weight(c, base + u) for c in range(5)]
            for w in range(planes):
                (cells, east, west, slope), slope_s, flux_s = state[w]
                ahead = rolled(w, base + u + 1)
                flux = weights[3] * (ahead[0] - cells)
                target[w, row_at(base + u), :] = (
                    (weights[0] * cells + weights[1] * east)
                    + (weights[2] * west + (flux - flux_s))
                    + weights[4] * (ahead[3] - slope_s)
                )
                state[w] = (ahead, slope, flux)
        return tuple(state)

    lax.fori_loop(0, blocks, block, tuple(state))


def diffuse(win, other, planes, coef, rows):
    def weight(c, index):
        return coef[c, pl.ds(index, 1), :]

    def two(t, carry):
        advance(win, other, planes, weight, rows)
        advance(other, win, planes, weight, rows)
        return carry

    for w in range(planes):
        other[w, :SUB, :] = jnp.zeros((SUB, LANES), jnp.float32)
        other[w, other.shape[1] - SUB * SUB :, :] = jnp.zeros((SUB * SUB, LANES), jnp.float32)
    lax.fori_loop(0, STEPS // 2, two, 0)


def own_kernel(field, above, below, coef, mid, win, other):
    groups = field.shape[0]
    rows = mid.shape[1] // SUB
    halo = STEPS * SUB
    extend(win, field, above, below)
    diffuse(win, other, groups, coef, rows)
    for g in range(groups):
        mid[g] = win[g, halo : halo + rows * SUB, :]


MERGE = 64


def strip_kernel(sizes, begin, aliased, earlier, *refs):
    loc, strips, from_west, from_east, coef, mid, low, high, norm_h = refs[:9]
    parts = refs[9 + aliased : 9 + aliased + earlier]
    refs = refs[9 + aliased + earlier :]
    if earlier:
        out_h, packed, sampled, turned = refs[:4]
    else:
        out_h, sampled = refs[:2]
    win, other, smooth, norm, out, sems = refs[-6:]
    groups = mid.shape[0]
    rows = mid.shape[1] // SUB
    levels = pl.ds(begin, sum(sizes))
    copy = pltpu.make_async_copy(norm_h.at[levels], norm, sems.at[0])
    copy.start()
    build_strips(win.at[0], strips, from_west, from_east)
    diffuse(win, other, 1, coef, rows)
    copy.wait()
    lane = iota((SUB, LANES), 1)
    outer = LANES - STEPS

    def merge(b, carry):
        done = []
        for u in range(MERGE):
            at = row_at(b * MERGE + u)
            strip = win[0, row_at(b * MERGE + u + STEPS), :]
            west = pltpu.roll(strip, outer, 1)
            east = pltpu.roll(strip, HALF + STEPS, 1)
            cells = mid[0, at, :]
            done.append((0, at, jnp.where(lane < STEPS, west, jnp.where(lane < outer, cells, east))))
            if groups == 2:
                both = pltpu.roll(jnp.where(lane < HALF, east, west), HALF, 1)
                cells = mid[1, at, :]
                done.append((1, at, jnp.where((lane < STEPS) | (lane >= outer), both, cells)))
        for g, at, value in done:
            smooth[g, at, :] = value
        return carry

    lax.fori_loop(0, rows // MERGE, merge, 0)

    def scale(i, carry):
        done = []
        for n in range(8):
            b = i * 8 + n
            own = pl.ds(pl.multiple_of(b * SUB, SUB), SUB)
            level = 0
            for g, size in enumerate(sizes):
                for l in range(size):
                    at = pl.ds(b * (SUB * SUB) + l, SUB, stride=SUB)
                    done.append((g, at, level, own, smooth[g, at, :] * norm[level, own, :]))
                    level += 1
        for g, at, level, own, value in done:
            out[level, own, :] = value
            smooth[g, at, :] = value
        return carry

    lax.fori_loop(0, rows // (8 * SUB), scale, 0)
    back = pltpu.make_async_copy(out, out_h.at[levels], sems.at[1])
    back.start()
    count = low.shape[0] // PER_ROW
    halves = count // LANES

    def samples(i, carry):
        h = i // PER_ROW
        k = i % PER_ROW
        kept = [[jnp.zeros((SUB, LANES), jnp.float32)] * 4 for _ in range(groups)]
        for seat in range(LANES):
            at = pl.multiple_of(loc[k, h * LANES + seat], SUB)
            lo = low[pl.ds(k * count + h * LANES + seat, 1), :]
            hi = high[pl.ds(k * count + h * LANES + seat, 1), :]
            for g in range(groups):
                value = smooth[g, pl.ds(at, SUB), :] * lo + smooth[g, pl.ds(at + SUB, SUB), :] * hi
                total = jnp.sum(value, axis=1, keepdims=True)
                kept[g][seat % 4] = jnp.where(lane == seat, total, kept[g][seat % 4])
        for g in range(groups):
            a, b, c, d = kept[g]
            sampled[h, g, row_at(k), :] = (a + b) + (c + d)
        return carry

    lax.fori_loop(0, halves * PER_ROW, samples, 0)
    if earlier:
        pack_samples(parts + (sampled,), packed, turned)
    back.wait()


def pack_samples(parts, out, turned):
    for h in range(turned.shape[0]):
        index = 0
        for part in parts:
            for g in range(part.shape[1]):
                for k in range(PER_ROW):
                    at = k * FEATS + index * SUB
                    turned[h, at : at + SUB, :] = part[h, g, k * SUB : (k + 1) * SUB, :]
                index += 1
        out[h * LANES : (h + 1) * LANES, :] = turned[h].T


def exchange_rows(up, down, n_lat):
    pairs = [(i, i + 1) for i in range(n_lat - 1)]
    back = [(i + 1, i) for i in range(n_lat - 1)]
    return lax.ppermute(up, "lat", pairs), lax.ppermute(down, "lat", back)


def exchange_columns(east, west, n_lon):
    pairs = [(i, (i + 1) % n_lon) for i in range(n_lon)]
    back = [((i + 1) % n_lon, i) for i in range(n_lon)]
    return lax.ppermute(east, "lon", pairs), lax.ppermute(west, "lon", back)


def on_device(
    innovations,
    owners,
    prof_row,
    prof_col,
    interp_weights,
    model_tiles,
    model_ids,
    face_x,
    face_y,
    cross_term,
    wet_mask,
    norm_factor,
):
    n_lat = lax.axis_size("lat")
    n_lon = lax.axis_size("lon")
    devices = n_lat * n_lon
    levels, lat_cells, lon_cells = norm_factor.shape
    tiles = model_tiles.shape[1]
    group = tiles // n_lon
    count = innovations.shape[1]
    cap = 2 * count // devices
    slots = devices * cap
    rows = slots // PER_ROW
    starts = group_starts()
    f32 = jnp.float32
    lat = lax.axis_index("lat").reshape(1)
    both = ("lat", "lon")
    span = span_of(lat_cells)
    ext_rows = SEATS * span
    win_rows = ext_rows + SUB

    def arrays(*shapes):
        return tuple(jax.ShapeDtypeStruct(shape, f32) for shape in shapes)

    def call(kernel, out_shape, micros, name, grant=SMALL, **kwargs):
        return pl.pallas_call(
            kernel,
            out_shape=out_shape,
            compiler_params=params(grant),
            cost_estimate=cost(micros),
            name=name,
            **kwargs,
        )

    def after(value, *others):
        return lax.optimization_barrier((value,) + others)[0]

    def tile_exchange(chunk, *others):
        first = sum(CHUNKS[:chunk])
        begin = starts[first]
        size = sum(GROUPS[first : first + CHUNKS[chunk]])
        piece = model_tiles[begin : begin + size].reshape(size, n_lon, group, SUB, LANES)
        piece = jnp.transpose(piece, (1, 0, 2, 3, 4))
        if others:
            piece = after(piece, *others)
        return lax.all_to_all(piece, "lon", split_axis=0, concat_axis=0, tiled=True)

    def halo(field, up, down, groups):
        above, below = exchange_rows(up, down, n_lat)
        strips, east, west = call(
            edges_kernel,
            arrays((ext_rows * SUB, LANES), (span * SUB, LANES), (span * SUB, LANES)),
            3,
            "edges",
            scratch_shapes=[pltpu.VMEM((groups, ext_rows * SUB, LANES), f32)],
        )(field, above, below)
        return (field, above, below, strips) + exchange_columns(east, west, n_lon)

    def field_shapes(groups):
        return arrays(
            (groups, lat_cells * SUB, LANES),
            (groups, STEPS * SUB, LANES),
            (groups, STEPS * SUB, LANES),
        )

    send, slot = call(
        functools.partial(route_kernel, cap, group, n_lat, starts),
        (jax.ShapeDtypeStruct((rows, LANES), f32), jax.ShapeDtypeStruct((1, count), jnp.int32)),
        3,
        "route",
        LARGE,
        scratch_shapes=[pltpu.VMEM((FEATS, count + devices * group), f32)],
    )(
        innovations,
        interp_weights,
        owners.reshape(1, count),
        prof_row.reshape(1, count),
        prof_col.reshape(1, count),
        model_ids,
    )
    stacked = call(stack_kernel, field_shapes(1), 3, "stack")(face_x, face_y, cross_term, wet_mask)
    stack, above, below, coef_strips, coef_west, coef_east = halo(*stacked, 1)
    own_coef = call(
        own_coef_kernel,
        arrays((5, win_rows, LANES))[0],
        3,
        "own_coef",
        scratch_shapes=[pltpu.VMEM((1, (win_rows + SUB) * SUB, LANES), f32)],
    )(stack, above, below)
    recv = lax.all_to_all(
        send.reshape(devices, rows // devices, LANES), both, split_axis=0, concat_axis=0, tiled=True
    ).reshape(rows, LANES)
    pieces = [tile_exchange(0, recv, stacked[0])]

    smem = pl.BlockSpec(memory_space=pltpu.SMEM)
    vmem = pl.BlockSpec(memory_space=pltpu.VMEM)
    hbm = pl.BlockSpec(memory_space=pltpu.HBM)
    turned = pltpu.VMEM((rows // LANES, LANES, LANES), f32)
    low, high, loc = call(
        place_kernel,
        arrays((slots, LANES), (slots, LANES)) + (jax.ShapeDtypeStruct((2 * PER_ROW, rows), jnp.int32),),
        2,
        "place",
        LARGE,
        scratch_shapes=[turned],
    )(recv)

    def scatter(chunk, grant):
        first = sum(CHUNKS[:chunk])
        return call(
            functools.partial(scatter_kernel, first),
            arrays((CHUNKS[chunk], lat_cells * SUB, LANES))[0],
            9,
            "scatter",
            grant,
            in_specs=[smem, vmem, vmem, vmem],
            scratch_shapes=[turned],
        )(loc, recv, low, high)

    observed = [scatter(0, LARGE), scatter(1, SMALL)]
    pieces.append(tile_exchange(1, pieces[0], observed[0], own_coef, coef_strips))
    smoothed = None
    sampled = []
    first = 0
    for chunk, groups in enumerate(CHUNKS):
        sizes = GROUPS[first : first + groups]
        begin = starts[first]
        own_levels = (sum(sizes), lat_cells, LANES)
        field = call(
            functools.partial(field_kernel, begin, sizes, n_lon, group, cap),
            field_shapes(groups),
            4,
            "field",
            in_specs=[smem, smem, vmem, vmem, hbm],
            scratch_shapes=[pltpu.VMEM(own_levels, f32), pltpu.SemaphoreType.DMA],
        )(loc, lat, pieces[chunk], observed[chunk], norm_factor)
        field, above, below, strips, from_west, from_east = halo(*field, groups)
        mid_shape = (groups, lat_cells * SUB, LANES)
        win_shape = (groups, win_rows * SUB, LANES)
        mid = call(
            own_kernel,
            arrays(mid_shape)[0],
            6 * groups,
            "own",
            scratch_shapes=[pltpu.VMEM(win_shape, f32), pltpu.VMEM(win_shape, f32)],
        )(after(field, strips), above, below, own_coef)
        if chunk == 0:
            strip_coef = call(
                strip_coef_kernel,
                arrays((5, win_rows, LANES))[0],
                3,
                "strip_coef",
                scratch_shapes=[pltpu.VMEM(((win_rows + SUB) * SUB, LANES), f32)],
            )(after(coef_strips, mid, *observed[1:]), coef_west, coef_east)
        operands = [loc, strips, from_west, from_east, strip_coef, mid, low, high, norm_factor]
        specs = [smem] + [vmem] * 7 + [hbm]
        aliases = {}
        if smoothed is not None:
            aliases = {len(operands): 0}
            operands.append(smoothed)
            specs.append(hbm)
        last = chunk + 1 == len(CHUNKS)
        earlier = sampled if last else []
        part_shape = (rows // LANES, groups, PER_ROW * SUB, LANES)
        gathered = [pltpu.VMEM(part_shape, f32), pltpu.VMEM((rows // LANES, LANES, LANES), f32)]
        smoothed, part = call(
            functools.partial(strip_kernel, sizes, begin, len(aliases), len(earlier)),
            arrays(norm_factor.shape, (rows, LANES) if earlier else part_shape),
            12,
            "strips",
            in_specs=specs + [vmem] * len(earlier),
            out_specs=(hbm, vmem),
            scratch_shapes=(gathered if earlier else [])
            + [
                pltpu.VMEM((1,) + win_shape[1:], f32),
                pltpu.VMEM((1,) + win_shape[1:], f32),
                pltpu.VMEM(mid_shape, f32),
                pltpu.VMEM(own_levels, f32),
                pltpu.VMEM(own_levels, f32),
                pltpu.SemaphoreType.DMA((2,)),
            ],
            input_output_aliases=aliases,
        )(*operands, *earlier)
        sampled.append(part)
        first += groups
        if not last:
            pieces[chunk + 1] = after(pieces[chunk + 1], part)

    back = sampled[-1]
    returned = lax.all_to_all(
        back.reshape(devices, rows // devices, LANES), both, split_axis=0, concat_axis=0, tiled=True
    ).reshape(rows, LANES)
    profile_values = call(
        functools.partial(unpack_kernel, starts),
        arrays((levels, count))[0],
        1,
        "unpack",
    )(returned, slot)
    return (smoothed, profile_values)


def solution(mesh):
    in_specs = (
        P(None, ("lat", "lon")),
        P(("lat", "lon"), None),
        P(("lat", "lon")),
        P(("lat", "lon")),
        P(None, ("lat", "lon")),
        P(None, ("lat", "lon"), None, None),
        P(None, ("lat", "lon")),
        P("lat", "lon"),
        P("lat", "lon"),
        P("lat", "lon"),
        P("lat", "lon"),
        P(None, "lat", "lon"),
    )
    out_specs = (P(None, "lat", "lon"), P(None, ("lat", "lon")))
    return jax.shard_map(
        on_device, mesh=mesh, in_specs=in_specs, out_specs=out_specs, check_vma=False
    )
```

```python
import functools
import jax
import jax.numpy as jnp
from jax import lax
from jax.experimental import pallas as pl
from jax.experimental.pallas import tpu as pltpu
from jax.sharding import PartitionSpec as P

STEPS = 10
SUB = 8
LANES = 128
FEATS = 32
PER_ROW = LANES // FEATS
GROUPS = (5, 4, 8, 8)
CHUNKS = (2, 2)
WEIGHT_ROWS = (5, 6, 12, 13)
LOC_ROW = 7
ID_ROW = 15
SMALL = 20 * 1024 * 1024
LARGE = 60 * 1024 * 1024


def group_starts():
    starts = []
    total = 0
    for count in GROUPS:
        starts.append(total)
        total += count
    return starts


def params(grant):
    return pltpu.CompilerParams(vmem_limit_bytes=grant)


def cost(micros):
    return pl.CostEstimate(flops=0, bytes_accessed=int(micros * 3.6e6), transcendentals=0)


def iota(shape, dim):
    return lax.broadcasted_iota(jnp.int32, shape, dim)


def split3(values):
    high = values.astype(jnp.bfloat16)
    rest = values - high.astype(jnp.float32)
    middle = rest.astype(jnp.bfloat16)
    low = (rest - middle.astype(jnp.float32)).astype(jnp.bfloat16)
    return high, middle, low


def route_kernel(cap, group, copies, starts, innov, weights, own_row, prow, pcol, ids, send, slot_out, pay):
    count = innov.shape[1]
    tiles = ids.shape[1]
    extra = tiles * copies
    owner = own_row[...]
    column = jnp.broadcast_to(owner.astype(jnp.float32), (SUB, count)).T[:, :1].astype(jnp.int32)
    same = column == owner
    before = iota((count, count), 0) < iota((count, count), 1)
    ones = jnp.where(same & before, 1.0, 0.0)
    rank = jnp.sum(ones, axis=0, keepdims=True).astype(jnp.int32)
    slot = owner * cap + rank
    slot_out[...] = slot
    number = iota((1, extra), 1)
    id_slot = (number // group) * cap + number % group
    pay[...] = jnp.zeros_like(pay)
    for index, count_in in enumerate(GROUPS):
        pay[index * SUB : index * SUB + count_in, :count] = innov[starts[index] : starts[index] + count_in, :]
    for corner, row in enumerate(WEIGHT_ROWS):
        pay[row : row + 1, :count] = weights[corner : corner + 1, :]
    pay[LOC_ROW : LOC_ROW + 1, :count] = (prow[...] * LANES + pcol[...]).astype(jnp.float32)
    for i in range(copies):
        at = count + i * tiles
        pay[ID_ROW : ID_ROW + 1, at : at + tiles] = ids[...].astype(jnp.float32)
    slots = jnp.concatenate([slot, id_slot], axis=1)
    values = pay[...]
    part = slots % PER_ROW
    spread = jnp.concatenate([jnp.where(part == k, values, 0.0) for k in range(PER_ROW)], axis=0)
    rows = send.shape[0]
    hot = jnp.where(iota((rows, count + extra), 0) == slots // PER_ROW, 1.0, 0.0).astype(jnp.bfloat16)
    total = None
    for piece in split3(spread):
        term = lax.dot_general(hot, piece, (((1,), (1,)), ((), ())), preferred_element_type=jnp.float32)
        total = term if total is None else total + term
    send[...] = total


def unpack_kernel(starts, recv, slot, out):
    slots = slot[...]
    rows = recv.shape[0]
    hot = jnp.where(iota((rows, slots.shape[1]), 0) == slots // PER_ROW, 1.0, 0.0).astype(jnp.bfloat16)
    total = None
    for piece in split3(recv[...]):
        term = lax.dot_general(piece, hot, (((0,), (0,)), ((), ())), preferred_element_type=jnp.float32)
        total = term if total is None else total + term
    part = slots % PER_ROW
    picked = jnp.zeros((FEATS, slots.shape[1]), jnp.float32)
    for k in range(PER_ROW):
        picked = jnp.where(part == k, total[k * FEATS : (k + 1) * FEATS], picked)
    for index, count_in in enumerate(GROUPS):
        out[starts[index] : starts[index] + count_in, :] = picked[index * SUB : index * SUB + count_in]


def turn_slots(recv, turned):
    for h in range(recv.shape[0] // LANES):
        turned[h] = recv[h * LANES : (h + 1) * LANES, :].T


def place_kernel(recv, low, high, loc_out, turned):
    rows = recv.shape[0]
    turn_slots(recv, turned)
    for k in range(PER_ROW):
        for h in range(rows // LANES):
            at = k * FEATS
            cut = slice(h * LANES, (h + 1) * LANES)
            cells = turned[h, at + LOC_ROW : at + LOC_ROW + 1, :].astype(jnp.int32)
            loc_out[k : k + 1, cut] = cells // LANES * SUB
            loc_out[PER_ROW + k : PER_ROW + k + 1, cut] = turned[h, at + ID_ROW : at + ID_ROW + 1, :].astype(jnp.int32)
    lane = iota((rows, LANES), 1)
    for k in range(PER_ROW):
        at = k * FEATS
        col = recv[:, at + LOC_ROW : at + LOC_ROW + 1].astype(jnp.int32) % LANES
        w = [recv[:, at + row : at + row + 1] for row in WEIGHT_ROWS]
        here = lane == col
        after = lane == col + 1
        low[k * rows : (k + 1) * rows, :] = jnp.where(here, w[0], jnp.where(after, w[1], 0.0))
        high[k * rows : (k + 1) * rows, :] = jnp.where(here, w[2], jnp.where(after, w[3], 0.0))


def scatter_kernel(first, loc, recv, low, high, obs, turned, odd):
    rows = recv.shape[0]
    groups = range(obs.shape[0])
    turn_slots(recv, turned)

    def clear(i, carry):
        for g in groups:
            at = pl.ds(pl.multiple_of(i * 64, 64), 64)
            obs[g, at, :] = jnp.zeros((64, LANES), jnp.float32)
            odd[g, at, :] = jnp.zeros((64, LANES), jnp.float32)
        return carry

    lax.fori_loop(0, obs.shape[1] // 64, clear, 0)

    def body(i, carry):
        h = i // PER_ROW
        k = i % PER_ROW
        size = len(groups) * SUB
        block = turned[h, pl.ds(pl.multiple_of(k * FEATS + first * SUB, SUB), size), :]
        for seat in range(0, LANES, 2):
            found = []
            for n, total in enumerate((obs, odd)):
                at = pl.multiple_of(loc[k, h * LANES + seat + n], SUB)
                lo = low[pl.ds(k * rows + h * LANES + seat + n, 1), :]
                hi = high[pl.ds(k * rows + h * LANES + seat + n, 1), :]
                for g in groups:
                    value = block[g * SUB : (g + 1) * SUB, seat + n : seat + n + 1]
                    here = total[g, pl.ds(at, SUB), :] + value * lo
                    north = total[g, pl.ds(at + SUB, SUB), :] + value * hi
                    found.append((total, g, at, here, north))
            for total, g, at, here, north in found:
                total[g, pl.ds(at, SUB), :] = here
                total[g, pl.ds(at + SUB, SUB), :] = north
        return carry

    lax.fori_loop(0, (rows // LANES) * PER_ROW, body, 0)

    def join(i, carry):
        for g in groups:
            at = pl.ds(pl.multiple_of(i * 64, 64), 64)
            obs[g, at, :] = obs[g, at, :] + odd[g, at, :]
        return carry

    lax.fori_loop(0, obs.shape[1] // 64, join, 0)


def row_at(index):
    return pl.ds(pl.multiple_of(index * SUB, SUB), SUB)


def rows_at(index, count):
    return pl.ds(pl.multiple_of(index * SUB, SUB), count * SUB)


def send_rows(field, up, down):
    edge = up.shape[1]
    total = field.shape[1]
    for g in range(field.shape[0]):
        up[g] = field[g, total - edge :, :]
        down[g] = field[g, :edge, :]


def field_kernel(begin, sizes, n_lon, group, cap, loc, lat, tiles, obs, norm_h, field, up, down, norm, sem):
    copy = pltpu.make_async_copy(norm_h.at[pl.ds(begin, sum(sizes))], norm, sem)
    copy.start()
    field[...] = jnp.zeros_like(field)
    copy.wait()

    def body(j, carry):
        done = []
        for c in range(group):
            slot = (lat[0] * n_lon + j) * cap + c
            t = loc[PER_ROW + slot % PER_ROW, slot // PER_ROW]
            own = pl.ds(pl.multiple_of(t * SUB, SUB), SUB)
            level = 0
            for g, size in enumerate(sizes):
                for l in range(size):
                    at = pl.ds(t * (SUB * SUB) + l, SUB, stride=SUB)
                    done.append((g, at, norm[level, own, :] * (obs[g, at, :] + tiles[j, level, c])))
                    level += 1
        for g, at, value in done:
            field[g, at, :] = value
        return carry

    lax.fori_loop(0, n_lon, body, 0)
    send_rows(field, up, down)


def stack_kernel(face_x, face_y, cross, wet, field, up, down):
    field[...] = jnp.zeros_like(field)
    sources = (face_x, face_y, cross, wet)

    def body(i, carry):
        values = []
        for n in range(4):
            t = i * 4 + n
            own = pl.ds(pl.multiple_of(t * SUB, SUB), SUB)
            values += [(t, l, source[own, :].astype(jnp.float32)) for l, source in enumerate(sources)]
        for t, l, value in values:
            field[0, pl.ds(t * (SUB * SUB) + l, SUB, stride=SUB), :] = value
        return carry

    lax.fori_loop(0, face_x.shape[0] // SUB // 4, body, 0)
    send_rows(field, up, down)


STRIP = 32
HALF = 2 * STRIP
SEAT = 16
SEATS = HALF // SEAT
TURNS = 10


def span_of(rows):
    return -(-(rows + 2 * STEPS) // (SEATS * TURNS)) * TURNS


def extend(ext, field, above, below):
    groups, total, _ = field.shape
    halo = STEPS * SUB
    for g in range(groups):
        ext[g, :halo, :] = above[g]
        ext[g, halo : halo + total, :] = field[g]
        ext[g, halo + total : 2 * halo + total, :] = below[g]
        ext[g, 2 * halo + total :, :] = jnp.zeros((ext.shape[1] - 2 * halo - total, LANES), jnp.float32)


def edges_kernel(field, above, below, strips, east, west, ext):
    groups = field.shape[0]
    extend(ext, field, above, below)
    span = east.shape[0] // SUB
    lane = iota((SUB, LANES), 1)
    place = lane % HALF

    def body(i, carry):
        for n in range(TURNS):
            m = i * TURNS + n
            to_east = None
            to_west = None
            for q in range(SEATS):
                first = ext[0, row_at(q * span + m), :]
                second = pltpu.roll(ext[groups - 1, row_at(q * span + m), :], HALF, 1)
                left = jnp.where(lane < HALF, first, second)
                right = jnp.where(lane < HALF, second, first)
                row = jnp.where(place < STRIP, pltpu.roll(left, STEPS, 1), pltpu.roll(right, HALF - STEPS, 1))
                strips[row_at(q * span + m), :] = row
                right = pltpu.roll(right, SEAT * q + SEAT, 1)
                if q:
                    left = pltpu.roll(left, SEAT * q, 1)
                mine = place // SEAT == q
                to_east = right if q == 0 else jnp.where(mine, right, to_east)
                to_west = left if q == 0 else jnp.where(mine, left, to_west)
            east[row_at(m), :] = to_east
            west[row_at(m), :] = to_west
        return carry

    lax.fori_loop(0, span // TURNS, body, 0)


def build_strips(win, strips, from_west, from_east):
    span = from_west.shape[0] // SUB
    place = iota((SUB, LANES), 1) % HALF

    def body(i, carry):
        for n in range(TURNS):
            m = i * TURNS + n
            west = from_west[row_at(m), :]
            east = from_east[row_at(m), :]
            for q in range(SEATS):
                a = pltpu.roll(west, (STEPS - SEAT - SEAT * q) % LANES, 1)
                b = pltpu.roll(east, (HALF - STEPS - SEAT * q) % LANES, 1)
                row = strips[row_at(q * span + m), :]
                row = jnp.where(place < STEPS, a, jnp.where(place < HALF - STEPS, row, b))
                win[row_at(q * span + m), :] = row
        return carry

    lax.fori_loop(0, span // TURNS, body, 0)
    first = SEATS * span * SUB
    win[first:, :] = jnp.zeros((win.shape[0] - first, LANES), jnp.float32)


def fill_coef(coef, win):
    rows = coef.shape[1]

    def body(i, carry):
        done = []
        for n in range(12):
            b = i * 12 + n
            base = b * (SUB * SUB)
            at = pl.ds(pl.multiple_of(b * SUB, SUB), SUB)
            fx, fy, ct, wet = (win[pl.ds(base + s, SUB, stride=SUB), :] for s in range(4))
            wet_n = win[pl.ds(base + SUB + 3, SUB, stride=SUB), :]
            x = fx * wet * pltpu.roll(wet, LANES - 1, 1)
            xw = pltpu.roll(x, 1, 1)
            y = fy * wet * wet_n
            twist = 0.25 * ct * wet
            for c, value in enumerate((1.0 - x - xw, x, xw, y, twist)):
                done.append((c, at, value))
        for c, at, value in done:
            coef[c, at, :] = value
        return carry

    lax.fori_loop(0, rows // (12 * SUB), body, 0)


def own_coef_kernel(field, above, below, coef, ext):
    extend(ext, field, above, below)
    fill_coef(coef, ext.at[0])


def strip_coef_kernel(strips, from_west, from_east, coef, win):
    build_strips(win, strips, from_west, from_east)
    fill_coef(coef, win)


BY_MATMUL = 0.25


def fill_shift(shift):
    row = iota(shift.shape, 0) % LANES
    col = iota(shift.shape, 1)
    near = jnp.where(col < LANES, col + 1, col + LANES - 1) % LANES
    shift[...] = jnp.where(row == near, 1.0, 0.0).astype(jnp.bfloat16)


def advance(source, target, planes, weight, shift, rows):
    last = rows + 2 * STEPS + 4
    unroll = last // planes
    blocks = last // unroll
    split = int(unroll * BY_MATMUL)

    def rolled(w, index):
        cells = source[w, row_at(index), :]
        east = pltpu.roll(cells, LANES - 1, 1)
        west = pltpu.roll(cells, 1, 1)
        return cells, east, west, east - west

    def shifted_rows(w, first):
        cells = source[w, rows_at(first, split), :]
        high = cells.astype(jnp.bfloat16)
        low = (cells - high.astype(jnp.float32)).astype(jnp.bfloat16)
        both = jnp.concatenate([high, low], axis=1)
        return jnp.dot(both, shift[...], preferred_element_type=jnp.float32)

    y_first = weight(3, 0)
    state = []
    for w in range(planes):
        before = rolled(w, 0)
        now = rolled(w, 1)
        state.append((now, before[3], y_first * (now[0] - before[0])))

    def block(b, state):
        base = 1 + b * unroll
        state = list(state)
        sides = [shifted_rows(w, base + 1) for w in range(planes)]
        for u in range(unroll):
            weights = [weight(c, base + u) for c in range(5)]
            for w in range(planes):
                (cells, east, west, slope), slope_s, flux_s = state[w]
                if u < split:
                    cells_n = source[w, row_at(base + u + 1), :]
                    east_n = sides[w][u * SUB : (u + 1) * SUB, :LANES]
                    west_n = sides[w][u * SUB : (u + 1) * SUB, LANES:]
                    ahead = (cells_n, east_n, west_n, east_n - west_n)
                else:
                    ahead = rolled(w, base + u + 1)
                flux = weights[3] * (ahead[0] - cells)
                target[w, row_at(base + u), :] = (
                    (weights[0] * cells + weights[1] * east)
                    + (weights[2] * west + (flux - flux_s))
                    + weights[4] * (ahead[3] - slope_s)
                )
                state[w] = (ahead, slope, flux)
        return tuple(state)

    lax.fori_loop(0, blocks, block, tuple(state))


def diffuse(win, other, planes, coef, shift, rows):
    fill_shift(shift)

    def weight(c, index):
        return coef[c, pl.ds(index, 1), :]

    def two(t, carry):
        advance(win, other, planes, weight, shift, rows)
        advance(other, win, planes, weight, shift, rows)
        return carry

    for w in range(planes):
        other[w, :SUB, :] = jnp.zeros((SUB, LANES), jnp.float32)
        other[w, other.shape[1] - SUB * SUB :, :] = jnp.zeros((SUB * SUB, LANES), jnp.float32)
    lax.fori_loop(0, STEPS // 2, two, 0)


def own_kernel(field, above, below, coef, mid, win, other, shift):
    groups = field.shape[0]
    rows = mid.shape[1] // SUB
    halo = STEPS * SUB
    extend(win, field, above, below)
    diffuse(win, other, groups, coef, shift, rows)
    for g in range(groups):
        mid[g] = win[g, halo : halo + rows * SUB, :]


MERGE = 32


def strip_kernel(sizes, begin, aliased, earlier, *refs):
    loc, strips, from_west, from_east, coef, mid, low, high, norm_h = refs[:9]
    parts = refs[9 + aliased : 9 + aliased + earlier]
    refs = refs[9 + aliased + earlier :]
    if earlier:
        out_h, packed, sampled, turned = refs[:4]
    else:
        out_h, sampled = refs[:2]
    win, other, shift, smooth, norm, out, sems = refs[-7:]
    groups = mid.shape[0]
    rows = mid.shape[1] // SUB
    levels = pl.ds(begin, sum(sizes))
    copy = pltpu.make_async_copy(norm_h.at[levels], norm, sems.at[0])
    copy.start()
    build_strips(win.at[0], strips, from_west, from_east)
    diffuse(win, other, 1, coef, shift, rows)
    copy.wait()
    lane = iota((SUB, LANES), 1)
    outer = LANES - STEPS

    def merge(b, carry):
        for u in range(MERGE):
            at = row_at(b * MERGE + u)
            strip = win[0, row_at(b * MERGE + u + STEPS), :]
            west = pltpu.roll(strip, outer, 1)
            east = pltpu.roll(strip, HALF + STEPS, 1)
            cells = mid[0, at, :]
            smooth[0, at, :] = jnp.where(lane < STEPS, west, jnp.where(lane < outer, cells, east))
            if groups == 2:
                both = pltpu.roll(jnp.where(lane < HALF, east, west), HALF, 1)
                cells = mid[1, at, :]
                smooth[1, at, :] = jnp.where((lane < STEPS) | (lane >= outer), both, cells)
        return carry

    lax.fori_loop(0, rows // MERGE, merge, 0)

    def scale(i, carry):
        done = []
        for n in range(4):
            b = i * 4 + n
            own = pl.ds(pl.multiple_of(b * SUB, SUB), SUB)
            level = 0
            for g, size in enumerate(sizes):
                for l in range(size):
                    at = pl.ds(b * (SUB * SUB) + l, SUB, stride=SUB)
                    done.append((g, at, level, own, smooth[g, at, :] * norm[level, own, :]))
                    level += 1
        for g, at, level, own, value in done:
            out[level, own, :] = value
            smooth[g, at, :] = value
        return carry

    lax.fori_loop(0, rows // (4 * SUB), scale, 0)
    back = pltpu.make_async_copy(out, out_h.at[levels], sems.at[1])
    back.start()
    count = low.shape[0] // PER_ROW
    halves = count // LANES

    def samples(i, carry):
        h = i // PER_ROW
        k = i % PER_ROW
        kept = [[jnp.zeros((SUB, LANES), jnp.float32)] * 4 for _ in range(groups)]
        for seat in range(LANES):
            at = pl.multiple_of(loc[k, h * LANES + seat], SUB)
            lo = low[pl.ds(k * count + h * LANES + seat, 1), :]
            hi = high[pl.ds(k * count + h * LANES + seat, 1), :]
            for g in range(groups):
                value = smooth[g, pl.ds(at, SUB), :] * lo + smooth[g, pl.ds(at + SUB, SUB), :] * hi
                total = jnp.sum(value, axis=1, keepdims=True)
                kept[g][seat % 4] = jnp.where(lane == seat, total, kept[g][seat % 4])
        for g in range(groups):
            a, b, c, d = kept[g]
            sampled[h, g, row_at(k), :] = (a + b) + (c + d)
        return carry

    lax.fori_loop(0, halves * PER_ROW, samples, 0)
    if earlier:
        pack_samples(parts + (sampled,), packed, turned)
    back.wait()


def pack_samples(parts, out, turned):
    for h in range(turned.shape[0]):
        index = 0
        for part in parts:
            for g in range(part.shape[1]):
                for k in range(PER_ROW):
                    at = k * FEATS + index * SUB
                    turned[h, at : at + SUB, :] = part[h, g, k * SUB : (k + 1) * SUB, :]
                index += 1
        out[h * LANES : (h + 1) * LANES, :] = turned[h].T


def exchange_rows(up, down, n_lat):
    pairs = [(i, i + 1) for i in range(n_lat - 1)]
    back = [(i + 1, i) for i in range(n_lat - 1)]
    return lax.ppermute(up, "lat", pairs), lax.ppermute(down, "lat", back)


def exchange_columns(east, west, n_lon):
    pairs = [(i, (i + 1) % n_lon) for i in range(n_lon)]
    back = [((i + 1) % n_lon, i) for i in range(n_lon)]
    return lax.ppermute(east, "lon", pairs), lax.ppermute(west, "lon", back)


def on_device(
    innovations,
    owners,
    prof_row,
    prof_col,
    interp_weights,
    model_tiles,
    model_ids,
    face_x,
    face_y,
    cross_term,
    wet_mask,
    norm_factor,
):
    n_lat = lax.axis_size("lat")
    n_lon = lax.axis_size("lon")
    devices = n_lat * n_lon
    levels, lat_cells, lon_cells = norm_factor.shape
    tiles = model_tiles.shape[1]
    group = tiles // n_lon
    count = innovations.shape[1]
    cap = 2 * count // devices
    slots = devices * cap
    rows = slots // PER_ROW
    starts = group_starts()
    f32 = jnp.float32
    lat = lax.axis_index("lat").reshape(1)
    both = ("lat", "lon")
    span = span_of(lat_cells)
    ext_rows = SEATS * span
    win_rows = ext_rows + SUB

    def arrays(*shapes):
        return tuple(jax.ShapeDtypeStruct(shape, f32) for shape in shapes)

    def call(kernel, out_shape, micros, name, grant=SMALL, **kwargs):
        return pl.pallas_call(
            kernel,
            out_shape=out_shape,
            compiler_params=params(grant),
            cost_estimate=cost(micros),
            name=name,
            **kwargs,
        )

    def after(value, *others):
        return lax.optimization_barrier((value,) + others)[0]

    def tile_exchange(chunk, *others):
        first = sum(CHUNKS[:chunk])
        begin = starts[first]
        size = sum(GROUPS[first : first + CHUNKS[chunk]])
        piece = model_tiles[begin : begin + size].reshape(size, n_lon, group, SUB, LANES)
        piece = jnp.transpose(piece, (1, 0, 2, 3, 4))
        if others:
            piece = after(piece, *others)
        return lax.all_to_all(piece, "lon", split_axis=0, concat_axis=0, tiled=True)

    def halo(field, up, down, groups):
        above, below = exchange_rows(up, down, n_lat)
        strips, east, west = call(
            edges_kernel,
            arrays((ext_rows * SUB, LANES), (span * SUB, LANES), (span * SUB, LANES)),
            3,
            "edges",
            scratch_shapes=[pltpu.VMEM((groups, ext_rows * SUB, LANES), f32)],
        )(field, above, below)
        return (field, above, below, strips) + exchange_columns(east, west, n_lon)

    def field_shapes(groups):
        return arrays(
            (groups, lat_cells * SUB, LANES),
            (groups, STEPS * SUB, LANES),
            (groups, STEPS * SUB, LANES),
        )

    send, slot = call(
        functools.partial(route_kernel, cap, group, n_lat, starts),
        (jax.ShapeDtypeStruct((rows, LANES), f32), jax.ShapeDtypeStruct((1, count), jnp.int32)),
        3,
        "route",
        LARGE,
        scratch_shapes=[pltpu.VMEM((FEATS, count + devices * group), f32)],
    )(
        innovations,
        interp_weights,
        owners.reshape(1, count),
        prof_row.reshape(1, count),
        prof_col.reshape(1, count),
        model_ids,
    )
    stacked = call(stack_kernel, field_shapes(1), 3, "stack")(face_x, face_y, cross_term, wet_mask)
    stack, above, below, coef_strips, coef_west, coef_east = halo(*stacked, 1)
    own_coef = call(
        own_coef_kernel,
        arrays((5, win_rows, LANES))[0],
        3,
        "own_coef",
        scratch_shapes=[pltpu.VMEM((1, (win_rows + SUB) * SUB, LANES), f32)],
    )(stack, above, below)
    recv = lax.all_to_all(
        send.reshape(devices, rows // devices, LANES), both, split_axis=0, concat_axis=0, tiled=True
    ).reshape(rows, LANES)
    pieces = [tile_exchange(0, recv, stacked[0])]

    smem = pl.BlockSpec(memory_space=pltpu.SMEM)
    vmem = pl.BlockSpec(memory_space=pltpu.VMEM)
    hbm = pl.BlockSpec(memory_space=pltpu.HBM)
    turned = pltpu.VMEM((rows // LANES, LANES, LANES), f32)
    low, high, loc = call(
        place_kernel,
        arrays((slots, LANES), (slots, LANES)) + (jax.ShapeDtypeStruct((2 * PER_ROW, rows), jnp.int32),),
        2,
        "place",
        LARGE,
        scratch_shapes=[turned],
    )(recv)

    def scatter(chunk, grant):
        first = sum(CHUNKS[:chunk])
        return call(
            functools.partial(scatter_kernel, first),
            arrays((CHUNKS[chunk], lat_cells * SUB, LANES))[0],
            9,
            "scatter",
            grant,
            in_specs=[smem, vmem, vmem, vmem],
            scratch_shapes=[turned, pltpu.VMEM((CHUNKS[chunk], lat_cells * SUB, LANES), f32)],
        )(loc, recv, low, high)

    observed = [scatter(0, LARGE), scatter(1, SMALL)]
    pieces.append(tile_exchange(1, pieces[0], observed[0], own_coef, coef_strips))
    shift_space = pltpu.VMEM((2 * LANES, 2 * LANES), jnp.bfloat16)
    smoothed = None
    sampled = []
    first = 0
    for chunk, groups in enumerate(CHUNKS):
        sizes = GROUPS[first : first + groups]
        begin = starts[first]
        own_levels = (sum(sizes), lat_cells, LANES)
        field = call(
            functools.partial(field_kernel, begin, sizes, n_lon, group, cap),
            field_shapes(groups),
            4,
            "field",
            in_specs=[smem, smem, vmem, vmem, hbm],
            scratch_shapes=[pltpu.VMEM(own_levels, f32), pltpu.SemaphoreType.DMA],
        )(loc, lat, pieces[chunk], observed[chunk], norm_factor)
        field, above, below, strips, from_west, from_east = halo(*field, groups)
        mid_shape = (groups, lat_cells * SUB, LANES)
        win_shape = (groups, win_rows * SUB, LANES)
        mid = call(
            own_kernel,
            arrays(mid_shape)[0],
            6 * groups,
            "own",
            scratch_shapes=[pltpu.VMEM(win_shape, f32), pltpu.VMEM(win_shape, f32), shift_space],
        )(after(field, strips), above, below, own_coef)
        if chunk == 0:
            strip_coef = call(
                strip_coef_kernel,
                arrays((5, win_rows, LANES))[0],
                3,
                "strip_coef",
                scratch_shapes=[pltpu.VMEM(((win_rows + SUB) * SUB, LANES), f32)],
            )(after(coef_strips, mid, *observed[1:]), coef_west, coef_east)
        operands = [loc, strips, from_west, from_east, strip_coef, mid, low, high, norm_factor]
        specs = [smem] + [vmem] * 7 + [hbm]
        aliases = {}
        if smoothed is not None:
            aliases = {len(operands): 0}
            operands.append(smoothed)
            specs.append(hbm)
        last = chunk + 1 == len(CHUNKS)
        earlier = sampled if last else []
        part_shape = (rows // LANES, groups, PER_ROW * SUB, LANES)
        gathered = [pltpu.VMEM(part_shape, f32), pltpu.VMEM((rows // LANES, LANES, LANES), f32)]
        smoothed, part = call(
            functools.partial(strip_kernel, sizes, begin, len(aliases), len(earlier)),
            arrays(norm_factor.shape, (rows, LANES) if earlier else part_shape),
            12,
            "strips",
            in_specs=specs + [vmem] * len(earlier),
            out_specs=(hbm, vmem),
            scratch_shapes=(gathered if earlier else [])
            + [
                pltpu.VMEM((1,) + win_shape[1:], f32),
                pltpu.VMEM((1,) + win_shape[1:], f32),
                shift_space,
                pltpu.VMEM(mid_shape, f32),
                pltpu.VMEM(own_levels, f32),
                pltpu.VMEM(own_levels, f32),
                pltpu.SemaphoreType.DMA((2,)),
            ],
            input_output_aliases=aliases,
        )(*operands, *earlier)
        sampled.append(part)
        first += groups
        if not last:
            pieces[chunk + 1] = after(pieces[chunk + 1], part)

    back = sampled[-1]
    returned = lax.all_to_all(
        back.reshape(devices, rows // devices, LANES), both, split_axis=0, concat_axis=0, tiled=True
    ).reshape(rows, LANES)
    profile_values = call(
        functools.partial(unpack_kernel, starts),
        arrays((levels, count))[0],
        1,
        "unpack",
    )(returned, slot)
    return (smoothed, profile_values)


def solution(mesh):
    in_specs = (
        P(None, ("lat", "lon")),
        P(("lat", "lon"), None),
        P(("lat", "lon")),
        P(("lat", "lon")),
        P(None, ("lat", "lon")),
        P(None, ("lat", "lon"), None, None),
        P(None, ("lat", "lon")),
        P("lat", "lon"),
        P("lat", "lon"),
        P("lat", "lon"),
        P("lat", "lon"),
        P(None, "lat", "lon"),
    )
    out_specs = (P(None, "lat", "lon"), P(None, ("lat", "lon")))
    return jax.shard_map(
        on_device, mesh=mesh, in_specs=in_specs, out_specs=out_specs, check_vma=False
    )
```

```python
import functools
import jax
import jax.numpy as jnp
from jax import lax
from jax.experimental import pallas as pl
from jax.experimental.pallas import tpu as pltpu
from jax.sharding import PartitionSpec as P

STEPS = 10
SUB = 8
LANES = 128
FEATS = 32
PER_ROW = LANES // FEATS
GROUPS = (5, 4, 8, 8)
CHUNKS = (2, 2)
WEIGHT_ROWS = (5, 6, 12, 13)
LOC_ROW = 7
ID_ROW = 15
SMALL = 20 * 1024 * 1024
LARGE = 60 * 1024 * 1024


def group_starts():
    starts = []
    total = 0
    for count in GROUPS:
        starts.append(total)
        total += count
    return starts


def params(grant):
    return pltpu.CompilerParams(vmem_limit_bytes=grant)


def cost(micros):
    return pl.CostEstimate(flops=0, bytes_accessed=int(micros * 3.6e6), transcendentals=0)


def iota(shape, dim):
    return lax.broadcasted_iota(jnp.int32, shape, dim)


def split3(values):
    high = values.astype(jnp.bfloat16)
    rest = values - high.astype(jnp.float32)
    middle = rest.astype(jnp.bfloat16)
    low = (rest - middle.astype(jnp.float32)).astype(jnp.bfloat16)
    return high, middle, low


def route_kernel(cap, group, copies, starts, innov, weights, own_row, prow, pcol, ids, send, slot_out, pay):
    count = innov.shape[1]
    tiles = ids.shape[1]
    extra = tiles * copies
    owner = own_row[...]
    column = jnp.broadcast_to(owner.astype(jnp.float32), (SUB, count)).T[:, :1].astype(jnp.int32)
    same = column == owner
    before = iota((count, count), 0) < iota((count, count), 1)
    ones = jnp.where(same & before, 1.0, 0.0)
    rank = jnp.sum(ones, axis=0, keepdims=True).astype(jnp.int32)
    slot = owner * cap + rank
    slot_out[...] = slot
    number = iota((1, extra), 1)
    id_slot = (number // group) * cap + number % group
    pay[...] = jnp.zeros_like(pay)
    for index, count_in in enumerate(GROUPS):
        pay[index * SUB : index * SUB + count_in, :count] = innov[starts[index] : starts[index] + count_in, :]
    for corner, row in enumerate(WEIGHT_ROWS):
        pay[row : row + 1, :count] = weights[corner : corner + 1, :]
    pay[LOC_ROW : LOC_ROW + 1, :count] = (prow[...] * LANES + pcol[...]).astype(jnp.float32)
    for i in range(copies):
        at = count + i * tiles
        pay[ID_ROW : ID_ROW + 1, at : at + tiles] = ids[...].astype(jnp.float32)
    slots = jnp.concatenate([slot, id_slot], axis=1)
    values = pay[...]
    part = slots % PER_ROW
    spread = jnp.concatenate([jnp.where(part == k, values, 0.0) for k in range(PER_ROW)], axis=0)
    rows = send.shape[0]
    hot = jnp.where(iota((rows, count + extra), 0) == slots // PER_ROW, 1.0, 0.0).astype(jnp.bfloat16)
    total = None
    for piece in split3(spread):
        term = lax.dot_general(hot, piece, (((1,), (1,)), ((), ())), preferred_element_type=jnp.float32)
        total = term if total is None else total + term
    send[...] = total


def unpack_kernel(starts, recv, slot, out):
    slots = slot[...]
    rows = recv.shape[0]
    hot = jnp.where(iota((rows, slots.shape[1]), 0) == slots // PER_ROW, 1.0, 0.0).astype(jnp.bfloat16)
    total = None
    for piece in split3(recv[...]):
        term = lax.dot_general(piece, hot, (((0,), (0,)), ((), ())), preferred_element_type=jnp.float32)
        total = term if total is None else total + term
    part = slots % PER_ROW
    picked = jnp.zeros((FEATS, slots.shape[1]), jnp.float32)
    for k in range(PER_ROW):
        picked = jnp.where(part == k, total[k * FEATS : (k + 1) * FEATS], picked)
    for index, count_in in enumerate(GROUPS):
        out[starts[index] : starts[index] + count_in, :] = picked[index * SUB : index * SUB + count_in]


def turn_slots(recv, turned):
    for h in range(recv.shape[0] // LANES):
        turned[h] = recv[h * LANES : (h + 1) * LANES, :].T


def place_kernel(recv, low, high, loc_out, turned):
    rows = recv.shape[0]
    turn_slots(recv, turned)
    for k in range(PER_ROW):
        for h in range(rows // LANES):
            at = k * FEATS
            cut = slice(h * LANES, (h + 1) * LANES)
            cells = turned[h, at + LOC_ROW : at + LOC_ROW + 1, :].astype(jnp.int32)
            loc_out[k : k + 1, cut] = cells // LANES * SUB
            loc_out[PER_ROW + k : PER_ROW + k + 1, cut] = turned[h, at + ID_ROW : at + ID_ROW + 1, :].astype(jnp.int32)
    lane = iota((rows, LANES), 1)
    for k in range(PER_ROW):
        at = k * FEATS
        col = recv[:, at + LOC_ROW : at + LOC_ROW + 1].astype(jnp.int32) % LANES
        w = [recv[:, at + row : at + row + 1] for row in WEIGHT_ROWS]
        here = lane == col
        after = lane == col + 1
        low[k * rows : (k + 1) * rows, :] = jnp.where(here, w[0], jnp.where(after, w[1], 0.0))
        high[k * rows : (k + 1) * rows, :] = jnp.where(here, w[2], jnp.where(after, w[3], 0.0))


def scatter_kernel(first, loc, recv, low, high, obs, turned, odd):
    rows = recv.shape[0]
    groups = range(obs.shape[0])
    turn_slots(recv, turned)

    def clear(i, carry):
        for g in groups:
            at = pl.ds(pl.multiple_of(i * 64, 64), 64)
            obs[g, at, :] = jnp.zeros((64, LANES), jnp.float32)
            odd[g, at, :] = jnp.zeros((64, LANES), jnp.float32)
        return carry

    lax.fori_loop(0, obs.shape[1] // 64, clear, 0)

    def body(i, carry):
        h = i // PER_ROW
        k = i % PER_ROW
        size = len(groups) * SUB
        block = turned[h, pl.ds(pl.multiple_of(k * FEATS + first * SUB, SUB), size), :]
        for seat in range(0, LANES, 2):
            found = []
            for n, total in enumerate((obs, odd)):
                at = pl.multiple_of(loc[k, h * LANES + seat + n], SUB)
                lo = low[pl.ds(k * rows + h * LANES + seat + n, 1), :]
                hi = high[pl.ds(k * rows + h * LANES + seat + n, 1), :]
                for g in groups:
                    value = block[g * SUB : (g + 1) * SUB, seat + n : seat + n + 1]
                    here = total[g, pl.ds(at, SUB), :] + value * lo
                    north = total[g, pl.ds(at + SUB, SUB), :] + value * hi
                    found.append((total, g, at, here, north))
            for total, g, at, here, north in found:
                total[g, pl.ds(at, SUB), :] = here
                total[g, pl.ds(at + SUB, SUB), :] = north
        return carry

    lax.fori_loop(0, (rows // LANES) * PER_ROW, body, 0)

    def join(i, carry):
        for g in groups:
            at = pl.ds(pl.multiple_of(i * 64, 64), 64)
            obs[g, at, :] = obs[g, at, :] + odd[g, at, :]
        return carry

    lax.fori_loop(0, obs.shape[1] // 64, join, 0)


def row_at(index):
    return pl.ds(pl.multiple_of(index * SUB, SUB), SUB)


def rows_at(index, count):
    return pl.ds(pl.multiple_of(index * SUB, SUB), count * SUB)


def send_rows(field, up, down):
    edge = up.shape[1]
    total = field.shape[1]
    for g in range(field.shape[0]):
        up[g] = field[g, total - edge :, :]
        down[g] = field[g, :edge, :]


def field_kernel(begin, sizes, n_lon, group, cap, loc, lat, tiles, obs, norm_h, field, up, down, norm, sem):
    copy = pltpu.make_async_copy(norm_h.at[pl.ds(begin, sum(sizes))], norm, sem)
    copy.start()
    field[...] = jnp.zeros_like(field)
    copy.wait()

    def body(j, carry):
        done = []
        for c in range(group):
            slot = (lat[0] * n_lon + j) * cap + c
            t = loc[PER_ROW + slot % PER_ROW, slot // PER_ROW]
            own = pl.ds(pl.multiple_of(t * SUB, SUB), SUB)
            level = 0
            for g, size in enumerate(sizes):
                for l in range(size):
                    at = pl.ds(t * (SUB * SUB) + l, SUB, stride=SUB)
                    done.append((g, at, norm[level, own, :] * (obs[g, at, :] + tiles[j, level, c])))
                    level += 1
        for g, at, value in done:
            field[g, at, :] = value
        return carry

    lax.fori_loop(0, n_lon, body, 0)
    send_rows(field, up, down)


def stack_kernel(face_x, face_y, cross, wet, field, up, down):
    field[...] = jnp.zeros_like(field)
    sources = (face_x, face_y, cross, wet)

    def body(i, carry):
        values = []
        for n in range(4):
            t = i * 4 + n
            own = pl.ds(pl.multiple_of(t * SUB, SUB), SUB)
            values += [(t, l, source[own, :].astype(jnp.float32)) for l, source in enumerate(sources)]
        for t, l, value in values:
            field[0, pl.ds(t * (SUB * SUB) + l, SUB, stride=SUB), :] = value
        return carry

    lax.fori_loop(0, face_x.shape[0] // SUB // 4, body, 0)
    send_rows(field, up, down)


STRIP = 32
HALF = 2 * STRIP
SEAT = 16
SEATS = HALF // SEAT
TURNS = 10


def span_of(rows):
    return -(-(rows + 2 * STEPS) // (SEATS * TURNS)) * TURNS


def extend(ext, field, above, below):
    groups, total, _ = field.shape
    halo = STEPS * SUB
    for g in range(groups):
        ext[g, :halo, :] = above[g]
        ext[g, halo : halo + total, :] = field[g]
        ext[g, halo + total : 2 * halo + total, :] = below[g]
        ext[g, 2 * halo + total :, :] = jnp.zeros((ext.shape[1] - 2 * halo - total, LANES), jnp.float32)


def edges_kernel(field, above, below, strips, east, west, ext):
    groups = field.shape[0]
    extend(ext, field, above, below)
    span = east.shape[0] // SUB
    lane = iota((SUB, LANES), 1)
    place = lane % HALF

    def body(i, carry):
        done = []
        for n in range(TURNS // 2):
            m = i * (TURNS // 2) + n
            to_east = None
            to_west = None
            for q in range(SEATS):
                first = ext[0, row_at(q * span + m), :]
                second = pltpu.roll(ext[groups - 1, row_at(q * span + m), :], HALF, 1)
                left = jnp.where(lane < HALF, first, second)
                right = jnp.where(lane < HALF, second, first)
                row = jnp.where(place < STRIP, pltpu.roll(left, STEPS, 1), pltpu.roll(right, HALF - STEPS, 1))
                done.append((strips, q * span + m, row))
                right = pltpu.roll(right, SEAT * q + SEAT, 1)
                if q:
                    left = pltpu.roll(left, SEAT * q, 1)
                mine = place // SEAT == q
                to_east = right if q == 0 else jnp.where(mine, right, to_east)
                to_west = left if q == 0 else jnp.where(mine, left, to_west)
            done.append((east, m, to_east))
            done.append((west, m, to_west))
        for ref, m, value in done:
            ref[row_at(m), :] = value
        return carry

    lax.fori_loop(0, span // (TURNS // 2), body, 0)


def build_strips(win, strips, from_west, from_east):
    span = from_west.shape[0] // SUB
    place = iota((SUB, LANES), 1) % HALF

    def body(i, carry):
        for n in range(TURNS):
            m = i * TURNS + n
            west = from_west[row_at(m), :]
            east = from_east[row_at(m), :]
            for q in range(SEATS):
                a = pltpu.roll(west, (STEPS - SEAT - SEAT * q) % LANES, 1)
                b = pltpu.roll(east, (HALF - STEPS - SEAT * q) % LANES, 1)
                row = strips[row_at(q * span + m), :]
                row = jnp.where(place < STEPS, a, jnp.where(place < HALF - STEPS, row, b))
                win[row_at(q * span + m), :] = row
        return carry

    lax.fori_loop(0, span // TURNS, body, 0)
    first = SEATS * span * SUB
    win[first:, :] = jnp.zeros((win.shape[0] - first, LANES), jnp.float32)


def fill_coef(coef, win):
    rows = coef.shape[1]

    def body(i, carry):
        done = []
        for n in range(12):
            b = i * 12 + n
            base = b * (SUB * SUB)
            at = pl.ds(pl.multiple_of(b * SUB, SUB), SUB)
            fx, fy, ct, wet = (win[pl.ds(base + s, SUB, stride=SUB), :] for s in range(4))
            wet_n = win[pl.ds(base + SUB + 3, SUB, stride=SUB), :]
            x = fx * wet * pltpu.roll(wet, LANES - 1, 1)
            xw = pltpu.roll(x, 1, 1)
            y = fy * wet * wet_n
            twist = 0.25 * ct * wet
            for c, value in enumerate((1.0 - x - xw, x, xw, y, twist)):
                done.append((c, at, value))
        for c, at, value in done:
            coef[c, at, :] = value
        return carry

    lax.fori_loop(0, rows // (12 * SUB), body, 0)


def own_coef_kernel(field, above, below, coef, ext):
    extend(ext, field, above, below)
    fill_coef(coef, ext.at[0])


def strip_coef_kernel(strips, from_west, from_east, coef, win):
    build_strips(win, strips, from_west, from_east)
    fill_coef(coef, win)


BY_MATMUL = 0.25


def fill_shift(shift):
    row = iota(shift.shape, 0) % LANES
    col = iota(shift.shape, 1)
    near = jnp.where(col < LANES, col + 1, col + LANES - 1) % LANES
    shift[...] = jnp.where(row == near, 1.0, 0.0).astype(jnp.bfloat16)


def advance(source, target, planes, weight, shift, rows):
    last = rows + 2 * STEPS + 4
    unroll = last // planes
    blocks = last // unroll
    split = int(unroll * BY_MATMUL)

    def rolled(w, index):
        cells = source[w, row_at(index), :]
        east = pltpu.roll(cells, LANES - 1, 1)
        west = pltpu.roll(cells, 1, 1)
        return cells, east, west, east - west

    def shifted_rows(w, first):
        cells = source[w, rows_at(first, split), :]
        high = cells.astype(jnp.bfloat16)
        low = (cells - high.astype(jnp.float32)).astype(jnp.bfloat16)
        both = jnp.concatenate([high, low], axis=1)
        return jnp.dot(both, shift[...], preferred_element_type=jnp.float32)

    y_first = weight(3, 0)
    state = []
    for w in range(planes):
        before = rolled(w, 0)
        now = rolled(w, 1)
        state.append((now, before[3], y_first * (now[0] - before[0])))

    def block(b, state):
        base = 1 + b * unroll
        state = list(state)
        sides = [shifted_rows(w, base + 1) for w in range(planes)]
        for u in range(unroll):
            weights = [weight(c, base + u) for c in range(5)]
            for w in range(planes):
                (cells, east, west, slope), slope_s, flux_s = state[w]
                if u < split:
                    cells_n = source[w, row_at(base + u + 1), :]
                    east_n = sides[w][u * SUB : (u + 1) * SUB, :LANES]
                    west_n = sides[w][u * SUB : (u + 1) * SUB, LANES:]
                    ahead = (cells_n, east_n, west_n, east_n - west_n)
                else:
                    ahead = rolled(w, base + u + 1)
                flux = weights[3] * (ahead[0] - cells)
                target[w, row_at(base + u), :] = (
                    (weights[0] * cells + weights[1] * east)
                    + (weights[2] * west + (flux - flux_s))
                    + weights[4] * (ahead[3] - slope_s)
                )
                state[w] = (ahead, slope, flux)
        return tuple(state)

    lax.fori_loop(0, blocks, block, tuple(state))


def diffuse(win, other, planes, coef, shift, rows):
    fill_shift(shift)

    def weight(c, index):
        return coef[c, pl.ds(index, 1), :]

    def two(t, carry):
        advance(win, other, planes, weight, shift, rows)
        advance(other, win, planes, weight, shift, rows)
        return carry

    for w in range(planes):
        other[w, :SUB, :] = jnp.zeros((SUB, LANES), jnp.float32)
        other[w, other.shape[1] - SUB * SUB :, :] = jnp.zeros((SUB * SUB, LANES), jnp.float32)
    lax.fori_loop(0, STEPS // 2, two, 0)


def own_kernel(field, above, below, coef, mid, win, other, shift):
    groups = field.shape[0]
    rows = mid.shape[1] // SUB
    halo = STEPS * SUB
    extend(win, field, above, below)
    diffuse(win, other, groups, coef, shift, rows)
    for g in range(groups):
        mid[g] = win[g, halo : halo + rows * SUB, :]


MERGE = 32


def strip_kernel(sizes, begin, aliased, earlier, *refs):
    loc, strips, from_west, from_east, coef, mid, low, high, norm_h = refs[:9]
    parts = refs[9 + aliased : 9 + aliased + earlier]
    refs = refs[9 + aliased + earlier :]
    if earlier:
        out_h, packed, sampled, turned = refs[:4]
    else:
        out_h, sampled = refs[:2]
    win, other, shift, smooth, norm, out, sems = refs[-7:]
    groups = mid.shape[0]
    rows = mid.shape[1] // SUB
    levels = pl.ds(begin, sum(sizes))
    copy = pltpu.make_async_copy(norm_h.at[levels], norm, sems.at[0])
    copy.start()
    build_strips(win.at[0], strips, from_west, from_east)
    diffuse(win, other, 1, coef, shift, rows)
    copy.wait()
    lane = iota((SUB, LANES), 1)
    outer = LANES - STEPS

    def merge(b, carry):
        for u in range(MERGE):
            at = row_at(b * MERGE + u)
            strip = win[0, row_at(b * MERGE + u + STEPS), :]
            west = pltpu.roll(strip, outer, 1)
            east = pltpu.roll(strip, HALF + STEPS, 1)
            cells = mid[0, at, :]
            smooth[0, at, :] = jnp.where(lane < STEPS, west, jnp.where(lane < outer, cells, east))
            if groups == 2:
                both = pltpu.roll(jnp.where(lane < HALF, east, west), HALF, 1)
                cells = mid[1, at, :]
                smooth[1, at, :] = jnp.where((lane < STEPS) | (lane >= outer), both, cells)
        return carry

    lax.fori_loop(0, rows // MERGE, merge, 0)

    def scale(i, carry):
        done = []
        for n in range(4):
            b = i * 4 + n
            own = pl.ds(pl.multiple_of(b * SUB, SUB), SUB)
            level = 0
            for g, size in enumerate(sizes):
                for l in range(size):
                    at = pl.ds(b * (SUB * SUB) + l, SUB, stride=SUB)
                    done.append((g, at, level, own, smooth[g, at, :] * norm[level, own, :]))
                    level += 1
        for g, at, level, own, value in done:
            out[level, own, :] = value
            smooth[g, at, :] = value
        return carry

    lax.fori_loop(0, rows // (4 * SUB), scale, 0)
    back = pltpu.make_async_copy(out, out_h.at[levels], sems.at[1])
    back.start()
    count = low.shape[0] // PER_ROW
    halves = count // LANES

    def samples(i, carry):
        h = i // PER_ROW
        k = i % PER_ROW
        kept = [[jnp.zeros((SUB, LANES), jnp.float32)] * 4 for _ in range(groups)]
        for seat in range(LANES):
            at = pl.multiple_of(loc[k, h * LANES + seat], SUB)
            lo = low[pl.ds(k * count + h * LANES + seat, 1), :]
            hi = high[pl.ds(k * count + h * LANES + seat, 1), :]
            for g in range(groups):
                value = smooth[g, pl.ds(at, SUB), :] * lo + smooth[g, pl.ds(at + SUB, SUB), :] * hi
                total = jnp.sum(value, axis=1, keepdims=True)
                kept[g][seat % 4] = jnp.where(lane == seat, total, kept[g][seat % 4])
        for g in range(groups):
            a, b, c, d = kept[g]
            sampled[h, g, row_at(k), :] = (a + b) + (c + d)
        return carry

    lax.fori_loop(0, halves * PER_ROW, samples, 0)
    if earlier:
        pack_samples(parts + (sampled,), packed, turned)
    back.wait()


def pack_samples(parts, out, turned):
    for h in range(turned.shape[0]):
        index = 0
        for part in parts:
            for g in range(part.shape[1]):
                for k in range(PER_ROW):
                    at = k * FEATS + index * SUB
                    turned[h, at : at + SUB, :] = part[h, g, k * SUB : (k + 1) * SUB, :]
                index += 1
        out[h * LANES : (h + 1) * LANES, :] = turned[h].T


def exchange_rows(up, down, n_lat):
    pairs = [(i, i + 1) for i in range(n_lat - 1)]
    back = [(i + 1, i) for i in range(n_lat - 1)]
    return lax.ppermute(up, "lat", pairs), lax.ppermute(down, "lat", back)


def exchange_columns(east, west, n_lon):
    pairs = [(i, (i + 1) % n_lon) for i in range(n_lon)]
    back = [((i + 1) % n_lon, i) for i in range(n_lon)]
    return lax.ppermute(east, "lon", pairs), lax.ppermute(west, "lon", back)


def on_device(
    innovations,
    owners,
    prof_row,
    prof_col,
    interp_weights,
    model_tiles,
    model_ids,
    face_x,
    face_y,
    cross_term,
    wet_mask,
    norm_factor,
):
    n_lat = lax.axis_size("lat")
    n_lon = lax.axis_size("lon")
    devices = n_lat * n_lon
    levels, lat_cells, lon_cells = norm_factor.shape
    tiles = model_tiles.shape[1]
    group = tiles // n_lon
    count = innovations.shape[1]
    cap = 2 * count // devices
    slots = devices * cap
    rows = slots // PER_ROW
    starts = group_starts()
    f32 = jnp.float32
    lat = lax.axis_index("lat").reshape(1)
    both = ("lat", "lon")
    span = span_of(lat_cells)
    ext_rows = SEATS * span
    win_rows = ext_rows + SUB

    def arrays(*shapes):
        return tuple(jax.ShapeDtypeStruct(shape, f32) for shape in shapes)

    def call(kernel, out_shape, micros, name, grant=SMALL, **kwargs):
        return pl.pallas_call(
            kernel,
            out_shape=out_shape,
            compiler_params=params(grant),
            cost_estimate=cost(micros),
            name=name,
            **kwargs,
        )

    def after(value, *others):
        return lax.optimization_barrier((value,) + others)[0]

    def tile_exchange(chunk, *others):
        first = sum(CHUNKS[:chunk])
        begin = starts[first]
        size = sum(GROUPS[first : first + CHUNKS[chunk]])
        piece = model_tiles[begin : begin + size].reshape(size, n_lon, group, SUB, LANES)
        piece = jnp.transpose(piece, (1, 0, 2, 3, 4))
        if others:
            piece = after(piece, *others)
        return lax.all_to_all(piece, "lon", split_axis=0, concat_axis=0, tiled=True)

    def halo(field, up, down, groups):
        above, below = exchange_rows(up, down, n_lat)
        strips, east, west = call(
            edges_kernel,
            arrays((ext_rows * SUB, LANES), (span * SUB, LANES), (span * SUB, LANES)),
            3,
            "edges",
            scratch_shapes=[pltpu.VMEM((groups, ext_rows * SUB, LANES), f32)],
        )(field, above, below)
        return (field, above, below, strips) + exchange_columns(east, west, n_lon)

    def field_shapes(groups):
        return arrays(
            (groups, lat_cells * SUB, LANES),
            (groups, STEPS * SUB, LANES),
            (groups, STEPS * SUB, LANES),
        )

    send, slot = call(
        functools.partial(route_kernel, cap, group, n_lat, starts),
        (jax.ShapeDtypeStruct((rows, LANES), f32), jax.ShapeDtypeStruct((1, count), jnp.int32)),
        3,
        "route",
        LARGE,
        scratch_shapes=[pltpu.VMEM((FEATS, count + devices * group), f32)],
    )(
        innovations,
        interp_weights,
        owners.reshape(1, count),
        prof_row.reshape(1, count),
        prof_col.reshape(1, count),
        model_ids,
    )
    stacked = call(stack_kernel, field_shapes(1), 3, "stack")(face_x, face_y, cross_term, wet_mask)
    stack, above, below, coef_strips, coef_west, coef_east = halo(*stacked, 1)
    own_coef = call(
        own_coef_kernel,
        arrays((5, win_rows, LANES))[0],
        3,
        "own_coef",
        scratch_shapes=[pltpu.VMEM((1, (win_rows + SUB) * SUB, LANES), f32)],
    )(stack, above, below)
    recv = lax.all_to_all(
        send.reshape(devices, rows // devices, LANES), both, split_axis=0, concat_axis=0, tiled=True
    ).reshape(rows, LANES)
    pieces = [tile_exchange(0, recv, stacked[0])]

    smem = pl.BlockSpec(memory_space=pltpu.SMEM)
    vmem = pl.BlockSpec(memory_space=pltpu.VMEM)
    hbm = pl.BlockSpec(memory_space=pltpu.HBM)
    turned = pltpu.VMEM((rows // LANES, LANES, LANES), f32)
    low, high, loc = call(
        place_kernel,
        arrays((slots, LANES), (slots, LANES)) + (jax.ShapeDtypeStruct((2 * PER_ROW, rows), jnp.int32),),
        2,
        "place",
        LARGE,
        scratch_shapes=[turned],
    )(recv)

    def scatter(chunk, grant):
        first = sum(CHUNKS[:chunk])
        return call(
            functools.partial(scatter_kernel, first),
            arrays((CHUNKS[chunk], lat_cells * SUB, LANES))[0],
            9,
            "scatter",
            grant,
            in_specs=[smem, vmem, vmem, vmem],
            scratch_shapes=[turned, pltpu.VMEM((CHUNKS[chunk], lat_cells * SUB, LANES), f32)],
        )(loc, recv, low, high)

    observed = [scatter(0, LARGE), scatter(1, SMALL)]
    pieces.append(tile_exchange(1, pieces[0], observed[0], own_coef, coef_west, coef_east))
    shift_space = pltpu.VMEM((2 * LANES, 2 * LANES), jnp.bfloat16)
    smoothed = None
    sampled = []
    first = 0
    for chunk, groups in enumerate(CHUNKS):
        sizes = GROUPS[first : first + groups]
        begin = starts[first]
        own_levels = (sum(sizes), lat_cells, LANES)
        field = call(
            functools.partial(field_kernel, begin, sizes, n_lon, group, cap),
            field_shapes(groups),
            4,
            "field",
            in_specs=[smem, smem, vmem, vmem, hbm],
            scratch_shapes=[pltpu.VMEM(own_levels, f32), pltpu.SemaphoreType.DMA],
        )(loc, lat, pieces[chunk], observed[chunk], norm_factor)
        field, above, below, strips, from_west, from_east = halo(*field, groups)
        mid_shape = (groups, lat_cells * SUB, LANES)
        win_shape = (groups, win_rows * SUB, LANES)
        mid = call(
            own_kernel,
            arrays(mid_shape)[0],
            6 * groups,
            "own",
            scratch_shapes=[pltpu.VMEM(win_shape, f32), pltpu.VMEM(win_shape, f32), shift_space],
        )(after(field, strips), above, below, own_coef)
        if chunk == 0:
            strip_coef = call(
                strip_coef_kernel,
                arrays((5, win_rows, LANES))[0],
                3,
                "strip_coef",
                scratch_shapes=[pltpu.VMEM(((win_rows + SUB) * SUB, LANES), f32)],
            )(after(coef_strips, mid, *observed[1:]), coef_west, coef_east)
        if chunk + 1 < len(CHUNKS):
            pieces[chunk + 1] = after(pieces[chunk + 1], mid)
        operands = [loc, strips, from_west, from_east, strip_coef, mid, low, high, norm_factor]
        specs = [smem] + [vmem] * 7 + [hbm]
        aliases = {}
        if smoothed is not None:
            aliases = {len(operands): 0}
            operands.append(smoothed)
            specs.append(hbm)
        last = chunk + 1 == len(CHUNKS)
        earlier = sampled if last else []
        part_shape = (rows // LANES, groups, PER_ROW * SUB, LANES)
        gathered = [pltpu.VMEM(part_shape, f32), pltpu.VMEM((rows // LANES, LANES, LANES), f32)]
        smoothed, part = call(
            functools.partial(strip_kernel, sizes, begin, len(aliases), len(earlier)),
            arrays(norm_factor.shape, (rows, LANES) if earlier else part_shape),
            12,
            "strips",
            in_specs=specs + [vmem] * len(earlier),
            out_specs=(hbm, vmem),
            scratch_shapes=(gathered if earlier else [])
            + [
                pltpu.VMEM((1,) + win_shape[1:], f32),
                pltpu.VMEM((1,) + win_shape[1:], f32),
                shift_space,
                pltpu.VMEM(mid_shape, f32),
                pltpu.VMEM(own_levels, f32),
                pltpu.VMEM(own_levels, f32),
                pltpu.SemaphoreType.DMA((2,)),
            ],
            input_output_aliases=aliases,
        )(*operands, *earlier)
        sampled.append(part)
        first += groups

    back = sampled[-1]
    returned = lax.all_to_all(
        back.reshape(devices, rows // devices, LANES), both, split_axis=0, concat_axis=0, tiled=True
    ).reshape(rows, LANES)
    profile_values = call(
        functools.partial(unpack_kernel, starts),
        arrays((levels, count))[0],
        1,
        "unpack",
    )(returned, slot)
    return (smoothed, profile_values)


def solution(mesh):
    in_specs = (
        P(None, ("lat", "lon")),
        P(("lat", "lon"), None),
        P(("lat", "lon")),
        P(("lat", "lon")),
        P(None, ("lat", "lon")),
        P(None, ("lat", "lon"), None, None),
        P(None, ("lat", "lon")),
        P("lat", "lon"),
        P("lat", "lon"),
        P("lat", "lon"),
        P("lat", "lon"),
        P(None, "lat", "lon"),
    )
    out_specs = (P(None, "lat", "lon"), P(None, ("lat", "lon")))
    return jax.shard_map(
        on_device, mesh=mesh, in_specs=in_specs, out_specs=out_specs, check_vma=False
    )
```

```python
import functools
import jax
import jax.numpy as jnp
from jax import lax
from jax.experimental import pallas as pl
from jax.experimental.pallas import tpu as pltpu
from jax.sharding import PartitionSpec as P

STEPS = 10
SUB = 8
LANES = 128
FEATS = 32
PER_ROW = LANES // FEATS
GROUPS = (5, 4, 8, 8)
CHUNKS = (2, 2)
EXCHANGES = ((0, 1), (2,), (3,))
WEIGHT_ROWS = (5, 6, 12, 13)
LOC_ROW = 7
ID_ROW = 15
SMALL = 20 * 1024 * 1024
LARGE = 60 * 1024 * 1024


def group_starts():
    starts = []
    total = 0
    for count in GROUPS:
        starts.append(total)
        total += count
    return starts


def params(grant):
    return pltpu.CompilerParams(vmem_limit_bytes=grant)


def cost(micros):
    return pl.CostEstimate(flops=0, bytes_accessed=int(micros * 2e5), transcendentals=0)


def iota(shape, dim):
    return lax.broadcasted_iota(jnp.int32, shape, dim)


def split3(values):
    high = values.astype(jnp.bfloat16)
    rest = values - high.astype(jnp.float32)
    middle = rest.astype(jnp.bfloat16)
    low = (rest - middle.astype(jnp.float32)).astype(jnp.bfloat16)
    return high, middle, low


def route_kernel(cap, group, copies, starts, innov, weights, own_row, prow, pcol, ids, send, slot_out, pay):
    count = innov.shape[1]
    tiles = ids.shape[1]
    extra = tiles * copies
    owner = own_row[...]
    column = jnp.broadcast_to(owner.astype(jnp.float32), (SUB, count)).T[:, :1].astype(jnp.int32)
    same = column == owner
    before = iota((count, count), 0) < iota((count, count), 1)
    ones = jnp.where(same & before, 1.0, 0.0)
    rank = jnp.sum(ones, axis=0, keepdims=True).astype(jnp.int32)
    slot = owner * cap + rank
    slot_out[...] = slot
    number = iota((1, extra), 1)
    id_slot = (number // group) * cap + number % group
    pay[...] = jnp.zeros_like(pay)
    for index, count_in in enumerate(GROUPS):
        pay[index * SUB : index * SUB + count_in, :count] = innov[starts[index] : starts[index] + count_in, :]
    for corner, row in enumerate(WEIGHT_ROWS):
        pay[row : row + 1, :count] = weights[corner : corner + 1, :]
    pay[LOC_ROW : LOC_ROW + 1, :count] = (prow[...] * LANES + pcol[...]).astype(jnp.float32)
    for i in range(copies):
        at = count + i * tiles
        pay[ID_ROW : ID_ROW + 1, at : at + tiles] = ids[...].astype(jnp.float32)
    slots = jnp.concatenate([slot, id_slot], axis=1)
    values = pay[...]
    part = slots % PER_ROW
    spread = jnp.concatenate([jnp.where(part == k, values, 0.0) for k in range(PER_ROW)], axis=0)
    rows = send.shape[0]
    hot = jnp.where(iota((rows, count + extra), 0) == slots // PER_ROW, 1.0, 0.0).astype(jnp.bfloat16)
    total = None
    for piece in split3(spread):
        term = lax.dot_general(hot, piece, (((1,), (1,)), ((), ())), preferred_element_type=jnp.float32)
        total = term if total is None else total + term
    send[...] = total


def unpack_kernel(starts, recv, slot, out):
    slots = slot[...]
    rows = recv.shape[0]
    hot = jnp.where(iota((rows, slots.shape[1]), 0) == slots // PER_ROW, 1.0, 0.0).astype(jnp.bfloat16)
    total = None
    for piece in split3(recv[...]):
        term = lax.dot_general(piece, hot, (((0,), (0,)), ((), ())), preferred_element_type=jnp.float32)
        total = term if total is None else total + term
    part = slots % PER_ROW
    picked = jnp.zeros((FEATS, slots.shape[1]), jnp.float32)
    for k in range(PER_ROW):
        picked = jnp.where(part == k, total[k * FEATS : (k + 1) * FEATS], picked)
    for index, count_in in enumerate(GROUPS):
        out[starts[index] : starts[index] + count_in, :] = picked[index * SUB : index * SUB + count_in]


def turn_slots(recv, turned):
    for h in range(recv.shape[0] // LANES):
        turned[h] = recv[h * LANES : (h + 1) * LANES, :].T


def place_kernel(recv, low, high, loc_out, turned):
    rows = recv.shape[0]
    turn_slots(recv, turned)
    for k in range(PER_ROW):
        for h in range(rows // LANES):
            at = k * FEATS
            cut = slice(h * LANES, (h + 1) * LANES)
            cells = turned[h, at + LOC_ROW : at + LOC_ROW + 1, :].astype(jnp.int32)
            loc_out[k : k + 1, cut] = cells // LANES * SUB
            loc_out[PER_ROW + k : PER_ROW + k + 1, cut] = turned[h, at + ID_ROW : at + ID_ROW + 1, :].astype(jnp.int32)
    lane = iota((rows, LANES), 1)
    for k in range(PER_ROW):
        at = k * FEATS
        col = recv[:, at + LOC_ROW : at + LOC_ROW + 1].astype(jnp.int32) % LANES
        w = [recv[:, at + row : at + row + 1] for row in WEIGHT_ROWS]
        here = lane == col
        after = lane == col + 1
        low[k * rows : (k + 1) * rows, :] = jnp.where(here, w[0], jnp.where(after, w[1], 0.0))
        high[k * rows : (k + 1) * rows, :] = jnp.where(here, w[2], jnp.where(after, w[3], 0.0))


def scatter_kernel(first, loc, recv, low, high, obs, turned, odd):
    rows = recv.shape[0]
    groups = range(obs.shape[0])
    turn_slots(recv, turned)

    def clear(i, carry):
        for g in groups:
            at = pl.ds(pl.multiple_of(i * 64, 64), 64)
            obs[g, at, :] = jnp.zeros((64, LANES), jnp.float32)
            odd[g, at, :] = jnp.zeros((64, LANES), jnp.float32)
        return carry

    lax.fori_loop(0, obs.shape[1] // 64, clear, 0)

    def body(i, carry):
        h = i // PER_ROW
        k = i % PER_ROW
        size = len(groups) * SUB
        block = turned[h, pl.ds(pl.multiple_of(k * FEATS + first * SUB, SUB), size), :]
        for seat in range(0, LANES, 2):
            found = []
            for n, total in enumerate((obs, odd)):
                at = pl.multiple_of(loc[k, h * LANES + seat + n], SUB)
                lo = low[pl.ds(k * rows + h * LANES + seat + n, 1), :]
                hi = high[pl.ds(k * rows + h * LANES + seat + n, 1), :]
                for g in groups:
                    value = block[g * SUB : (g + 1) * SUB, seat + n : seat + n + 1]
                    here = total[g, pl.ds(at, SUB), :] + value * lo
                    north = total[g, pl.ds(at + SUB, SUB), :] + value * hi
                    found.append((total, g, at, here, north))
            for total, g, at, here, north in found:
                total[g, pl.ds(at, SUB), :] = here
                total[g, pl.ds(at + SUB, SUB), :] = north
        return carry

    lax.fori_loop(0, (rows // LANES) * PER_ROW, body, 0)

    def join(i, carry):
        for g in groups:
            at = pl.ds(pl.multiple_of(i * 64, 64), 64)
            obs[g, at, :] = obs[g, at, :] + odd[g, at, :]
        return carry

    lax.fori_loop(0, obs.shape[1] // 64, join, 0)


def row_at(index):
    return pl.ds(pl.multiple_of(index * SUB, SUB), SUB)


def rows_at(index, count):
    return pl.ds(pl.multiple_of(index * SUB, SUB), count * SUB)


def send_rows(field, up, down):
    edge = up.shape[1]
    total = field.shape[1]
    for g in range(field.shape[0]):
        up[g] = field[g, total - edge :, :]
        down[g] = field[g, :edge, :]


def field_kernel(begin, sizes, places, n_lon, group, cap, loc, lat, obs, norm_h, *refs):
    tiles = refs[:-5]
    field, up, down, norm, sem = refs[-5:]
    copy = pltpu.make_async_copy(norm_h.at[pl.ds(begin, sum(sizes))], norm, sem)
    copy.start()
    field[...] = jnp.zeros_like(field)
    copy.wait()

    def body(j, carry):
        done = []
        for c in range(group):
            slot = (lat[0] * n_lon + j) * cap + c
            t = loc[PER_ROW + slot % PER_ROW, slot // PER_ROW]
            own = pl.ds(pl.multiple_of(t * SUB, SUB), SUB)
            level = 0
            for g, size in enumerate(sizes):
                source, offset = places[g]
                for l in range(size):
                    at = pl.ds(t * (SUB * SUB) + l, SUB, stride=SUB)
                    cells = tiles[source][j, offset + l, c]
                    done.append((g, at, norm[level, own, :] * (obs[g, at, :] + cells)))
                    level += 1
        for g, at, value in done:
            field[g, at, :] = value
        return carry

    lax.fori_loop(0, n_lon, body, 0)
    send_rows(field, up, down)


def stack_kernel(face_x, face_y, cross, wet, field, up, down):
    field[...] = jnp.zeros_like(field)
    sources = (face_x, face_y, cross, wet)

    def body(i, carry):
        values = []
        for n in range(4):
            t = i * 4 + n
            own = pl.ds(pl.multiple_of(t * SUB, SUB), SUB)
            values += [(t, l, source[own, :].astype(jnp.float32)) for l, source in enumerate(sources)]
        for t, l, value in values:
            field[0, pl.ds(t * (SUB * SUB) + l, SUB, stride=SUB), :] = value
        return carry

    lax.fori_loop(0, face_x.shape[0] // SUB // 4, body, 0)
    send_rows(field, up, down)


STRIP = 32
HALF = 2 * STRIP
SEAT = 16
SEATS = HALF // SEAT
TURNS = 10


def span_of(rows):
    return -(-(rows + 2 * STEPS) // (SEATS * TURNS)) * TURNS


def extend(ext, field, above, below):
    groups, total, _ = field.shape
    halo = STEPS * SUB
    for g in range(groups):
        ext[g, :halo, :] = above[g]
        ext[g, halo : halo + total, :] = field[g]
        ext[g, halo + total : 2 * halo + total, :] = below[g]
        ext[g, 2 * halo + total :, :] = jnp.zeros((ext.shape[1] - 2 * halo - total, LANES), jnp.float32)


def edges_kernel(field, above, below, strips, east, west, ext):
    groups = field.shape[0]
    extend(ext, field, above, below)
    span = east.shape[0] // SUB
    lane = iota((SUB, LANES), 1)
    place = lane % HALF

    def body(i, carry):
        done = []
        for n in range(TURNS // 2):
            m = i * (TURNS // 2) + n
            to_east = None
            to_west = None
            for q in range(SEATS):
                first = ext[0, row_at(q * span + m), :]
                second = pltpu.roll(ext[groups - 1, row_at(q * span + m), :], HALF, 1)
                left = jnp.where(lane < HALF, first, second)
                right = jnp.where(lane < HALF, second, first)
                row = jnp.where(place < STRIP, pltpu.roll(left, STEPS, 1), pltpu.roll(right, HALF - STEPS, 1))
                done.append((strips, q * span + m, row))
                right = pltpu.roll(right, SEAT * q + SEAT, 1)
                if q:
                    left = pltpu.roll(left, SEAT * q, 1)
                mine = place // SEAT == q
                to_east = right if q == 0 else jnp.where(mine, right, to_east)
                to_west = left if q == 0 else jnp.where(mine, left, to_west)
            done.append((east, m, to_east))
            done.append((west, m, to_west))
        for ref, m, value in done:
            ref[row_at(m), :] = value
        return carry

    lax.fori_loop(0, span // (TURNS // 2), body, 0)


def build_strips(win, strips, from_west, from_east):
    span = from_west.shape[0] // SUB
    place = iota((SUB, LANES), 1) % HALF

    def body(i, carry):
        for n in range(TURNS):
            m = i * TURNS + n
            west = from_west[row_at(m), :]
            east = from_east[row_at(m), :]
            for q in range(SEATS):
                a = pltpu.roll(west, (STEPS - SEAT - SEAT * q) % LANES, 1)
                b = pltpu.roll(east, (HALF - STEPS - SEAT * q) % LANES, 1)
                row = strips[row_at(q * span + m), :]
                row = jnp.where(place < STEPS, a, jnp.where(place < HALF - STEPS, row, b))
                win[row_at(q * span + m), :] = row
        return carry

    lax.fori_loop(0, span // TURNS, body, 0)
    first = SEATS * span * SUB
    win[first:, :] = jnp.zeros((win.shape[0] - first, LANES), jnp.float32)


def fill_coef(coef, win):
    rows = coef.shape[1]

    def body(i, carry):
        done = []
        for n in range(12):
            b = i * 12 + n
            base = b * (SUB * SUB)
            at = pl.ds(pl.multiple_of(b * SUB, SUB), SUB)
            fx, fy, ct, wet = (win[pl.ds(base + s, SUB, stride=SUB), :] for s in range(4))
            wet_n = win[pl.ds(base + SUB + 3, SUB, stride=SUB), :]
            x = fx * wet * pltpu.roll(wet, LANES - 1, 1)
            xw = pltpu.roll(x, 1, 1)
            y = fy * wet * wet_n
            twist = 0.25 * ct * wet
            for c, value in enumerate((1.0 - x - xw, x, xw, y, twist)):
                done.append((c, at, value))
        for c, at, value in done:
            coef[c, at, :] = value
        return carry

    lax.fori_loop(0, rows // (12 * SUB), body, 0)


def own_coef_kernel(field, above, below, coef, ext):
    extend(ext, field, above, below)
    fill_coef(coef, ext.at[0])


def strip_coef_kernel(strips, from_west, from_east, coef, win):
    build_strips(win, strips, from_west, from_east)
    fill_coef(coef, win)


BY_MATMUL = 0.25


def fill_shift(shift):
    row = iota(shift.shape, 0) % LANES
    col = iota(shift.shape, 1)
    near = jnp.where(col < LANES, col + 1, col + LANES - 1) % LANES
    shift[...] = jnp.where(row == near, 1.0, 0.0).astype(jnp.bfloat16)


def advance(source, target, planes, weight, shift, rows):
    last = rows + 2 * STEPS + 4
    unroll = last // planes
    blocks = last // unroll
    split = int(unroll * BY_MATMUL)

    def rolled(w, index):
        cells = source[w, row_at(index), :]
        east = pltpu.roll(cells, LANES - 1, 1)
        west = pltpu.roll(cells, 1, 1)
        return cells, east, west, east - west

    def shifted_rows(w, first):
        cells = source[w, rows_at(first, split), :]
        high = cells.astype(jnp.bfloat16)
        low = (cells - high.astype(jnp.float32)).astype(jnp.bfloat16)
        both = jnp.concatenate([high, low], axis=1)
        return jnp.dot(both, shift[...], preferred_element_type=jnp.float32)

    y_first = weight(3, 0)
    state = []
    for w in range(planes):
        before = rolled(w, 0)
        now = rolled(w, 1)
        state.append((now, before[3], y_first * (now[0] - before[0])))

    def block(b, state):
        base = 1 + b * unroll
        state = list(state)
        sides = [shifted_rows(w, base + 1) for w in range(planes)]
        for u in range(unroll):
            weights = [weight(c, base + u) for c in range(5)]
            for w in range(planes):
                (cells, east, west, slope), slope_s, flux_s = state[w]
                if u < split:
                    cells_n = source[w, row_at(base + u + 1), :]
                    east_n = sides[w][u * SUB : (u + 1) * SUB, :LANES]
                    west_n = sides[w][u * SUB : (u + 1) * SUB, LANES:]
                    ahead = (cells_n, east_n, west_n, east_n - west_n)
                else:
                    ahead = rolled(w, base + u + 1)
                flux = weights[3] * (ahead[0] - cells)
                target[w, row_at(base + u), :] = (
                    (weights[0] * cells + weights[1] * east)
                    + (weights[2] * west + (flux - flux_s))
                    + weights[4] * (ahead[3] - slope_s)
                )
                state[w] = (ahead, slope, flux)
        return tuple(state)

    lax.fori_loop(0, blocks, block, tuple(state))


def diffuse(win, other, planes, coef, shift, rows):
    fill_shift(shift)

    def weight(c, index):
        return coef[c, pl.ds(index, 1), :]

    def two(t, carry):
        advance(win, other, planes, weight, shift, rows)
        advance(other, win, planes, weight, shift, rows)
        return carry

    for w in range(planes):
        other[w, :SUB, :] = jnp.zeros((SUB, LANES), jnp.float32)
        other[w, other.shape[1] - SUB * SUB :, :] = jnp.zeros((SUB * SUB, LANES), jnp.float32)
    lax.fori_loop(0, STEPS // 2, two, 0)


def own_kernel(field, above, below, coef, mid, win, other, shift):
    groups = field.shape[0]
    rows = mid.shape[1] // SUB
    halo = STEPS * SUB
    extend(win, field, above, below)
    diffuse(win, other, groups, coef, shift, rows)
    for g in range(groups):
        mid[g] = win[g, halo : halo + rows * SUB, :]


MERGE = 32


def strip_kernel(sizes, begin, aliased, earlier, *refs):
    loc, strips, from_west, from_east, coef, mid, low, high, norm_h = refs[:9]
    parts = refs[9 + aliased : 9 + aliased + earlier]
    refs = refs[9 + aliased + earlier :]
    if earlier:
        out_h, packed, sampled, turned = refs[:4]
    else:
        out_h, sampled = refs[:2]
    win, other, shift, smooth, norm, out, sems = refs[-7:]
    groups = mid.shape[0]
    rows = mid.shape[1] // SUB
    levels = pl.ds(begin, sum(sizes))
    copy = pltpu.make_async_copy(norm_h.at[levels], norm, sems.at[0])
    copy.start()
    build_strips(win.at[0], strips, from_west, from_east)
    diffuse(win, other, 1, coef, shift, rows)
    copy.wait()
    lane = iota((SUB, LANES), 1)
    outer = LANES - STEPS

    def merge(b, carry):
        for u in range(MERGE):
            at = row_at(b * MERGE + u)
            strip = win[0, row_at(b * MERGE + u + STEPS), :]
            west = pltpu.roll(strip, outer, 1)
            east = pltpu.roll(strip, HALF + STEPS, 1)
            cells = mid[0, at, :]
            smooth[0, at, :] = jnp.where(lane < STEPS, west, jnp.where(lane < outer, cells, east))
            if groups == 2:
                both = pltpu.roll(jnp.where(lane < HALF, east, west), HALF, 1)
                cells = mid[1, at, :]
                smooth[1, at, :] = jnp.where((lane < STEPS) | (lane >= outer), both, cells)
        return carry

    lax.fori_loop(0, rows // MERGE, merge, 0)

    def scale(i, carry):
        done = []
        for n in range(4):
            b = i * 4 + n
            own = pl.ds(pl.multiple_of(b * SUB, SUB), SUB)
            level = 0
            for g, size in enumerate(sizes):
                for l in range(size):
                    at = pl.ds(b * (SUB * SUB) + l, SUB, stride=SUB)
                    done.append((g, at, level, own, smooth[g, at, :] * norm[level, own, :]))
                    level += 1
        for g, at, level, own, value in done:
            out[level, own, :] = value
            smooth[g, at, :] = value
        return carry

    lax.fori_loop(0, rows // (4 * SUB), scale, 0)
    back = pltpu.make_async_copy(out, out_h.at[levels], sems.at[1])
    back.start()
    count = low.shape[0] // PER_ROW
    halves = count // LANES

    def samples(i, carry):
        h = i // PER_ROW
        k = i % PER_ROW
        kept = [[jnp.zeros((SUB, LANES), jnp.float32)] * 4 for _ in range(groups)]
        for seat in range(LANES):
            at = pl.multiple_of(loc[k, h * LANES + seat], SUB)
            lo = low[pl.ds(k * count + h * LANES + seat, 1), :]
            hi = high[pl.ds(k * count + h * LANES + seat, 1), :]
            for g in range(groups):
                value = smooth[g, pl.ds(at, SUB), :] * lo + smooth[g, pl.ds(at + SUB, SUB), :] * hi
                total = jnp.sum(value, axis=1, keepdims=True)
                kept[g][seat % 4] = jnp.where(lane == seat, total, kept[g][seat % 4])
        for g in range(groups):
            a, b, c, d = kept[g]
            sampled[h, g, row_at(k), :] = (a + b) + (c + d)
        return carry

    lax.fori_loop(0, halves * PER_ROW, samples, 0)
    if earlier:
        pack_samples(parts + (sampled,), packed, turned)
    back.wait()


def pack_samples(parts, out, turned):
    for h in range(turned.shape[0]):
        index = 0
        for part in parts:
            for g in range(part.shape[1]):
                for k in range(PER_ROW):
                    at = k * FEATS + index * SUB
                    turned[h, at : at + SUB, :] = part[h, g, k * SUB : (k + 1) * SUB, :]
                index += 1
        out[h * LANES : (h + 1) * LANES, :] = turned[h].T


def exchange_rows(up, down, n_lat):
    pairs = [(i, i + 1) for i in range(n_lat - 1)]
    back = [(i + 1, i) for i in range(n_lat - 1)]
    return lax.ppermute(up, "lat", pairs), lax.ppermute(down, "lat", back)


def exchange_columns(east, west, n_lon):
    pairs = [(i, (i + 1) % n_lon) for i in range(n_lon)]
    back = [((i + 1) % n_lon, i) for i in range(n_lon)]
    return lax.ppermute(east, "lon", pairs), lax.ppermute(west, "lon", back)


def on_device(
    innovations,
    owners,
    prof_row,
    prof_col,
    interp_weights,
    model_tiles,
    model_ids,
    face_x,
    face_y,
    cross_term,
    wet_mask,
    norm_factor,
):
    n_lat = lax.axis_size("lat")
    n_lon = lax.axis_size("lon")
    devices = n_lat * n_lon
    levels, lat_cells, lon_cells = norm_factor.shape
    tiles = model_tiles.shape[1]
    group = tiles // n_lon
    count = innovations.shape[1]
    cap = 2 * count // devices
    slots = devices * cap
    rows = slots // PER_ROW
    starts = group_starts()
    f32 = jnp.float32
    lat = lax.axis_index("lat").reshape(1)
    both = ("lat", "lon")
    span = span_of(lat_cells)
    ext_rows = SEATS * span
    win_rows = ext_rows + SUB

    def arrays(*shapes):
        return tuple(jax.ShapeDtypeStruct(shape, f32) for shape in shapes)

    def call(kernel, out_shape, micros, name, grant=SMALL, **kwargs):
        return pl.pallas_call(
            kernel,
            out_shape=out_shape,
            compiler_params=params(grant),
            cost_estimate=cost(micros),
            name=name,
            **kwargs,
        )

    def after(value, *others):
        return lax.optimization_barrier((value,) + others)[0]

    def tile_exchange(number, *others):
        members = EXCHANGES[number]
        begin = starts[members[0]]
        size = sum(GROUPS[index] for index in members)
        piece = model_tiles[begin : begin + size].reshape(size, n_lon, group, SUB, LANES)
        piece = jnp.transpose(piece, (1, 0, 2, 3, 4))
        if others:
            piece = after(piece, *others)
        return lax.all_to_all(piece, "lon", split_axis=0, concat_axis=0, tiled=True)

    def halo(field, up, down, groups):
        above, below = exchange_rows(up, down, n_lat)
        strips, east, west = call(
            edges_kernel,
            arrays((ext_rows * SUB, LANES), (span * SUB, LANES), (span * SUB, LANES)),
            3,
            "edges",
            scratch_shapes=[pltpu.VMEM((groups, ext_rows * SUB, LANES), f32)],
        )(field, above, below)
        return (field, above, below, strips) + exchange_columns(east, west, n_lon)

    def field_shapes(groups):
        return arrays(
            (groups, lat_cells * SUB, LANES),
            (groups, STEPS * SUB, LANES),
            (groups, STEPS * SUB, LANES),
        )

    send, slot = call(
        functools.partial(route_kernel, cap, group, n_lat, starts),
        (jax.ShapeDtypeStruct((rows, LANES), f32), jax.ShapeDtypeStruct((1, count), jnp.int32)),
        3,
        "route",
        LARGE,
        scratch_shapes=[pltpu.VMEM((FEATS, count + devices * group), f32)],
    )(
        innovations,
        interp_weights,
        owners.reshape(1, count),
        prof_row.reshape(1, count),
        prof_col.reshape(1, count),
        model_ids,
    )
    stacked = call(stack_kernel, field_shapes(1), 3, "stack")(face_x, face_y, cross_term, wet_mask)
    stack, above, below, coef_strips, coef_west, coef_east = halo(*stacked, 1)
    own_coef = call(
        own_coef_kernel,
        arrays((5, win_rows, LANES))[0],
        3,
        "own_coef",
        scratch_shapes=[pltpu.VMEM((1, (win_rows + SUB) * SUB, LANES), f32)],
    )(stack, above, below)
    recv = lax.all_to_all(
        send.reshape(devices, rows // devices, LANES), both, split_axis=0, concat_axis=0, tiled=True
    ).reshape(rows, LANES)
    pieces = [tile_exchange(0, recv, stacked[0])]

    smem = pl.BlockSpec(memory_space=pltpu.SMEM)
    vmem = pl.BlockSpec(memory_space=pltpu.VMEM)
    hbm = pl.BlockSpec(memory_space=pltpu.HBM)
    turned = pltpu.VMEM((rows // LANES, LANES, LANES), f32)
    low, high, loc = call(
        place_kernel,
        arrays((slots, LANES), (slots, LANES)) + (jax.ShapeDtypeStruct((2 * PER_ROW, rows), jnp.int32),),
        2,
        "place",
        LARGE,
        scratch_shapes=[turned],
    )(recv)

    def scatter(chunk, grant):
        first = sum(CHUNKS[:chunk])
        return call(
            functools.partial(scatter_kernel, first),
            arrays((CHUNKS[chunk], lat_cells * SUB, LANES))[0],
            9,
            "scatter",
            grant,
            in_specs=[smem, vmem, vmem, vmem],
            scratch_shapes=[turned, pltpu.VMEM((CHUNKS[chunk], lat_cells * SUB, LANES), f32)],
        )(loc, recv, low, high)

    observed = [scatter(0, LARGE), scatter(1, SMALL)]
    pieces.append(tile_exchange(1, pieces[0], observed[0], own_coef))
    shift_space = pltpu.VMEM((2 * LANES, 2 * LANES), jnp.bfloat16)
    smoothed = None
    sampled = []
    first = 0
    for chunk, groups in enumerate(CHUNKS):
        sizes = GROUPS[first : first + groups]
        begin = starts[first]
        own_levels = (sum(sizes), lat_cells, LANES)
        used = []
        places = []
        for index in range(first, first + groups):
            number = [index in members for members in EXCHANGES].index(True)
            if number not in used:
                used.append(number)
            places.append((used.index(number), starts[index] - starts[EXCHANGES[number][0]]))
        arrived = [pieces[number] for number in used]
        if chunk:
            arrived[-1] = after(arrived[-1], sampled[-1])
        field = call(
            functools.partial(field_kernel, begin, sizes, places, n_lon, group, cap),
            field_shapes(groups),
            4,
            "field",
            in_specs=[smem, smem, vmem, hbm] + [vmem] * len(arrived),
            scratch_shapes=[pltpu.VMEM(own_levels, f32), pltpu.SemaphoreType.DMA],
        )(loc, lat, observed[chunk], norm_factor, *arrived)
        field, above, below, strips, from_west, from_east = halo(*field, groups)
        mid_shape = (groups, lat_cells * SUB, LANES)
        win_shape = (groups, win_rows * SUB, LANES)
        mid = call(
            own_kernel,
            arrays(mid_shape)[0],
            6 * groups,
            "own",
            scratch_shapes=[pltpu.VMEM(win_shape, f32), pltpu.VMEM(win_shape, f32), shift_space],
        )(after(field, strips), above, below, own_coef)
        if chunk == 0:
            strip_coef = call(
                strip_coef_kernel,
                arrays((5, win_rows, LANES))[0],
                3,
                "strip_coef",
                scratch_shapes=[pltpu.VMEM(((win_rows + SUB) * SUB, LANES), f32)],
            )(after(coef_strips, mid, *observed[1:]), coef_west, coef_east)
        if chunk == 0:
            pieces.append(tile_exchange(2, pieces[1], from_west, from_east, coef_west, coef_east))
        operands = [loc, strips, from_west, from_east, strip_coef, mid, low, high, norm_factor]
        specs = [smem] + [vmem] * 7 + [hbm]
        aliases = {}
        if smoothed is not None:
            aliases = {len(operands): 0}
            operands.append(smoothed)
            specs.append(hbm)
        last = chunk + 1 == len(CHUNKS)
        earlier = sampled if last else []
        part_shape = (rows // LANES, groups, PER_ROW * SUB, LANES)
        gathered = [pltpu.VMEM(part_shape, f32), pltpu.VMEM((rows // LANES, LANES, LANES), f32)]
        smoothed, part = call(
            functools.partial(strip_kernel, sizes, begin, len(aliases), len(earlier)),
            arrays(norm_factor.shape, (rows, LANES) if earlier else part_shape),
            12,
            "strips",
            in_specs=specs + [vmem] * len(earlier),
            out_specs=(hbm, vmem),
            scratch_shapes=(gathered if earlier else [])
            + [
                pltpu.VMEM((1,) + win_shape[1:], f32),
                pltpu.VMEM((1,) + win_shape[1:], f32),
                shift_space,
                pltpu.VMEM(mid_shape, f32),
                pltpu.VMEM(own_levels, f32),
                pltpu.VMEM(own_levels, f32),
                pltpu.SemaphoreType.DMA((2,)),
            ],
            input_output_aliases=aliases,
        )(*operands, *earlier)
        sampled.append(part)
        first += groups

    back = sampled[-1]
    returned = lax.all_to_all(
        back.reshape(devices, rows // devices, LANES), both, split_axis=0, concat_axis=0, tiled=True
    ).reshape(rows, LANES)
    profile_values = call(
        functools.partial(unpack_kernel, starts),
        arrays((levels, count))[0],
        1,
        "unpack",
    )(returned, slot)
    return (smoothed, profile_values)


def solution(mesh):
    in_specs = (
        P(None, ("lat", "lon")),
        P(("lat", "lon"), None),
        P(("lat", "lon")),
        P(("lat", "lon")),
        P(None, ("lat", "lon")),
        P(None, ("lat", "lon"), None, None),
        P(None, ("lat", "lon")),
        P("lat", "lon"),
        P("lat", "lon"),
        P("lat", "lon"),
        P("lat", "lon"),
        P(None, "lat", "lon"),
    )
    out_specs = (P(None, "lat", "lon"), P(None, ("lat", "lon")))
    return jax.shard_map(
        on_device, mesh=mesh, in_specs=in_specs, out_specs=out_specs, check_vma=False
    )
```

```python
import functools
import jax
import jax.numpy as jnp
from jax import lax
from jax.experimental import pallas as pl
from jax.experimental.pallas import tpu as pltpu
from jax.sharding import PartitionSpec as P

STEPS = 10
SUB = 8
LANES = 128
FEATS = 32
PER_ROW = LANES // FEATS
GROUPS = (5, 4, 8, 8)
CHUNKS = (2, 2)
EXCHANGES = ((0, 1), (2,), (3,))
WEIGHT_ROWS = (5, 6, 12, 13)
LOC_ROW = 7
ID_ROW = 15
SMALL = 20 * 1024 * 1024
LARGE = 60 * 1024 * 1024


def group_starts():
    starts = []
    total = 0
    for count in GROUPS:
        starts.append(total)
        total += count
    return starts


def params(grant):
    return pltpu.CompilerParams(vmem_limit_bytes=grant)


def cost(micros):
    return pl.CostEstimate(flops=0, bytes_accessed=int(micros * 2e5), transcendentals=0)


def iota(shape, dim):
    return lax.broadcasted_iota(jnp.int32, shape, dim)


def split3(values):
    high = values.astype(jnp.bfloat16)
    rest = values - high.astype(jnp.float32)
    middle = rest.astype(jnp.bfloat16)
    low = (rest - middle.astype(jnp.float32)).astype(jnp.bfloat16)
    return high, middle, low


def route_kernel(cap, group, copies, starts, innov, weights, own_row, prow, pcol, ids, send, slot_out, pay):
    count = innov.shape[1]
    tiles = ids.shape[1]
    extra = tiles * copies
    owner = own_row[...]
    column = jnp.broadcast_to(owner.astype(jnp.float32), (SUB, count)).T[:, :1].astype(jnp.int32)
    same = column == owner
    before = iota((count, count), 0) < iota((count, count), 1)
    ones = jnp.where(same & before, 1.0, 0.0)
    rank = jnp.sum(ones, axis=0, keepdims=True).astype(jnp.int32)
    slot = owner * cap + rank
    slot_out[...] = slot
    number = iota((1, extra), 1)
    id_slot = (number // group) * cap + number % group
    pay[...] = jnp.zeros_like(pay)
    for index, count_in in enumerate(GROUPS):
        pay[index * SUB : index * SUB + count_in, :count] = innov[starts[index] : starts[index] + count_in, :]
    for corner, row in enumerate(WEIGHT_ROWS):
        pay[row : row + 1, :count] = weights[corner : corner + 1, :]
    pay[LOC_ROW : LOC_ROW + 1, :count] = (prow[...] * LANES + pcol[...]).astype(jnp.float32)
    for i in range(copies):
        at = count + i * tiles
        pay[ID_ROW : ID_ROW + 1, at : at + tiles] = ids[...].astype(jnp.float32)
    slots = jnp.concatenate([slot, id_slot], axis=1)
    values = pay[...]
    part = slots % PER_ROW
    spread = jnp.concatenate([jnp.where(part == k, values, 0.0) for k in range(PER_ROW)], axis=0)
    rows = send.shape[0]
    hot = jnp.where(iota((rows, count + extra), 0) == slots // PER_ROW, 1.0, 0.0).astype(jnp.bfloat16)
    total = None
    for piece in split3(spread):
        term = lax.dot_general(hot, piece, (((1,), (1,)), ((), ())), preferred_element_type=jnp.float32)
        total = term if total is None else total + term
    send[...] = total


def unpack_kernel(starts, recv, slot, out):
    slots = slot[...]
    rows = recv.shape[0]
    hot = jnp.where(iota((rows, slots.shape[1]), 0) == slots // PER_ROW, 1.0, 0.0).astype(jnp.bfloat16)
    total = None
    for piece in split3(recv[...]):
        term = lax.dot_general(piece, hot, (((0,), (0,)), ((), ())), preferred_element_type=jnp.float32)
        total = term if total is None else total + term
    part = slots % PER_ROW
    picked = jnp.zeros((FEATS, slots.shape[1]), jnp.float32)
    for k in range(PER_ROW):
        picked = jnp.where(part == k, total[k * FEATS : (k + 1) * FEATS], picked)
    for index, count_in in enumerate(GROUPS):
        out[starts[index] : starts[index] + count_in, :] = picked[index * SUB : index * SUB + count_in]


def turn_slots(recv, turned):
    for h in range(recv.shape[0] // LANES):
        turned[h] = recv[h * LANES : (h + 1) * LANES, :].T


def place_kernel(recv, low, high, loc_out, turned):
    rows = recv.shape[0]
    turn_slots(recv, turned)
    for k in range(PER_ROW):
        for h in range(rows // LANES):
            at = k * FEATS
            cut = slice(h * LANES, (h + 1) * LANES)
            cells = turned[h, at + LOC_ROW : at + LOC_ROW + 1, :].astype(jnp.int32)
            loc_out[k : k + 1, cut] = cells // LANES * SUB
            loc_out[PER_ROW + k : PER_ROW + k + 1, cut] = turned[h, at + ID_ROW : at + ID_ROW + 1, :].astype(jnp.int32)
    lane = iota((rows, LANES), 1)
    for k in range(PER_ROW):
        at = k * FEATS
        col = recv[:, at + LOC_ROW : at + LOC_ROW + 1].astype(jnp.int32) % LANES
        w = [recv[:, at + row : at + row + 1] for row in WEIGHT_ROWS]
        here = lane == col
        after = lane == col + 1
        low[k * rows : (k + 1) * rows, :] = jnp.where(here, w[0], jnp.where(after, w[1], 0.0))
        high[k * rows : (k + 1) * rows, :] = jnp.where(here, w[2], jnp.where(after, w[3], 0.0))


def scatter_kernel(first, loc, recv, low, high, obs, turned, odd):
    rows = recv.shape[0]
    groups = range(obs.shape[0])
    turn_slots(recv, turned)

    def clear(i, carry):
        for g in groups:
            at = pl.ds(pl.multiple_of(i * 64, 64), 64)
            obs[g, at, :] = jnp.zeros((64, LANES), jnp.float32)
            odd[g, at, :] = jnp.zeros((64, LANES), jnp.float32)
        return carry

    lax.fori_loop(0, obs.shape[1] // 64, clear, 0)

    def body(i, carry):
        h = i // PER_ROW
        k = i % PER_ROW
        size = len(groups) * SUB
        block = turned[h, pl.ds(pl.multiple_of(k * FEATS + first * SUB, SUB), size), :]
        for seat in range(0, LANES, 2):
            found = []
            for n, total in enumerate((obs, odd)):
                at = pl.multiple_of(loc[k, h * LANES + seat + n], SUB)
                lo = low[pl.ds(k * rows + h * LANES + seat + n, 1), :]
                hi = high[pl.ds(k * rows + h * LANES + seat + n, 1), :]
                for g in groups:
                    value = block[g * SUB : (g + 1) * SUB, seat + n : seat + n + 1]
                    here = total[g, pl.ds(at, SUB), :] + value * lo
                    north = total[g, pl.ds(at + SUB, SUB), :] + value * hi
                    found.append((total, g, at, here, north))
            for total, g, at, here, north in found:
                total[g, pl.ds(at, SUB), :] = here
                total[g, pl.ds(at + SUB, SUB), :] = north
        return carry

    lax.fori_loop(0, (rows // LANES) * PER_ROW, body, 0)

    def join(i, carry):
        for g in groups:
            at = pl.ds(pl.multiple_of(i * 64, 64), 64)
            obs[g, at, :] = obs[g, at, :] + odd[g, at, :]
        return carry

    lax.fori_loop(0, obs.shape[1] // 64, join, 0)


def row_at(index):
    return pl.ds(pl.multiple_of(index * SUB, SUB), SUB)


def rows_at(index, count):
    return pl.ds(pl.multiple_of(index * SUB, SUB), count * SUB)


def send_rows(field, up, down):
    edge = up.shape[1]
    total = field.shape[1]
    for g in range(field.shape[0]):
        up[g] = field[g, total - edge :, :]
        down[g] = field[g, :edge, :]


def field_kernel(begin, sizes, places, n_lon, group, cap, loc, lat, obs, norm_h, *refs):
    tiles = refs[:-5]
    field, up, down, norm, sem = refs[-5:]
    copy = pltpu.make_async_copy(norm_h.at[pl.ds(begin, sum(sizes))], norm, sem)
    copy.start()
    field[...] = jnp.zeros_like(field)
    copy.wait()

    def body(j, carry):
        done = []
        for c in range(group):
            slot = (lat[0] * n_lon + j) * cap + c
            t = loc[PER_ROW + slot % PER_ROW, slot // PER_ROW]
            own = pl.ds(pl.multiple_of(t * SUB, SUB), SUB)
            level = 0
            for g, size in enumerate(sizes):
                source, offset = places[g]
                for l in range(size):
                    at = pl.ds(t * (SUB * SUB) + l, SUB, stride=SUB)
                    cells = tiles[source][j, offset + l, c]
                    done.append((g, at, norm[level, own, :] * (obs[g, at, :] + cells)))
                    level += 1
        for g, at, value in done:
            field[g, at, :] = value
        return carry

    lax.fori_loop(0, n_lon, body, 0)
    send_rows(field, up, down)


def stack_kernel(face_x, face_y, cross, wet, field, up, down):
    field[...] = jnp.zeros_like(field)
    sources = (face_x, face_y, cross, wet)

    def body(i, carry):
        values = []
        for n in range(4):
            t = i * 4 + n
            own = pl.ds(pl.multiple_of(t * SUB, SUB), SUB)
            values += [(t, l, source[own, :].astype(jnp.float32)) for l, source in enumerate(sources)]
        for t, l, value in values:
            field[0, pl.ds(t * (SUB * SUB) + l, SUB, stride=SUB), :] = value
        return carry

    lax.fori_loop(0, face_x.shape[0] // SUB // 4, body, 0)
    send_rows(field, up, down)


STRIP = 32
HALF = 2 * STRIP
SEAT = 16
SEATS = HALF // SEAT
TURNS = 10


def span_of(rows):
    return -(-(rows + 2 * STEPS) // (SEATS * TURNS)) * TURNS


def extend(ext, field, above, below):
    groups, total, _ = field.shape
    halo = STEPS * SUB
    for g in range(groups):
        ext[g, :halo, :] = above[g]
        ext[g, halo : halo + total, :] = field[g]
        ext[g, halo + total : 2 * halo + total, :] = below[g]
        ext[g, 2 * halo + total :, :] = jnp.zeros((ext.shape[1] - 2 * halo - total, LANES), jnp.float32)


def edges_kernel(field, above, below, strips, east, west, ext):
    groups = field.shape[0]
    extend(ext, field, above, below)
    span = east.shape[0] // SUB
    lane = iota((SUB, LANES), 1)
    place = lane % HALF

    def body(i, carry):
        done = []
        for n in range(TURNS // 2):
            m = i * (TURNS // 2) + n
            to_east = None
            to_west = None
            for q in range(SEATS):
                first = ext[0, row_at(q * span + m), :]
                second = pltpu.roll(ext[groups - 1, row_at(q * span + m), :], HALF, 1)
                left = jnp.where(lane < HALF, first, second)
                right = jnp.where(lane < HALF, second, first)
                row = jnp.where(place < STRIP, pltpu.roll(left, STEPS, 1), pltpu.roll(right, HALF - STEPS, 1))
                done.append((strips, q * span + m, row))
                right = pltpu.roll(right, SEAT * q + SEAT, 1)
                if q:
                    left = pltpu.roll(left, SEAT * q, 1)
                mine = place // SEAT == q
                to_east = right if q == 0 else jnp.where(mine, right, to_east)
                to_west = left if q == 0 else jnp.where(mine, left, to_west)
            done.append((east, m, to_east))
            done.append((west, m, to_west))
        for ref, m, value in done:
            ref[row_at(m), :] = value
        return carry

    lax.fori_loop(0, span // (TURNS // 2), body, 0)


def build_strips(win, strips, from_west, from_east):
    span = from_west.shape[0] // SUB
    place = iota((SUB, LANES), 1) % HALF

    def body(i, carry):
        for n in range(TURNS):
            m = i * TURNS + n
            west = from_west[row_at(m), :]
            east = from_east[row_at(m), :]
            for q in range(SEATS):
                a = pltpu.roll(west, (STEPS - SEAT - SEAT * q) % LANES, 1)
                b = pltpu.roll(east, (HALF - STEPS - SEAT * q) % LANES, 1)
                row = strips[row_at(q * span + m), :]
                row = jnp.where(place < STEPS, a, jnp.where(place < HALF - STEPS, row, b))
                win[row_at(q * span + m), :] = row
        return carry

    lax.fori_loop(0, span // TURNS, body, 0)
    first = SEATS * span * SUB
    win[first:, :] = jnp.zeros((win.shape[0] - first, LANES), jnp.float32)


def fill_coef(coef, win):
    rows = coef.shape[1]

    def body(i, carry):
        done = []
        for n in range(12):
            b = i * 12 + n
            base = b * (SUB * SUB)
            at = pl.ds(pl.multiple_of(b * SUB, SUB), SUB)
            fx, fy, ct, wet = (win[pl.ds(base + s, SUB, stride=SUB), :] for s in range(4))
            wet_n = win[pl.ds(base + SUB + 3, SUB, stride=SUB), :]
            x = fx * wet * pltpu.roll(wet, LANES - 1, 1)
            xw = pltpu.roll(x, 1, 1)
            y = fy * wet * wet_n
            twist = 0.25 * ct * wet
            for c, value in enumerate((1.0 - x - xw, x, xw, y, twist)):
                done.append((c, at, value))
        for c, at, value in done:
            coef[c, at, :] = value
        return carry

    lax.fori_loop(0, rows // (12 * SUB), body, 0)


def own_coef_kernel(field, above, below, coef, ext):
    extend(ext, field, above, below)
    fill_coef(coef, ext.at[0])


def strip_coef_kernel(strips, from_west, from_east, coef, win):
    build_strips(win, strips, from_west, from_east)
    fill_coef(coef, win)


BY_MATMUL = 0.25


def fill_shift(shift):
    row = iota(shift.shape, 0) % LANES
    col = iota(shift.shape, 1)
    near = jnp.where(col < LANES, col + 1, col + LANES - 1) % LANES
    shift[...] = jnp.where(row == near, 1.0, 0.0).astype(jnp.bfloat16)


def advance(source, target, planes, weight, shift, rows):
    last = rows + 2 * STEPS + 4
    unroll = last // planes
    blocks = last // unroll
    split = int(unroll * BY_MATMUL)

    def rolled(w, index):
        cells = source[w, row_at(index), :]
        east = pltpu.roll(cells, LANES - 1, 1)
        west = pltpu.roll(cells, 1, 1)
        return cells, east, west, east - west

    def shifted_rows(w, first):
        cells = source[w, rows_at(first, split), :]
        high = cells.astype(jnp.bfloat16)
        low = (cells - high.astype(jnp.float32)).astype(jnp.bfloat16)
        both = jnp.concatenate([high, low], axis=1)
        return jnp.dot(both, shift[...], preferred_element_type=jnp.float32)

    y_first = weight(3, 0)
    state = []
    for w in range(planes):
        before = rolled(w, 0)
        now = rolled(w, 1)
        state.append((now, before[3], y_first * (now[0] - before[0])))

    def block(b, state):
        base = 1 + b * unroll
        state = list(state)
        sides = [shifted_rows(w, base + 1) for w in range(planes)]
        for u in range(unroll):
            weights = [weight(c, base + u) for c in range(5)]
            for w in range(planes):
                (cells, east, west, slope), slope_s, flux_s = state[w]
                if u < split:
                    cells_n = source[w, row_at(base + u + 1), :]
                    east_n = sides[w][u * SUB : (u + 1) * SUB, :LANES]
                    west_n = sides[w][u * SUB : (u + 1) * SUB, LANES:]
                    ahead = (cells_n, east_n, west_n, east_n - west_n)
                else:
                    ahead = rolled(w, base + u + 1)
                flux = weights[3] * (ahead[0] - cells)
                target[w, row_at(base + u), :] = (
                    (weights[0] * cells + weights[1] * east)
                    + (weights[2] * west + (flux - flux_s))
                    + weights[4] * (ahead[3] - slope_s)
                )
                state[w] = (ahead, slope, flux)
        return tuple(state)

    lax.fori_loop(0, blocks, block, tuple(state))


def diffuse(win, other, planes, coef, shift, rows):
    fill_shift(shift)

    def weight(c, index):
        return coef[c, pl.ds(index, 1), :]

    def two(t, carry):
        advance(win, other, planes, weight, shift, rows)
        advance(other, win, planes, weight, shift, rows)
        return carry

    for w in range(planes):
        other[w, :SUB, :] = jnp.zeros((SUB, LANES), jnp.float32)
        other[w, other.shape[1] - SUB * SUB :, :] = jnp.zeros((SUB * SUB, LANES), jnp.float32)
    lax.fori_loop(0, STEPS // 2, two, 0)


def own_kernel(field, above, below, coef, mid, win, other, shift):
    groups = field.shape[0]
    rows = mid.shape[1] // SUB
    halo = STEPS * SUB
    extend(win, field, above, below)
    diffuse(win, other, groups, coef, shift, rows)
    for g in range(groups):
        mid[g] = win[g, halo : halo + rows * SUB, :]


MERGE = 32


def strip_kernel(sizes, begin, aliased, earlier, *refs):
    loc, strips, from_west, from_east, coef, mid, low, high, norm_h = refs[:9]
    parts = refs[9 + aliased : 9 + aliased + earlier]
    refs = refs[9 + aliased + earlier :]
    if earlier:
        out_h, packed, sampled, turned = refs[:4]
    else:
        out_h, sampled = refs[:2]
    win, other, shift, smooth, norm, out, sems = refs[-7:]
    groups = mid.shape[0]
    rows = mid.shape[1] // SUB
    levels = pl.ds(begin, sum(sizes))
    copy = pltpu.make_async_copy(norm_h.at[levels], norm, sems.at[0])
    copy.start()
    build_strips(win.at[0], strips, from_west, from_east)
    diffuse(win, other, 1, coef, shift, rows)
    copy.wait()
    lane = iota((SUB, LANES), 1)
    outer = LANES - STEPS

    def merge(b, carry):
        for u in range(MERGE):
            at = row_at(b * MERGE + u)
            strip = win[0, row_at(b * MERGE + u + STEPS), :]
            west = pltpu.roll(strip, outer, 1)
            east = pltpu.roll(strip, HALF + STEPS, 1)
            cells = mid[0, at, :]
            smooth[0, at, :] = jnp.where(lane < STEPS, west, jnp.where(lane < outer, cells, east))
            if groups == 2:
                both = pltpu.roll(jnp.where(lane < HALF, east, west), HALF, 1)
                cells = mid[1, at, :]
                smooth[1, at, :] = jnp.where((lane < STEPS) | (lane >= outer), both, cells)
        return carry

    lax.fori_loop(0, rows // MERGE, merge, 0)

    def scale(i, carry):
        done = []
        for n in range(4):
            b = i * 4 + n
            own = pl.ds(pl.multiple_of(b * SUB, SUB), SUB)
            level = 0
            for g, size in enumerate(sizes):
                for l in range(size):
                    at = pl.ds(b * (SUB * SUB) + l, SUB, stride=SUB)
                    done.append((g, at, level, own, smooth[g, at, :] * norm[level, own, :]))
                    level += 1
        for g, at, level, own, value in done:
            out[level, own, :] = value
            smooth[g, at, :] = value
        return carry

    lax.fori_loop(0, rows // (4 * SUB), scale, 0)
    back = pltpu.make_async_copy(out, out_h.at[levels], sems.at[1])
    back.start()
    count = low.shape[0] // PER_ROW
    halves = count // LANES

    def samples(i, carry):
        h = i // PER_ROW
        k = i % PER_ROW
        kept = [[jnp.zeros((SUB, LANES), jnp.float32)] * 4 for _ in range(groups)]
        for seat in range(LANES):
            at = pl.multiple_of(loc[k, h * LANES + seat], SUB)
            lo = low[pl.ds(k * count + h * LANES + seat, 1), :]
            hi = high[pl.ds(k * count + h * LANES + seat, 1), :]
            for g in range(groups):
                value = smooth[g, pl.ds(at, SUB), :] * lo + smooth[g, pl.ds(at + SUB, SUB), :] * hi
                total = jnp.sum(value, axis=1, keepdims=True)
                kept[g][seat % 4] = jnp.where(lane == seat, total, kept[g][seat % 4])
        for g in range(groups):
            a, b, c, d = kept[g]
            sampled[h, g, row_at(k), :] = (a + b) + (c + d)
        return carry

    lax.fori_loop(0, halves * PER_ROW, samples, 0)
    if earlier:
        pack_samples(parts + (sampled,), packed, turned)
    back.wait()


def pack_samples(parts, out, turned):
    for h in range(turned.shape[0]):
        index = 0
        for part in parts:
            for g in range(part.shape[1]):
                for k in range(PER_ROW):
                    at = k * FEATS + index * SUB
                    turned[h, at : at + SUB, :] = part[h, g, k * SUB : (k + 1) * SUB, :]
                index += 1
        out[h * LANES : (h + 1) * LANES, :] = turned[h].T


def exchange_rows(up, down, n_lat):
    pairs = [(i, i + 1) for i in range(n_lat - 1)]
    back = [(i + 1, i) for i in range(n_lat - 1)]
    return lax.ppermute(up, "lat", pairs), lax.ppermute(down, "lat", back)


def exchange_columns(east, west, n_lon):
    pairs = [(i, (i + 1) % n_lon) for i in range(n_lon)]
    back = [((i + 1) % n_lon, i) for i in range(n_lon)]
    return lax.ppermute(east, "lon", pairs), lax.ppermute(west, "lon", back)


def on_device(
    innovations,
    owners,
    prof_row,
    prof_col,
    interp_weights,
    model_tiles,
    model_ids,
    face_x,
    face_y,
    cross_term,
    wet_mask,
    norm_factor,
):
    n_lat = lax.axis_size("lat")
    n_lon = lax.axis_size("lon")
    devices = n_lat * n_lon
    levels, lat_cells, lon_cells = norm_factor.shape
    tiles = model_tiles.shape[1]
    group = tiles // n_lon
    count = innovations.shape[1]
    cap = 2 * count // devices
    slots = devices * cap
    rows = slots // PER_ROW
    starts = group_starts()
    f32 = jnp.float32
    lat = lax.axis_index("lat").reshape(1)
    both = ("lat", "lon")
    span = span_of(lat_cells)
    ext_rows = SEATS * span
    win_rows = ext_rows + SUB

    def arrays(*shapes):
        return tuple(jax.ShapeDtypeStruct(shape, f32) for shape in shapes)

    def call(kernel, out_shape, micros, name, grant=SMALL, **kwargs):
        return pl.pallas_call(
            kernel,
            out_shape=out_shape,
            compiler_params=params(grant),
            cost_estimate=cost(micros),
            name=name,
            **kwargs,
        )

    def after(value, *others):
        return lax.optimization_barrier((value,) + others)[0]

    def tile_exchange(number, *others):
        members = EXCHANGES[number]
        begin = starts[members[0]]
        size = sum(GROUPS[index] for index in members)
        piece = model_tiles[begin : begin + size].reshape(size, n_lon, group, SUB, LANES)
        piece = jnp.transpose(piece, (1, 0, 2, 3, 4))
        if others:
            piece = after(piece, *others)
        return lax.all_to_all(piece, "lon", split_axis=0, concat_axis=0, tiled=True)

    def halo(field, up, down, groups):
        above, below = exchange_rows(up, down, n_lat)
        strips, east, west = call(
            edges_kernel,
            arrays((ext_rows * SUB, LANES), (span * SUB, LANES), (span * SUB, LANES)),
            3,
            "edges",
            scratch_shapes=[pltpu.VMEM((groups, ext_rows * SUB, LANES), f32)],
        )(field, above, below)
        return (field, above, below, strips) + exchange_columns(east, west, n_lon)

    def field_shapes(groups):
        return arrays(
            (groups, lat_cells * SUB, LANES),
            (groups, STEPS * SUB, LANES),
            (groups, STEPS * SUB, LANES),
        )

    send, slot = call(
        functools.partial(route_kernel, cap, group, n_lat, starts),
        (jax.ShapeDtypeStruct((rows, LANES), f32), jax.ShapeDtypeStruct((1, count), jnp.int32)),
        3,
        "route",
        LARGE,
        scratch_shapes=[pltpu.VMEM((FEATS, count + devices * group), f32)],
    )(
        innovations,
        interp_weights,
        owners.reshape(1, count),
        prof_row.reshape(1, count),
        prof_col.reshape(1, count),
        model_ids,
    )
    stacked = call(stack_kernel, field_shapes(1), 3, "stack")(face_x, face_y, cross_term, wet_mask)
    stack, above, below, coef_strips, coef_west, coef_east = halo(*stacked, 1)
    own_coef = call(
        own_coef_kernel,
        arrays((5, win_rows, LANES))[0],
        3,
        "own_coef",
        scratch_shapes=[pltpu.VMEM((1, (win_rows + SUB) * SUB, LANES), f32)],
    )(stack, above, below)
    recv = lax.all_to_all(
        send.reshape(devices, rows // devices, LANES), both, split_axis=0, concat_axis=0, tiled=True
    ).reshape(rows, LANES)
    pieces = [tile_exchange(0, recv, stacked[0])]

    smem = pl.BlockSpec(memory_space=pltpu.SMEM)
    vmem = pl.BlockSpec(memory_space=pltpu.VMEM)
    hbm = pl.BlockSpec(memory_space=pltpu.HBM)
    turned = pltpu.VMEM((rows // LANES, LANES, LANES), f32)
    low, high, loc = call(
        place_kernel,
        arrays((slots, LANES), (slots, LANES)) + (jax.ShapeDtypeStruct((2 * PER_ROW, rows), jnp.int32),),
        2,
        "place",
        LARGE,
        scratch_shapes=[turned],
    )(recv)

    def scatter(chunk, grant):
        first = sum(CHUNKS[:chunk])
        return call(
            functools.partial(scatter_kernel, first),
            arrays((CHUNKS[chunk], lat_cells * SUB, LANES))[0],
            9,
            "scatter",
            grant,
            in_specs=[smem, vmem, vmem, vmem],
            scratch_shapes=[turned, pltpu.VMEM((CHUNKS[chunk], lat_cells * SUB, LANES), f32)],
        )(loc, recv, low, high)

    observed = [scatter(0, LARGE), scatter(1, SMALL)]
    pieces.append(tile_exchange(1, pieces[0], observed[0], own_coef))
    shift_space = pltpu.VMEM((2 * LANES, 2 * LANES), jnp.bfloat16)
    smoothed = None
    sampled = []
    first = 0
    for chunk, groups in enumerate(CHUNKS):
        sizes = GROUPS[first : first + groups]
        begin = starts[first]
        own_levels = (sum(sizes), lat_cells, LANES)
        used = []
        places = []
        for index in range(first, first + groups):
            number = [index in members for members in EXCHANGES].index(True)
            if number not in used:
                used.append(number)
            places.append((used.index(number), starts[index] - starts[EXCHANGES[number][0]]))
        arrived = [pieces[number] for number in used]
        if chunk:
            arrived[-1] = after(arrived[-1], sampled[-1])
        field = call(
            functools.partial(field_kernel, begin, sizes, places, n_lon, group, cap),
            field_shapes(groups),
            4,
            "field",
            in_specs=[smem, smem, vmem, hbm] + [vmem] * len(arrived),
            scratch_shapes=[pltpu.VMEM(own_levels, f32), pltpu.SemaphoreType.DMA],
        )(loc, lat, observed[chunk], norm_factor, *arrived)
        field, above, below, strips, from_west, from_east = halo(*field, groups)
        mid_shape = (groups, lat_cells * SUB, LANES)
        win_shape = (groups, win_rows * SUB, LANES)
        mid = call(
            own_kernel,
            arrays(mid_shape)[0],
            6 * groups,
            "own",
            scratch_shapes=[pltpu.VMEM(win_shape, f32), pltpu.VMEM(win_shape, f32), shift_space],
        )(after(field, strips), above, below, own_coef)
        if chunk == 0:
            strip_coef = call(
                strip_coef_kernel,
                arrays((5, win_rows, LANES))[0],
                3,
                "strip_coef",
                scratch_shapes=[pltpu.VMEM(((win_rows + SUB) * SUB, LANES), f32)],
            )(after(coef_strips, mid, *observed[1:]), coef_west, coef_east)
        if chunk == 0:
            pieces.append(tile_exchange(2, pieces[1], mid, from_west, from_east, coef_west, coef_east))
        operands = [loc, strips, from_west, from_east, strip_coef, mid, low, high, norm_factor]
        specs = [smem] + [vmem] * 7 + [hbm]
        aliases = {}
        if smoothed is not None:
            aliases = {len(operands): 0}
            operands.append(smoothed)
            specs.append(hbm)
        last = chunk + 1 == len(CHUNKS)
        earlier = sampled if last else []
        part_shape = (rows // LANES, groups, PER_ROW * SUB, LANES)
        gathered = [pltpu.VMEM(part_shape, f32), pltpu.VMEM((rows // LANES, LANES, LANES), f32)]
        smoothed, part = call(
            functools.partial(strip_kernel, sizes, begin, len(aliases), len(earlier)),
            arrays(norm_factor.shape, (rows, LANES) if earlier else part_shape),
            12,
            "strips",
            in_specs=specs + [vmem] * len(earlier),
            out_specs=(hbm, vmem),
            scratch_shapes=(gathered if earlier else [])
            + [
                pltpu.VMEM((1,) + win_shape[1:], f32),
                pltpu.VMEM((1,) + win_shape[1:], f32),
                shift_space,
                pltpu.VMEM(mid_shape, f32),
                pltpu.VMEM(own_levels, f32),
                pltpu.VMEM(own_levels, f32),
                pltpu.SemaphoreType.DMA((2,)),
            ],
            input_output_aliases=aliases,
        )(*operands, *earlier)
        sampled.append(part)
        first += groups

    back = sampled[-1]
    returned = lax.all_to_all(
        back.reshape(devices, rows // devices, LANES), both, split_axis=0, concat_axis=0, tiled=True
    ).reshape(rows, LANES)
    profile_values = call(
        functools.partial(unpack_kernel, starts),
        arrays((levels, count))[0],
        1,
        "unpack",
    )(returned, slot)
    return (smoothed, profile_values)


def solution(mesh):
    in_specs = (
        P(None, ("lat", "lon")),
        P(("lat", "lon"), None),
        P(("lat", "lon")),
        P(("lat", "lon")),
        P(None, ("lat", "lon")),
        P(None, ("lat", "lon"), None, None),
        P(None, ("lat", "lon")),
        P("lat", "lon"),
        P("lat", "lon"),
        P("lat", "lon"),
        P("lat", "lon"),
        P(None, "lat", "lon"),
    )
    out_specs = (P(None, "lat", "lon"), P(None, ("lat", "lon")))
    return jax.shard_map(
        on_device, mesh=mesh, in_specs=in_specs, out_specs=out_specs, check_vma=False
    )
```

```python
import functools
import jax
import jax.numpy as jnp
from jax import lax
from jax.experimental import pallas as pl
from jax.experimental.pallas import tpu as pltpu
from jax.sharding import PartitionSpec as P

STEPS = 10
SUB = 8
LANES = 128
FEATS = 32
PER_ROW = LANES // FEATS
GROUPS = (5, 4, 8, 8)
CHUNKS = (2, 2)
WEIGHT_ROWS = (5, 6, 12, 13)
LOC_ROW = 7
ID_ROW = 15
SMALL = 20 * 1024 * 1024
LARGE = 60 * 1024 * 1024


def group_starts():
    starts = []
    total = 0
    for count in GROUPS:
        starts.append(total)
        total += count
    return starts


def params(grant):
    return pltpu.CompilerParams(vmem_limit_bytes=grant)


def cost(micros):
    return pl.CostEstimate(flops=0, bytes_accessed=int(micros * 2e5), transcendentals=0)


def iota(shape, dim):
    return lax.broadcasted_iota(jnp.int32, shape, dim)


def split3(values):
    high = values.astype(jnp.bfloat16)
    rest = values - high.astype(jnp.float32)
    middle = rest.astype(jnp.bfloat16)
    low = (rest - middle.astype(jnp.float32)).astype(jnp.bfloat16)
    return high, middle, low


def route_kernel(cap, group, copies, starts, innov, weights, own_row, prow, pcol, ids, send, slot_out, pay):
    count = innov.shape[1]
    tiles = ids.shape[1]
    extra = tiles * copies
    owner = own_row[...]
    column = jnp.broadcast_to(owner.astype(jnp.float32), (SUB, count)).T[:, :1].astype(jnp.int32)
    same = column == owner
    before = iota((count, count), 0) < iota((count, count), 1)
    ones = jnp.where(same & before, 1.0, 0.0)
    rank = jnp.sum(ones, axis=0, keepdims=True).astype(jnp.int32)
    slot = owner * cap + rank
    slot_out[...] = slot
    number = iota((1, extra), 1)
    id_slot = (number // group) * cap + number % group
    pay[...] = jnp.zeros_like(pay)
    for index, count_in in enumerate(GROUPS):
        pay[index * SUB : index * SUB + count_in, :count] = innov[starts[index] : starts[index] + count_in, :]
    for corner, row in enumerate(WEIGHT_ROWS):
        pay[row : row + 1, :count] = weights[corner : corner + 1, :]
    pay[LOC_ROW : LOC_ROW + 1, :count] = (prow[...] * LANES + pcol[...]).astype(jnp.float32)
    for i in range(copies):
        at = count + i * tiles
        pay[ID_ROW : ID_ROW + 1, at : at + tiles] = ids[...].astype(jnp.float32)
    slots = jnp.concatenate([slot, id_slot], axis=1)
    values = pay[...]
    part = slots % PER_ROW
    spread = jnp.concatenate([jnp.where(part == k, values, 0.0) for k in range(PER_ROW)], axis=0)
    rows = send.shape[0]
    hot = jnp.where(iota((rows, count + extra), 0) == slots // PER_ROW, 1.0, 0.0).astype(jnp.bfloat16)
    total = None
    for piece in split3(spread):
        term = lax.dot_general(hot, piece, (((1,), (1,)), ((), ())), preferred_element_type=jnp.float32)
        total = term if total is None else total + term
    send[...] = total


def unpack_kernel(starts, recv, slot, out):
    slots = slot[...]
    rows = recv.shape[0]
    hot = jnp.where(iota((rows, slots.shape[1]), 0) == slots // PER_ROW, 1.0, 0.0).astype(jnp.bfloat16)
    total = None
    for piece in split3(recv[...]):
        term = lax.dot_general(piece, hot, (((0,), (0,)), ((), ())), preferred_element_type=jnp.float32)
        total = term if total is None else total + term
    part = slots % PER_ROW
    picked = jnp.zeros((FEATS, slots.shape[1]), jnp.float32)
    for k in range(PER_ROW):
        picked = jnp.where(part == k, total[k * FEATS : (k + 1) * FEATS], picked)
    for index, count_in in enumerate(GROUPS):
        out[starts[index] : starts[index] + count_in, :] = picked[index * SUB : index * SUB + count_in]


def turn_slots(recv, turned):
    for h in range(recv.shape[0] // LANES):
        turned[h] = recv[h * LANES : (h + 1) * LANES, :].T


def place_kernel(recv, low, high, loc_out, turned):
    rows = recv.shape[0]
    turn_slots(recv, turned)
    for k in range(PER_ROW):
        for h in range(rows // LANES):
            at = k * FEATS
            cut = slice(h * LANES, (h + 1) * LANES)
            cells = turned[h, at + LOC_ROW : at + LOC_ROW + 1, :].astype(jnp.int32)
            loc_out[k : k + 1, cut] = cells // LANES * SUB
            loc_out[PER_ROW + k : PER_ROW + k + 1, cut] = turned[h, at + ID_ROW : at + ID_ROW + 1, :].astype(jnp.int32)
    lane = iota((rows, LANES), 1)
    for k in range(PER_ROW):
        at = k * FEATS
        col = recv[:, at + LOC_ROW : at + LOC_ROW + 1].astype(jnp.int32) % LANES
        w = [recv[:, at + row : at + row + 1] for row in WEIGHT_ROWS]
        here = lane == col
        after = lane == col + 1
        low[k * rows : (k + 1) * rows, :] = jnp.where(here, w[0], jnp.where(after, w[1], 0.0))
        high[k * rows : (k + 1) * rows, :] = jnp.where(here, w[2], jnp.where(after, w[3], 0.0))


def scatter_kernel(first, loc, recv, low, high, obs, turned, odd):
    rows = recv.shape[0]
    groups = range(obs.shape[0])
    turn_slots(recv, turned)

    def clear(i, carry):
        for g in groups:
            at = pl.ds(pl.multiple_of(i * 64, 64), 64)
            obs[g, at, :] = jnp.zeros((64, LANES), jnp.float32)
            odd[g, at, :] = jnp.zeros((64, LANES), jnp.float32)
        return carry

    lax.fori_loop(0, obs.shape[1] // 64, clear, 0)

    def body(i, carry):
        h = i // PER_ROW
        k = i % PER_ROW
        size = len(groups) * SUB
        block = turned[h, pl.ds(pl.multiple_of(k * FEATS + first * SUB, SUB), size), :]
        for seat in range(0, LANES, 2):
            found = []
            for n, total in enumerate((obs, odd)):
                at = pl.multiple_of(loc[k, h * LANES + seat + n], SUB)
                lo = low[pl.ds(k * rows + h * LANES + seat + n, 1), :]
                hi = high[pl.ds(k * rows + h * LANES + seat + n, 1), :]
                for g in groups:
                    value = block[g * SUB : (g + 1) * SUB, seat + n : seat + n + 1]
                    here = total[g, pl.ds(at, SUB), :] + value * lo
                    north = total[g, pl.ds(at + SUB, SUB), :] + value * hi
                    found.append((total, g, at, here, north))
            for total, g, at, here, north in found:
                total[g, pl.ds(at, SUB), :] = here
                total[g, pl.ds(at + SUB, SUB), :] = north
        return carry

    lax.fori_loop(0, (rows // LANES) * PER_ROW, body, 0)

    def join(i, carry):
        for g in groups:
            at = pl.ds(pl.multiple_of(i * 64, 64), 64)
            obs[g, at, :] = obs[g, at, :] + odd[g, at, :]
        return carry

    lax.fori_loop(0, obs.shape[1] // 64, join, 0)


def row_at(index):
    return pl.ds(pl.multiple_of(index * SUB, SUB), SUB)


def rows_at(index, count):
    return pl.ds(pl.multiple_of(index * SUB, SUB), count * SUB)


def send_rows(field, up, down):
    edge = up.shape[1]
    total = field.shape[1]
    for g in range(field.shape[0]):
        up[g] = field[g, total - edge :, :]
        down[g] = field[g, :edge, :]


def field_kernel(begin, sizes, n_lon, group, cap, loc, lat, tiles, obs, norm_h, field, up, down, norm, sem):
    copy = pltpu.make_async_copy(norm_h.at[pl.ds(begin, sum(sizes))], norm, sem)
    copy.start()
    field[...] = jnp.zeros_like(field)
    copy.wait()

    def body(j, carry):
        done = []
        for c in range(group):
            slot = (lat[0] * n_lon + j) * cap + c
            t = loc[PER_ROW + slot % PER_ROW, slot // PER_ROW]
            own = pl.ds(pl.multiple_of(t * SUB, SUB), SUB)
            level = 0
            for g, size in enumerate(sizes):
                for l in range(size):
                    at = pl.ds(t * (SUB * SUB) + l, SUB, stride=SUB)
                    done.append((g, at, norm[level, own, :] * (obs[g, at, :] + tiles[j, level, c])))
                    level += 1
        for g, at, value in done:
            field[g, at, :] = value
        return carry

    lax.fori_loop(0, n_lon, body, 0)
    send_rows(field, up, down)


def stack_kernel(face_x, face_y, cross, wet, field, up, down):
    field[...] = jnp.zeros_like(field)
    sources = (face_x, face_y, cross, wet)

    def body(i, carry):
        values = []
        for n in range(4):
            t = i * 4 + n
            own = pl.ds(pl.multiple_of(t * SUB, SUB), SUB)
            values += [(t, l, source[own, :].astype(jnp.float32)) for l, source in enumerate(sources)]
        for t, l, value in values:
            field[0, pl.ds(t * (SUB * SUB) + l, SUB, stride=SUB), :] = value
        return carry

    lax.fori_loop(0, face_x.shape[0] // SUB // 4, body, 0)
    send_rows(field, up, down)


STRIP = 32
HALF = 2 * STRIP
SEAT = 16
SEATS = HALF // SEAT
TURNS = 10


def span_of(rows):
    return -(-(rows + 2 * STEPS) // (SEATS * TURNS)) * TURNS


def extend(ext, field, above, below):
    groups, total, _ = field.shape
    halo = STEPS * SUB
    for g in range(groups):
        ext[g, :halo, :] = above[g]
        ext[g, halo : halo + total, :] = field[g]
        ext[g, halo + total : 2 * halo + total, :] = below[g]
        ext[g, 2 * halo + total :, :] = jnp.zeros((ext.shape[1] - 2 * halo - total, LANES), jnp.float32)


def edges_kernel(field, above, below, strips, east, west, ext):
    groups = field.shape[0]
    extend(ext, field, above, below)
    span = east.shape[0] // SUB
    lane = iota((SUB, LANES), 1)
    place = lane % HALF

    def body(i, carry):
        done = []
        for n in range(TURNS // 2):
            m = i * (TURNS // 2) + n
            to_east = None
            to_west = None
            for q in range(SEATS):
                first = ext[0, row_at(q * span + m), :]
                second = pltpu.roll(ext[groups - 1, row_at(q * span + m), :], HALF, 1)
                left = jnp.where(lane < HALF, first, second)
                right = jnp.where(lane < HALF, second, first)
                row = jnp.where(place < STRIP, pltpu.roll(left, STEPS, 1), pltpu.roll(right, HALF - STEPS, 1))
                done.append((strips, q * span + m, row))
                right = pltpu.roll(right, SEAT * q + SEAT, 1)
                if q:
                    left = pltpu.roll(left, SEAT * q, 1)
                mine = place // SEAT == q
                to_east = right if q == 0 else jnp.where(mine, right, to_east)
                to_west = left if q == 0 else jnp.where(mine, left, to_west)
            done.append((east, m, to_east))
            done.append((west, m, to_west))
        for ref, m, value in done:
            ref[row_at(m), :] = value
        return carry

    lax.fori_loop(0, span // (TURNS // 2), body, 0)


def build_strips(win, strips, from_west, from_east):
    span = from_west.shape[0] // SUB
    place = iota((SUB, LANES), 1) % HALF

    def body(i, carry):
        for n in range(TURNS):
            m = i * TURNS + n
            west = from_west[row_at(m), :]
            east = from_east[row_at(m), :]
            for q in range(SEATS):
                a = pltpu.roll(west, (STEPS - SEAT - SEAT * q) % LANES, 1)
                b = pltpu.roll(east, (HALF - STEPS - SEAT * q) % LANES, 1)
                row = strips[row_at(q * span + m), :]
                row = jnp.where(place < STEPS, a, jnp.where(place < HALF - STEPS, row, b))
                win[row_at(q * span + m), :] = row
        return carry

    lax.fori_loop(0, span // TURNS, body, 0)
    first = SEATS * span * SUB
    win[first:, :] = jnp.zeros((win.shape[0] - first, LANES), jnp.float32)


def fill_coef(coef, win):
    rows = coef.shape[1]

    def body(i, carry):
        done = []
        for n in range(12):
            b = i * 12 + n
            base = b * (SUB * SUB)
            at = pl.ds(pl.multiple_of(b * SUB, SUB), SUB)
            fx, fy, ct, wet = (win[pl.ds(base + s, SUB, stride=SUB), :] for s in range(4))
            wet_n = win[pl.ds(base + SUB + 3, SUB, stride=SUB), :]
            x = fx * wet * pltpu.roll(wet, LANES - 1, 1)
            xw = pltpu.roll(x, 1, 1)
            y = fy * wet * wet_n
            twist = 0.25 * ct * wet
            for c, value in enumerate((1.0 - x - xw, x, xw, y, twist)):
                done.append((c, at, value))
        for c, at, value in done:
            coef[c, at, :] = value
        return carry

    lax.fori_loop(0, rows // (12 * SUB), body, 0)


def own_coef_kernel(field, above, below, coef, ext):
    extend(ext, field, above, below)
    fill_coef(coef, ext.at[0])


def strip_coef_kernel(strips, from_west, from_east, coef, win):
    build_strips(win, strips, from_west, from_east)
    fill_coef(coef, win)


BY_MATMUL = 0.25


def fill_shift(shift):
    row = iota(shift.shape, 0) % LANES
    col = iota(shift.shape, 1)
    near = jnp.where(col < LANES, col + 1, col + LANES - 1) % LANES
    shift[...] = jnp.where(row == near, 1.0, 0.0).astype(jnp.bfloat16)


def advance(source, target, planes, weight, shift, rows):
    last = rows + 2 * STEPS + 4
    unroll = last // planes
    blocks = last // unroll
    split = int(unroll * BY_MATMUL)

    def rolled(w, index):
        cells = source[w, row_at(index), :]
        east = pltpu.roll(cells, LANES - 1, 1)
        west = pltpu.roll(cells, 1, 1)
        return cells, east, west, east - west

    def shifted_rows(w, first):
        cells = source[w, rows_at(first, split), :]
        high = cells.astype(jnp.bfloat16)
        low = (cells - high.astype(jnp.float32)).astype(jnp.bfloat16)
        both = jnp.concatenate([high, low], axis=1)
        return jnp.dot(both, shift[...], preferred_element_type=jnp.float32)

    y_first = weight(3, 0)
    state = []
    for w in range(planes):
        before = rolled(w, 0)
        now = rolled(w, 1)
        state.append((now, before[3], y_first * (now[0] - before[0])))

    def block(b, state):
        base = 1 + b * unroll
        state = list(state)
        sides = [shifted_rows(w, base + 1) for w in range(planes)]
        for u in range(unroll):
            weights = [weight(c, base + u) for c in range(5)]
            for w in range(planes):
                (cells, east, west, slope), slope_s, flux_s = state[w]
                if u < split:
                    cells_n = source[w, row_at(base + u + 1), :]
                    east_n = sides[w][u * SUB : (u + 1) * SUB, :LANES]
                    west_n = sides[w][u * SUB : (u + 1) * SUB, LANES:]
                    ahead = (cells_n, east_n, west_n, east_n - west_n)
                else:
                    ahead = rolled(w, base + u + 1)
                flux = weights[3] * (ahead[0] - cells)
                target[w, row_at(base + u), :] = (
                    (weights[0] * cells + weights[1] * east)
                    + (weights[2] * west + (flux - flux_s))
                    + weights[4] * (ahead[3] - slope_s)
                )
                state[w] = (ahead, slope, flux)
        return tuple(state)

    lax.fori_loop(0, blocks, block, tuple(state))


def diffuse(win, other, planes, coef, shift, rows):
    fill_shift(shift)

    def weight(c, index):
        return coef[c, pl.ds(index, 1), :]

    def two(t, carry):
        advance(win, other, planes, weight, shift, rows)
        advance(other, win, planes, weight, shift, rows)
        return carry

    for w in range(planes):
        other[w, :SUB, :] = jnp.zeros((SUB, LANES), jnp.float32)
        other[w, other.shape[1] - SUB * SUB :, :] = jnp.zeros((SUB * SUB, LANES), jnp.float32)
    lax.fori_loop(0, STEPS // 2, two, 0)


def own_kernel(field, above, below, coef, mid, win, other, shift):
    groups = field.shape[0]
    rows = mid.shape[1] // SUB
    halo = STEPS * SUB
    extend(win, field, above, below)
    diffuse(win, other, groups, coef, shift, rows)
    for g in range(groups):
        mid[g] = win[g, halo : halo + rows * SUB, :]


MERGE = 32


def strip_kernel(sizes, begin, aliased, earlier, *refs):
    loc, strips, from_west, from_east, coef, mid, low, high, norm_h = refs[:9]
    parts = refs[9 + aliased : 9 + aliased + earlier]
    refs = refs[9 + aliased + earlier :]
    if earlier:
        out_h, packed, sampled, turned = refs[:4]
    else:
        out_h, sampled = refs[:2]
    win, other, shift, smooth, norm, out, sems = refs[-7:]
    groups = mid.shape[0]
    rows = mid.shape[1] // SUB
    levels = pl.ds(begin, sum(sizes))
    copy = pltpu.make_async_copy(norm_h.at[levels], norm, sems.at[0])
    copy.start()
    build_strips(win.at[0], strips, from_west, from_east)
    diffuse(win, other, 1, coef, shift, rows)
    copy.wait()
    lane = iota((SUB, LANES), 1)
    outer = LANES - STEPS

    def merge(b, carry):
        for u in range(MERGE):
            at = row_at(b * MERGE + u)
            strip = win[0, row_at(b * MERGE + u + STEPS), :]
            west = pltpu.roll(strip, outer, 1)
            east = pltpu.roll(strip, HALF + STEPS, 1)
            cells = mid[0, at, :]
            smooth[0, at, :] = jnp.where(lane < STEPS, west, jnp.where(lane < outer, cells, east))
            if groups == 2:
                both = pltpu.roll(jnp.where(lane < HALF, east, west), HALF, 1)
                cells = mid[1, at, :]
                smooth[1, at, :] = jnp.where((lane < STEPS) | (lane >= outer), both, cells)
        return carry

    lax.fori_loop(0, rows // MERGE, merge, 0)

    def scale(i, carry):
        done = []
        for n in range(4):
            b = i * 4 + n
            own = pl.ds(pl.multiple_of(b * SUB, SUB), SUB)
            level = 0
            for g, size in enumerate(sizes):
                for l in range(size):
                    at = pl.ds(b * (SUB * SUB) + l, SUB, stride=SUB)
                    done.append((g, at, level, own, smooth[g, at, :] * norm[level, own, :]))
                    level += 1
        for g, at, level, own, value in done:
            out[level, own, :] = value
            smooth[g, at, :] = value
        return carry

    lax.fori_loop(0, rows // (4 * SUB), scale, 0)
    back = pltpu.make_async_copy(out, out_h.at[levels], sems.at[1])
    back.start()
    count = low.shape[0] // PER_ROW
    halves = count // LANES

    def samples(i, carry):
        h = i // PER_ROW
        k = i % PER_ROW
        kept = [[jnp.zeros((SUB, LANES), jnp.float32)] * 4 for _ in range(groups)]
        for seat in range(LANES):
            at = pl.multiple_of(loc[k, h * LANES + seat], SUB)
            lo = low[pl.ds(k * count + h * LANES + seat, 1), :]
            hi = high[pl.ds(k * count + h * LANES + seat, 1), :]
            for g in range(groups):
                value = smooth[g, pl.ds(at, SUB), :] * lo + smooth[g, pl.ds(at + SUB, SUB), :] * hi
                total = jnp.sum(value, axis=1, keepdims=True)
                kept[g][seat % 4] = jnp.where(lane == seat, total, kept[g][seat % 4])
        for g in range(groups):
            a, b, c, d = kept[g]
            sampled[h, g, row_at(k), :] = (a + b) + (c + d)
        return carry

    lax.fori_loop(0, halves * PER_ROW, samples, 0)
    if earlier:
        pack_samples(parts + (sampled,), packed, turned)
    back.wait()


def pack_samples(parts, out, turned):
    for h in range(turned.shape[0]):
        index = 0
        for part in parts:
            for g in range(part.shape[1]):
                for k in range(PER_ROW):
                    at = k * FEATS + index * SUB
                    turned[h, at : at + SUB, :] = part[h, g, k * SUB : (k + 1) * SUB, :]
                index += 1
        out[h * LANES : (h + 1) * LANES, :] = turned[h].T


def exchange_rows(up, down, n_lat):
    pairs = [(i, i + 1) for i in range(n_lat - 1)]
    back = [(i + 1, i) for i in range(n_lat - 1)]
    return lax.ppermute(up, "lat", pairs), lax.ppermute(down, "lat", back)


def exchange_columns(east, west, n_lon):
    pairs = [(i, (i + 1) % n_lon) for i in range(n_lon)]
    back = [((i + 1) % n_lon, i) for i in range(n_lon)]
    return lax.ppermute(east, "lon", pairs), lax.ppermute(west, "lon", back)


def on_device(
    innovations,
    owners,
    prof_row,
    prof_col,
    interp_weights,
    model_tiles,
    model_ids,
    face_x,
    face_y,
    cross_term,
    wet_mask,
    norm_factor,
):
    n_lat = lax.axis_size("lat")
    n_lon = lax.axis_size("lon")
    devices = n_lat * n_lon
    levels, lat_cells, lon_cells = norm_factor.shape
    tiles = model_tiles.shape[1]
    group = tiles // n_lon
    count = innovations.shape[1]
    cap = 2 * count // devices
    slots = devices * cap
    rows = slots // PER_ROW
    starts = group_starts()
    f32 = jnp.float32
    lat = lax.axis_index("lat").reshape(1)
    both = ("lat", "lon")
    span = span_of(lat_cells)
    ext_rows = SEATS * span
    win_rows = ext_rows + SUB

    def arrays(*shapes):
        return tuple(jax.ShapeDtypeStruct(shape, f32) for shape in shapes)

    def call(kernel, out_shape, micros, name, grant=SMALL, **kwargs):
        return pl.pallas_call(
            kernel,
            out_shape=out_shape,
            compiler_params=params(grant),
            cost_estimate=cost(micros),
            name=name,
            **kwargs,
        )

    def after(value, *others):
        return lax.optimization_barrier((value,) + others)[0]

    def tile_exchange(chunk, *others):
        first = sum(CHUNKS[:chunk])
        begin = starts[first]
        size = sum(GROUPS[first : first + CHUNKS[chunk]])
        piece = model_tiles[begin : begin + size].reshape(size, n_lon, group, SUB, LANES)
        piece = jnp.transpose(piece, (1, 0, 2, 3, 4))
        if others:
            piece = after(piece, *others)
        return lax.all_to_all(piece, "lon", split_axis=0, concat_axis=0, tiled=True)

    def halo(field, up, down, groups):
        above, below = exchange_rows(up, down, n_lat)
        strips, east, west = call(
            edges_kernel,
            arrays((ext_rows * SUB, LANES), (span * SUB, LANES), (span * SUB, LANES)),
            3,
            "edges",
            scratch_shapes=[pltpu.VMEM((groups, ext_rows * SUB, LANES), f32)],
        )(field, above, below)
        return (field, above, below, strips) + exchange_columns(east, west, n_lon)

    def field_shapes(groups):
        return arrays(
            (groups, lat_cells * SUB, LANES),
            (groups, STEPS * SUB, LANES),
            (groups, STEPS * SUB, LANES),
        )

    send, slot = call(
        functools.partial(route_kernel, cap, group, n_lat, starts),
        (jax.ShapeDtypeStruct((rows, LANES), f32), jax.ShapeDtypeStruct((1, count), jnp.int32)),
        3,
        "route",
        LARGE,
        scratch_shapes=[pltpu.VMEM((FEATS, count + devices * group), f32)],
    )(
        innovations,
        interp_weights,
        owners.reshape(1, count),
        prof_row.reshape(1, count),
        prof_col.reshape(1, count),
        model_ids,
    )
    stacked = call(stack_kernel, field_shapes(1), 3, "stack")(face_x, face_y, cross_term, wet_mask)
    stack, above, below, coef_strips, coef_west, coef_east = halo(*stacked, 1)
    own_coef = call(
        own_coef_kernel,
        arrays((5, win_rows, LANES))[0],
        3,
        "own_coef",
        scratch_shapes=[pltpu.VMEM((1, (win_rows + SUB) * SUB, LANES), f32)],
    )(stack, above, below)
    recv = lax.all_to_all(
        send.reshape(devices, rows // devices, LANES), both, split_axis=0, concat_axis=0, tiled=True
    ).reshape(rows, LANES)
    pieces = [tile_exchange(0, recv, stacked[0])]

    smem = pl.BlockSpec(memory_space=pltpu.SMEM)
    vmem = pl.BlockSpec(memory_space=pltpu.VMEM)
    hbm = pl.BlockSpec(memory_space=pltpu.HBM)
    turned = pltpu.VMEM((rows // LANES, LANES, LANES), f32)
    low, high, loc = call(
        place_kernel,
        arrays((slots, LANES), (slots, LANES)) + (jax.ShapeDtypeStruct((2 * PER_ROW, rows), jnp.int32),),
        2,
        "place",
        LARGE,
        scratch_shapes=[turned],
    )(recv)

    def scatter(chunk, grant):
        first = sum(CHUNKS[:chunk])
        return call(
            functools.partial(scatter_kernel, first),
            arrays((CHUNKS[chunk], lat_cells * SUB, LANES))[0],
            9,
            "scatter",
            grant,
            in_specs=[smem, vmem, vmem, vmem],
            scratch_shapes=[turned, pltpu.VMEM((CHUNKS[chunk], lat_cells * SUB, LANES), f32)],
        )(loc, recv, low, high)

    observed = [scatter(0, LARGE), scatter(1, SMALL)]
    pieces.append(tile_exchange(1, pieces[0], observed[0], own_coef))
    shift_space = pltpu.VMEM((2 * LANES, 2 * LANES), jnp.bfloat16)
    def first_field(chunk, piece):
        first = sum(CHUNKS[:chunk])
        sizes = GROUPS[first : first + CHUNKS[chunk]]
        return call(
            functools.partial(field_kernel, starts[first], sizes, n_lon, group, cap),
            field_shapes(CHUNKS[chunk]),
            4,
            "field",
            in_specs=[smem, smem, vmem, vmem, hbm],
            scratch_shapes=[pltpu.VMEM((sum(sizes), lat_cells, LANES), f32), pltpu.SemaphoreType.DMA],
        )(loc, lat, piece, observed[chunk], norm_factor)

    fields = [first_field(0, pieces[0])]
    smoothed = None
    sampled = []
    first = 0
    for chunk, groups in enumerate(CHUNKS):
        sizes = GROUPS[first : first + groups]
        begin = starts[first]
        own_levels = (sum(sizes), lat_cells, LANES)
        field = fields[chunk]
        field, above, below, strips, from_west, from_east = halo(*field, groups)
        mid_shape = (groups, lat_cells * SUB, LANES)
        win_shape = (groups, win_rows * SUB, LANES)
        mid = call(
            own_kernel,
            arrays(mid_shape)[0],
            6 * groups,
            "own",
            scratch_shapes=[pltpu.VMEM(win_shape, f32), pltpu.VMEM(win_shape, f32), shift_space],
        )(after(field, strips), above, below, own_coef)
        if chunk == 0:
            fields.append(first_field(1, after(pieces[1], mid)))
            strip_coef = call(
                strip_coef_kernel,
                arrays((5, win_rows, LANES))[0],
                3,
                "strip_coef",
                scratch_shapes=[pltpu.VMEM(((win_rows + SUB) * SUB, LANES), f32)],
            )(after(coef_strips, mid, fields[1][1]), coef_west, coef_east)
        operands = [loc, strips, from_west, from_east, strip_coef, mid, low, high, norm_factor]
        specs = [smem] + [vmem] * 7 + [hbm]
        aliases = {}
        if smoothed is not None:
            aliases = {len(operands): 0}
            operands.append(smoothed)
            specs.append(hbm)
        last = chunk + 1 == len(CHUNKS)
        earlier = sampled if last else []
        part_shape = (rows // LANES, groups, PER_ROW * SUB, LANES)
        gathered = [pltpu.VMEM(part_shape, f32), pltpu.VMEM((rows // LANES, LANES, LANES), f32)]
        smoothed, part = call(
            functools.partial(strip_kernel, sizes, begin, len(aliases), len(earlier)),
            arrays(norm_factor.shape, (rows, LANES) if earlier else part_shape),
            12,
            "strips",
            in_specs=specs + [vmem] * len(earlier),
            out_specs=(hbm, vmem),
            scratch_shapes=(gathered if earlier else [])
            + [
                pltpu.VMEM((1,) + win_shape[1:], f32),
                pltpu.VMEM((1,) + win_shape[1:], f32),
                shift_space,
                pltpu.VMEM(mid_shape, f32),
                pltpu.VMEM(own_levels, f32),
                pltpu.VMEM(own_levels, f32),
                pltpu.SemaphoreType.DMA((2,)),
            ],
            input_output_aliases=aliases,
        )(*operands, *earlier)
        sampled.append(part)
        first += groups

    back = sampled[-1]
    returned = lax.all_to_all(
        back.reshape(devices, rows // devices, LANES), both, split_axis=0, concat_axis=0, tiled=True
    ).reshape(rows, LANES)
    profile_values = call(
        functools.partial(unpack_kernel, starts),
        arrays((levels, count))[0],
        1,
        "unpack",
    )(returned, slot)
    return (smoothed, profile_values)


def solution(mesh):
    in_specs = (
        P(None, ("lat", "lon")),
        P(("lat", "lon"), None),
        P(("lat", "lon")),
        P(("lat", "lon")),
        P(None, ("lat", "lon")),
        P(None, ("lat", "lon"), None, None),
        P(None, ("lat", "lon")),
        P("lat", "lon"),
        P("lat", "lon"),
        P("lat", "lon"),
        P("lat", "lon"),
        P(None, "lat", "lon"),
    )
    out_specs = (P(None, "lat", "lon"), P(None, ("lat", "lon")))
    return jax.shard_map(
        on_device, mesh=mesh, in_specs=in_specs, out_specs=out_specs, check_vma=False
    )
```

```python
import functools
import jax
import jax.numpy as jnp
from jax import lax
from jax.experimental import pallas as pl
from jax.experimental.pallas import tpu as pltpu
from jax.sharding import PartitionSpec as P

STEPS = 10
SUB = 8
LANES = 128
FEATS = 32
PER_ROW = LANES // FEATS
GROUPS = (5, 4, 8, 8)
CHUNKS = (2, 2)
WEIGHT_ROWS = (5, 6, 12, 13)
LOC_ROW = 7
ID_ROW = 15
SMALL = 20 * 1024 * 1024
LARGE = 60 * 1024 * 1024


def group_starts():
    starts = []
    total = 0
    for count in GROUPS:
        starts.append(total)
        total += count
    return starts


def params(grant):
    return pltpu.CompilerParams(vmem_limit_bytes=grant)


def cost(micros):
    return pl.CostEstimate(flops=0, bytes_accessed=int(micros * 3.6e6), transcendentals=0)


def iota(shape, dim):
    return lax.broadcasted_iota(jnp.int32, shape, dim)


def split3(values):
    high = values.astype(jnp.bfloat16)
    rest = values - high.astype(jnp.float32)
    middle = rest.astype(jnp.bfloat16)
    low = (rest - middle.astype(jnp.float32)).astype(jnp.bfloat16)
    return high, middle, low


def route_kernel(cap, group, copies, starts, innov, weights, own_row, prow, pcol, ids, send, slot_out, pay):
    count = innov.shape[1]
    tiles = ids.shape[1]
    extra = tiles * copies
    owner = own_row[...]
    column = jnp.broadcast_to(owner.astype(jnp.float32), (SUB, count)).T[:, :1].astype(jnp.int32)
    same = column == owner
    before = iota((count, count), 0) < iota((count, count), 1)
    ones = jnp.where(same & before, 1.0, 0.0)
    rank = jnp.sum(ones, axis=0, keepdims=True).astype(jnp.int32)
    slot = owner * cap + rank
    slot_out[...] = slot
    number = iota((1, extra), 1)
    id_slot = (number // group) * cap + number % group
    pay[...] = jnp.zeros_like(pay)
    for index, count_in in enumerate(GROUPS):
        pay[index * SUB : index * SUB + count_in, :count] = innov[starts[index] : starts[index] + count_in, :]
    for corner, row in enumerate(WEIGHT_ROWS):
        pay[row : row + 1, :count] = weights[corner : corner + 1, :]
    pay[LOC_ROW : LOC_ROW + 1, :count] = (prow[...] * LANES + pcol[...]).astype(jnp.float32)
    for i in range(copies):
        at = count + i * tiles
        pay[ID_ROW : ID_ROW + 1, at : at + tiles] = ids[...].astype(jnp.float32)
    slots = jnp.concatenate([slot, id_slot], axis=1)
    values = pay[...]
    part = slots % PER_ROW
    spread = jnp.concatenate([jnp.where(part == k, values, 0.0) for k in range(PER_ROW)], axis=0)
    rows = send.shape[0]
    hot = jnp.where(iota((rows, count + extra), 0) == slots // PER_ROW, 1.0, 0.0).astype(jnp.bfloat16)
    total = None
    for piece in split3(spread):
        term = lax.dot_general(hot, piece, (((1,), (1,)), ((), ())), preferred_element_type=jnp.float32)
        total = term if total is None else total + term
    send[...] = total


def unpack_kernel(starts, recv, slot, out):
    slots = slot[...]
    rows = recv.shape[0]
    hot = jnp.where(iota((rows, slots.shape[1]), 0) == slots // PER_ROW, 1.0, 0.0).astype(jnp.bfloat16)
    total = None
    for piece in split3(recv[...]):
        term = lax.dot_general(piece, hot, (((0,), (0,)), ((), ())), preferred_element_type=jnp.float32)
        total = term if total is None else total + term
    part = slots % PER_ROW
    picked = jnp.zeros((FEATS, slots.shape[1]), jnp.float32)
    for k in range(PER_ROW):
        picked = jnp.where(part == k, total[k * FEATS : (k + 1) * FEATS], picked)
    for index, count_in in enumerate(GROUPS):
        out[starts[index] : starts[index] + count_in, :] = picked[index * SUB : index * SUB + count_in]


def turn_slots(recv, turned):
    for h in range(recv.shape[0] // LANES):
        turned[h] = recv[h * LANES : (h + 1) * LANES, :].T


def place_kernel(recv, low, high, loc_out, turned):
    rows = recv.shape[0]
    turn_slots(recv, turned)
    for k in range(PER_ROW):
        for h in range(rows // LANES):
            at = k * FEATS
            cut = slice(h * LANES, (h + 1) * LANES)
            cells = turned[h, at + LOC_ROW : at + LOC_ROW + 1, :].astype(jnp.int32)
            loc_out[k : k + 1, cut] = cells // LANES * SUB
            loc_out[PER_ROW + k : PER_ROW + k + 1, cut] = turned[h, at + ID_ROW : at + ID_ROW + 1, :].astype(jnp.int32)
    lane = iota((rows, LANES), 1)
    for k in range(PER_ROW):
        at = k * FEATS
        col = recv[:, at + LOC_ROW : at + LOC_ROW + 1].astype(jnp.int32) % LANES
        w = [recv[:, at + row : at + row + 1] for row in WEIGHT_ROWS]
        here = lane == col
        after = lane == col + 1
        low[k * rows : (k + 1) * rows, :] = jnp.where(here, w[0], jnp.where(after, w[1], 0.0))
        high[k * rows : (k + 1) * rows, :] = jnp.where(here, w[2], jnp.where(after, w[3], 0.0))


def scatter_kernel(first, loc, recv, low, high, obs, turned, odd):
    rows = recv.shape[0]
    groups = range(obs.shape[0])
    turn_slots(recv, turned)

    def clear(i, carry):
        for g in groups:
            at = pl.ds(pl.multiple_of(i * 64, 64), 64)
            obs[g, at, :] = jnp.zeros((64, LANES), jnp.float32)
            odd[g, at, :] = jnp.zeros((64, LANES), jnp.float32)
        return carry

    lax.fori_loop(0, obs.shape[1] // 64, clear, 0)

    def body(i, carry):
        h = i // PER_ROW
        k = i % PER_ROW
        size = len(groups) * SUB
        block = turned[h, pl.ds(pl.multiple_of(k * FEATS + first * SUB, SUB), size), :]
        for seat in range(0, LANES, 2):
            found = []
            for n, total in enumerate((obs, odd)):
                at = pl.multiple_of(loc[k, h * LANES + seat + n], SUB)
                lo = low[pl.ds(k * rows + h * LANES + seat + n, 1), :]
                hi = high[pl.ds(k * rows + h * LANES + seat + n, 1), :]
                for g in groups:
                    value = block[g * SUB : (g + 1) * SUB, seat + n : seat + n + 1]
                    here = total[g, pl.ds(at, SUB), :] + value * lo
                    north = total[g, pl.ds(at + SUB, SUB), :] + value * hi
                    found.append((total, g, at, here, north))
            for total, g, at, here, north in found:
                total[g, pl.ds(at, SUB), :] = here
                total[g, pl.ds(at + SUB, SUB), :] = north
        return carry

    lax.fori_loop(0, (rows // LANES) * PER_ROW, body, 0)

    def join(i, carry):
        for g in groups:
            at = pl.ds(pl.multiple_of(i * 64, 64), 64)
            obs[g, at, :] = obs[g, at, :] + odd[g, at, :]
        return carry

    lax.fori_loop(0, obs.shape[1] // 64, join, 0)


def row_at(index):
    return pl.ds(pl.multiple_of(index * SUB, SUB), SUB)


def rows_at(index, count):
    return pl.ds(pl.multiple_of(index * SUB, SUB), count * SUB)


def send_rows(field, up, down):
    edge = up.shape[1]
    total = field.shape[1]
    for g in range(field.shape[0]):
        up[g] = field[g, total - edge :, :]
        down[g] = field[g, :edge, :]


def field_kernel(begin, sizes, n_lon, group, cap, loc, lat, tiles, obs, norm_h, field, up, down, norm, sem):
    copy = pltpu.make_async_copy(norm_h.at[pl.ds(begin, sum(sizes))], norm, sem)
    copy.start()
    field[...] = jnp.zeros_like(field)
    copy.wait()

    def body(j, carry):
        done = []
        for c in range(group):
            slot = (lat[0] * n_lon + j) * cap + c
            t = loc[PER_ROW + slot % PER_ROW, slot // PER_ROW]
            own = pl.ds(pl.multiple_of(t * SUB, SUB), SUB)
            level = 0
            for g, size in enumerate(sizes):
                for l in range(size):
                    at = pl.ds(t * (SUB * SUB) + l, SUB, stride=SUB)
                    done.append((g, at, norm[level, own, :] * (obs[g, at, :] + tiles[j, level, c])))
                    level += 1
        for g, at, value in done:
            field[g, at, :] = value
        return carry

    lax.fori_loop(0, n_lon, body, 0)
    send_rows(field, up, down)


def stack_kernel(face_x, face_y, cross, wet, field, up, down):
    field[...] = jnp.zeros_like(field)
    sources = (face_x, face_y, cross, wet)

    def body(i, carry):
        values = []
        for n in range(4):
            t = i * 4 + n
            own = pl.ds(pl.multiple_of(t * SUB, SUB), SUB)
            values += [(t, l, source[own, :].astype(jnp.float32)) for l, source in enumerate(sources)]
        for t, l, value in values:
            field[0, pl.ds(t * (SUB * SUB) + l, SUB, stride=SUB), :] = value
        return carry

    lax.fori_loop(0, face_x.shape[0] // SUB // 4, body, 0)
    send_rows(field, up, down)


STRIP = 32
HALF = 2 * STRIP
SEAT = 16
SEATS = HALF // SEAT
TURNS = 10


def span_of(rows):
    return -(-(rows + 2 * STEPS) // (SEATS * TURNS)) * TURNS


def extend(ext, field, above, below):
    groups, total, _ = field.shape
    halo = STEPS * SUB
    for g in range(groups):
        ext[g, :halo, :] = above[g]
        ext[g, halo : halo + total, :] = field[g]
        ext[g, halo + total : 2 * halo + total, :] = below[g]
        ext[g, 2 * halo + total :, :] = jnp.zeros((ext.shape[1] - 2 * halo - total, LANES), jnp.float32)


def edges_kernel(field, above, below, strips, east, west, ext):
    groups = field.shape[0]
    extend(ext, field, above, below)
    span = east.shape[0] // SUB
    lane = iota((SUB, LANES), 1)
    place = lane % HALF

    def body(i, carry):
        done = []
        for n in range(TURNS // 2):
            m = i * (TURNS // 2) + n
            to_east = None
            to_west = None
            for q in range(SEATS):
                first = ext[0, row_at(q * span + m), :]
                second = pltpu.roll(ext[groups - 1, row_at(q * span + m), :], HALF, 1)
                left = jnp.where(lane < HALF, first, second)
                right = jnp.where(lane < HALF, second, first)
                row = jnp.where(place < STRIP, pltpu.roll(left, STEPS, 1), pltpu.roll(right, HALF - STEPS, 1))
                done.append((strips, q * span + m, row))
                right = pltpu.roll(right, SEAT * q + SEAT, 1)
                if q:
                    left = pltpu.roll(left, SEAT * q, 1)
                mine = place // SEAT == q
                to_east = right if q == 0 else jnp.where(mine, right, to_east)
                to_west = left if q == 0 else jnp.where(mine, left, to_west)
            done.append((east, m, to_east))
            done.append((west, m, to_west))
        for ref, m, value in done:
            ref[row_at(m), :] = value
        return carry

    lax.fori_loop(0, span // (TURNS // 2), body, 0)


def build_strips(win, strips, from_west, from_east):
    span = from_west.shape[0] // SUB
    place = iota((SUB, LANES), 1) % HALF

    def body(i, carry):
        for n in range(TURNS):
            m = i * TURNS + n
            west = from_west[row_at(m), :]
            east = from_east[row_at(m), :]
            for q in range(SEATS):
                a = pltpu.roll(west, (STEPS - SEAT - SEAT * q) % LANES, 1)
                b = pltpu.roll(east, (HALF - STEPS - SEAT * q) % LANES, 1)
                row = strips[row_at(q * span + m), :]
                row = jnp.where(place < STEPS, a, jnp.where(place < HALF - STEPS, row, b))
                win[row_at(q * span + m), :] = row
        return carry

    lax.fori_loop(0, span // TURNS, body, 0)
    first = SEATS * span * SUB
    win[first:, :] = jnp.zeros((win.shape[0] - first, LANES), jnp.float32)


def fill_coef(coef, win):
    rows = coef.shape[1]

    def body(i, carry):
        done = []
        for n in range(12):
            b = i * 12 + n
            base = b * (SUB * SUB)
            at = pl.ds(pl.multiple_of(b * SUB, SUB), SUB)
            fx, fy, ct, wet = (win[pl.ds(base + s, SUB, stride=SUB), :] for s in range(4))
            wet_n = win[pl.ds(base + SUB + 3, SUB, stride=SUB), :]
            x = fx * wet * pltpu.roll(wet, LANES - 1, 1)
            xw = pltpu.roll(x, 1, 1)
            y = fy * wet * wet_n
            twist = 0.25 * ct * wet
            for c, value in enumerate((1.0 - x - xw, x, xw, y, twist)):
                done.append((c, at, value))
        for c, at, value in done:
            coef[c, at, :] = value
        return carry

    lax.fori_loop(0, rows // (12 * SUB), body, 0)


def own_coef_kernel(field, above, below, coef, ext):
    extend(ext, field, above, below)
    fill_coef(coef, ext.at[0])


def strip_coef_kernel(strips, from_west, from_east, coef, win):
    build_strips(win, strips, from_west, from_east)
    fill_coef(coef, win)


BY_MATMUL = 0.25


def fill_shift(shift):
    row = iota(shift.shape, 0) % LANES
    col = iota(shift.shape, 1)
    near = jnp.where(col < LANES, col + 1, col + LANES - 1) % LANES
    shift[...] = jnp.where(row == near, 1.0, 0.0).astype(jnp.bfloat16)


def advance(source, target, planes, weight, shift, rows):
    last = rows + 2 * STEPS + 4
    unroll = last // planes
    blocks = last // unroll
    split = int(unroll * BY_MATMUL)

    def rolled(w, index):
        cells = source[w, row_at(index), :]
        east = pltpu.roll(cells, LANES - 1, 1)
        west = pltpu.roll(cells, 1, 1)
        return cells, east, west, east - west

    def shifted_rows(w, first):
        cells = source[w, rows_at(first, split), :]
        high = cells.astype(jnp.bfloat16)
        low = (cells - high.astype(jnp.float32)).astype(jnp.bfloat16)
        both = jnp.concatenate([high, low], axis=1)
        return jnp.dot(both, shift[...], preferred_element_type=jnp.float32)

    y_first = weight(3, 0)
    state = []
    for w in range(planes):
        before = rolled(w, 0)
        now = rolled(w, 1)
        state.append((now, before[3], y_first * (now[0] - before[0])))

    def block(b, state):
        base = 1 + b * unroll
        state = list(state)
        sides = [shifted_rows(w, base + 1) for w in range(planes)]
        for u in range(unroll):
            weights = [weight(c, base + u) for c in range(5)]
            for w in range(planes):
                (cells, east, west, slope), slope_s, flux_s = state[w]
                if u < split:
                    cells_n = source[w, row_at(base + u + 1), :]
                    east_n = sides[w][u * SUB : (u + 1) * SUB, :LANES]
                    west_n = sides[w][u * SUB : (u + 1) * SUB, LANES:]
                    ahead = (cells_n, east_n, west_n, east_n - west_n)
                else:
                    ahead = rolled(w, base + u + 1)
                flux = weights[3] * (ahead[0] - cells)
                target[w, row_at(base + u), :] = (
                    (weights[0] * cells + weights[1] * east)
                    + (weights[2] * west + (flux - flux_s))
                    + weights[4] * (ahead[3] - slope_s)
                )
                state[w] = (ahead, slope, flux)
        return tuple(state)

    lax.fori_loop(0, blocks, block, tuple(state))


def diffuse(win, other, planes, coef, shift, rows):
    fill_shift(shift)

    def weight(c, index):
        return coef[c, pl.ds(index, 1), :]

    def two(t, carry):
        advance(win, other, planes, weight, shift, rows)
        advance(other, win, planes, weight, shift, rows)
        return carry

    for w in range(planes):
        other[w, :SUB, :] = jnp.zeros((SUB, LANES), jnp.float32)
        other[w, other.shape[1] - SUB * SUB :, :] = jnp.zeros((SUB * SUB, LANES), jnp.float32)
    lax.fori_loop(0, STEPS // 2, two, 0)


def own_kernel(field, above, below, coef, mid, win, other, shift):
    groups = field.shape[0]
    rows = mid.shape[1] // SUB
    halo = STEPS * SUB
    extend(win, field, above, below)
    diffuse(win, other, groups, coef, shift, rows)
    for g in range(groups):
        mid[g] = win[g, halo : halo + rows * SUB, :]


MERGE = 32


def strip_kernel(sizes, begin, aliased, earlier, *refs):
    loc, strips, from_west, from_east, coef, mid, low, high, norm_h = refs[:9]
    parts = refs[9 + aliased : 9 + aliased + earlier]
    refs = refs[9 + aliased + earlier :]
    if earlier:
        out_h, packed, sampled, turned = refs[:4]
    else:
        out_h, sampled = refs[:2]
    win, other, shift, smooth, norm, out, sems = refs[-7:]
    groups = mid.shape[0]
    rows = mid.shape[1] // SUB
    levels = pl.ds(begin, sum(sizes))
    copy = pltpu.make_async_copy(norm_h.at[levels], norm, sems.at[0])
    copy.start()
    build_strips(win.at[0], strips, from_west, from_east)
    diffuse(win, other, 1, coef, shift, rows)
    copy.wait()
    lane = iota((SUB, LANES), 1)
    outer = LANES - STEPS

    def merge(b, carry):
        for u in range(MERGE):
            at = row_at(b * MERGE + u)
            strip = win[0, row_at(b * MERGE + u + STEPS), :]
            west = pltpu.roll(strip, outer, 1)
            east = pltpu.roll(strip, HALF + STEPS, 1)
            cells = mid[0, at, :]
            smooth[0, at, :] = jnp.where(lane < STEPS, west, jnp.where(lane < outer, cells, east))
            if groups == 2:
                both = pltpu.roll(jnp.where(lane < HALF, east, west), HALF, 1)
                cells = mid[1, at, :]
                smooth[1, at, :] = jnp.where((lane < STEPS) | (lane >= outer), both, cells)
        return carry

    lax.fori_loop(0, rows // MERGE, merge, 0)

    def scale(i, carry):
        done = []
        for n in range(4):
            b = i * 4 + n
            own = pl.ds(pl.multiple_of(b * SUB, SUB), SUB)
            level = 0
            for g, size in enumerate(sizes):
                for l in range(size):
                    at = pl.ds(b * (SUB * SUB) + l, SUB, stride=SUB)
                    done.append((g, at, level, own, smooth[g, at, :] * norm[level, own, :]))
                    level += 1
        for g, at, level, own, value in done:
            out[level, own, :] = value
            smooth[g, at, :] = value
        return carry

    lax.fori_loop(0, rows // (4 * SUB), scale, 0)
    back = pltpu.make_async_copy(out, out_h.at[levels], sems.at[1])
    back.start()
    count = low.shape[0] // PER_ROW
    halves = count // LANES

    def samples(i, carry):
        h = i // PER_ROW
        k = i % PER_ROW
        kept = [[jnp.zeros((SUB, LANES), jnp.float32)] * 4 for _ in range(groups)]
        for seat in range(LANES):
            at = pl.multiple_of(loc[k, h * LANES + seat], SUB)
            lo = low[pl.ds(k * count + h * LANES + seat, 1), :]
            hi = high[pl.ds(k * count + h * LANES + seat, 1), :]
            for g in range(groups):
                value = smooth[g, pl.ds(at, SUB), :] * lo + smooth[g, pl.ds(at + SUB, SUB), :] * hi
                total = jnp.sum(value, axis=1, keepdims=True)
                kept[g][seat % 4] = jnp.where(lane == seat, total, kept[g][seat % 4])
        for g in range(groups):
            a, b, c, d = kept[g]
            sampled[h, g, row_at(k), :] = (a + b) + (c + d)
        return carry

    lax.fori_loop(0, halves * PER_ROW, samples, 0)
    if earlier:
        pack_samples(parts + (sampled,), packed, turned)
    back.wait()


def pack_samples(parts, out, turned):
    for h in range(turned.shape[0]):
        index = 0
        for part in parts:
            for g in range(part.shape[1]):
                for k in range(PER_ROW):
                    at = k * FEATS + index * SUB
                    turned[h, at : at + SUB, :] = part[h, g, k * SUB : (k + 1) * SUB, :]
                index += 1
        out[h * LANES : (h + 1) * LANES, :] = turned[h].T


def exchange_rows(up, down, n_lat):
    pairs = [(i, i + 1) for i in range(n_lat - 1)]
    back = [(i + 1, i) for i in range(n_lat - 1)]
    return lax.ppermute(up, "lat", pairs), lax.ppermute(down, "lat", back)


def exchange_columns(east, west, n_lon):
    pairs = [(i, (i + 1) % n_lon) for i in range(n_lon)]
    back = [((i + 1) % n_lon, i) for i in range(n_lon)]
    return lax.ppermute(east, "lon", pairs), lax.ppermute(west, "lon", back)


def on_device(
    innovations,
    owners,
    prof_row,
    prof_col,
    interp_weights,
    model_tiles,
    model_ids,
    face_x,
    face_y,
    cross_term,
    wet_mask,
    norm_factor,
):
    n_lat = lax.axis_size("lat")
    n_lon = lax.axis_size("lon")
    devices = n_lat * n_lon
    levels, lat_cells, lon_cells = norm_factor.shape
    tiles = model_tiles.shape[1]
    group = tiles // n_lon
    count = innovations.shape[1]
    cap = 2 * count // devices
    slots = devices * cap
    rows = slots // PER_ROW
    starts = group_starts()
    f32 = jnp.float32
    lat = lax.axis_index("lat").reshape(1)
    both = ("lat", "lon")
    span = span_of(lat_cells)
    ext_rows = SEATS * span
    win_rows = ext_rows + SUB

    def arrays(*shapes):
        return tuple(jax.ShapeDtypeStruct(shape, f32) for shape in shapes)

    def call(kernel, out_shape, micros, name, grant=SMALL, **kwargs):
        return pl.pallas_call(
            kernel,
            out_shape=out_shape,
            compiler_params=params(grant),
            cost_estimate=cost(micros),
            name=name,
            **kwargs,
        )

    def after(value, *others):
        return lax.optimization_barrier((value,) + others)[0]

    def tile_exchange(chunk, *others):
        first = sum(CHUNKS[:chunk])
        begin = starts[first]
        size = sum(GROUPS[first : first + CHUNKS[chunk]])
        piece = model_tiles[begin : begin + size].reshape(size, n_lon, group, SUB, LANES)
        piece = jnp.transpose(piece, (1, 0, 2, 3, 4))
        if others:
            piece = after(piece, *others)
        return lax.all_to_all(piece, "lon", split_axis=0, concat_axis=0, tiled=True)

    def halo(field, up, down, groups):
        above, below = exchange_rows(up, down, n_lat)
        strips, east, west = call(
            edges_kernel,
            arrays((ext_rows * SUB, LANES), (span * SUB, LANES), (span * SUB, LANES)),
            3,
            "edges",
            scratch_shapes=[pltpu.VMEM((groups, ext_rows * SUB, LANES), f32)],
        )(field, above, below)
        return (field, above, below, strips) + exchange_columns(east, west, n_lon)

    def field_shapes(groups):
        return arrays(
            (groups, lat_cells * SUB, LANES),
            (groups, STEPS * SUB, LANES),
            (groups, STEPS * SUB, LANES),
        )

    send, slot = call(
        functools.partial(route_kernel, cap, group, n_lat, starts),
        (jax.ShapeDtypeStruct((rows, LANES), f32), jax.ShapeDtypeStruct((1, count), jnp.int32)),
        3,
        "route",
        LARGE,
        scratch_shapes=[pltpu.VMEM((FEATS, count + devices * group), f32)],
    )(
        innovations,
        interp_weights,
        owners.reshape(1, count),
        prof_row.reshape(1, count),
        prof_col.reshape(1, count),
        model_ids,
    )
    stacked = call(stack_kernel, field_shapes(1), 3, "stack")(face_x, face_y, cross_term, wet_mask)
    stack, above, below, coef_strips, coef_west, coef_east = halo(*stacked, 1)
    own_coef = call(
        own_coef_kernel,
        arrays((5, win_rows, LANES))[0],
        3,
        "own_coef",
        scratch_shapes=[pltpu.VMEM((1, (win_rows + SUB) * SUB, LANES), f32)],
    )(stack, above, below)
    recv = lax.all_to_all(
        send.reshape(devices, rows // devices, LANES), both, split_axis=0, concat_axis=0, tiled=True
    ).reshape(rows, LANES)
    pieces = [tile_exchange(0, recv, stacked[0])]

    smem = pl.BlockSpec(memory_space=pltpu.SMEM)
    vmem = pl.BlockSpec(memory_space=pltpu.VMEM)
    hbm = pl.BlockSpec(memory_space=pltpu.HBM)
    turned = pltpu.VMEM((rows // LANES, LANES, LANES), f32)
    low, high, loc = call(
        place_kernel,
        arrays((slots, LANES), (slots, LANES)) + (jax.ShapeDtypeStruct((2 * PER_ROW, rows), jnp.int32),),
        2,
        "place",
        LARGE,
        scratch_shapes=[turned],
    )(recv)

    def scatter(chunk, grant):
        first = sum(CHUNKS[:chunk])
        return call(
            functools.partial(scatter_kernel, first),
            arrays((CHUNKS[chunk], lat_cells * SUB, LANES))[0],
            9,
            "scatter",
            grant,
            in_specs=[smem, vmem, vmem, vmem],
            scratch_shapes=[turned, pltpu.VMEM((CHUNKS[chunk], lat_cells * SUB, LANES), f32)],
        )(loc, recv, low, high)

    observed = [scatter(0, LARGE), scatter(1, SMALL)]
    pieces.append(tile_exchange(1, pieces[0], observed[0], own_coef, coef_west, coef_east))
    shift_space = pltpu.VMEM((2 * LANES, 2 * LANES), jnp.bfloat16)
    smoothed = None
    sampled = []
    first = 0
    for chunk, groups in enumerate(CHUNKS):
        sizes = GROUPS[first : first + groups]
        begin = starts[first]
        own_levels = (sum(sizes), lat_cells, LANES)
        field = call(
            functools.partial(field_kernel, begin, sizes, n_lon, group, cap),
            field_shapes(groups),
            4,
            "field",
            in_specs=[smem, smem, vmem, vmem, hbm],
            scratch_shapes=[pltpu.VMEM(own_levels, f32), pltpu.SemaphoreType.DMA],
        )(loc, lat, pieces[chunk], observed[chunk], norm_factor)
        field, above, below, strips, from_west, from_east = halo(*field, groups)
        mid_shape = (groups, lat_cells * SUB, LANES)
        win_shape = (groups, win_rows * SUB, LANES)
        mid = call(
            own_kernel,
            arrays(mid_shape)[0],
            6 * groups,
            "own",
            scratch_shapes=[pltpu.VMEM(win_shape, f32), pltpu.VMEM(win_shape, f32), shift_space],
        )(after(field, strips), above, below, own_coef)
        if chunk == 0:
            strip_coef = call(
                strip_coef_kernel,
                arrays((5, win_rows, LANES))[0],
                3,
                "strip_coef",
                scratch_shapes=[pltpu.VMEM(((win_rows + SUB) * SUB, LANES), f32)],
            )(after(coef_strips, mid, *observed[1:]), coef_west, coef_east)
        if chunk + 1 < len(CHUNKS):
            pieces[chunk + 1] = after(pieces[chunk + 1], mid, strip_coef)
        operands = [loc, strips, from_west, from_east, strip_coef, mid, low, high, norm_factor]
        specs = [smem] + [vmem] * 7 + [hbm]
        aliases = {}
        if smoothed is not None:
            aliases = {len(operands): 0}
            operands.append(smoothed)
            specs.append(hbm)
        last = chunk + 1 == len(CHUNKS)
        earlier = sampled if last else []
        part_shape = (rows // LANES, groups, PER_ROW * SUB, LANES)
        gathered = [pltpu.VMEM(part_shape, f32), pltpu.VMEM((rows // LANES, LANES, LANES), f32)]
        smoothed, part = call(
            functools.partial(strip_kernel, sizes, begin, len(aliases), len(earlier)),
            arrays(norm_factor.shape, (rows, LANES) if earlier else part_shape),
            12,
            "strips",
            in_specs=specs + [vmem] * len(earlier),
            out_specs=(hbm, vmem),
            scratch_shapes=(gathered if earlier else [])
            + [
                pltpu.VMEM((1,) + win_shape[1:], f32),
                pltpu.VMEM((1,) + win_shape[1:], f32),
                shift_space,
                pltpu.VMEM(mid_shape, f32),
                pltpu.VMEM(own_levels, f32),
                pltpu.VMEM(own_levels, f32),
                pltpu.SemaphoreType.DMA((2,)),
            ],
            input_output_aliases=aliases,
        )(*operands, *earlier)
        sampled.append(part)
        first += groups

    back = sampled[-1]
    returned = lax.all_to_all(
        back.reshape(devices, rows // devices, LANES), both, split_axis=0, concat_axis=0, tiled=True
    ).reshape(rows, LANES)
    profile_values = call(
        functools.partial(unpack_kernel, starts),
        arrays((levels, count))[0],
        1,
        "unpack",
    )(returned, slot)
    return (smoothed, profile_values)


def solution(mesh):
    in_specs = (
        P(None, ("lat", "lon")),
        P(("lat", "lon"), None),
        P(("lat", "lon")),
        P(("lat", "lon")),
        P(None, ("lat", "lon")),
        P(None, ("lat", "lon"), None, None),
        P(None, ("lat", "lon")),
        P("lat", "lon"),
        P("lat", "lon"),
        P("lat", "lon"),
        P("lat", "lon"),
        P(None, "lat", "lon"),
    )
    out_specs = (P(None, "lat", "lon"), P(None, ("lat", "lon")))
    return jax.shard_map(
        on_device, mesh=mesh, in_specs=in_specs, out_specs=out_specs, check_vma=False
    )
```
